32 devices in a mesh: section: 2 (over y), sample: 4 (over z), seq: 4 (over x, core).
Axes of the slice: x: 2, y: 2, z: 4, core: 2. Of those that a mesh axis runs over, the one named last changes fastest.
Arguments:
- first_rows: bfloat16 [2, 4, 512, 2048], P('section', 'sample', 'seq'), may hold values from -10 to 10
- second_rows: bfloat16 [2, 4, 512, 2048], P('section', 'sample', 'seq'), may hold values from -6 to 6
- alignment: int32 [4, 4, 2], P('sample', 'seq'), may hold values from 0 to 3, as said below
- diffusion_mask: int32 [4, 512], P('sample', 'seq'), may hold values 0 or 1
- source_length: int32 [4], P('sample'), may hold values from 256 to 512, as said below
- target_length: int32 [4], P('sample'), may hold values from 256 to 512
Outputs:
- grad_first: bfloat16 [2, 4, 512, 2048], P('section', 'sample', 'seq')
- grad_second: bfloat16 [2, 4, 512, 2048], P('section', 'sample', 'seq')
The draws below stay inside these ranges and needn't reach their ends.
Inputs may be any that keep to these rules, and one draw needn't show every extreme that they name: `alignment`: each list names 2 different blocks from t - 1 to t + 1 for target block t; where block t holds a target position below the target length, every listed block starts below the source length. `source_length`: at least the sample's target length.
All inputs are finite; a program needn't handle non-finite values. No bound on the sum of `diffusion_mask` on one device may be relied on, other than what follows from the above.
Results may differ from the reference program's by a relative error of at most 0.013.
Values may be sent and summed in bfloat16 or wider, within the bound.
No kernel may reach another device: no remote copies, remote signals or barrier semaphores. Data moves between devices by JAX's collectives and lax.ppermute only.
A program may use at most 64 MiB of HBM per device.

```python
import jax
import jax.numpy as jnp
from jax import lax

HEADS = 32
HDIM = 64
INNER = 2048
BLK = 128
NLIST = 2
WIN = 1
SAMPLES = 4
SEQLEN = 512
NBLK = 4


def plan_integers(key):
    base = jax.random.fold_in(key, 4099)
    key_target, key_order, key_spread, key_lists = jax.random.split(base, 4)
    sample_ids = jnp.arange(SAMPLES, dtype=jnp.int32)
    target_len = jax.random.randint(key_target, (SAMPLES,), SEQLEN // 2, SEQLEN + 1)
    order = jax.random.permutation(key_order, SAMPLES)
    longest = order[0]
    shortest = order[1]
    target_len = jnp.where(sample_ids == longest, SEQLEN, target_len)
    target_len = jnp.where(sample_ids == shortest, SEQLEN // 2, target_len)
    spread = jax.random.randint(key_spread, (SAMPLES,), 0, 1 << 20)
    source_len = target_len + spread % (SEQLEN - target_len + 1)
    source_len = jnp.where(sample_ids == shortest, target_len, source_len)
    valid_blocks = (source_len + BLK - 1) // BLK
    blocks = jnp.arange(NBLK, dtype=jnp.int32)
    width = 2 * WIN + 1
    offsets = jnp.arange(width, dtype=jnp.int32) - WIN
    candidate = blocks[:, None] + offsets[None, :]
    in_range = (candidate >= 0) & (candidate < NBLK)
    holds_rows = blocks[None, :] * BLK < target_len[:, None]
    allowed = in_range[None, :, :] & (~holds_rows[:, :, None] | (candidate[None, :, :] < valid_blocks[:, None, None]))
    noise = jax.random.randint(key_lists, (SAMPLES, NBLK, width), 0, 1 << 20) * width + offsets[None, None, :] + WIN
    ranking = jnp.where(allowed, noise, -1)
    unused, picks = lax.top_k(ranking, NLIST)
    lists = blocks[None, :, None] + picks.astype(jnp.int32) - WIN
    return (lists.astype(jnp.int32), source_len.astype(jnp.int32), target_len.astype(jnp.int32))


def draw_alignment(key, part):
    return plan_integers(key)[0]


def draw_source_length(key, part):
    return plan_integers(key)[1]


def draw_target_length(key, part):
    return plan_integers(key)[2]


def draw_first_rows(key, part):
    key_base = jax.random.fold_in(jax.random.fold_in(key, 17), 0)
    shape = (2, SAMPLES, SEQLEN, INNER)
    base = jnp.clip(jax.random.normal(key_base, shape, jnp.float32), -4.0, 4.0)
    return base.astype(jnp.bfloat16)


def with_ends(values, stream_key, least, high):
    place = [jax.random.randint(jax.random.fold_in(stream_key, axis), (), 0, length) for axis, length in enumerate(values.shape)]
    main_axis = values.shape.index(max(values.shape))
    next_to = place[:main_axis] + [(place[main_axis] + 1) % values.shape[main_axis]] + place[main_axis + 1:]
    return values.at[tuple(place)].set(least).at[tuple(next_to)].set(high)


def steps_of(own_key, shape, cuts, smallest, high):
    def one(position, blocks):
        draws = jax.random.uniform(jax.random.fold_in(jax.random.fold_in(own_key, 6), position), (blocks,), jnp.float32, smallest / len(cuts), high / len(cuts))
        return jnp.repeat(jnp.exp(draws), shape[position] // blocks).reshape((-1,) + (1,) * (len(shape) - position - 1))

    gain = one(*cuts[0])
    for cut in cuts[1:]:
        gain = gain * one(*cut)
    return gain


def gaussian(own_key, extent, scale, bound, pieces=(), kind=jnp.bfloat16):
    values = jax.random.normal(own_key, extent, jnp.float32) * scale
    if len(pieces) > 0:
        values = steps_of(own_key, extent, pieces, -0.22, 0.18) * values
    return jnp.clip(values, min=-bound, max=bound).astype(kind)


def setup_inputs(seed: int = 0) -> dict:
    key_list = jax.random.split(jax.random.key(seed), 7)
    first_rows = draw_first_rows(jax.random.fold_in(key_list[6], 71), 0)
    second_rows = gaussian(key_list[1], (2, SAMPLES, SEQLEN, INNER), 1.0, 6.0, ((0, 2), (1, 4), (2, 4)))
    alignment = draw_alignment(jax.random.fold_in(key_list[6], 71), 0)
    diffusion_mask = with_ends((jax.random.randint(key_list[3], (SAMPLES, SEQLEN), 0, 2) < 1).astype(jnp.int32), jax.random.fold_in(key_list[3], 1), 0, 1)
    source_length = draw_source_length(jax.random.fold_in(key_list[6], 71), 0)
    target_length = draw_target_length(jax.random.fold_in(key_list[6], 71), 0)
    return dict(first_rows=first_rows, second_rows=second_rows, alignment=alignment, diffusion_mask=diffusion_mask, source_length=source_length, target_length=target_length)


NEG_FILL = -1e30


def attend_block(query_blk, cot_blk, key_rows, value_rows, key_valid, query_valid, cot_keep):
    scale = HDIM ** -0.5
    queries = query_blk.reshape(BLK, HEADS, HDIM).astype(jnp.float32)
    keys = key_rows.reshape(NLIST * BLK, HEADS, HDIM).astype(jnp.float32)
    values = value_rows.reshape(NLIST * BLK, HEADS, HDIM).astype(jnp.float32)
    scores = jnp.einsum("qhd,khd->hqk", queries, keys) * scale
    scores = jnp.where(key_valid[None, None, :], scores, NEG_FILL)
    peak = jnp.max(scores, axis=-1, keepdims=True)
    expo = jnp.exp(scores - peak)
    probs = expo / jnp.sum(expo, axis=-1, keepdims=True)
    probs_low = lax.optimization_barrier(probs.astype(jnp.bfloat16)).astype(jnp.float32)
    attended = jnp.einsum("hqk,khd->qhd", probs_low, values)
    attended = jnp.where(query_valid[:, None, None], attended, jnp.float32(0.0))
    out_low = attended.astype(jnp.bfloat16)
    out_wide = lax.optimization_barrier(out_low).astype(jnp.float32)
    cot = jnp.where(cot_keep[:, None], cot_blk, jnp.zeros_like(cot_blk))
    cot_wide = cot.reshape(BLK, HEADS, HDIM).astype(jnp.float32)
    delta = jnp.sum(cot_wide * out_wide, axis=-1).T[:, :, None]
    dprob = jnp.einsum("qhd,khd->hqk", cot_wide, values)
    dscore = probs * (dprob - delta)
    dscore_low = lax.optimization_barrier(dscore.astype(jnp.bfloat16)).astype(jnp.float32)
    dvalue = jnp.einsum("hqk,qhd->khd", probs_low, cot_wide)
    dquery = scale * jnp.einsum("hqk,khd->qhd", dscore_low, keys)
    dkey = scale * jnp.einsum("hqk,qhd->khd", dscore_low, queries)
    return (out_low.reshape(BLK, INNER), dquery.astype(jnp.bfloat16).reshape(BLK, INNER),
            dkey.reshape(NLIST, BLK, INNER), dvalue.reshape(NLIST, BLK, INNER))


def one_sample(first_pair, second_pair, lists, mask_row, source_len, target_len):
    key_blocks = first_pair[0].reshape(NBLK, BLK, INNER)
    query_blocks = first_pair[1].reshape(NBLK, BLK, INNER)
    value_blocks = second_pair[0].reshape(NBLK, BLK, INNER)
    cot_blocks = second_pair[1].reshape(NBLK, BLK, INNER)
    mask_blocks = mask_row.reshape(NBLK, BLK)
    inside = jnp.arange(BLK, dtype=jnp.int32)

    def step(carry, index):
        key_acc, value_acc = carry
        chosen = lists[index]
        key_rows = key_blocks[chosen].reshape(NLIST * BLK, INNER)
        value_rows = value_blocks[chosen].reshape(NLIST * BLK, INNER)
        key_pos = (chosen[:, None] * BLK + inside[None, :]).reshape(NLIST * BLK)
        key_valid = key_pos < source_len
        row_pos = index * BLK + inside
        query_valid = row_pos < target_len
        cot_keep = query_valid & (mask_blocks[index] == 1)
        out_low, dquery, dkey, dvalue = attend_block(query_blocks[index], cot_blocks[index], key_rows,
                                                     value_rows, key_valid, query_valid, cot_keep)
        key_acc = key_acc.at[chosen].add(dkey)
        value_acc = value_acc.at[chosen].add(dvalue)
        return (key_acc, value_acc), (out_low, dquery)

    start = (jnp.zeros((NBLK, BLK, INNER), jnp.float32), jnp.zeros((NBLK, BLK, INNER), jnp.float32))
    (key_acc, value_acc), (outs, dqueries) = lax.scan(step, start, jnp.arange(NBLK, dtype=jnp.int32))
    return (key_acc.reshape(SEQLEN, INNER).astype(jnp.bfloat16), dqueries.reshape(SEQLEN, INNER),
            value_acc.reshape(SEQLEN, INNER).astype(jnp.bfloat16), outs.reshape(SEQLEN, INNER))


def reference(first_rows, second_rows, alignment, diffusion_mask, source_length, target_length):
    firsts = jnp.moveaxis(first_rows, 1, 0)
    seconds = jnp.moveaxis(second_rows, 1, 0)

    def per_sample(packed):
        return one_sample(packed[0], packed[1], packed[2], packed[3], packed[4], packed[5])

    key_grad, query_grad, value_grad, outs = lax.map(
        per_sample, (firsts, seconds, alignment, diffusion_mask, source_length, target_length))
    return jnp.stack([key_grad, query_grad], 0), jnp.stack([value_grad, outs], 0)
```

```python
import functools

import jax
import jax.numpy as jnp
from jax import lax
from jax.experimental import pallas as pl
from jax.experimental.pallas import tpu as pltpu
from jax.sharding import PartitionSpec as P

HDIM = 64
BLK = 128
NLIST = 2
LANES = 128
SCALE = HDIM ** (-0.5)
FLOOR = -1e30


def contract(left, right, left_dim, right_dim):
    return lax.dot_general(
        left, right, (((left_dim,), (right_dim,)), ((), ())), preferred_element_type=jnp.float32
    )


def attend_kernel(seq_count, lists, lengths, rows, out, key_grad, value_grad):
    per_device = rows.shape[2] // BLK
    block_count = seq_count * per_device
    width = rows.shape[3]
    tile = min(width, LANES)
    heads = tile // HDIM
    source_len = lengths[0]
    target_len = lengths[1]
    key_grad[...] = jnp.zeros_like(key_grad)
    value_grad[...] = jnp.zeros_like(value_grad)
    key_inside = lax.broadcasted_iota(jnp.int32, (BLK, 1), 0)
    lane_head = lax.broadcasted_iota(jnp.int32, (BLK, tile), 1) // HDIM

    def place(block):
        if per_device == 1:
            return block, pl.ds(0, BLK)
        return block // per_device, pl.ds((block % per_device) * BLK, BLK)

    def step(block, carry):
        chosen = [lists[block, slot] for slot in range(NLIST)]
        places = [place(index) for index in chosen]
        target, target_rows = place(block)
        key_valid = jnp.concatenate(
            [index * BLK + key_inside < source_len for index in chosen], axis=0
        )
        live = block * BLK + key_inside < target_len
        for first in range(0, width, tile):
            lanes = pl.ds(first, tile)
            keys = jnp.concatenate([rows[dev, 0, here, lanes] for dev, here in places], axis=0)
            values = jnp.concatenate([rows[dev, 1, here, lanes] for dev, here in places], axis=0)
            queries = rows[seq_count + target, 0, target_rows, lanes] * jnp.bfloat16(SCALE)
            cots = rows[seq_count + target, 1, target_rows, lanes]
            none = jnp.zeros_like(queries)
            queries = jnp.concatenate(
                [jnp.where(lane_head == head, queries, none) for head in range(heads)], axis=0
            )
            cots = jnp.concatenate(
                [jnp.where(lane_head == head, cots, none) for head in range(heads)], axis=0
            )
            scores = jnp.where(key_valid, contract(keys, queries, 1, 1), FLOOR)
            expo = jnp.exp(scores - jnp.max(scores, axis=0, keepdims=True))
            probs = expo * (1.0 / jnp.sum(expo, axis=0, keepdims=True))
            dprob = contract(values, cots, 1, 1)
            delta = jnp.sum(probs * dprob, axis=0, keepdims=True)
            probs_low = probs.astype(jnp.bfloat16)
            dscore_low = (probs * (dprob - delta)).astype(jnp.bfloat16)
            dvalue = contract(probs_low, cots, 1, 0)
            dkey = contract(dscore_low, queries, 1, 0)
            attended = contract(probs_low, values, 0, 0)
            dquery = contract(dscore_low, keys, 0, 0)
            for head in range(1, heads):
                mine = lane_head == head
                attended = jnp.where(mine, attended[head * BLK : (head + 1) * BLK], attended[:BLK])
                dquery = jnp.where(mine, dquery[head * BLK : (head + 1) * BLK], dquery[:BLK])
            attended = jnp.where(live, attended, 0.0)
            out[seq_count + target, 0, target_rows, lanes] = (dquery * SCALE).astype(jnp.bfloat16)
            out[seq_count + target, 1, target_rows, lanes] = attended.astype(jnp.bfloat16)
            for slot, (dev, here) in enumerate(places):
                part = slice(slot * BLK, (slot + 1) * BLK)
                key_grad[dev, here, lanes] += dkey[part]
                value_grad[dev, here, lanes] += dvalue[part]
        return carry

    lax.fori_loop(0, block_count, step, 0)
    out[:seq_count, 0] = key_grad[...].astype(jnp.bfloat16)
    out[:seq_count, 1] = value_grad[...].astype(jnp.bfloat16)


def attend(seq_count, lists, lengths, rows):
    grads = (seq_count, rows.shape[2], rows.shape[3])
    block_count = lists.shape[0]
    pairs = block_count * NLIST * BLK * BLK * rows.shape[3]
    vmem = pl.BlockSpec(memory_space=pltpu.VMEM)
    smem = pl.BlockSpec(memory_space=pltpu.SMEM)
    return pl.pallas_call(
        functools.partial(attend_kernel, seq_count),
        out_shape=jax.ShapeDtypeStruct(rows.shape, rows.dtype),
        in_specs=[smem, smem, vmem],
        out_specs=vmem,
        scratch_shapes=[pltpu.VMEM(grads, jnp.float32), pltpu.VMEM(grads, jnp.float32)],
        compiler_params=pltpu.CompilerParams(vmem_limit_bytes=32 * 1024 * 1024),
        cost_estimate=pl.CostEstimate(
            flops=10 * pairs, bytes_accessed=4 * rows.size, transcendentals=pairs // HDIM
        ),
        name="attend",
    )(lists, lengths, rows)


def on_device(first_rows, second_rows, alignment, diffusion_mask, source_length, target_length):
    axes = ("section", "seq")
    seq_count = lax.axis_size("seq")
    parts = lax.axis_size("section") * seq_count
    rows_here = first_rows.shape[2]
    width = first_rows.shape[3]
    on_encoder = lax.axis_index("section") == 0
    row_pos = lax.axis_index("seq") * rows_here + jnp.arange(rows_here, dtype=jnp.int32)
    keep = on_encoder | ((row_pos < target_length[0]) & (diffusion_mask[0] == 1))
    second = jnp.where(keep[:, None], second_rows[0, 0], jnp.zeros_like(second_rows[0, 0]))
    held = jnp.stack([first_rows[0, 0], second])
    held = held.reshape(2, rows_here, parts, width // parts).transpose(2, 0, 1, 3)
    lists = lax.all_gather(alignment[0], "seq", axis=0, tiled=True)
    lengths = jnp.concatenate([source_length, target_length])
    rows = lax.all_to_all(held, axes, 0, 0, tiled=True)
    grads = attend(seq_count, lists, lengths, rows)
    grads = lax.all_to_all(grads, axes, 0, 0, tiled=True)
    grads = grads.transpose(1, 2, 0, 3).reshape(2, rows_here, width)
    return (grads[0][None, None], grads[1][None, None])


def solution(mesh):
    placed = (
        P("section", "sample", "seq", None),
        P("section", "sample", "seq", None),
        P("sample", "seq", None),
        P("sample", "seq"),
        P("sample"),
        P("sample"),
    )
    return jax.shard_map(
        on_device,
        mesh=mesh,
        in_specs=placed,
        out_specs=(P("section", "sample", "seq", None), P("section", "sample", "seq", None)),
        check_vma=False,
    )
```

```python
import functools

import jax
import jax.numpy as jnp
from jax import lax
from jax.experimental import pallas as pl
from jax.experimental.pallas import tpu as pltpu
from jax.sharding import PartitionSpec as P

HDIM = 64
BLK = 128
NLIST = 2
WIN = 1
SPAN = 2 * WIN + 1
LANES = 128
TAIL = 16
SCALE = HDIM ** (-0.5)
FLOOR = -1e30
VMEM_LIMIT = 32 * 1024 * 1024
AXES = ("section", "seq")


def contract(left, right, left_dim, right_dim):
    return lax.dot_general(
        left, right, (((left_dim,), (right_dim,)), ((), ())), preferred_element_type=jnp.float32
    )


def attend_sample(seq_count, listed, source_len, target_len, rows, out, key_grad, value_grad):
    per_device = rows.shape[2] // BLK
    block_count = seq_count * per_device
    width = rows.shape[3]
    tile = min(width, LANES)
    heads = tile // HDIM
    key_grad[...] = jnp.zeros_like(key_grad)
    value_grad[...] = jnp.zeros_like(value_grad)
    inside = lax.broadcasted_iota(jnp.int32, (BLK, 1), 0)
    lane_head = lax.broadcasted_iota(jnp.int32, (BLK, tile), 1) // HDIM

    def place(block):
        if per_device == 1:
            return block, pl.ds(0, BLK)
        return block // per_device, pl.ds((block % per_device) * BLK, BLK)

    def step(block, carry):
        chosen = [listed(block, slot) for slot in range(NLIST)]
        places = [place(index) for index in chosen]
        target, target_rows = place(block)
        key_valid = jnp.concatenate(
            [index * BLK + inside < source_len for index in chosen], axis=0
        )
        live = block * BLK + inside < target_len
        for first in range(0, width, tile):
            lanes = pl.ds(first, tile)
            keys = jnp.concatenate([rows[dev, 0, here, lanes] for dev, here in places], axis=0)
            values = jnp.concatenate([rows[dev, 1, here, lanes] for dev, here in places], axis=0)
            queries = rows[seq_count + target, 0, target_rows, lanes] * jnp.bfloat16(SCALE)
            cots = rows[seq_count + target, 1, target_rows, lanes]
            none = jnp.zeros_like(queries)
            queries = jnp.concatenate(
                [jnp.where(lane_head == head, queries, none) for head in range(heads)], axis=0
            )
            cots = jnp.concatenate(
                [jnp.where(lane_head == head, cots, none) for head in range(heads)], axis=0
            )
            scores = jnp.where(key_valid, contract(keys, queries, 1, 1), FLOOR)
            expo = jnp.exp(scores - jnp.max(scores, axis=0, keepdims=True))
            probs = expo * (1.0 / jnp.sum(expo, axis=0, keepdims=True))
            dprob = contract(values, cots, 1, 1)
            delta = jnp.sum(probs * dprob, axis=0, keepdims=True)
            probs_low = probs.astype(jnp.bfloat16)
            dscore_low = (probs * (dprob - delta)).astype(jnp.bfloat16)
            dvalue = contract(probs_low, cots, 1, 0)
            dkey = contract(dscore_low, queries, 1, 0)
            attended = contract(probs_low, values, 0, 0)
            dquery = contract(dscore_low, keys, 0, 0)
            for head in range(1, heads):
                mine = lane_head == head
                attended = jnp.where(mine, attended[head * BLK : (head + 1) * BLK], attended[:BLK])
                dquery = jnp.where(mine, dquery[head * BLK : (head + 1) * BLK], dquery[:BLK])
            attended = jnp.where(live, attended, 0.0)
            out[seq_count + target, 0, target_rows, lanes] = (dquery * SCALE).astype(jnp.bfloat16)
            out[seq_count + target, 1, target_rows, lanes] = attended.astype(jnp.bfloat16)
            for slot, (dev, here) in enumerate(places):
                part = slice(slot * BLK, (slot + 1) * BLK)
                key_grad[dev, here, lanes] += dkey[part]
                value_grad[dev, here, lanes] += dvalue[part]
        return carry

    lax.fori_loop(0, block_count, step, 0)
    out[:seq_count, 0] = key_grad[...].astype(jnp.bfloat16)
    out[:seq_count, 1] = value_grad[...].astype(jnp.bfloat16)


def attend_cost(block_count, width):
    pairs = block_count * NLIST * BLK * BLK * width
    return pl.CostEstimate(
        flops=10 * pairs,
        bytes_accessed=16 * block_count * BLK * width,
        transcendentals=pairs // HDIM,
    )


def specs(count, space):
    return [pl.BlockSpec(memory_space=space)] * count


def gathered_kernel(seq_count, lists, lengths, rows, out, key_grad, value_grad):
    def listed(block, slot):
        return lists[block, slot]

    attend_sample(
        seq_count, listed, lengths[0], lengths[1], rows, out, key_grad, value_grad
    )


def by_all_to_all(first_rows, second_rows, alignment, diffusion_mask, lengths):
    seq_count = lax.axis_size("seq")
    parts = lax.axis_size("section") * seq_count
    rows_here = first_rows.shape[2]
    width = first_rows.shape[3]
    on_encoder = lax.axis_index("section") == 0
    row_pos = lax.axis_index("seq") * rows_here + jnp.arange(rows_here, dtype=jnp.int32)
    keep = on_encoder | ((row_pos < lengths[1]) & (diffusion_mask[0] == 1))
    second = jnp.where(keep[:, None], second_rows[0, 0], jnp.zeros_like(second_rows[0, 0]))
    held = jnp.stack([first_rows[0, 0], second])
    held = held.reshape(2, rows_here, parts, width // parts).transpose(2, 0, 1, 3)
    lists = lax.all_gather(alignment[0], "seq", axis=0, tiled=True)
    rows = lax.all_to_all(held, AXES, 0, 0, tiled=True)
    grads = pltpu.VMEM((seq_count, rows_here, width // parts), jnp.float32)
    grads = pl.pallas_call(
        functools.partial(gathered_kernel, seq_count),
        out_shape=jax.ShapeDtypeStruct(rows.shape, rows.dtype),
        in_specs=specs(2, pltpu.SMEM) + specs(1, pltpu.VMEM),
        out_specs=pl.BlockSpec(memory_space=pltpu.VMEM),
        scratch_shapes=[grads, grads],
        compiler_params=pltpu.CompilerParams(vmem_limit_bytes=VMEM_LIMIT),
        cost_estimate=attend_cost(lists.shape[0], width // parts),
        name="attend_gathered",
    )(lists, lengths, rows)
    grads = lax.all_to_all(grads, AXES, 0, 0, tiled=True)
    grads = grads.transpose(1, 2, 0, 3).reshape(2, rows_here, width)
    return (grads[0][None, None], grads[1][None, None])


def pack_kernel(seq_count, me, lengths, lists, mask, first, second, *outs):
    here = me[0] % seq_count
    share = outs[0].shape[1]
    positions = here * BLK + lax.broadcasted_iota(jnp.int32, (1, BLK), 1)
    keep = ((positions < lengths[1]) & (mask[...] == 1)) | (me[0] < seq_count)
    keep = jnp.broadcast_to(jnp.where(keep, 1.0, 0.0), (BLK, BLK)).T.astype(jnp.bfloat16)
    keep = jnp.concatenate([keep] * (share // LANES), axis=1)
    base = here - WIN
    code = (lists[0, 0, 0] - base) * SPAN + lists[0, 0, 1] - base
    for step, out in enumerate(outs):
        lanes = pl.ds(pl.multiple_of((me[0] ^ step) * share, LANES), share)
        out[:BLK] = first[0, 0, :, lanes]
        out[BLK : 2 * BLK] = second[0, 0, :, lanes] * keep
        if step < seq_count:
            out[2 * BLK :] = jnp.full((TAIL, share), code, jnp.int32).astype(
                jnp.float32
            ).astype(jnp.bfloat16)


def attend_kernel(seq_count, me, lengths, *refs):
    parts = 2 * seq_count
    shares, outs = refs[:parts], refs[parts : 2 * parts]
    rows, result, key_grad, value_grad, lists = refs[2 * parts :]
    here = me[0] % seq_count
    for step, share in enumerate(shares):
        source = me[0] ^ step
        rows[source, 0] = share[:BLK]
        rows[source, 1] = share[BLK : 2 * BLK]
        if step < seq_count:
            tail = share[2 * BLK :, :LANES].astype(jnp.float32)
            lists[here ^ step] = jnp.max(tail).astype(jnp.int32)

    def listed(block, slot):
        code = lists[block]
        return block - WIN + (code // SPAN if slot == 0 else code % SPAN)

    attend_sample(
        seq_count, listed, lengths[0], lengths[1], rows, result, key_grad, value_grad
    )
    for step, out in enumerate(outs):
        out[:BLK] = result[me[0] ^ step, 0]
        out[BLK:] = result[me[0] ^ step, 1]


def unpack_kernel(me, *refs):
    shares, (first, second) = refs[:-2], refs[-2:]
    width = shares[0].shape[1]
    for step, share in enumerate(shares):
        lanes = pl.ds(pl.multiple_of((me[0] ^ step) * width, LANES), width)
        first[0, 0, :, lanes] = share[:BLK]
        second[0, 0, :, lanes] = share[BLK:]


def swapped(shares, order):
    moved = list(shares)
    for step in order:
        pairs = [(dev, dev ^ step) for dev in range(len(shares))]
        moved[step] = lax.ppermute(shares[step], AXES, pairs)
    return moved


def by_pairs(first_rows, second_rows, alignment, diffusion_mask, lengths):
    seq_count = lax.axis_size("seq")
    parts = 2 * seq_count
    width = first_rows.shape[3]
    share = width // parts
    kind = first_rows.dtype
    me = (lax.axis_index("section") * seq_count + lax.axis_index("seq")).reshape(1)
    params = pltpu.CompilerParams(vmem_limit_bytes=VMEM_LIMIT)
    order = [*range(seq_count, parts), *range(seq_count - 1, 0, -1)]
    tails = [TAIL if step < seq_count else 0 for step in range(parts)]
    shares = pl.pallas_call(
        functools.partial(pack_kernel, seq_count),
        out_shape=[jax.ShapeDtypeStruct((2 * BLK + tail, share), kind) for tail in tails],
        in_specs=specs(3, pltpu.SMEM) + specs(3, pltpu.VMEM),
        out_specs=specs(parts, pltpu.VMEM),
        compiler_params=params,
        name="pack",
    )(me, lengths, alignment, diffusion_mask, first_rows, second_rows)
    shares = swapped(shares, order)
    rows = pltpu.VMEM((parts, 2, BLK, share), kind)
    grads = pltpu.VMEM((seq_count, BLK, share), jnp.float32)
    shares = pl.pallas_call(
        functools.partial(attend_kernel, seq_count),
        out_shape=[jax.ShapeDtypeStruct((2 * BLK, share), kind)] * parts,
        in_specs=specs(2, pltpu.SMEM) + specs(parts, pltpu.VMEM),
        out_specs=specs(parts, pltpu.VMEM),
        scratch_shapes=[rows, rows, grads, grads, pltpu.SMEM((seq_count,), jnp.int32)],
        compiler_params=params,
        cost_estimate=attend_cost(seq_count, share),
        name="attend",
    )(me, lengths, *shares)
    shares = swapped(shares, order)
    out_shape = jax.ShapeDtypeStruct((1, 1, BLK, width), kind)
    return pl.pallas_call(
        unpack_kernel,
        out_shape=[out_shape, out_shape],
        in_specs=specs(1, pltpu.SMEM) + specs(parts, pltpu.VMEM),
        out_specs=specs(2, pltpu.VMEM),
        compiler_params=params,
        name="unpack",
    )(me, *shares)


def on_device(first_rows, second_rows, alignment, diffusion_mask, source_length, target_length):
    seq_count = lax.axis_size("seq")
    parts = lax.axis_size("section") * seq_count
    lengths = jnp.concatenate([source_length, target_length])
    paired = (
        parts == 2 * seq_count
        and seq_count & (seq_count - 1) == 0
        and first_rows.shape[2] == BLK
        and first_rows.shape[3] % (parts * LANES) == 0
    )
    work = by_pairs if paired else by_all_to_all
    return tuple(work(first_rows, second_rows, alignment, diffusion_mask, lengths))


def solution(mesh):
    placed = (
        P("section", "sample", "seq", None),
        P("section", "sample", "seq", None),
        P("sample", "seq", None),
        P("sample", "seq"),
        P("sample"),
        P("sample"),
    )
    return jax.shard_map(
        on_device,
        mesh=mesh,
        in_specs=placed,
        out_specs=(P("section", "sample", "seq", None), P("section", "sample", "seq", None)),
        check_vma=False,
    )
```

```python
import functools

import jax
import jax.numpy as jnp
from jax import lax
from jax.experimental import pallas as pl
from jax.experimental.pallas import tpu as pltpu
from jax.sharding import PartitionSpec as P

HDIM = 64
BLK = 128
NLIST = 2
WIN = 1
SPAN = 2 * WIN + 1
LANES = 128
TAIL = 16
SCALE = HDIM ** (-0.5)
FLOOR = -1e30
VMEM_LIMIT = 32 * 1024 * 1024
AXES = ("section", "seq")


def contract(left, right, left_dim, right_dim):
    return lax.dot_general(
        left, right, (((left_dim,), (right_dim,)), ((), ())), preferred_element_type=jnp.float32
    )


def attend_sample(seq_count, listed, source_len, target_len, rows, out, key_grad, value_grad):
    per_device = rows.shape[2] // BLK
    block_count = seq_count * per_device
    width = rows.shape[3]
    tile = min(width, LANES)
    heads = tile // HDIM
    key_grad[...] = jnp.zeros_like(key_grad)
    value_grad[...] = jnp.zeros_like(value_grad)
    inside = lax.broadcasted_iota(jnp.int32, (BLK, 1), 0)
    lane_head = lax.broadcasted_iota(jnp.int32, (BLK, tile), 1) // HDIM

    def place(block):
        if per_device == 1:
            return block, pl.ds(0, BLK)
        return block // per_device, pl.ds((block % per_device) * BLK, BLK)

    def step(block, carry):
        chosen = [listed(block, slot) for slot in range(NLIST)]
        places = [place(index) for index in chosen]
        target, target_rows = place(block)
        key_valid = jnp.concatenate(
            [index * BLK + inside < source_len for index in chosen], axis=0
        )
        live = block * BLK + inside < target_len
        for first in range(0, width, tile):
            lanes = pl.ds(first, tile)
            keys = jnp.concatenate([rows[dev, 0, here, lanes] for dev, here in places], axis=0)
            values = jnp.concatenate([rows[dev, 1, here, lanes] for dev, here in places], axis=0)
            queries = rows[seq_count + target, 0, target_rows, lanes] * jnp.bfloat16(SCALE)
            cots = rows[seq_count + target, 1, target_rows, lanes]
            none = jnp.zeros_like(queries)
            queries = jnp.concatenate(
                [jnp.where(lane_head == head, queries, none) for head in range(heads)], axis=0
            )
            cots = jnp.concatenate(
                [jnp.where(lane_head == head, cots, none) for head in range(heads)], axis=0
            )
            scores = jnp.where(key_valid, contract(keys, queries, 1, 1), FLOOR)
            expo = jnp.exp(scores - jnp.max(scores, axis=0, keepdims=True))
            probs = expo * (1.0 / jnp.sum(expo, axis=0, keepdims=True))
            dprob = contract(values, cots, 1, 1)
            delta = jnp.sum(probs * dprob, axis=0, keepdims=True)
            probs_low = probs.astype(jnp.bfloat16)
            dscore_low = (probs * (dprob - delta)).astype(jnp.bfloat16)
            dvalue = contract(probs_low, cots, 1, 0)
            dkey = contract(dscore_low, queries, 1, 0)
            attended = contract(probs_low, values, 0, 0)
            dquery = contract(dscore_low, keys, 0, 0)
            for head in range(1, heads):
                mine = lane_head == head
                attended = jnp.where(mine, attended[head * BLK : (head + 1) * BLK], attended[:BLK])
                dquery = jnp.where(mine, dquery[head * BLK : (head + 1) * BLK], dquery[:BLK])
            attended = jnp.where(live, attended, 0.0)
            out[seq_count + target, 0, target_rows, lanes] = (dquery * SCALE).astype(jnp.bfloat16)
            out[seq_count + target, 1, target_rows, lanes] = attended.astype(jnp.bfloat16)
            for slot, (dev, here) in enumerate(places):
                part = slice(slot * BLK, (slot + 1) * BLK)
                key_grad[dev, here, lanes] += dkey[part]
                value_grad[dev, here, lanes] += dvalue[part]
        return carry

    lax.fori_loop(0, block_count, step, 0)
    out[:seq_count, 0] = key_grad[...].astype(jnp.bfloat16)
    out[:seq_count, 1] = value_grad[...].astype(jnp.bfloat16)


def attend_cost(block_count, width):
    pairs = block_count * NLIST * BLK * BLK * width
    return pl.CostEstimate(
        flops=10 * pairs,
        bytes_accessed=16 * block_count * BLK * width,
        transcendentals=pairs // HDIM,
    )


def specs(count, space):
    return [pl.BlockSpec(memory_space=space)] * count


def gathered_kernel(seq_count, lists, source_len, target_len, rows, out, key_grad, value_grad):
    def listed(block, slot):
        return lists[block, slot]

    attend_sample(
        seq_count, listed, source_len[0], target_len[0], rows, out, key_grad, value_grad
    )


def by_all_to_all(first_rows, second_rows, alignment, diffusion_mask, source_length, target_length):
    seq_count = lax.axis_size("seq")
    parts = lax.axis_size("section") * seq_count
    rows_here = first_rows.shape[2]
    width = first_rows.shape[3]
    on_encoder = lax.axis_index("section") == 0
    row_pos = lax.axis_index("seq") * rows_here + jnp.arange(rows_here, dtype=jnp.int32)
    keep = on_encoder | ((row_pos < target_length[0]) & (diffusion_mask[0] == 1))
    second = jnp.where(keep[:, None], second_rows[0, 0], jnp.zeros_like(second_rows[0, 0]))
    held = jnp.stack([first_rows[0, 0], second])
    held = held.reshape(2, rows_here, parts, width // parts).transpose(2, 0, 1, 3)
    lists = lax.all_gather(alignment[0], "seq", axis=0, tiled=True)
    rows = lax.all_to_all(held, AXES, 0, 0, tiled=True)
    grads = pltpu.VMEM((seq_count, rows_here, width // parts), jnp.float32)
    grads = pl.pallas_call(
        functools.partial(gathered_kernel, seq_count),
        out_shape=jax.ShapeDtypeStruct(rows.shape, rows.dtype),
        in_specs=specs(3, pltpu.SMEM) + specs(1, pltpu.VMEM),
        out_specs=pl.BlockSpec(memory_space=pltpu.VMEM),
        scratch_shapes=[grads, grads],
        compiler_params=pltpu.CompilerParams(vmem_limit_bytes=VMEM_LIMIT),
        cost_estimate=attend_cost(lists.shape[0], width // parts),
        name="attend_gathered",
    )(lists, source_length, target_length, rows)
    grads = lax.all_to_all(grads, AXES, 0, 0, tiled=True)
    grads = grads.transpose(1, 2, 0, 3).reshape(2, rows_here, width)
    return (grads[0][None, None], grads[1][None, None])


def device_index(seq_count):
    return lax.axis_index("section") * seq_count + lax.axis_index("seq")


def pack_kernel(seq_count, order, target_len, lists, mask, first, second, *refs):
    outs, sem = refs[:-1], refs[-1]
    me = device_index(seq_count)
    here = me % seq_count
    share = outs[0].shape[1]
    copies = []
    for slot, (step, out) in enumerate(zip(order, outs)):
        lanes = pl.ds(pl.multiple_of((me ^ step) * share, LANES), share)
        pair = [
            pltpu.make_async_copy(
                source.at[0, 0, :, lanes], out.at[pl.ds(half * BLK, BLK)], sem.at[half, slot]
            )
            for half, source in enumerate((first, second))
        ]
        for copy in pair:
            copy.start()
        copies.append(pair)
    positions = here * BLK + lax.broadcasted_iota(jnp.int32, (1, BLK), 1)
    keep = ((positions < target_len[0]) & (mask[...] == 1)) | (me < seq_count)
    keep = jnp.broadcast_to(jnp.where(keep, 1.0, 0.0), (BLK, BLK)).T.astype(jnp.bfloat16)
    keep = jnp.concatenate([keep] * (share // LANES), axis=1)
    base = here - WIN
    code = (lists[0, 0, 0] - base) * SPAN + lists[0, 0, 1] - base
    tail = jnp.full((TAIL, share), code, jnp.int32).astype(jnp.float32).astype(jnp.bfloat16)
    for out, pair in zip(outs, copies):
        for copy in pair:
            copy.wait()
        out[BLK : 2 * BLK] = out[BLK : 2 * BLK] * keep
        out[2 * BLK :] = tail


def attend_kernel(seq_count, order, source_len, target_len, *refs):
    parts = 2 * seq_count
    shares, outs = refs[:parts], refs[parts : 2 * parts]
    rows, result, key_grad, value_grad, lists = refs[2 * parts :]
    me = device_index(seq_count)
    here = me % seq_count
    for step, share in zip(order, shares):
        source = me ^ step
        rows[source, 0] = share[:BLK]
        rows[source, 1] = share[BLK : 2 * BLK]
        if step < seq_count:
            tail = share[2 * BLK :, :LANES].astype(jnp.float32)
            lists[here ^ step] = jnp.max(tail).astype(jnp.int32)

    def listed(block, slot):
        code = lists[block]
        return block - WIN + (code // SPAN if slot == 0 else code % SPAN)

    attend_sample(
        seq_count, listed, source_len[0], target_len[0], rows, result, key_grad, value_grad
    )
    for step, out in zip(order, outs):
        out[:BLK] = result[me ^ step, 0]
        out[BLK:] = result[me ^ step, 1]


def unpack_kernel(seq_count, order, *refs):
    shares, (first, second, sem) = refs[:-3], refs[-3:]
    width = shares[0].shape[1]
    me = device_index(seq_count)
    copies = []
    for slot, (step, share) in enumerate(zip(order, shares)):
        lanes = pl.ds(pl.multiple_of((me ^ step) * width, LANES), width)
        for half, result in enumerate((first, second)):
            copy = pltpu.make_async_copy(
                share.at[pl.ds(half * BLK, BLK)], result.at[0, 0, :, lanes], sem.at[half, slot]
            )
            copy.start()
            copies.append(copy)
    for copy in copies:
        copy.wait()


def swapped(shares, order):
    parts = len(order)
    return [
        lax.ppermute(share, AXES, [(dev, dev ^ step) for dev in range(parts)]) if step else share
        for step, share in zip(order, shares)
    ]


def by_pairs(first_rows, second_rows, alignment, diffusion_mask, source_length, target_length):
    seq_count = lax.axis_size("seq")
    parts = 2 * seq_count
    width = first_rows.shape[3]
    share = width // parts
    kind = first_rows.dtype
    params = pltpu.CompilerParams(vmem_limit_bytes=VMEM_LIMIT)
    order = sorted(range(parts), key=lambda step: (-(step >= seq_count), -(step >> 1 & 1), step))
    order = [step for step in order if step > 1] + [1, 0]
    sems = pltpu.SemaphoreType.DMA((2, parts))
    shares = pl.pallas_call(
        functools.partial(pack_kernel, seq_count, order),
        out_shape=[jax.ShapeDtypeStruct((2 * BLK + TAIL, share), kind)] * parts,
        in_specs=specs(2, pltpu.SMEM) + specs(1, pltpu.VMEM) + specs(2, pltpu.HBM),
        out_specs=specs(parts, pltpu.VMEM),
        scratch_shapes=[sems],
        compiler_params=params,
        name="pack",
    )(target_length, alignment, diffusion_mask, first_rows, second_rows)
    shares = swapped(shares, order)
    rows = pltpu.VMEM((parts, 2, BLK, share), kind)
    grads = pltpu.VMEM((seq_count, BLK, share), jnp.float32)
    shares = pl.pallas_call(
        functools.partial(attend_kernel, seq_count, order),
        out_shape=[jax.ShapeDtypeStruct((2 * BLK, share), kind)] * parts,
        in_specs=specs(2, pltpu.SMEM) + specs(parts, pltpu.VMEM),
        out_specs=specs(parts, pltpu.VMEM),
        scratch_shapes=[rows, rows, grads, grads, pltpu.SMEM((seq_count,), jnp.int32)],
        compiler_params=params,
        cost_estimate=attend_cost(seq_count, share),
        name="attend",
    )(source_length, target_length, *shares)
    shares = swapped(shares, order)
    out_shape = jax.ShapeDtypeStruct((1, 1, BLK, width), kind)
    return pl.pallas_call(
        functools.partial(unpack_kernel, seq_count, order),
        out_shape=[out_shape, out_shape],
        in_specs=specs(parts, pltpu.VMEM),
        out_specs=specs(2, pltpu.HBM),
        scratch_shapes=[sems],
        compiler_params=params,
        name="unpack",
    )(*shares)


def on_device(first_rows, second_rows, alignment, diffusion_mask, source_length, target_length):
    seq_count = lax.axis_size("seq")
    parts = lax.axis_size("section") * seq_count
    paired = (
        parts == 2 * seq_count
        and seq_count & (seq_count - 1) == 0
        and first_rows.shape[2] == BLK
        and first_rows.shape[3] % (parts * LANES) == 0
    )
    work = by_pairs if paired else by_all_to_all
    return tuple(
        work(first_rows, second_rows, alignment, diffusion_mask, source_length, target_length)
    )


def solution(mesh):
    placed = (
        P("section", "sample", "seq", None),
        P("section", "sample", "seq", None),
        P("sample", "seq", None),
        P("sample", "seq"),
        P("sample"),
        P("sample"),
    )
    return jax.shard_map(
        on_device,
        mesh=mesh,
        in_specs=placed,
        out_specs=(P("section", "sample", "seq", None), P("section", "sample", "seq", None)),
        check_vma=False,
    )
```

```python
import functools

import jax
import jax.numpy as jnp
from jax import lax
from jax.experimental import pallas as pl
from jax.experimental.pallas import tpu as pltpu
from jax.sharding import PartitionSpec as P

HDIM = 64
BLK = 128
NLIST = 2
WIN = 1
SPAN = 2 * WIN + 1
LANES = 128
TAIL = 16
SCALE = HDIM ** (-0.5)
FLOOR = -1e30
VMEM_LIMIT = 32 * 1024 * 1024
AXES = ("section", "seq")


def contract(left, right, left_dim, right_dim):
    return lax.dot_general(
        left, right, (((left_dim,), (right_dim,)), ((), ())), preferred_element_type=jnp.float32
    )


def attend_sample(seq_count, listed, source_len, target_len, rows, out, key_grad, value_grad):
    per_device = rows.shape[2] // BLK
    block_count = seq_count * per_device
    width = rows.shape[3]
    tile = min(width, LANES)
    heads = tile // HDIM
    key_grad[...] = jnp.zeros_like(key_grad)
    value_grad[...] = jnp.zeros_like(value_grad)
    inside = lax.broadcasted_iota(jnp.int32, (BLK, 1), 0)
    lane_head = lax.broadcasted_iota(jnp.int32, (BLK, tile), 1) // HDIM

    def place(block):
        if per_device == 1:
            return block, pl.ds(0, BLK)
        return block // per_device, pl.ds((block % per_device) * BLK, BLK)

    def step(block, carry):
        chosen = [listed(block, slot) for slot in range(NLIST)]
        places = [place(index) for index in chosen]
        target, target_rows = place(block)
        key_valid = jnp.concatenate(
            [index * BLK + inside < source_len for index in chosen], axis=0
        )
        live = block * BLK + inside < target_len
        for first in range(0, width, tile):
            lanes = pl.ds(first, tile)
            keys = jnp.concatenate([rows[dev, 0, here, lanes] for dev, here in places], axis=0)
            values = jnp.concatenate([rows[dev, 1, here, lanes] for dev, here in places], axis=0)
            queries = rows[seq_count + target, 0, target_rows, lanes] * jnp.bfloat16(SCALE)
            cots = rows[seq_count + target, 1, target_rows, lanes]
            none = jnp.zeros_like(queries)
            queries = jnp.concatenate(
                [jnp.where(lane_head == head, queries, none) for head in range(heads)], axis=0
            )
            cots = jnp.concatenate(
                [jnp.where(lane_head == head, cots, none) for head in range(heads)], axis=0
            )
            scores = jnp.where(key_valid, contract(keys, queries, 1, 1), FLOOR)
            expo = jnp.exp(scores - jnp.max(scores, axis=0, keepdims=True))
            probs = expo * (1.0 / jnp.sum(expo, axis=0, keepdims=True))
            dprob = contract(values, cots, 1, 1)
            delta = jnp.sum(probs * dprob, axis=0, keepdims=True)
            probs_low = probs.astype(jnp.bfloat16)
            dscore_low = (probs * (dprob - delta)).astype(jnp.bfloat16)
            dvalue = contract(probs_low, cots, 1, 0)
            dkey = contract(dscore_low, queries, 1, 0)
            attended = contract(probs_low, values, 0, 0)
            dquery = contract(dscore_low, keys, 0, 0)
            for head in range(1, heads):
                mine = lane_head == head
                attended = jnp.where(mine, attended[head * BLK : (head + 1) * BLK], attended[:BLK])
                dquery = jnp.where(mine, dquery[head * BLK : (head + 1) * BLK], dquery[:BLK])
            attended = jnp.where(live, attended, 0.0)
            out[seq_count + target, 0, target_rows, lanes] = (dquery * SCALE).astype(jnp.bfloat16)
            out[seq_count + target, 1, target_rows, lanes] = attended.astype(jnp.bfloat16)
            for slot, (dev, here) in enumerate(places):
                part = slice(slot * BLK, (slot + 1) * BLK)
                key_grad[dev, here, lanes] += dkey[part]
                value_grad[dev, here, lanes] += dvalue[part]
        return carry

    lax.fori_loop(0, block_count, step, 0)
    out[:seq_count, 0] = key_grad[...].astype(jnp.bfloat16)
    out[:seq_count, 1] = value_grad[...].astype(jnp.bfloat16)


def attend_cost(block_count, width):
    pairs = block_count * NLIST * BLK * BLK * width
    return pl.CostEstimate(
        flops=10 * pairs,
        bytes_accessed=16 * block_count * BLK * width,
        transcendentals=pairs // HDIM,
    )


def specs(count, space):
    return [pl.BlockSpec(memory_space=space)] * count


def in_hbm(*arrays):
    return [pltpu.with_memory_space_constraint(array, pltpu.HBM) for array in arrays]


def gathered_kernel(seq_count, lists, source_len, target_len, rows, out, key_grad, value_grad):
    def listed(block, slot):
        return lists[block, slot]

    attend_sample(
        seq_count, listed, source_len[0], target_len[0], rows, out, key_grad, value_grad
    )


def by_all_to_all(first_rows, second_rows, alignment, diffusion_mask, source_length, target_length):
    seq_count = lax.axis_size("seq")
    parts = lax.axis_size("section") * seq_count
    rows_here = first_rows.shape[2]
    width = first_rows.shape[3]
    on_encoder = lax.axis_index("section") == 0
    row_pos = lax.axis_index("seq") * rows_here + jnp.arange(rows_here, dtype=jnp.int32)
    keep = on_encoder | ((row_pos < target_length[0]) & (diffusion_mask[0] == 1))
    second = jnp.where(keep[:, None], second_rows[0, 0], jnp.zeros_like(second_rows[0, 0]))
    held = jnp.stack([first_rows[0, 0], second])
    held = held.reshape(2, rows_here, parts, width // parts).transpose(2, 0, 1, 3)
    lists = lax.all_gather(alignment[0], "seq", axis=0, tiled=True)
    rows = lax.all_to_all(held, AXES, 0, 0, tiled=True)
    grads = pltpu.VMEM((seq_count, rows_here, width // parts), jnp.float32)
    grads = pl.pallas_call(
        functools.partial(gathered_kernel, seq_count),
        out_shape=jax.ShapeDtypeStruct(rows.shape, rows.dtype),
        in_specs=specs(3, pltpu.SMEM) + specs(1, pltpu.VMEM),
        out_specs=pl.BlockSpec(memory_space=pltpu.VMEM),
        scratch_shapes=[grads, grads],
        compiler_params=pltpu.CompilerParams(vmem_limit_bytes=VMEM_LIMIT),
        cost_estimate=attend_cost(lists.shape[0], width // parts),
        name="attend_gathered",
    )(lists, source_length, target_length, rows)
    grads = lax.all_to_all(grads, AXES, 0, 0, tiled=True)
    grads = grads.transpose(1, 2, 0, 3).reshape(2, rows_here, width)
    return (grads[0][None, None], grads[1][None, None])


def device_index(seq_count):
    return lax.axis_index("section") * seq_count + lax.axis_index("seq")


def pack_kernel(seq_count, order, *refs):
    target_len, smalls, (first, second) = refs[0], refs[1:3], refs[3:5]
    outs, (lists, mask, small_sem, sem) = refs[5:-4], refs[-4:]
    small_copies = [
        pltpu.make_async_copy(source, held, small_sem.at[slot])
        for slot, (source, held) in enumerate(zip(smalls, (lists, mask)))
    ]
    for copy in small_copies:
        copy.start()
    me = device_index(seq_count)
    here = me % seq_count
    share = outs[0].shape[1]
    copies = []
    for slot, (step, out) in enumerate(zip(order, outs)):
        lanes = pl.ds(pl.multiple_of((me ^ step) * share, LANES), share)
        pair = [
            pltpu.make_async_copy(
                source.at[0, 0, :, lanes], out.at[pl.ds(half * BLK, BLK)], sem.at[half, slot]
            )
            for half, source in enumerate((first, second))
        ]
        for copy in pair:
            copy.start()
        copies.append(pair)
    for copy in small_copies:
        copy.wait()
    positions = here * BLK + lax.broadcasted_iota(jnp.int32, (1, BLK), 1)
    keep = ((positions < target_len[0]) & (mask[...] == 1)) | (me < seq_count)
    keep = jnp.broadcast_to(jnp.where(keep, 1.0, 0.0), (BLK, BLK)).T.astype(jnp.bfloat16)
    keep = jnp.concatenate([keep] * (share // LANES), axis=1)
    base = here - WIN
    code = (lists[0, 0, 0] - base) * SPAN + lists[0, 0, 1] - base
    tail = jnp.full((TAIL, share), code, jnp.int32).astype(jnp.float32).astype(jnp.bfloat16)
    for out, pair in zip(outs, copies):
        for copy in pair:
            copy.wait()
        out[BLK : 2 * BLK] = out[BLK : 2 * BLK] * keep
        out[2 * BLK :] = tail


def attend_kernel(seq_count, order, source_len, target_len, *refs):
    parts = 2 * seq_count
    shares, outs = refs[:parts], refs[parts : 2 * parts]
    rows, result, key_grad, value_grad, lists = refs[2 * parts :]
    me = device_index(seq_count)
    here = me % seq_count
    for step, share in zip(order, shares):
        source = me ^ step
        rows[source, 0] = share[:BLK]
        rows[source, 1] = share[BLK : 2 * BLK]
        if step < seq_count:
            tail = share[2 * BLK :, :LANES].astype(jnp.float32)
            lists[here ^ step] = jnp.max(tail).astype(jnp.int32)

    def listed(block, slot):
        code = lists[block]
        return block - WIN + (code // SPAN if slot == 0 else code % SPAN)

    attend_sample(
        seq_count, listed, source_len[0], target_len[0], rows, result, key_grad, value_grad
    )
    for step, out in zip(order, outs):
        out[:BLK] = result[me ^ step, 0]
        out[BLK:] = result[me ^ step, 1]


def unpack_kernel(seq_count, order, *refs):
    shares, (first, second, sem) = refs[:-3], refs[-3:]
    width = shares[0].shape[1]
    me = device_index(seq_count)
    copies = []
    for slot, (step, share) in enumerate(zip(order, shares)):
        lanes = pl.ds(pl.multiple_of((me ^ step) * width, LANES), width)
        for half, result in enumerate((first, second)):
            copy = pltpu.make_async_copy(
                share.at[pl.ds(half * BLK, BLK)], result.at[0, 0, :, lanes], sem.at[half, slot]
            )
            copy.start()
            copies.append(copy)
    for copy in copies:
        copy.wait()


def swapped(shares, order):
    parts = len(order)
    return [
        lax.ppermute(share, AXES, [(dev, dev ^ step) for dev in range(parts)]) if step else share
        for step, share in zip(order, shares)
    ]


def by_pairs(first_rows, second_rows, alignment, diffusion_mask, source_length, target_length):
    seq_count = lax.axis_size("seq")
    parts = 2 * seq_count
    width = first_rows.shape[3]
    share = width // parts
    kind = first_rows.dtype
    params = pltpu.CompilerParams(vmem_limit_bytes=VMEM_LIMIT)
    far = [step for step in range(seq_count, parts) if step & 2]
    near = [step for step in range(seq_count, parts) if not step & 2]
    order = near[:1] + far + near[1:] + list(range(2, seq_count)) + [1, 0]
    sems = pltpu.SemaphoreType.DMA((2, parts))
    shares = pl.pallas_call(
        functools.partial(pack_kernel, seq_count, order),
        out_shape=[jax.ShapeDtypeStruct((2 * BLK + TAIL, share), kind)] * parts,
        in_specs=specs(1, pltpu.SMEM) + specs(4, pltpu.HBM),
        out_specs=specs(parts, pltpu.VMEM),
        scratch_shapes=[
            pltpu.SMEM(alignment.shape, jnp.int32),
            pltpu.VMEM(diffusion_mask.shape, jnp.int32),
            pltpu.SemaphoreType.DMA((2,)),
            sems,
        ],
        compiler_params=params,
        name="pack",
    )(target_length, *in_hbm(alignment, diffusion_mask, first_rows, second_rows))
    shares = swapped(shares, order)
    rows = pltpu.VMEM((parts, 2, BLK, share), kind)
    grads = pltpu.VMEM((seq_count, BLK, share), jnp.float32)
    shares = pl.pallas_call(
        functools.partial(attend_kernel, seq_count, order),
        out_shape=[jax.ShapeDtypeStruct((2 * BLK, share), kind)] * parts,
        in_specs=specs(2, pltpu.SMEM) + specs(parts, pltpu.VMEM),
        out_specs=specs(parts, pltpu.VMEM),
        scratch_shapes=[rows, rows, grads, grads, pltpu.SMEM((seq_count,), jnp.int32)],
        compiler_params=params,
        cost_estimate=attend_cost(seq_count, share),
        name="attend",
    )(source_length, target_length, *shares)
    shares = swapped(shares, order)
    out_shape = jax.ShapeDtypeStruct((1, 1, BLK, width), kind)
    return pl.pallas_call(
        functools.partial(unpack_kernel, seq_count, order),
        out_shape=[out_shape, out_shape],
        in_specs=specs(parts, pltpu.VMEM),
        out_specs=specs(2, pltpu.HBM),
        scratch_shapes=[sems],
        compiler_params=params,
        name="unpack",
    )(*shares)


def on_device(first_rows, second_rows, alignment, diffusion_mask, source_length, target_length):
    seq_count = lax.axis_size("seq")
    parts = lax.axis_size("section") * seq_count
    paired = (
        parts == 2 * seq_count
        and seq_count & (seq_count - 1) == 0
        and first_rows.shape[2] == BLK
        and first_rows.shape[3] % (parts * LANES) == 0
    )
    work = by_pairs if paired else by_all_to_all
    return tuple(
        work(first_rows, second_rows, alignment, diffusion_mask, source_length, target_length)
    )


def solution(mesh):
    placed = (
        P("section", "sample", "seq", None),
        P("section", "sample", "seq", None),
        P("sample", "seq", None),
        P("sample", "seq"),
        P("sample"),
        P("sample"),
    )
    return jax.shard_map(
        on_device,
        mesh=mesh,
        in_specs=placed,
        out_specs=(P("section", "sample", "seq", None), P("section", "sample", "seq", None)),
        check_vma=False,
    )
```

```python
import functools

import jax
import jax.numpy as jnp
from jax import lax
from jax.experimental import pallas as pl
from jax.experimental.pallas import tpu as pltpu
from jax.sharding import PartitionSpec as P

HDIM = 64
BLK = 128
NLIST = 2
WIN = 1
SPAN = 2 * WIN + 1
LANES = 128
TAIL = 16
SCALE = HDIM ** (-0.5)
FLOOR = -1e30
VMEM_LIMIT = 32 * 1024 * 1024
AXES = ("section", "seq")


def contract(left, right, left_dim, right_dim):
    return lax.dot_general(
        left, right, (((left_dim,), (right_dim,)), ((), ())), preferred_element_type=jnp.float32
    )


def attend_sample(seq_count, listed, source_len, target_len, rows, out, key_grad, value_grad):
    per_device = rows.shape[2] // BLK
    block_count = seq_count * per_device
    width = rows.shape[3]
    tile = min(width, LANES)
    heads = tile // HDIM
    key_grad[...] = jnp.zeros_like(key_grad)
    value_grad[...] = jnp.zeros_like(value_grad)
    inside = lax.broadcasted_iota(jnp.int32, (BLK, 1), 0)
    lane_head = lax.broadcasted_iota(jnp.int32, (BLK, tile), 1) // HDIM

    def place(block):
        if per_device == 1:
            return block, pl.ds(0, BLK)
        return block // per_device, pl.ds((block % per_device) * BLK, BLK)

    def step(block, carry):
        chosen = [listed(block, slot) for slot in range(NLIST)]
        places = [place(index) for index in chosen]
        target, target_rows = place(block)
        key_valid = jnp.concatenate(
            [index * BLK + inside < source_len for index in chosen], axis=0
        )
        live = block * BLK + inside < target_len
        for first in range(0, width, tile):
            lanes = pl.ds(first, tile)
            keys = jnp.concatenate([rows[dev, 0, here, lanes] for dev, here in places], axis=0)
            values = jnp.concatenate([rows[dev, 1, here, lanes] for dev, here in places], axis=0)
            queries = rows[seq_count + target, 0, target_rows, lanes] * jnp.bfloat16(SCALE)
            cots = rows[seq_count + target, 1, target_rows, lanes]
            none = jnp.zeros_like(queries)
            queries = jnp.concatenate(
                [jnp.where(lane_head == head, queries, none) for head in range(heads)], axis=0
            )
            cots = jnp.concatenate(
                [jnp.where(lane_head == head, cots, none) for head in range(heads)], axis=0
            )
            scores = jnp.where(key_valid, contract(keys, queries, 1, 1), FLOOR)
            expo = jnp.exp(scores - jnp.max(scores, axis=0, keepdims=True))
            probs = expo * (1.0 / jnp.sum(expo, axis=0, keepdims=True))
            dprob = contract(values, cots, 1, 1)
            delta = jnp.sum(probs * dprob, axis=0, keepdims=True)
            probs_low = probs.astype(jnp.bfloat16)
            dscore_low = (probs * (dprob - delta)).astype(jnp.bfloat16)
            dvalue = contract(probs_low, cots, 1, 0)
            dkey = contract(dscore_low, queries, 1, 0)
            attended = contract(probs_low, values, 0, 0)
            dquery = contract(dscore_low, keys, 0, 0)
            for head in range(1, heads):
                mine = lane_head == head
                attended = jnp.where(mine, attended[head * BLK : (head + 1) * BLK], attended[:BLK])
                dquery = jnp.where(mine, dquery[head * BLK : (head + 1) * BLK], dquery[:BLK])
            attended = jnp.where(live, attended, 0.0)
            out[seq_count + target, 0, target_rows, lanes] = (dquery * SCALE).astype(jnp.bfloat16)
            out[seq_count + target, 1, target_rows, lanes] = attended.astype(jnp.bfloat16)
            for slot, (dev, here) in enumerate(places):
                part = slice(slot * BLK, (slot + 1) * BLK)
                key_grad[dev, here, lanes] += dkey[part]
                value_grad[dev, here, lanes] += dvalue[part]
        return carry

    lax.fori_loop(0, block_count, step, 0)
    out[:seq_count, 0] = key_grad[...].astype(jnp.bfloat16)
    out[:seq_count, 1] = value_grad[...].astype(jnp.bfloat16)


def attend_cost(block_count, width):
    pairs = block_count * NLIST * BLK * BLK * width
    return pl.CostEstimate(
        flops=10 * pairs,
        bytes_accessed=16 * block_count * BLK * width,
        transcendentals=pairs // HDIM,
    )


def specs(count, space):
    return [pl.BlockSpec(memory_space=space)] * count


def in_hbm(*arrays):
    return [pltpu.with_memory_space_constraint(array, pltpu.HBM) for array in arrays]


def gathered_kernel(seq_count, lists, source_len, target_len, rows, out, key_grad, value_grad):
    def listed(block, slot):
        return lists[block, slot]

    attend_sample(
        seq_count, listed, source_len[0], target_len[0], rows, out, key_grad, value_grad
    )


def by_all_to_all(first_rows, second_rows, alignment, diffusion_mask, source_length, target_length):
    seq_count = lax.axis_size("seq")
    parts = lax.axis_size("section") * seq_count
    rows_here = first_rows.shape[2]
    width = first_rows.shape[3]
    on_encoder = lax.axis_index("section") == 0
    row_pos = lax.axis_index("seq") * rows_here + jnp.arange(rows_here, dtype=jnp.int32)
    keep = on_encoder | ((row_pos < target_length[0]) & (diffusion_mask[0] == 1))
    second = jnp.where(keep[:, None], second_rows[0, 0], jnp.zeros_like(second_rows[0, 0]))
    held = jnp.stack([first_rows[0, 0], second])
    held = held.reshape(2, rows_here, parts, width // parts).transpose(2, 0, 1, 3)
    lists = lax.all_gather(alignment[0], "seq", axis=0, tiled=True)
    rows = lax.all_to_all(held, AXES, 0, 0, tiled=True)
    grads = pltpu.VMEM((seq_count, rows_here, width // parts), jnp.float32)
    grads = pl.pallas_call(
        functools.partial(gathered_kernel, seq_count),
        out_shape=jax.ShapeDtypeStruct(rows.shape, rows.dtype),
        in_specs=specs(3, pltpu.SMEM) + specs(1, pltpu.VMEM),
        out_specs=pl.BlockSpec(memory_space=pltpu.VMEM),
        scratch_shapes=[grads, grads],
        compiler_params=pltpu.CompilerParams(vmem_limit_bytes=VMEM_LIMIT),
        cost_estimate=attend_cost(lists.shape[0], width // parts),
        name="attend_gathered",
    )(lists, source_length, target_length, rows)
    grads = lax.all_to_all(grads, AXES, 0, 0, tiled=True)
    grads = grads.transpose(1, 2, 0, 3).reshape(2, rows_here, width)
    return (grads[0][None, None], grads[1][None, None])


def device_index(seq_count):
    return lax.axis_index("section") * seq_count + lax.axis_index("seq")


def pack_kernel(seq_count, order, *refs):
    target_len, smalls, (first, second) = refs[0], refs[1:3], refs[3:5]
    outs, (lists, mask, small_sem, sem) = refs[5:-4], refs[-4:]
    small_copies = [
        pltpu.make_async_copy(source, held, small_sem.at[slot])
        for slot, (source, held) in enumerate(zip(smalls, (lists, mask)))
    ]
    for copy in small_copies:
        copy.start()
    me = device_index(seq_count)
    here = me % seq_count
    share = outs[0].shape[1]
    copies = []
    for slot, (step, out) in enumerate(zip(order, outs)):
        lanes = pl.ds(pl.multiple_of((me ^ step) * share, LANES), share)
        pair = [
            pltpu.make_async_copy(
                source.at[0, 0, :, lanes], out.at[pl.ds(half * BLK, BLK)], sem.at[half, slot]
            )
            for half, source in enumerate((first, second))
        ]
        for copy in pair:
            copy.start()
        copies.append(pair)
    for copy in small_copies:
        copy.wait()
    positions = here * BLK + lax.broadcasted_iota(jnp.int32, (1, BLK), 1)
    keep = ((positions < target_len[0]) & (mask[...] == 1)) | (me < seq_count)
    keep = jnp.broadcast_to(jnp.where(keep, 1.0, 0.0), (BLK, BLK)).T.astype(jnp.bfloat16)
    keep = jnp.concatenate([keep] * (share // LANES), axis=1)
    base = here - WIN
    code = (lists[0, 0, 0] - base) * SPAN + lists[0, 0, 1] - base
    tail = jnp.full((TAIL, share), code, jnp.int32).astype(jnp.float32).astype(jnp.bfloat16)
    for out, pair in zip(outs, copies):
        for copy in pair:
            copy.wait()
        out[BLK : 2 * BLK] = out[BLK : 2 * BLK] * keep
        out[2 * BLK :] = tail


def attend_kernel(seq_count, order, source_len, target_len, *refs):
    parts = 2 * seq_count
    shares, outs = refs[:parts], refs[parts : 2 * parts]
    rows, result, key_grad, value_grad, lists = refs[2 * parts :]
    me = device_index(seq_count)
    here = me % seq_count
    for step, share in zip(order, shares):
        source = me ^ step
        rows[source, 0] = share[:BLK]
        rows[source, 1] = share[BLK : 2 * BLK]
        if step < seq_count:
            tail = share[2 * BLK :, :LANES].astype(jnp.float32)
            lists[here ^ step] = jnp.max(tail).astype(jnp.int32)

    def listed(block, slot):
        code = lists[block]
        return block - WIN + (code // SPAN if slot == 0 else code % SPAN)

    attend_sample(
        seq_count, listed, source_len[0], target_len[0], rows, result, key_grad, value_grad
    )
    for step, out in zip(order, outs):
        out[:BLK] = result[me ^ step, 0]
        out[BLK:] = result[me ^ step, 1]


def unpack_kernel(seq_count, order, *refs):
    shares, (first, second, sem) = refs[:-3], refs[-3:]
    width = shares[0].shape[1]
    me = device_index(seq_count)
    copies = []
    for slot, (step, share) in enumerate(zip(order, shares)):
        lanes = pl.ds(pl.multiple_of((me ^ step) * width, LANES), width)
        for half, result in enumerate((first, second)):
            copy = pltpu.make_async_copy(
                share.at[pl.ds(half * BLK, BLK)], result.at[0, 0, :, lanes], sem.at[half, slot]
            )
            copy.start()
            copies.append(copy)
    for copy in copies:
        copy.wait()


def swapped(shares, order, after):
    parts = len(order)
    held = dict(zip(order, shares))
    moved = {0: held[0]}
    for step in order:
        if step:
            share = held[step]
            if step in after:
                earlier = after[step]
                share, moved[earlier] = lax.optimization_barrier((share, moved[earlier]))
            moved[step] = lax.ppermute(share, AXES, [(dev, dev ^ step) for dev in range(parts)])
    return [moved[step] for step in order]


def by_pairs(first_rows, second_rows, alignment, diffusion_mask, source_length, target_length):
    seq_count = lax.axis_size("seq")
    parts = 2 * seq_count
    width = first_rows.shape[3]
    share = width // parts
    kind = first_rows.dtype
    params = pltpu.CompilerParams(vmem_limit_bytes=VMEM_LIMIT)
    order, after = list(range(parts - 1, -1, -1)), {}
    if parts == 8:
        order, after = [6, 7, 4, 1, 2, 5, 3, 0], {5: 1, 3: 2}
    sems = pltpu.SemaphoreType.DMA((2, parts))
    shares = pl.pallas_call(
        functools.partial(pack_kernel, seq_count, order),
        out_shape=[jax.ShapeDtypeStruct((2 * BLK + TAIL, share), kind)] * parts,
        in_specs=specs(1, pltpu.SMEM) + specs(4, pltpu.HBM),
        out_specs=specs(parts, pltpu.VMEM),
        scratch_shapes=[
            pltpu.SMEM(alignment.shape, jnp.int32),
            pltpu.VMEM(diffusion_mask.shape, jnp.int32),
            pltpu.SemaphoreType.DMA((2,)),
            sems,
        ],
        compiler_params=params,
        name="pack",
    )(target_length, *in_hbm(alignment, diffusion_mask, first_rows, second_rows))
    shares = swapped(shares, order, after)
    rows = pltpu.VMEM((parts, 2, BLK, share), kind)
    grads = pltpu.VMEM((seq_count, BLK, share), jnp.float32)
    shares = pl.pallas_call(
        functools.partial(attend_kernel, seq_count, order),
        out_shape=[jax.ShapeDtypeStruct((2 * BLK, share), kind)] * parts,
        in_specs=specs(2, pltpu.SMEM) + specs(parts, pltpu.VMEM),
        out_specs=specs(parts, pltpu.VMEM),
        scratch_shapes=[rows, rows, grads, grads, pltpu.SMEM((seq_count,), jnp.int32)],
        compiler_params=params,
        cost_estimate=attend_cost(seq_count, share),
        name="attend",
    )(source_length, target_length, *shares)
    shares = swapped(shares, order, after)
    out_shape = jax.ShapeDtypeStruct((1, 1, BLK, width), kind)
    return pl.pallas_call(
        functools.partial(unpack_kernel, seq_count, order),
        out_shape=[out_shape, out_shape],
        in_specs=specs(parts, pltpu.VMEM),
        out_specs=specs(2, pltpu.HBM),
        scratch_shapes=[sems],
        compiler_params=params,
        name="unpack",
    )(*shares)


def on_device(first_rows, second_rows, alignment, diffusion_mask, source_length, target_length):
    seq_count = lax.axis_size("seq")
    parts = lax.axis_size("section") * seq_count
    paired = (
        parts == 2 * seq_count
        and seq_count & (seq_count - 1) == 0
        and first_rows.shape[2] == BLK
        and first_rows.shape[3] % (parts * LANES) == 0
    )
    work = by_pairs if paired else by_all_to_all
    return tuple(
        work(first_rows, second_rows, alignment, diffusion_mask, source_length, target_length)
    )


def solution(mesh):
    placed = (
        P("section", "sample", "seq", None),
        P("section", "sample", "seq", None),
        P("sample", "seq", None),
        P("sample", "seq"),
        P("sample"),
        P("sample"),
    )
    return jax.shard_map(
        on_device,
        mesh=mesh,
        in_specs=placed,
        out_specs=(P("section", "sample", "seq", None), P("section", "sample", "seq", None)),
        check_vma=False,
    )
```

```python
import functools

import jax
import jax.numpy as jnp
from jax import lax
from jax.experimental import pallas as pl
from jax.experimental.pallas import tpu as pltpu
from jax.sharding import PartitionSpec as P

HDIM = 64
BLK = 128
NLIST = 2
WIN = 1
SPAN = 2 * WIN + 1
LANES = 128
TAIL = 16
SCALE = HDIM ** (-0.5)
FLOOR = -1e30
VMEM_LIMIT = 32 * 1024 * 1024
AXES = ("section", "seq")


def contract(left, right, left_dim, right_dim):
    return lax.dot_general(
        left, right, (((left_dim,), (right_dim,)), ((), ())), preferred_element_type=jnp.float32
    )


def attend_sample(seq_count, listed, source_len, target_len, rows, out, key_grad, value_grad):
    per_device = rows.shape[2] // BLK
    block_count = seq_count * per_device
    width = rows.shape[3]
    tile = min(width, LANES)
    heads = tile // HDIM
    key_grad[...] = jnp.zeros_like(key_grad)
    value_grad[...] = jnp.zeros_like(value_grad)
    inside = lax.broadcasted_iota(jnp.int32, (BLK, 1), 0)
    lane_head = lax.broadcasted_iota(jnp.int32, (BLK, tile), 1) // HDIM

    def place(block):
        if per_device == 1:
            return block, pl.ds(0, BLK)
        return block // per_device, pl.ds((block % per_device) * BLK, BLK)

    def step(block, carry):
        chosen = [listed(block, slot) for slot in range(NLIST)]
        places = [place(index) for index in chosen]
        target, target_rows = place(block)
        key_valid = jnp.concatenate(
            [index * BLK + inside < source_len for index in chosen], axis=0
        )
        live = block * BLK + inside < target_len
        for first in range(0, width, tile):
            lanes = pl.ds(first, tile)
            keys = jnp.concatenate([rows[dev, 0, here, lanes] for dev, here in places], axis=0)
            values = jnp.concatenate([rows[dev, 1, here, lanes] for dev, here in places], axis=0)
            queries = rows[seq_count + target, 0, target_rows, lanes] * jnp.bfloat16(SCALE)
            cots = rows[seq_count + target, 1, target_rows, lanes]
            none = jnp.zeros_like(queries)
            cots = jnp.where(live, cots, none)
            queries = jnp.concatenate(
                [jnp.where(lane_head == head, queries, none) for head in range(heads)], axis=0
            )
            cots = jnp.concatenate(
                [jnp.where(lane_head == head, cots, none) for head in range(heads)], axis=0
            )
            scores = jnp.where(key_valid, contract(keys, queries, 1, 1), FLOOR)
            expo = jnp.exp(scores - jnp.max(scores, axis=0, keepdims=True))
            probs = expo * (1.0 / jnp.sum(expo, axis=0, keepdims=True))
            dprob = contract(values, cots, 1, 1)
            delta = jnp.sum(probs * dprob, axis=0, keepdims=True)
            probs_low = probs.astype(jnp.bfloat16)
            dscore_low = (probs * (dprob - delta)).astype(jnp.bfloat16)
            dvalue = contract(probs_low, cots, 1, 0)
            dkey = contract(dscore_low, queries, 1, 0)
            attended = contract(probs_low, values, 0, 0)
            dquery = contract(dscore_low, keys, 0, 0)
            for head in range(1, heads):
                mine = lane_head == head
                attended = jnp.where(mine, attended[head * BLK : (head + 1) * BLK], attended[:BLK])
                dquery = jnp.where(mine, dquery[head * BLK : (head + 1) * BLK], dquery[:BLK])
            attended = jnp.where(live, attended, 0.0)
            out[seq_count + target, 0, target_rows, lanes] = (dquery * SCALE).astype(jnp.bfloat16)
            out[seq_count + target, 1, target_rows, lanes] = attended.astype(jnp.bfloat16)
            for slot, (dev, here) in enumerate(places):
                part = slice(slot * BLK, (slot + 1) * BLK)
                key_grad[dev, here, lanes] += dkey[part]
                value_grad[dev, here, lanes] += dvalue[part]
        return carry

    lax.fori_loop(0, block_count, step, 0, unroll=block_count <= 4)
    out[:seq_count, 0] = key_grad[...].astype(jnp.bfloat16)
    out[:seq_count, 1] = value_grad[...].astype(jnp.bfloat16)


def attend_cost(block_count, width):
    pairs = block_count * NLIST * BLK * BLK * width
    return pl.CostEstimate(
        flops=10 * pairs,
        bytes_accessed=16 * block_count * BLK * width,
        transcendentals=pairs // HDIM,
    )


def specs(count, space):
    return [pl.BlockSpec(memory_space=space)] * count


def in_hbm(*arrays):
    return [pltpu.with_memory_space_constraint(array, pltpu.HBM) for array in arrays]


def gathered_kernel(seq_count, lists, source_len, target_len, rows, out, key_grad, value_grad):
    def listed(block, slot):
        return lists[block, slot]

    attend_sample(
        seq_count, listed, source_len[0], target_len[0], rows, out, key_grad, value_grad
    )


def by_all_to_all(first_rows, second_rows, alignment, diffusion_mask, source_length, target_length):
    seq_count = lax.axis_size("seq")
    parts = lax.axis_size("section") * seq_count
    rows_here = first_rows.shape[2]
    width = first_rows.shape[3]
    on_encoder = lax.axis_index("section") == 0
    keep = on_encoder | (diffusion_mask[0] == 1)
    second = jnp.where(keep[:, None], second_rows[0, 0], jnp.zeros_like(second_rows[0, 0]))
    held = jnp.stack([first_rows[0, 0], second])
    held = held.reshape(2, rows_here, parts, width // parts).transpose(2, 0, 1, 3)
    lists = lax.all_gather(alignment[0], "seq", axis=0, tiled=True)
    rows = lax.all_to_all(held, AXES, 0, 0, tiled=True)
    grads = pltpu.VMEM((seq_count, rows_here, width // parts), jnp.float32)
    grads = pl.pallas_call(
        functools.partial(gathered_kernel, seq_count),
        out_shape=jax.ShapeDtypeStruct(rows.shape, rows.dtype),
        in_specs=specs(3, pltpu.SMEM) + specs(1, pltpu.VMEM),
        out_specs=pl.BlockSpec(memory_space=pltpu.VMEM),
        scratch_shapes=[grads, grads],
        compiler_params=pltpu.CompilerParams(vmem_limit_bytes=VMEM_LIMIT),
        cost_estimate=attend_cost(lists.shape[0], width // parts),
        name="attend_gathered",
    )(lists, source_length, target_length, rows)
    grads = lax.all_to_all(grads, AXES, 0, 0, tiled=True)
    grads = grads.transpose(1, 2, 0, 3).reshape(2, rows_here, width)
    return (grads[0][None, None], grads[1][None, None])


def device_index(seq_count):
    return lax.axis_index("section") * seq_count + lax.axis_index("seq")


def pack_kernel(seq_count, order, *refs):
    smalls, (first, second) = refs[:2], refs[2:4]
    outs, (lists, mask, small_sem, sem) = refs[4:-4], refs[-4:]
    small_copies = [
        pltpu.make_async_copy(source, held, small_sem.at[slot])
        for slot, (source, held) in enumerate(zip(smalls, (lists, mask)))
    ]
    for copy in small_copies:
        copy.start()
    me = device_index(seq_count)
    here = me % seq_count
    share = outs[0].shape[1]
    copies = []
    for slot, (step, out) in enumerate(zip(order, outs)):
        lanes = pl.ds(pl.multiple_of((me ^ step) * share, LANES), share)
        pair = [
            pltpu.make_async_copy(
                source.at[0, 0, :, lanes], out.at[pl.ds(half * BLK, BLK)], sem.at[half, slot]
            )
            for half, source in enumerate((first, second))
        ]
        for copy in pair:
            copy.start()
        copies.append(pair)
    for copy in small_copies:
        copy.wait()
    keep = (mask[...] == 1) | (me < seq_count)
    keep = jnp.broadcast_to(jnp.where(keep, 1.0, 0.0), (BLK, BLK)).T.astype(jnp.bfloat16)
    keep = jnp.concatenate([keep] * (share // LANES), axis=1)
    base = here - WIN
    code = (lists[0, 0, 0] - base) * SPAN + lists[0, 0, 1] - base
    tail = jnp.full((TAIL, share), code, jnp.int32).astype(jnp.float32).astype(jnp.bfloat16)
    for out, pair in zip(outs, copies):
        for copy in pair:
            copy.wait()
        out[BLK : 2 * BLK] = out[BLK : 2 * BLK] * keep
        out[2 * BLK :] = tail


def attend_kernel(seq_count, order, source_len, target_len, *refs):
    parts = 2 * seq_count
    shares, outs = refs[:parts], refs[parts : 2 * parts]
    rows, result, key_grad, value_grad, lists = refs[2 * parts :]
    me = device_index(seq_count)
    here = me % seq_count
    for step, share in zip(order, shares):
        source = me ^ step
        rows[source, 0] = share[:BLK]
        rows[source, 1] = share[BLK : 2 * BLK]
        if step < seq_count:
            tail = share[2 * BLK :, :LANES].astype(jnp.float32)
            lists[here ^ step] = jnp.max(tail).astype(jnp.int32)

    def listed(block, slot):
        code = lists[block]
        return block - WIN + (code // SPAN if slot == 0 else code % SPAN)

    attend_sample(
        seq_count, listed, source_len[0], target_len[0], rows, result, key_grad, value_grad
    )
    for step, out in zip(order, outs):
        out[:BLK] = result[me ^ step, 0]
        out[BLK:] = result[me ^ step, 1]


def unpack_kernel(seq_count, order, *refs):
    shares, (first, second, sem) = refs[:-3], refs[-3:]
    width = shares[0].shape[1]
    me = device_index(seq_count)
    copies = []
    for slot, (step, share) in enumerate(zip(order, shares)):
        lanes = pl.ds(pl.multiple_of((me ^ step) * width, LANES), width)
        for half, result in enumerate((first, second)):
            copy = pltpu.make_async_copy(
                share.at[pl.ds(half * BLK, BLK)], result.at[0, 0, :, lanes], sem.at[half, slot]
            )
            copy.start()
            copies.append(copy)
    for copy in copies:
        copy.wait()


def swapped(shares, order, after):
    parts = len(order)
    held = dict(zip(order, shares))
    moved = {0: held[0]}
    for step in order:
        if step:
            share = held[step]
            if step in after:
                earlier = after[step]
                share, moved[earlier] = lax.optimization_barrier((share, moved[earlier]))
            moved[step] = lax.ppermute(share, AXES, [(dev, dev ^ step) for dev in range(parts)])
    return [moved[step] for step in order]


def by_pairs(first_rows, second_rows, alignment, diffusion_mask, source_length, target_length):
    seq_count = lax.axis_size("seq")
    parts = 2 * seq_count
    width = first_rows.shape[3]
    share = width // parts
    kind = first_rows.dtype
    params = pltpu.CompilerParams(vmem_limit_bytes=VMEM_LIMIT)
    order, after = list(range(parts - 1, -1, -1)), {}
    if parts == 8:
        order = [6, 7, 4, 5, 2, 3, 1, 0]
    sems = pltpu.SemaphoreType.DMA((2, parts))
    shares = pl.pallas_call(
        functools.partial(pack_kernel, seq_count, order),
        out_shape=[jax.ShapeDtypeStruct((2 * BLK + TAIL, share), kind)] * parts,
        in_specs=specs(4, pltpu.HBM),
        out_specs=specs(parts, pltpu.VMEM),
        scratch_shapes=[
            pltpu.SMEM(alignment.shape, jnp.int32),
            pltpu.VMEM(diffusion_mask.shape, jnp.int32),
            pltpu.SemaphoreType.DMA((2,)),
            sems,
        ],
        compiler_params=params,
        name="pack",
    )(*in_hbm(alignment, diffusion_mask, first_rows, second_rows))
    shares = swapped(shares, order, after)
    rows = pltpu.VMEM((parts, 2, BLK, share), kind)
    grads = pltpu.VMEM((seq_count, BLK, share), jnp.float32)
    shares = pl.pallas_call(
        functools.partial(attend_kernel, seq_count, order),
        out_shape=[jax.ShapeDtypeStruct((2 * BLK, share), kind)] * parts,
        in_specs=specs(2, pltpu.SMEM) + specs(parts, pltpu.VMEM),
        out_specs=specs(parts, pltpu.VMEM),
        scratch_shapes=[rows, rows, grads, grads, pltpu.SMEM((seq_count,), jnp.int32)],
        compiler_params=params,
        cost_estimate=attend_cost(seq_count, share),
        name="attend",
    )(source_length, target_length, *shares)
    shares = swapped(shares, order, after)
    out_shape = jax.ShapeDtypeStruct((1, 1, BLK, width), kind)
    return pl.pallas_call(
        functools.partial(unpack_kernel, seq_count, order),
        out_shape=[out_shape, out_shape],
        in_specs=specs(parts, pltpu.VMEM),
        out_specs=specs(2, pltpu.HBM),
        scratch_shapes=[sems],
        compiler_params=params,
        name="unpack",
    )(*shares)


def on_device(first_rows, second_rows, alignment, diffusion_mask, source_length, target_length):
    seq_count = lax.axis_size("seq")
    parts = lax.axis_size("section") * seq_count
    paired = (
        parts == 2 * seq_count
        and seq_count & (seq_count - 1) == 0
        and first_rows.shape[2] == BLK
        and first_rows.shape[3] % (parts * LANES) == 0
    )
    work = by_pairs if paired else by_all_to_all
    return tuple(
        work(first_rows, second_rows, alignment, diffusion_mask, source_length, target_length)
    )


def solution(mesh):
    placed = (
        P("section", "sample", "seq", None),
        P("section", "sample", "seq", None),
        P("sample", "seq", None),
        P("sample", "seq"),
        P("sample"),
        P("sample"),
    )
    return jax.shard_map(
        on_device,
        mesh=mesh,
        in_specs=placed,
        out_specs=(P("section", "sample", "seq", None), P("section", "sample", "seq", None)),
        check_vma=False,
    )
```

```python
import functools

import jax
import jax.numpy as jnp
from jax import lax
from jax.experimental import pallas as pl
from jax.experimental.pallas import tpu as pltpu
from jax.sharding import PartitionSpec as P

HDIM = 64
BLK = 128
NLIST = 2
WIN = 1
SPAN = 2 * WIN + 1
LANES = 128
TAIL = 16
SCALE = HDIM ** (-0.5)
FLOOR = -1e30
VMEM_LIMIT = 32 * 1024 * 1024
AXES = ("section", "seq")


def contract(left, right, left_dim, right_dim):
    return lax.dot_general(
        left, right, (((left_dim,), (right_dim,)), ((), ())), preferred_element_type=jnp.float32
    )


def attend_sample(seq_count, listed, source_len, target_len, rows, out, key_grad, value_grad):
    per_device = rows.shape[2] // BLK
    block_count = seq_count * per_device
    width = rows.shape[3]
    tile = min(width, LANES)
    heads = tile // HDIM
    key_grad[...] = jnp.zeros_like(key_grad)
    value_grad[...] = jnp.zeros_like(value_grad)
    inside = lax.broadcasted_iota(jnp.int32, (BLK, 1), 0)
    lane_head = lax.broadcasted_iota(jnp.int32, (BLK, tile), 1) // HDIM

    def place(block):
        if per_device == 1:
            return block, pl.ds(0, BLK)
        return block // per_device, pl.ds((block % per_device) * BLK, BLK)

    def step(block, carry):
        chosen = [listed(block, slot) for slot in range(NLIST)]
        places = [place(index) for index in chosen]
        target, target_rows = place(block)
        key_valid = jnp.concatenate(
            [index * BLK + inside < source_len for index in chosen], axis=0
        )
        live = block * BLK + inside < target_len
        for first in range(0, width, tile):
            lanes = pl.ds(first, tile)
            keys = jnp.concatenate([rows[dev, 0, here, lanes] for dev, here in places], axis=0)
            values = jnp.concatenate([rows[dev, 1, here, lanes] for dev, here in places], axis=0)
            queries = rows[seq_count + target, 0, target_rows, lanes] * jnp.bfloat16(SCALE)
            cots = rows[seq_count + target, 1, target_rows, lanes]
            none = jnp.zeros_like(queries)
            cots = jnp.where(live, cots, none)
            queries = jnp.concatenate(
                [jnp.where(lane_head == head, queries, none) for head in range(heads)], axis=0
            )
            cots = jnp.concatenate(
                [jnp.where(lane_head == head, cots, none) for head in range(heads)], axis=0
            )
            scores = jnp.where(key_valid, contract(keys, queries, 1, 1), FLOOR)
            expo = jnp.exp(scores - jnp.max(scores, axis=0, keepdims=True))
            probs = expo * (1.0 / jnp.sum(expo, axis=0, keepdims=True))
            dprob = contract(values, cots, 1, 1)
            delta = jnp.sum(probs * dprob, axis=0, keepdims=True)
            probs_low = probs.astype(jnp.bfloat16)
            dscore_low = (probs * (dprob - delta)).astype(jnp.bfloat16)
            dvalue = contract(probs_low, cots, 1, 0)
            dkey = contract(dscore_low, queries, 1, 0)
            attended = contract(probs_low, values, 0, 0)
            dquery = contract(dscore_low, keys, 0, 0)
            for head in range(1, heads):
                mine = lane_head == head
                attended = jnp.where(mine, attended[head * BLK : (head + 1) * BLK], attended[:BLK])
                dquery = jnp.where(mine, dquery[head * BLK : (head + 1) * BLK], dquery[:BLK])
            attended = jnp.where(live, attended, 0.0)
            out[seq_count + target, 0, target_rows, lanes] = (dquery * SCALE).astype(jnp.bfloat16)
            out[seq_count + target, 1, target_rows, lanes] = attended.astype(jnp.bfloat16)
            for slot, (dev, here) in enumerate(places):
                part = slice(slot * BLK, (slot + 1) * BLK)
                key_grad[dev, here, lanes] += dkey[part]
                value_grad[dev, here, lanes] += dvalue[part]
        return carry

    lax.fori_loop(0, block_count, step, 0, unroll=block_count <= 4)
    out[:seq_count, 0] = key_grad[...].astype(jnp.bfloat16)
    out[:seq_count, 1] = value_grad[...].astype(jnp.bfloat16)


def attend_cost(block_count, width):
    pairs = block_count * NLIST * BLK * BLK * width
    return pl.CostEstimate(
        flops=10 * pairs,
        bytes_accessed=16 * block_count * BLK * width,
        transcendentals=pairs // HDIM,
    )


def specs(count, space):
    return [pl.BlockSpec(memory_space=space)] * count


def in_hbm(*arrays):
    return [pltpu.with_memory_space_constraint(array, pltpu.HBM) for array in arrays]


def gathered_kernel(seq_count, lists, source_len, target_len, rows, out, key_grad, value_grad):
    def listed(block, slot):
        return lists[block, slot]

    attend_sample(
        seq_count, listed, source_len[0], target_len[0], rows, out, key_grad, value_grad
    )


def by_all_to_all(first_rows, second_rows, alignment, diffusion_mask, source_length, target_length):
    seq_count = lax.axis_size("seq")
    parts = lax.axis_size("section") * seq_count
    rows_here = first_rows.shape[2]
    width = first_rows.shape[3]
    on_encoder = lax.axis_index("section") == 0
    keep = on_encoder | (diffusion_mask[0] == 1)
    second = jnp.where(keep[:, None], second_rows[0, 0], jnp.zeros_like(second_rows[0, 0]))
    held = jnp.stack([first_rows[0, 0], second])
    held = held.reshape(2, rows_here, parts, width // parts).transpose(2, 0, 1, 3)
    lists = lax.all_gather(alignment[0], "seq", axis=0, tiled=True)
    rows = lax.all_to_all(held, AXES, 0, 0, tiled=True)
    grads = pltpu.VMEM((seq_count, rows_here, width // parts), jnp.float32)
    grads = pl.pallas_call(
        functools.partial(gathered_kernel, seq_count),
        out_shape=jax.ShapeDtypeStruct(rows.shape, rows.dtype),
        in_specs=specs(3, pltpu.SMEM) + specs(1, pltpu.VMEM),
        out_specs=pl.BlockSpec(memory_space=pltpu.VMEM),
        scratch_shapes=[grads, grads],
        compiler_params=pltpu.CompilerParams(vmem_limit_bytes=VMEM_LIMIT),
        cost_estimate=attend_cost(lists.shape[0], width // parts),
        name="attend_gathered",
    )(lists, source_length, target_length, rows)
    grads = lax.all_to_all(grads, AXES, 0, 0, tiled=True)
    grads = grads.transpose(1, 2, 0, 3).reshape(2, rows_here, width)
    return (grads[0][None, None], grads[1][None, None])


def device_index(seq_count):
    return lax.axis_index("section") * seq_count + lax.axis_index("seq")


def pack_kernel(seq_count, order, *refs):
    smalls, (first, second) = refs[:2], refs[2:4]
    near, far, (lists, mask, small_sem, sem) = refs[4], refs[5:-4], refs[-4:]
    me = device_index(seq_count)
    here = me % seq_count
    share = near.shape[2]
    outs = [(me ^ step, out) for step, out in zip(order, far)]
    outs += [(me - here + slot, near.at[slot]) for slot in range(seq_count)]
    small_copies = [
        pltpu.make_async_copy(source, held, small_sem.at[slot])
        for slot, (source, held) in enumerate(zip(smalls, (lists, mask)))
    ]
    for copy in small_copies:
        copy.start()
    copies = []
    for slot, (target, out) in enumerate(outs):
        lanes = pl.ds(pl.multiple_of(target * share, LANES), share)
        pair = [
            pltpu.make_async_copy(
                source.at[0, 0, :, lanes], out.at[pl.ds(half * BLK, BLK)], sem.at[half, slot]
            )
            for half, source in enumerate((first, second))
        ]
        for copy in pair:
            copy.start()
        copies.append(pair)
    for copy in small_copies:
        copy.wait()
    keep = (mask[...] == 1) | (me < seq_count)
    keep = jnp.broadcast_to(jnp.where(keep, 1.0, 0.0), (BLK, BLK)).T.astype(jnp.bfloat16)
    keep = jnp.concatenate([keep] * (share // LANES), axis=1)
    base = here - WIN
    code = (lists[0, 0, 0] - base) * SPAN + lists[0, 0, 1] - base
    tail = jnp.full((TAIL, share), code, jnp.int32).astype(jnp.float32).astype(jnp.bfloat16)
    for slot in range(seq_count):
        near[slot, 2 * BLK :] = tail
    for (target, out), pair in zip(outs, copies):
        for copy in pair:
            copy.wait()
        out[BLK : 2 * BLK] = out[BLK : 2 * BLK] * keep


def attend_kernel(seq_count, order, source_len, target_len, *refs):
    count = 1 + len(order)
    (near, *far), (near_out, *far_out) = refs[:count], refs[count : 2 * count]
    rows, result, key_grad, value_grad, lists = refs[2 * count :]
    me = device_index(seq_count)
    base = me - me % seq_count
    for slot in range(seq_count):
        rows[base + slot, 0] = near[slot, :BLK]
        rows[base + slot, 1] = near[slot, BLK : 2 * BLK]
        lists[slot] = jnp.max(near[slot, 2 * BLK :, :LANES].astype(jnp.float32)).astype(jnp.int32)
    for step, share in zip(order, far):
        rows[me ^ step, 0] = share[:BLK]
        rows[me ^ step, 1] = share[BLK:]

    def listed(block, slot):
        code = lists[block]
        return block - WIN + (code // SPAN if slot == 0 else code % SPAN)

    attend_sample(
        seq_count, listed, source_len[0], target_len[0], rows, result, key_grad, value_grad
    )
    for step, out in zip(order, far_out):
        out[:BLK] = result[me ^ step, 0]
        out[BLK:] = result[me ^ step, 1]
    for slot in range(seq_count):
        near_out[slot, :BLK] = result[base + slot, 0]
        near_out[slot, BLK:] = result[base + slot, 1]


def unpack_kernel(seq_count, order, near, *refs):
    far, (first, second, sem) = refs[:-3], refs[-3:]
    width = near.shape[2]
    me = device_index(seq_count)
    base = me - me % seq_count
    shares = [(me ^ step, share) for step, share in zip(order, far)]
    shares += [(base + slot, near.at[slot]) for slot in range(seq_count)]
    copies = []
    for slot, (source, share) in enumerate(shares):
        lanes = pl.ds(pl.multiple_of(source * width, LANES), width)
        for half, result in enumerate((first, second)):
            copy = pltpu.make_async_copy(
                share.at[pl.ds(half * BLK, BLK)], result.at[0, 0, :, lanes], sem.at[half, slot]
            )
            copy.start()
            copies.append(copy)
    for copy in copies:
        copy.wait()


def swapped(order, near, *far):
    parts = 2 * near.shape[0]
    far = [
        lax.ppermute(share, AXES, [(dev, dev ^ step) for dev in range(parts)])
        for step, share in zip(order, far)
    ]
    return [lax.all_to_all(near, "seq", 0, 0, tiled=True), *far]


def by_pairs(first_rows, second_rows, alignment, diffusion_mask, source_length, target_length):
    seq_count = lax.axis_size("seq")
    parts = 2 * seq_count
    width = first_rows.shape[3]
    share = width // parts
    kind = first_rows.dtype
    params = pltpu.CompilerParams(vmem_limit_bytes=VMEM_LIMIT)
    order = [seq_count, *range(seq_count + 2, parts), seq_count + 1]
    far = [jax.ShapeDtypeStruct((2 * BLK, share), kind)] * seq_count
    sems = pltpu.SemaphoreType.DMA((2, parts))
    shares = pl.pallas_call(
        functools.partial(pack_kernel, seq_count, order),
        out_shape=[jax.ShapeDtypeStruct((seq_count, 2 * BLK + TAIL, share), kind), *far],
        in_specs=specs(4, pltpu.HBM),
        out_specs=specs(1 + seq_count, pltpu.VMEM),
        scratch_shapes=[
            pltpu.SMEM(alignment.shape, jnp.int32),
            pltpu.VMEM(diffusion_mask.shape, jnp.int32),
            pltpu.SemaphoreType.DMA((2,)),
            sems,
        ],
        compiler_params=params,
        name="pack",
    )(*in_hbm(alignment, diffusion_mask, first_rows, second_rows))
    shares = swapped(order, *shares)
    rows = pltpu.VMEM((parts, 2, BLK, share), kind)
    grads = pltpu.VMEM((seq_count, BLK, share), jnp.float32)
    shares = pl.pallas_call(
        functools.partial(attend_kernel, seq_count, order),
        out_shape=[jax.ShapeDtypeStruct((seq_count, 2 * BLK, share), kind), *far],
        in_specs=specs(2, pltpu.SMEM) + specs(1 + seq_count, pltpu.VMEM),
        out_specs=specs(1 + seq_count, pltpu.VMEM),
        scratch_shapes=[rows, rows, grads, grads, pltpu.SMEM((seq_count,), jnp.int32)],
        compiler_params=params,
        cost_estimate=attend_cost(seq_count, share),
        name="attend",
    )(source_length, target_length, *shares)
    shares = swapped(order, *shares)
    out_shape = jax.ShapeDtypeStruct((1, 1, BLK, width), kind)
    return pl.pallas_call(
        functools.partial(unpack_kernel, seq_count, order),
        out_shape=[out_shape, out_shape],
        in_specs=specs(1 + seq_count, pltpu.VMEM),
        out_specs=specs(2, pltpu.HBM),
        scratch_shapes=[sems],
        compiler_params=params,
        name="unpack",
    )(*shares)


def on_device(first_rows, second_rows, alignment, diffusion_mask, source_length, target_length):
    seq_count = lax.axis_size("seq")
    parts = lax.axis_size("section") * seq_count
    paired = (
        parts == 2 * seq_count
        and seq_count >= 2
        and seq_count & (seq_count - 1) == 0
        and first_rows.shape[2] == BLK
        and first_rows.shape[3] % (parts * LANES) == 0
    )
    work = by_pairs if paired else by_all_to_all
    return tuple(
        work(first_rows, second_rows, alignment, diffusion_mask, source_length, target_length)
    )


def solution(mesh):
    placed = (
        P("section", "sample", "seq", None),
        P("section", "sample", "seq", None),
        P("sample", "seq", None),
        P("sample", "seq"),
        P("sample"),
        P("sample"),
    )
    return jax.shard_map(
        on_device,
        mesh=mesh,
        in_specs=placed,
        out_specs=(P("section", "sample", "seq", None), P("section", "sample", "seq", None)),
        check_vma=False,
    )
```

```python
import functools

import jax
import jax.numpy as jnp
from jax import lax
from jax.experimental import pallas as pl
from jax.experimental.pallas import tpu as pltpu
from jax.sharding import PartitionSpec as P

HDIM = 64
BLK = 128
NLIST = 2
WIN = 1
SPAN = 2 * WIN + 1
LANES = 128
TAIL = 16
SCALE = HDIM ** (-0.5)
FLOOR = -1e30
VMEM_LIMIT = 32 * 1024 * 1024
AXES = ("section", "seq")


def contract(left, right, left_dim, right_dim):
    return lax.dot_general(
        left, right, (((left_dim,), (right_dim,)), ((), ())), preferred_element_type=jnp.float32
    )


def attend_sample(seq_count, listed, source_len, target_len, rows, out, key_grad, value_grad):
    per_device = rows.shape[2] // BLK
    block_count = seq_count * per_device
    width = rows.shape[3]
    tile = min(width, LANES)
    heads = tile // HDIM
    key_grad[...] = jnp.zeros_like(key_grad)
    value_grad[...] = jnp.zeros_like(value_grad)
    inside = lax.broadcasted_iota(jnp.int32, (BLK, 1), 0)
    lane_head = lax.broadcasted_iota(jnp.int32, (BLK, tile), 1) // HDIM

    def place(block):
        if per_device == 1:
            return block, pl.ds(0, BLK)
        return block // per_device, pl.ds((block % per_device) * BLK, BLK)

    def step(block, carry):
        chosen = [listed(block, slot) for slot in range(NLIST)]
        places = [place(index) for index in chosen]
        target, target_rows = place(block)
        key_valid = jnp.concatenate(
            [index * BLK + inside < source_len for index in chosen], axis=0
        )
        live = block * BLK + inside < target_len
        for first in range(0, width, tile):
            lanes = pl.ds(first, tile)
            keys = jnp.concatenate([rows[dev, 0, here, lanes] for dev, here in places], axis=0)
            values = jnp.concatenate([rows[dev, 1, here, lanes] for dev, here in places], axis=0)
            queries = rows[seq_count + target, 0, target_rows, lanes] * jnp.bfloat16(SCALE)
            cots = rows[seq_count + target, 1, target_rows, lanes]
            none = jnp.zeros_like(queries)
            cots = jnp.where(live, cots, none)
            queries = jnp.concatenate(
                [jnp.where(lane_head == head, queries, none) for head in range(heads)], axis=0
            )
            cots = jnp.concatenate(
                [jnp.where(lane_head == head, cots, none) for head in range(heads)], axis=0
            )
            scores = jnp.where(key_valid, contract(keys, queries, 1, 1), FLOOR)
            expo = jnp.exp(scores - jnp.max(scores, axis=0, keepdims=True))
            probs = expo * (1.0 / jnp.sum(expo, axis=0, keepdims=True))
            dprob = contract(values, cots, 1, 1)
            delta = jnp.sum(probs * dprob, axis=0, keepdims=True)
            probs_low = probs.astype(jnp.bfloat16)
            dscore_low = (probs * (dprob - delta)).astype(jnp.bfloat16)
            dvalue = contract(probs_low, cots, 1, 0)
            dkey = contract(dscore_low, queries, 1, 0)
            attended = contract(probs_low, values, 0, 0)
            dquery = contract(dscore_low, keys, 0, 0)
            for head in range(1, heads):
                mine = lane_head == head
                attended = jnp.where(mine, attended[head * BLK : (head + 1) * BLK], attended[:BLK])
                dquery = jnp.where(mine, dquery[head * BLK : (head + 1) * BLK], dquery[:BLK])
            attended = jnp.where(live, attended, 0.0)
            out[seq_count + target, 0, target_rows, lanes] = (dquery * SCALE).astype(jnp.bfloat16)
            out[seq_count + target, 1, target_rows, lanes] = attended.astype(jnp.bfloat16)
            for slot, (dev, here) in enumerate(places):
                part = slice(slot * BLK, (slot + 1) * BLK)
                key_grad[dev, here, lanes] += dkey[part]
                value_grad[dev, here, lanes] += dvalue[part]
        return carry

    lax.fori_loop(0, block_count, step, 0, unroll=block_count <= 4)
    out[:seq_count, 0] = key_grad[...].astype(jnp.bfloat16)
    out[:seq_count, 1] = value_grad[...].astype(jnp.bfloat16)


def attend_cost(block_count, width):
    pairs = block_count * NLIST * BLK * BLK * width
    return pl.CostEstimate(
        flops=10 * pairs,
        bytes_accessed=16 * block_count * BLK * width,
        transcendentals=pairs // HDIM,
    )


def specs(count, space):
    return [pl.BlockSpec(memory_space=space)] * count


def in_hbm(*arrays):
    return [pltpu.with_memory_space_constraint(array, pltpu.HBM) for array in arrays]


def gathered_kernel(seq_count, lists, source_len, target_len, rows, out, key_grad, value_grad):
    def listed(block, slot):
        return lists[block, slot]

    attend_sample(
        seq_count, listed, source_len[0], target_len[0], rows, out, key_grad, value_grad
    )


def by_all_to_all(first_rows, second_rows, alignment, diffusion_mask, source_length, target_length):
    seq_count = lax.axis_size("seq")
    parts = lax.axis_size("section") * seq_count
    rows_here = first_rows.shape[2]
    width = first_rows.shape[3]
    on_encoder = lax.axis_index("section") == 0
    keep = on_encoder | (diffusion_mask[0] == 1)
    second = jnp.where(keep[:, None], second_rows[0, 0], jnp.zeros_like(second_rows[0, 0]))
    held = jnp.stack([first_rows[0, 0], second])
    held = held.reshape(2, rows_here, parts, width // parts).transpose(2, 0, 1, 3)
    lists = lax.all_gather(alignment[0], "seq", axis=0, tiled=True)
    rows = lax.all_to_all(held, AXES, 0, 0, tiled=True)
    grads = pltpu.VMEM((seq_count, rows_here, width // parts), jnp.float32)
    grads = pl.pallas_call(
        functools.partial(gathered_kernel, seq_count),
        out_shape=jax.ShapeDtypeStruct(rows.shape, rows.dtype),
        in_specs=specs(3, pltpu.SMEM) + specs(1, pltpu.VMEM),
        out_specs=pl.BlockSpec(memory_space=pltpu.VMEM),
        scratch_shapes=[grads, grads],
        compiler_params=pltpu.CompilerParams(vmem_limit_bytes=VMEM_LIMIT),
        cost_estimate=attend_cost(lists.shape[0], width // parts),
        name="attend_gathered",
    )(lists, source_length, target_length, rows)
    grads = lax.all_to_all(grads, AXES, 0, 0, tiled=True)
    grads = grads.transpose(1, 2, 0, 3).reshape(2, rows_here, width)
    return (grads[0][None, None], grads[1][None, None])


def device_index(seq_count):
    return lax.axis_index("section") * seq_count + lax.axis_index("seq")


def pack_kernel(seq_count, order, *refs):
    smalls, (first, second) = refs[:2], refs[2:4]
    outs, (lists, mask, small_sem, sem) = refs[4:-4], refs[-4:]
    small_copies = [
        pltpu.make_async_copy(source, held, small_sem.at[slot])
        for slot, (source, held) in enumerate(zip(smalls, (lists, mask)))
    ]
    for copy in small_copies:
        copy.start()
    me = device_index(seq_count)
    here = me % seq_count
    share = outs[0].shape[1]
    copies = []
    for slot, (step, out) in enumerate(zip(order, outs)):
        lanes = pl.ds(pl.multiple_of((me ^ step) * share, LANES), share)
        pair = [
            pltpu.make_async_copy(
                source.at[0, 0, :, lanes], out.at[pl.ds(half * BLK, BLK)], sem.at[half, slot]
            )
            for half, source in enumerate((first, second))
        ]
        for copy in pair:
            copy.start()
        copies.append(pair)
    for copy in small_copies:
        copy.wait()
    keep = (mask[...] == 1) | (me < seq_count)
    keep = jnp.broadcast_to(jnp.where(keep, 1.0, 0.0), (BLK, BLK)).T.astype(jnp.bfloat16)
    keep = jnp.concatenate([keep] * (share // LANES), axis=1)
    base = here - WIN
    code = (lists[0, 0, 0] - base) * SPAN + lists[0, 0, 1] - base
    tail = jnp.full((TAIL, share), code, jnp.int32).astype(jnp.float32).astype(jnp.bfloat16)
    for out, pair in zip(outs, copies):
        for copy in pair:
            copy.wait()
        out[BLK : 2 * BLK] = out[BLK : 2 * BLK] * keep
        out[2 * BLK :] = tail


def attend_kernel(seq_count, order, source_len, target_len, *refs):
    parts = 2 * seq_count
    shares, outs = refs[:parts], refs[parts : 2 * parts]
    rows, result, key_grad, value_grad, lists = refs[2 * parts :]
    me = device_index(seq_count)
    here = me % seq_count
    for step, share in zip(order, shares):
        source = me ^ step
        rows[source, 0] = share[:BLK]
        rows[source, 1] = share[BLK : 2 * BLK]
        if step < seq_count:
            tail = share[2 * BLK :, :LANES].astype(jnp.float32)
            lists[here ^ step] = jnp.max(tail).astype(jnp.int32)

    def listed(block, slot):
        code = lists[block]
        return block - WIN + (code // SPAN if slot == 0 else code % SPAN)

    attend_sample(
        seq_count, listed, source_len[0], target_len[0], rows, result, key_grad, value_grad
    )
    for step, out in zip(order, outs):
        out[:BLK] = result[me ^ step, 0]
        out[BLK:] = result[me ^ step, 1]


def unpack_kernel(seq_count, order, *refs):
    shares, (first, second, sem) = refs[:-3], refs[-3:]
    width = shares[0].shape[1]
    me = device_index(seq_count)
    copies = []
    for slot, (step, share) in enumerate(zip(order, shares)):
        lanes = pl.ds(pl.multiple_of((me ^ step) * width, LANES), width)
        for half, result in enumerate((first, second)):
            copy = pltpu.make_async_copy(
                share.at[pl.ds(half * BLK, BLK)], result.at[0, 0, :, lanes], sem.at[half, slot]
            )
            copy.start()
            copies.append(copy)
    for copy in copies:
        copy.wait()


def swapped(shares, order, after):
    parts = len(order)
    held = dict(zip(order, shares))
    moved = {0: held[0]}
    for step in order:
        if step:
            share = held[step]
            if step in after:
                earlier = after[step]
                share, moved[earlier] = lax.optimization_barrier((share, moved[earlier]))
            moved[step] = lax.ppermute(share, AXES, [(dev, dev ^ step) for dev in range(parts)])
    return [moved[step] for step in order]


def by_pairs(first_rows, second_rows, alignment, diffusion_mask, source_length, target_length):
    seq_count = lax.axis_size("seq")
    parts = 2 * seq_count
    width = first_rows.shape[3]
    share = width // parts
    kind = first_rows.dtype
    params = pltpu.CompilerParams(vmem_limit_bytes=VMEM_LIMIT)
    order, after = list(range(parts - 1, -1, -1)), {}
    if parts == 8:
        order = [1, 6, 4, 7, 2, 5, 3, 0]
    sems = pltpu.SemaphoreType.DMA((2, parts))
    shares = pl.pallas_call(
        functools.partial(pack_kernel, seq_count, order),
        out_shape=[jax.ShapeDtypeStruct((2 * BLK + TAIL, share), kind)] * parts,
        in_specs=specs(4, pltpu.HBM),
        out_specs=specs(parts, pltpu.VMEM),
        scratch_shapes=[
            pltpu.SMEM(alignment.shape, jnp.int32),
            pltpu.VMEM(diffusion_mask.shape, jnp.int32),
            pltpu.SemaphoreType.DMA((2,)),
            sems,
        ],
        compiler_params=params,
        name="pack",
    )(*in_hbm(alignment, diffusion_mask, first_rows, second_rows))
    shares = swapped(shares, order, after)
    rows = pltpu.VMEM((parts, 2, BLK, share), kind)
    grads = pltpu.VMEM((seq_count, BLK, share), jnp.float32)
    shares = pl.pallas_call(
        functools.partial(attend_kernel, seq_count, order),
        out_shape=[jax.ShapeDtypeStruct((2 * BLK, share), kind)] * parts,
        in_specs=specs(2, pltpu.SMEM) + specs(parts, pltpu.VMEM),
        out_specs=specs(parts, pltpu.VMEM),
        scratch_shapes=[rows, rows, grads, grads, pltpu.SMEM((seq_count,), jnp.int32)],
        compiler_params=params,
        cost_estimate=attend_cost(seq_count, share),
        name="attend",
    )(source_length, target_length, *shares)
    shares = swapped(shares, order, after)
    out_shape = jax.ShapeDtypeStruct((1, 1, BLK, width), kind)
    return pl.pallas_call(
        functools.partial(unpack_kernel, seq_count, order),
        out_shape=[out_shape, out_shape],
        in_specs=specs(parts, pltpu.VMEM),
        out_specs=specs(2, pltpu.HBM),
        scratch_shapes=[sems],
        compiler_params=params,
        name="unpack",
    )(*shares)


def on_device(first_rows, second_rows, alignment, diffusion_mask, source_length, target_length):
    seq_count = lax.axis_size("seq")
    parts = lax.axis_size("section") * seq_count
    paired = (
        parts == 2 * seq_count
        and seq_count & (seq_count - 1) == 0
        and first_rows.shape[2] == BLK
        and first_rows.shape[3] % (parts * LANES) == 0
    )
    work = by_pairs if paired else by_all_to_all
    return tuple(
        work(first_rows, second_rows, alignment, diffusion_mask, source_length, target_length)
    )


def solution(mesh):
    placed = (
        P("section", "sample", "seq", None),
        P("section", "sample", "seq", None),
        P("sample", "seq", None),
        P("sample", "seq"),
        P("sample"),
        P("sample"),
    )
    return jax.shard_map(
        on_device,
        mesh=mesh,
        in_specs=placed,
        out_specs=(P("section", "sample", "seq", None), P("section", "sample", "seq", None)),
        check_vma=False,
    )
```

```python
import functools

import jax
import jax.numpy as jnp
from jax import lax
from jax.experimental import pallas as pl
from jax.experimental.pallas import tpu as pltpu
from jax.sharding import PartitionSpec as P

HDIM = 64
BLK = 128
NLIST = 2
WIN = 1
SPAN = 2 * WIN + 1
LANES = 128
TAIL = 16
SCALE = HDIM ** (-0.5)
FLOOR = -1e30
VMEM_LIMIT = 32 * 1024 * 1024
AXES = ("section", "seq")


def contract(left, right, left_dim, right_dim):
    return lax.dot_general(
        left, right, (((left_dim,), (right_dim,)), ((), ())), preferred_element_type=jnp.float32
    )


def attend_sample(
    seq_count, listed, source_len, target_len, rows, out, key_grad, value_grad, turned
):
    per_device = rows.shape[2] // BLK
    block_count = seq_count * per_device
    width = rows.shape[3]
    tile = min(width, LANES)
    heads = tile // HDIM
    key_grad[...] = jnp.zeros_like(key_grad)
    value_grad[...] = jnp.zeros_like(value_grad)
    inside = lax.broadcasted_iota(jnp.int32, (BLK, 1), 0)
    lane_head = lax.broadcasted_iota(jnp.int32, (BLK, tile), 1) // HDIM

    def place(block):
        if per_device == 1:
            return block, pl.ds(0, BLK)
        return block // per_device, pl.ds((block % per_device) * BLK, BLK)

    def own_heads(turned_result):
        return jnp.concatenate(
            [
                turned_result[head * HDIM : (head + 1) * HDIM, head * BLK : (head + 1) * BLK]
                for head in range(heads)
            ],
            axis=0,
        )

    def turn(block, carry):
        dev, here = place(block)
        for first in range(0, width, tile):
            for half in range(2):
                turned[block, half, pl.ds(first, tile)] = rows[
                    dev, half, here, pl.ds(first, tile)
                ].T
        return carry

    def step(block, carry):
        chosen = [listed(block, slot) for slot in range(NLIST)]
        places = [place(index) for index in chosen]
        target, target_rows = place(block)
        key_valid = jnp.concatenate(
            [index * BLK + inside < source_len for index in chosen], axis=0
        )
        live = block * BLK + inside < target_len
        for first in range(0, width, tile):
            lanes = pl.ds(first, tile)
            keys = jnp.concatenate([rows[dev, 0, here, lanes] for dev, here in places], axis=0)
            values = jnp.concatenate([rows[dev, 1, here, lanes] for dev, here in places], axis=0)
            queries = rows[seq_count + target, 0, target_rows, lanes] * jnp.bfloat16(SCALE)
            cots = rows[seq_count + target, 1, target_rows, lanes]
            none = jnp.zeros_like(queries)
            cots = jnp.where(live, cots, none)
            queries = jnp.concatenate(
                [jnp.where(lane_head == head, queries, none) for head in range(heads)], axis=0
            )
            cots = jnp.concatenate(
                [jnp.where(lane_head == head, cots, none) for head in range(heads)], axis=0
            )
            scores = jnp.where(key_valid, contract(keys, queries, 1, 1), FLOOR)
            expo = jnp.exp(scores - jnp.max(scores, axis=0, keepdims=True))
            probs = expo * (1.0 / jnp.sum(expo, axis=0, keepdims=True))
            dprob = contract(values, cots, 1, 1)
            delta = jnp.sum(probs * dprob, axis=0, keepdims=True)
            probs_low = probs.astype(jnp.bfloat16)
            dscore_low = (probs * (dprob - delta)).astype(jnp.bfloat16)
            dvalue = contract(probs_low, cots, 1, 0)
            dkey = contract(dscore_low, queries, 1, 0)
            keys_turned = jnp.concatenate([turned[index, 0, lanes] for index in chosen], axis=1)
            values_turned = jnp.concatenate([turned[index, 1, lanes] for index in chosen], axis=1)
            attended = own_heads(contract(values_turned, probs_low, 1, 0))
            dquery = own_heads(contract(keys_turned, dscore_low, 1, 0)) * SCALE
            attended = jnp.where(live, attended.astype(jnp.bfloat16).T, none)
            out[seq_count + target, 0, target_rows, lanes] = dquery.astype(jnp.bfloat16).T
            out[seq_count + target, 1, target_rows, lanes] = attended
            for slot, (dev, here) in enumerate(places):
                part = slice(slot * BLK, (slot + 1) * BLK)
                key_grad[dev, here, lanes] += dkey[part]
                value_grad[dev, here, lanes] += dvalue[part]
        return carry

    lax.fori_loop(0, block_count, turn, 0, unroll=block_count <= 4)
    lax.fori_loop(0, block_count, step, 0, unroll=block_count <= 4)
    out[:seq_count, 0] = key_grad[...].astype(jnp.bfloat16)
    out[:seq_count, 1] = value_grad[...].astype(jnp.bfloat16)


def attend_cost(block_count, width):
    pairs = block_count * NLIST * BLK * BLK * width
    return pl.CostEstimate(
        flops=10 * pairs,
        bytes_accessed=16 * block_count * BLK * width,
        transcendentals=pairs // HDIM,
    )


def specs(count, space):
    return [pl.BlockSpec(memory_space=space)] * count


def in_hbm(*arrays):
    return [pltpu.with_memory_space_constraint(array, pltpu.HBM) for array in arrays]


def gathered_kernel(
    seq_count, lists, source_len, target_len, rows, out, key_grad, value_grad, turned
):
    def listed(block, slot):
        return lists[block, slot]

    attend_sample(
        seq_count, listed, source_len[0], target_len[0], rows, out, key_grad, value_grad, turned
    )


def by_all_to_all(first_rows, second_rows, alignment, diffusion_mask, source_length, target_length):
    seq_count = lax.axis_size("seq")
    parts = lax.axis_size("section") * seq_count
    rows_here = first_rows.shape[2]
    width = first_rows.shape[3]
    on_encoder = lax.axis_index("section") == 0
    keep = on_encoder | (diffusion_mask[0] == 1)
    second = jnp.where(keep[:, None], second_rows[0, 0], jnp.zeros_like(second_rows[0, 0]))
    held = jnp.stack([first_rows[0, 0], second])
    held = held.reshape(2, rows_here, parts, width // parts).transpose(2, 0, 1, 3)
    lists = lax.all_gather(alignment[0], "seq", axis=0, tiled=True)
    rows = lax.all_to_all(held, AXES, 0, 0, tiled=True)
    grads = pltpu.VMEM((seq_count, rows_here, width // parts), jnp.float32)
    turned = pltpu.VMEM((lists.shape[0], 2, width // parts, BLK), rows.dtype)
    grads = pl.pallas_call(
        functools.partial(gathered_kernel, seq_count),
        out_shape=jax.ShapeDtypeStruct(rows.shape, rows.dtype),
        in_specs=specs(3, pltpu.SMEM) + specs(1, pltpu.VMEM),
        out_specs=pl.BlockSpec(memory_space=pltpu.VMEM),
        scratch_shapes=[grads, grads, turned],
        compiler_params=pltpu.CompilerParams(vmem_limit_bytes=VMEM_LIMIT),
        cost_estimate=attend_cost(lists.shape[0], width // parts),
        name="attend_gathered",
    )(lists, source_length, target_length, rows)
    grads = lax.all_to_all(grads, AXES, 0, 0, tiled=True)
    grads = grads.transpose(1, 2, 0, 3).reshape(2, rows_here, width)
    return (grads[0][None, None], grads[1][None, None])


def device_index(seq_count):
    return lax.axis_index("section") * seq_count + lax.axis_index("seq")


def pack_kernel(seq_count, order, *refs):
    smalls, (first, second) = refs[:2], refs[2:4]
    outs, (lists, mask, small_sem, sem) = refs[4:-4], refs[-4:]
    small_copies = [
        pltpu.make_async_copy(source, held, small_sem.at[slot])
        for slot, (source, held) in enumerate(zip(smalls, (lists, mask)))
    ]
    for copy in small_copies:
        copy.start()
    me = device_index(seq_count)
    here = me % seq_count
    share = outs[0].shape[1]
    copies = []
    for slot, (step, out) in enumerate(zip(order, outs)):
        lanes = pl.ds(pl.multiple_of((me ^ step) * share, LANES), share)
        pair = [
            pltpu.make_async_copy(
                source.at[0, 0, :, lanes], out.at[pl.ds(half * BLK, BLK)], sem.at[half, slot]
            )
            for half, source in enumerate((first, second))
        ]
        for copy in pair:
            copy.start()
        copies.append(pair)
    for copy in small_copies:
        copy.wait()
    keep = (mask[...] == 1) | (me < seq_count)
    keep = jnp.broadcast_to(jnp.where(keep, 1.0, 0.0), (BLK, BLK)).T.astype(jnp.bfloat16)
    keep = jnp.concatenate([keep] * (share // LANES), axis=1)
    base = here - WIN
    code = (lists[0, 0, 0] - base) * SPAN + lists[0, 0, 1] - base
    tail = jnp.full((TAIL, share), code, jnp.int32).astype(jnp.float32).astype(jnp.bfloat16)
    for out, pair in zip(outs, copies):
        for copy in pair:
            copy.wait()
        out[BLK : 2 * BLK] = out[BLK : 2 * BLK] * keep
        out[2 * BLK :] = tail


def attend_kernel(seq_count, order, source_len, target_len, *refs):
    parts = 2 * seq_count
    shares, outs = refs[:parts], refs[parts : 2 * parts]
    rows, result, key_grad, value_grad, turned, lists = refs[2 * parts :]
    me = device_index(seq_count)
    here = me % seq_count
    for step, share in zip(order, shares):
        source = me ^ step
        rows[source, 0] = share[:BLK]
        rows[source, 1] = share[BLK : 2 * BLK]
        if step < seq_count:
            tail = share[2 * BLK :, :LANES].astype(jnp.float32)
            lists[here ^ step] = jnp.max(tail).astype(jnp.int32)

    def listed(block, slot):
        code = lists[block]
        return block - WIN + (code // SPAN if slot == 0 else code % SPAN)

    attend_sample(
        seq_count,
        listed,
        source_len[0],
        target_len[0],
        rows,
        result,
        key_grad,
        value_grad,
        turned,
    )
    for step, out in zip(order, outs):
        out[:BLK] = result[me ^ step, 0]
        out[BLK:] = result[me ^ step, 1]


def unpack_kernel(seq_count, order, *refs):
    shares, (first, second, sem) = refs[:-3], refs[-3:]
    width = shares[0].shape[1]
    me = device_index(seq_count)
    copies = []
    for slot, (step, share) in enumerate(zip(order, shares)):
        lanes = pl.ds(pl.multiple_of((me ^ step) * width, LANES), width)
        for half, result in enumerate((first, second)):
            copy = pltpu.make_async_copy(
                share.at[pl.ds(half * BLK, BLK)], result.at[0, 0, :, lanes], sem.at[half, slot]
            )
            copy.start()
            copies.append(copy)
    for copy in copies:
        copy.wait()


def swapped(shares, order, after):
    parts = len(order)
    held = dict(zip(order, shares))
    moved = {0: held[0]}
    for step in order:
        if step:
            share = held[step]
            if step in after:
                earlier = after[step]
                share, moved[earlier] = lax.optimization_barrier((share, moved[earlier]))
            moved[step] = lax.ppermute(share, AXES, [(dev, dev ^ step) for dev in range(parts)])
    return [moved[step] for step in order]


def by_pairs(first_rows, second_rows, alignment, diffusion_mask, source_length, target_length):
    seq_count = lax.axis_size("seq")
    parts = 2 * seq_count
    width = first_rows.shape[3]
    share = width // parts
    kind = first_rows.dtype
    params = pltpu.CompilerParams(vmem_limit_bytes=VMEM_LIMIT)
    order, after = list(range(parts - 1, -1, -1)), {}
    if parts == 8:
        order = [6, 7, 4, 5, 2, 3, 1, 0]
    sems = pltpu.SemaphoreType.DMA((2, parts))
    shares = pl.pallas_call(
        functools.partial(pack_kernel, seq_count, order),
        out_shape=[jax.ShapeDtypeStruct((2 * BLK + TAIL, share), kind)] * parts,
        in_specs=specs(4, pltpu.HBM),
        out_specs=specs(parts, pltpu.VMEM),
        scratch_shapes=[
            pltpu.SMEM(alignment.shape, jnp.int32),
            pltpu.VMEM(diffusion_mask.shape, jnp.int32),
            pltpu.SemaphoreType.DMA((2,)),
            sems,
        ],
        compiler_params=params,
        name="pack",
    )(*in_hbm(alignment, diffusion_mask, first_rows, second_rows))
    shares = swapped(shares, order, after)
    rows = pltpu.VMEM((parts, 2, BLK, share), kind)
    grads = pltpu.VMEM((seq_count, BLK, share), jnp.float32)
    turned = pltpu.VMEM((seq_count, 2, share, BLK), kind)
    shares = pl.pallas_call(
        functools.partial(attend_kernel, seq_count, order),
        out_shape=[jax.ShapeDtypeStruct((2 * BLK, share), kind)] * parts,
        in_specs=specs(2, pltpu.SMEM) + specs(parts, pltpu.VMEM),
        out_specs=specs(parts, pltpu.VMEM),
        scratch_shapes=[rows, rows, grads, grads, turned, pltpu.SMEM((seq_count,), jnp.int32)],
        compiler_params=params,
        cost_estimate=attend_cost(seq_count, share),
        name="attend",
    )(source_length, target_length, *shares)
    shares = swapped(shares, order, after)
    out_shape = jax.ShapeDtypeStruct((1, 1, BLK, width), kind)
    return pl.pallas_call(
        functools.partial(unpack_kernel, seq_count, order),
        out_shape=[out_shape, out_shape],
        in_specs=specs(parts, pltpu.VMEM),
        out_specs=specs(2, pltpu.HBM),
        scratch_shapes=[sems],
        compiler_params=params,
        name="unpack",
    )(*shares)


def on_device(first_rows, second_rows, alignment, diffusion_mask, source_length, target_length):
    seq_count = lax.axis_size("seq")
    parts = lax.axis_size("section") * seq_count
    paired = (
        parts == 2 * seq_count
        and seq_count & (seq_count - 1) == 0
        and first_rows.shape[2] == BLK
        and first_rows.shape[3] % (parts * LANES) == 0
    )
    work = by_pairs if paired else by_all_to_all
    return tuple(
        work(first_rows, second_rows, alignment, diffusion_mask, source_length, target_length)
    )


def solution(mesh):
    placed = (
        P("section", "sample", "seq", None),
        P("section", "sample", "seq", None),
        P("sample", "seq", None),
        P("sample", "seq"),
        P("sample"),
        P("sample"),
    )
    return jax.shard_map(
        on_device,
        mesh=mesh,
        in_specs=placed,
        out_specs=(P("section", "sample", "seq", None), P("section", "sample", "seq", None)),
        check_vma=False,
    )
```

```python
import functools

import jax
import jax.numpy as jnp
from jax import lax
from jax.experimental import pallas as pl
from jax.experimental.pallas import tpu as pltpu
from jax.sharding import PartitionSpec as P

HDIM = 64
BLK = 128
NLIST = 2
WIN = 1
SPAN = 2 * WIN + 1
LANES = 128
TAIL = 16
SCALE = HDIM ** (-0.5)
FLOOR = -1e30
VMEM_LIMIT = 32 * 1024 * 1024
AXES = ("section", "seq")


def contract(left, right, left_dim, right_dim):
    return lax.dot_general(
        left, right, (((left_dim,), (right_dim,)), ((), ())), preferred_element_type=jnp.float32
    )


def attend_sample(
    seq_count, listed, source_len, target_len, rows, out, key_grad, value_grad, turned
):
    per_device = rows.shape[2] // BLK
    block_count = seq_count * per_device
    width = rows.shape[3]
    tile = min(width, LANES)
    heads = tile // HDIM
    key_grad[...] = jnp.zeros_like(key_grad)
    value_grad[...] = jnp.zeros_like(value_grad)
    inside = lax.broadcasted_iota(jnp.int32, (BLK, 1), 0)
    lane_head = lax.broadcasted_iota(jnp.int32, (BLK, tile), 1) // HDIM

    def place(block):
        if per_device == 1:
            return block, pl.ds(0, BLK)
        return block // per_device, pl.ds((block % per_device) * BLK, BLK)

    def own_heads(turned_result):
        return jnp.concatenate(
            [
                turned_result[head * HDIM : (head + 1) * HDIM, head * BLK : (head + 1) * BLK]
                for head in range(heads)
            ],
            axis=0,
        )

    def turn(block, carry):
        dev, here = place(block)
        for first in range(0, width, tile):
            for half in range(2):
                turned[block, half, pl.ds(first, tile)] = rows[
                    dev, half, here, pl.ds(first, tile)
                ].T
        return carry

    def step(block, carry):
        chosen = [listed(block, slot) for slot in range(NLIST)]
        places = [place(index) for index in chosen]
        target, target_rows = place(block)
        key_valid = jnp.concatenate(
            [index * BLK + inside < source_len for index in chosen], axis=0
        )
        live = block * BLK + inside < target_len
        for first in range(0, width, tile):
            lanes = pl.ds(first, tile)
            keys = jnp.concatenate([rows[dev, 0, here, lanes] for dev, here in places], axis=0)
            values = jnp.concatenate([rows[dev, 1, here, lanes] for dev, here in places], axis=0)
            queries = rows[seq_count + target, 0, target_rows, lanes] * jnp.bfloat16(SCALE)
            cots = rows[seq_count + target, 1, target_rows, lanes]
            none = jnp.zeros_like(queries)
            cots = jnp.where(live, cots, none)
            queries = jnp.concatenate(
                [jnp.where(lane_head == head, queries, none) for head in range(heads)], axis=0
            )
            cots = jnp.concatenate(
                [jnp.where(lane_head == head, cots, none) for head in range(heads)], axis=0
            )
            scores = contract(keys, queries, 1, 1)
            dprob = contract(values, cots, 1, 1)
            probs_low, dscore_low = [], []
            for head in range(heads):
                part = slice(head * BLK, (head + 1) * BLK)
                mine = jnp.where(key_valid, scores[:, part], FLOOR)
                expo = jnp.exp(mine - jnp.max(mine, axis=0, keepdims=True))
                probs = expo * (1.0 / jnp.sum(expo, axis=0, keepdims=True))
                delta = jnp.sum(probs * dprob[:, part], axis=0, keepdims=True)
                dscore = probs * (dprob[:, part] - delta)
                probs_low.append(probs.astype(jnp.bfloat16))
                dscore_low.append(dscore.astype(jnp.bfloat16))
            probs_low = jnp.concatenate(probs_low, axis=1)
            dscore_low = jnp.concatenate(dscore_low, axis=1)
            dvalue = contract(probs_low, cots, 1, 0)
            dkey = contract(dscore_low, queries, 1, 0)
            keys_turned = jnp.concatenate([turned[index, 0, lanes] for index in chosen], axis=1)
            values_turned = jnp.concatenate([turned[index, 1, lanes] for index in chosen], axis=1)
            attended = own_heads(contract(values_turned, probs_low, 1, 0))
            dquery = own_heads(contract(keys_turned, dscore_low, 1, 0)) * SCALE
            attended = jnp.where(live, attended.astype(jnp.bfloat16).T, none)
            out[seq_count + target, 0, target_rows, lanes] = dquery.astype(jnp.bfloat16).T
            out[seq_count + target, 1, target_rows, lanes] = attended
            for slot, (dev, here) in enumerate(places):
                part = slice(slot * BLK, (slot + 1) * BLK)
                key_grad[dev, here, lanes] += dkey[part]
                value_grad[dev, here, lanes] += dvalue[part]
        return carry

    lax.fori_loop(0, block_count, turn, 0, unroll=block_count <= 4)
    lax.fori_loop(0, block_count, step, 0, unroll=block_count <= 4)
    out[:seq_count, 0] = key_grad[...].astype(jnp.bfloat16)
    out[:seq_count, 1] = value_grad[...].astype(jnp.bfloat16)


def attend_cost(block_count, width):
    pairs = block_count * NLIST * BLK * BLK * width
    return pl.CostEstimate(
        flops=10 * pairs,
        bytes_accessed=16 * block_count * BLK * width,
        transcendentals=pairs // HDIM,
    )


def specs(count, space):
    return [pl.BlockSpec(memory_space=space)] * count


def in_hbm(*arrays):
    return [pltpu.with_memory_space_constraint(array, pltpu.HBM) for array in arrays]


def gathered_kernel(
    seq_count, lists, source_len, target_len, rows, out, key_grad, value_grad, turned
):
    def listed(block, slot):
        return lists[block, slot]

    attend_sample(
        seq_count, listed, source_len[0], target_len[0], rows, out, key_grad, value_grad, turned
    )


def by_all_to_all(first_rows, second_rows, alignment, diffusion_mask, source_length, target_length):
    seq_count = lax.axis_size("seq")
    parts = lax.axis_size("section") * seq_count
    rows_here = first_rows.shape[2]
    width = first_rows.shape[3]
    on_encoder = lax.axis_index("section") == 0
    keep = on_encoder | (diffusion_mask[0] == 1)
    second = jnp.where(keep[:, None], second_rows[0, 0], jnp.zeros_like(second_rows[0, 0]))
    held = jnp.stack([first_rows[0, 0], second])
    held = held.reshape(2, rows_here, parts, width // parts).transpose(2, 0, 1, 3)
    lists = lax.all_gather(alignment[0], "seq", axis=0, tiled=True)
    rows = lax.all_to_all(held, AXES, 0, 0, tiled=True)
    grads = pltpu.VMEM((seq_count, rows_here, width // parts), jnp.float32)
    turned = pltpu.VMEM((lists.shape[0], 2, width // parts, BLK), rows.dtype)
    grads = pl.pallas_call(
        functools.partial(gathered_kernel, seq_count),
        out_shape=jax.ShapeDtypeStruct(rows.shape, rows.dtype),
        in_specs=specs(3, pltpu.SMEM) + specs(1, pltpu.VMEM),
        out_specs=pl.BlockSpec(memory_space=pltpu.VMEM),
        scratch_shapes=[grads, grads, turned],
        compiler_params=pltpu.CompilerParams(vmem_limit_bytes=VMEM_LIMIT),
        cost_estimate=attend_cost(lists.shape[0], width // parts),
        name="attend_gathered",
    )(lists, source_length, target_length, rows)
    grads = lax.all_to_all(grads, AXES, 0, 0, tiled=True)
    grads = grads.transpose(1, 2, 0, 3).reshape(2, rows_here, width)
    return (grads[0][None, None], grads[1][None, None])


def device_index(seq_count):
    return lax.axis_index("section") * seq_count + lax.axis_index("seq")


def pack_kernel(seq_count, order, *refs):
    smalls, (first, second) = refs[:2], refs[2:4]
    outs, (lists, mask, small_sem, sem) = refs[4:-4], refs[-4:]
    small_copies = [
        pltpu.make_async_copy(source, held, small_sem.at[slot])
        for slot, (source, held) in enumerate(zip(smalls, (lists, mask)))
    ]
    for copy in small_copies:
        copy.start()
    me = device_index(seq_count)
    here = me % seq_count
    share = outs[0].shape[1]
    copies = []
    for slot, (step, out) in enumerate(zip(order, outs)):
        lanes = pl.ds(pl.multiple_of((me ^ step) * share, LANES), share)
        pair = [
            pltpu.make_async_copy(
                source.at[0, 0, :, lanes], out.at[pl.ds(half * BLK, BLK)], sem.at[half, slot]
            )
            for half, source in enumerate((first, second))
        ]
        for copy in pair:
            copy.start()
        copies.append(pair)
    for copy in small_copies:
        copy.wait()
    keep = (mask[...] == 1) | (me < seq_count)
    keep = jnp.broadcast_to(jnp.where(keep, 1.0, 0.0), (BLK, BLK)).T.astype(jnp.bfloat16)
    keep = jnp.concatenate([keep] * (share // LANES), axis=1)
    base = here - WIN
    code = (lists[0, 0, 0] - base) * SPAN + lists[0, 0, 1] - base
    tail = jnp.full((TAIL, share), code, jnp.int32).astype(jnp.float32).astype(jnp.bfloat16)
    for out, pair in zip(outs, copies):
        for copy in pair:
            copy.wait()
        out[BLK : 2 * BLK] = out[BLK : 2 * BLK] * keep
        out[2 * BLK :] = tail


def attend_kernel(seq_count, order, back, source_len, target_len, *refs):
    parts = 2 * seq_count
    shares, outs = refs[:parts], refs[parts : 2 * parts]
    rows, result, key_grad, value_grad, turned, lists = refs[2 * parts :]
    me = device_index(seq_count)
    here = me % seq_count
    for step, share in zip(order, shares):
        source = me ^ step
        rows[source, 0] = share[:BLK]
        rows[source, 1] = share[BLK : 2 * BLK]
        if step < seq_count:
            tail = share[2 * BLK :, :LANES].astype(jnp.float32)
            lists[here ^ step] = jnp.max(tail).astype(jnp.int32)

    def listed(block, slot):
        code = lists[block]
        return block - WIN + (code // SPAN if slot == 0 else code % SPAN)

    attend_sample(
        seq_count,
        listed,
        source_len[0],
        target_len[0],
        rows,
        result,
        key_grad,
        value_grad,
        turned,
    )
    for step, out in zip(back, outs):
        out[:BLK] = result[me ^ step, 0]
        out[BLK:] = result[me ^ step, 1]


def unpack_kernel(seq_count, order, *refs):
    shares, (first, second, sem) = refs[:-3], refs[-3:]
    width = shares[0].shape[1]
    me = device_index(seq_count)
    copies = []
    for slot, (step, share) in enumerate(zip(order, shares)):
        lanes = pl.ds(pl.multiple_of((me ^ step) * width, LANES), width)
        for half, result in enumerate((first, second)):
            copy = pltpu.make_async_copy(
                share.at[pl.ds(half * BLK, BLK)], result.at[0, 0, :, lanes], sem.at[half, slot]
            )
            copy.start()
            copies.append(copy)
    for copy in copies:
        copy.wait()


def swapped(shares, order):
    parts = len(order)
    return [
        lax.ppermute(share, AXES, [(dev, dev ^ step) for dev in range(parts)]) if step else share
        for step, share in zip(order, shares)
    ]


def by_pairs(first_rows, second_rows, alignment, diffusion_mask, source_length, target_length):
    seq_count = lax.axis_size("seq")
    parts = 2 * seq_count
    width = first_rows.shape[3]
    share = width // parts
    kind = first_rows.dtype
    params = pltpu.CompilerParams(vmem_limit_bytes=VMEM_LIMIT)
    order = back = list(range(parts - 1, -1, -1))
    if parts == 8:
        order, back = [6, 4, 7, 5, 2, 3, 1, 0], [1, 4, 6, 7, 2, 3, 5, 0]
    sems = pltpu.SemaphoreType.DMA((2, parts))
    shares = pl.pallas_call(
        functools.partial(pack_kernel, seq_count, order),
        out_shape=[jax.ShapeDtypeStruct((2 * BLK + TAIL, share), kind)] * parts,
        in_specs=specs(4, pltpu.HBM),
        out_specs=specs(parts, pltpu.VMEM),
        scratch_shapes=[
            pltpu.SMEM(alignment.shape, jnp.int32),
            pltpu.VMEM(diffusion_mask.shape, jnp.int32),
            pltpu.SemaphoreType.DMA((2,)),
            sems,
        ],
        compiler_params=params,
        name="pack",
    )(*in_hbm(alignment, diffusion_mask, first_rows, second_rows))
    shares = swapped(shares, order)
    rows = pltpu.VMEM((parts, 2, BLK, share), kind)
    grads = pltpu.VMEM((seq_count, BLK, share), jnp.float32)
    turned = pltpu.VMEM((seq_count, 2, share, BLK), kind)
    shares = pl.pallas_call(
        functools.partial(attend_kernel, seq_count, order, back),
        out_shape=[jax.ShapeDtypeStruct((2 * BLK, share), kind)] * parts,
        in_specs=specs(2, pltpu.SMEM) + specs(parts, pltpu.VMEM),
        out_specs=specs(parts, pltpu.VMEM),
        scratch_shapes=[rows, rows, grads, grads, turned, pltpu.SMEM((seq_count,), jnp.int32)],
        compiler_params=params,
        cost_estimate=attend_cost(seq_count, share),
        name="attend",
    )(source_length, target_length, *shares)
    shares = swapped(shares, back)
    out_shape = jax.ShapeDtypeStruct((1, 1, BLK, width), kind)
    return pl.pallas_call(
        functools.partial(unpack_kernel, seq_count, back),
        out_shape=[out_shape, out_shape],
        in_specs=specs(parts, pltpu.VMEM),
        out_specs=specs(2, pltpu.HBM),
        scratch_shapes=[sems],
        compiler_params=params,
        name="unpack",
    )(*shares)


def on_device(first_rows, second_rows, alignment, diffusion_mask, source_length, target_length):
    seq_count = lax.axis_size("seq")
    parts = lax.axis_size("section") * seq_count
    paired = (
        parts == 2 * seq_count
        and seq_count & (seq_count - 1) == 0
        and first_rows.shape[2] == BLK
        and first_rows.shape[3] % (parts * LANES) == 0
    )
    work = by_pairs if paired else by_all_to_all
    return tuple(
        work(first_rows, second_rows, alignment, diffusion_mask, source_length, target_length)
    )


def solution(mesh):
    placed = (
        P("section", "sample", "seq", None),
        P("section", "sample", "seq", None),
        P("sample", "seq", None),
        P("sample", "seq"),
        P("sample"),
        P("sample"),
    )
    return jax.shard_map(
        on_device,
        mesh=mesh,
        in_specs=placed,
        out_specs=(P("section", "sample", "seq", None), P("section", "sample", "seq", None)),
        check_vma=False,
    )
```

```python
import functools

import jax
import jax.numpy as jnp
from jax import lax
from jax.experimental import pallas as pl
from jax.experimental.pallas import tpu as pltpu
from jax.sharding import PartitionSpec as P

HDIM = 64
BLK = 128
NLIST = 2
WIN = 1
SPAN = 2 * WIN + 1
LANES = 128
TAIL = 16
SCALE = HDIM ** (-0.5)
FLOOR = -1e30
VMEM_LIMIT = 32 * 1024 * 1024
AXES = ("section", "seq")


def contract(left, right, left_dim, right_dim):
    return lax.dot_general(
        left, right, (((left_dim,), (right_dim,)), ((), ())), preferred_element_type=jnp.float32
    )


def attend_sample(
    seq_count, listed, source_len, target_len, rows, out, key_grad, value_grad, turned
):
    per_device = rows.shape[2] // BLK
    block_count = seq_count * per_device
    width = rows.shape[3]
    tile = min(width, LANES)
    heads = tile // HDIM
    key_grad[...] = jnp.zeros_like(key_grad)
    value_grad[...] = jnp.zeros_like(value_grad)
    inside = lax.broadcasted_iota(jnp.int32, (BLK, 1), 0)
    inside_turned = lax.broadcasted_iota(jnp.int32, (1, BLK), 1)
    lane_head = lax.broadcasted_iota(jnp.int32, (BLK, tile), 1) // HDIM
    row_head = lax.broadcasted_iota(jnp.int32, (tile, BLK), 0) // HDIM

    def place(block):
        if per_device == 1:
            return block, pl.ds(0, BLK)
        return block // per_device, pl.ds((block % per_device) * BLK, BLK)

    def own_heads(turned_result):
        return jnp.concatenate(
            [
                turned_result[head * HDIM : (head + 1) * HDIM, head * BLK : (head + 1) * BLK]
                for head in range(heads)
            ],
            axis=0,
        )

    def turn(block, carry):
        dev, here = place(block)
        for first in range(0, width, tile):
            lanes = pl.ds(first, tile)
            for kind in range(4):
                section, half = divmod(kind, 2)
                turned[block, kind, lanes] = rows[section * seq_count + dev, half, here, lanes].T
        return carry

    def step(block, carry):
        chosen = [listed(block, slot) for slot in range(NLIST)]
        places = [place(index) for index in chosen]
        target, target_rows = place(block)
        key_valid = jnp.concatenate(
            [index * BLK + inside < source_len for index in chosen], axis=0
        )
        live = block * BLK + inside < target_len
        live_turned = block * BLK + inside_turned < target_len
        for first in range(0, width, tile):
            lanes = pl.ds(first, tile)
            keys = jnp.concatenate([rows[dev, 0, here, lanes] for dev, here in places], axis=0)
            values = jnp.concatenate([rows[dev, 1, here, lanes] for dev, here in places], axis=0)
            queries = rows[seq_count + target, 0, target_rows, lanes] * jnp.bfloat16(SCALE)
            cots = rows[seq_count + target, 1, target_rows, lanes]
            none = jnp.zeros_like(queries)
            none_turned = jnp.zeros((tile, BLK), queries.dtype)
            cots = jnp.where(live, cots, none)
            queries = jnp.concatenate(
                [jnp.where(lane_head == head, queries, none) for head in range(heads)], axis=0
            )
            cots = jnp.concatenate(
                [jnp.where(lane_head == head, cots, none) for head in range(heads)], axis=0
            )
            queries_turned = turned[block, 2, lanes] * jnp.bfloat16(SCALE)
            cots_turned = jnp.where(live_turned, turned[block, 3, lanes], none_turned)
            queries_turned = jnp.concatenate(
                [jnp.where(row_head == head, queries_turned, none_turned) for head in range(heads)],
                axis=1,
            )
            cots_turned = jnp.concatenate(
                [jnp.where(row_head == head, cots_turned, none_turned) for head in range(heads)],
                axis=1,
            )
            scores = jnp.where(key_valid, contract(keys, queries_turned, 1, 0), FLOOR)
            expo = jnp.exp(scores - jnp.max(scores, axis=0, keepdims=True))
            probs = expo * (1.0 / jnp.sum(expo, axis=0, keepdims=True))
            dprob = contract(values, cots_turned, 1, 0)
            delta = jnp.sum(probs * dprob, axis=0, keepdims=True)
            probs_low = probs.astype(jnp.bfloat16)
            dscore_low = (probs * (dprob - delta)).astype(jnp.bfloat16)
            dvalue = contract(probs_low, cots, 1, 0)
            dkey = contract(dscore_low, queries, 1, 0)
            keys_turned = jnp.concatenate([turned[index, 0, lanes] for index in chosen], axis=1)
            values_turned = jnp.concatenate([turned[index, 1, lanes] for index in chosen], axis=1)
            attended = own_heads(contract(values_turned, probs_low, 1, 0))
            dquery = own_heads(contract(keys_turned, dscore_low, 1, 0)) * SCALE
            attended = jnp.where(live, attended.astype(jnp.bfloat16).T, none)
            out[seq_count + target, 0, target_rows, lanes] = dquery.astype(jnp.bfloat16).T
            out[seq_count + target, 1, target_rows, lanes] = attended
            for slot, (dev, here) in enumerate(places):
                part = slice(slot * BLK, (slot + 1) * BLK)
                key_grad[dev, here, lanes] += dkey[part]
                value_grad[dev, here, lanes] += dvalue[part]
        return carry

    lax.fori_loop(0, block_count, turn, 0, unroll=block_count <= 4)
    lax.fori_loop(0, block_count, step, 0, unroll=block_count <= 4)
    out[:seq_count, 0] = key_grad[...].astype(jnp.bfloat16)
    out[:seq_count, 1] = value_grad[...].astype(jnp.bfloat16)


def attend_cost(block_count, width):
    pairs = block_count * NLIST * BLK * BLK * width
    return pl.CostEstimate(
        flops=10 * pairs,
        bytes_accessed=16 * block_count * BLK * width,
        transcendentals=pairs // HDIM,
    )


def specs(count, space):
    return [pl.BlockSpec(memory_space=space)] * count


def in_hbm(*arrays):
    return [pltpu.with_memory_space_constraint(array, pltpu.HBM) for array in arrays]


def gathered_kernel(
    seq_count, lists, source_len, target_len, rows, out, key_grad, value_grad, turned
):
    def listed(block, slot):
        return lists[block, slot]

    attend_sample(
        seq_count, listed, source_len[0], target_len[0], rows, out, key_grad, value_grad, turned
    )


def by_all_to_all(first_rows, second_rows, alignment, diffusion_mask, source_length, target_length):
    seq_count = lax.axis_size("seq")
    parts = lax.axis_size("section") * seq_count
    rows_here = first_rows.shape[2]
    width = first_rows.shape[3]
    on_encoder = lax.axis_index("section") == 0
    keep = on_encoder | (diffusion_mask[0] == 1)
    second = jnp.where(keep[:, None], second_rows[0, 0], jnp.zeros_like(second_rows[0, 0]))
    held = jnp.stack([first_rows[0, 0], second])
    held = held.reshape(2, rows_here, parts, width // parts).transpose(2, 0, 1, 3)
    lists = lax.all_gather(alignment[0], "seq", axis=0, tiled=True)
    rows = lax.all_to_all(held, AXES, 0, 0, tiled=True)
    grads = pltpu.VMEM((seq_count, rows_here, width // parts), jnp.float32)
    turned = pltpu.VMEM((lists.shape[0], 4, width // parts, BLK), rows.dtype)
    grads = pl.pallas_call(
        functools.partial(gathered_kernel, seq_count),
        out_shape=jax.ShapeDtypeStruct(rows.shape, rows.dtype),
        in_specs=specs(3, pltpu.SMEM) + specs(1, pltpu.VMEM),
        out_specs=pl.BlockSpec(memory_space=pltpu.VMEM),
        scratch_shapes=[grads, grads, turned],
        compiler_params=pltpu.CompilerParams(vmem_limit_bytes=VMEM_LIMIT),
        cost_estimate=attend_cost(lists.shape[0], width // parts),
        name="attend_gathered",
    )(lists, source_length, target_length, rows)
    grads = lax.all_to_all(grads, AXES, 0, 0, tiled=True)
    grads = grads.transpose(1, 2, 0, 3).reshape(2, rows_here, width)
    return (grads[0][None, None], grads[1][None, None])


def device_index(seq_count):
    return lax.axis_index("section") * seq_count + lax.axis_index("seq")


def pack_kernel(seq_count, order, *refs):
    smalls, (first, second) = refs[:2], refs[2:4]
    outs, (lists, mask, small_sem, sem) = refs[4:-4], refs[-4:]
    small_copies = [
        pltpu.make_async_copy(source, held, small_sem.at[slot])
        for slot, (source, held) in enumerate(zip(smalls, (lists, mask)))
    ]
    for copy in small_copies:
        copy.start()
    me = device_index(seq_count)
    here = me % seq_count
    share = outs[0].shape[1]
    copies = []
    for slot, (step, out) in enumerate(zip(order, outs)):
        lanes = pl.ds(pl.multiple_of((me ^ step) * share, LANES), share)
        pair = [
            pltpu.make_async_copy(
                source.at[0, 0, :, lanes], out.at[pl.ds(half * BLK, BLK)], sem.at[half, slot]
            )
            for half, source in enumerate((first, second))
        ]
        for copy in pair:
            copy.start()
        copies.append(pair)
    for copy in small_copies:
        copy.wait()
    keep = (mask[...] == 1) | (me < seq_count)
    keep = jnp.broadcast_to(jnp.where(keep, 1.0, 0.0), (BLK, BLK)).T.astype(jnp.bfloat16)
    keep = jnp.concatenate([keep] * (share // LANES), axis=1)
    base = here - WIN
    code = (lists[0, 0, 0] - base) * SPAN + lists[0, 0, 1] - base
    tail = jnp.full((TAIL, share), code, jnp.int32).astype(jnp.float32).astype(jnp.bfloat16)
    for out, pair in zip(outs, copies):
        for copy in pair:
            copy.wait()
        out[BLK : 2 * BLK] = out[BLK : 2 * BLK] * keep
        out[2 * BLK :] = tail


def attend_kernel(seq_count, order, source_len, target_len, *refs):
    parts = 2 * seq_count
    shares, outs = refs[:parts], refs[parts : 2 * parts]
    rows, result, key_grad, value_grad, turned, lists = refs[2 * parts :]
    me = device_index(seq_count)
    here = me % seq_count
    for step, share in zip(order, shares):
        source = me ^ step
        rows[source, 0] = share[:BLK]
        rows[source, 1] = share[BLK : 2 * BLK]
        if step < seq_count:
            tail = share[2 * BLK :, :LANES].astype(jnp.float32)
            lists[here ^ step] = jnp.max(tail).astype(jnp.int32)

    def listed(block, slot):
        code = lists[block]
        return block - WIN + (code // SPAN if slot == 0 else code % SPAN)

    attend_sample(
        seq_count,
        listed,
        source_len[0],
        target_len[0],
        rows,
        result,
        key_grad,
        value_grad,
        turned,
    )
    for step, out in zip(order, outs):
        out[:BLK] = result[me ^ step, 0]
        out[BLK:] = result[me ^ step, 1]


def unpack_kernel(seq_count, order, *refs):
    shares, (first, second, sem) = refs[:-3], refs[-3:]
    width = shares[0].shape[1]
    me = device_index(seq_count)
    copies = []
    for slot, (step, share) in enumerate(zip(order, shares)):
        lanes = pl.ds(pl.multiple_of((me ^ step) * width, LANES), width)
        for half, result in enumerate((first, second)):
            copy = pltpu.make_async_copy(
                share.at[pl.ds(half * BLK, BLK)], result.at[0, 0, :, lanes], sem.at[half, slot]
            )
            copy.start()
            copies.append(copy)
    for copy in copies:
        copy.wait()


def swapped(shares, order, after):
    parts = len(order)
    held = dict(zip(order, shares))
    moved = {0: held[0]}
    for step in order:
        if step:
            share = held[step]
            if step in after:
                earlier = after[step]
                share, moved[earlier] = lax.optimization_barrier((share, moved[earlier]))
            moved[step] = lax.ppermute(share, AXES, [(dev, dev ^ step) for dev in range(parts)])
    return [moved[step] for step in order]


def by_pairs(first_rows, second_rows, alignment, diffusion_mask, source_length, target_length):
    seq_count = lax.axis_size("seq")
    parts = 2 * seq_count
    width = first_rows.shape[3]
    share = width // parts
    kind = first_rows.dtype
    params = pltpu.CompilerParams(vmem_limit_bytes=VMEM_LIMIT)
    order, after = list(range(parts - 1, -1, -1)), {}
    if parts == 8:
        order = [6, 4, 7, 5, 2, 3, 1, 0]
    sems = pltpu.SemaphoreType.DMA((2, parts))
    shares = pl.pallas_call(
        functools.partial(pack_kernel, seq_count, order),
        out_shape=[jax.ShapeDtypeStruct((2 * BLK + TAIL, share), kind)] * parts,
        in_specs=specs(4, pltpu.HBM),
        out_specs=specs(parts, pltpu.VMEM),
        scratch_shapes=[
            pltpu.SMEM(alignment.shape, jnp.int32),
            pltpu.VMEM(diffusion_mask.shape, jnp.int32),
            pltpu.SemaphoreType.DMA((2,)),
            sems,
        ],
        compiler_params=params,
        name="pack",
    )(*in_hbm(alignment, diffusion_mask, first_rows, second_rows))
    shares = swapped(shares, order, after)
    rows = pltpu.VMEM((parts, 2, BLK, share), kind)
    grads = pltpu.VMEM((seq_count, BLK, share), jnp.float32)
    turned = pltpu.VMEM((seq_count, 4, share, BLK), kind)
    shares = pl.pallas_call(
        functools.partial(attend_kernel, seq_count, order),
        out_shape=[jax.ShapeDtypeStruct((2 * BLK, share), kind)] * parts,
        in_specs=specs(2, pltpu.SMEM) + specs(parts, pltpu.VMEM),
        out_specs=specs(parts, pltpu.VMEM),
        scratch_shapes=[rows, rows, grads, grads, turned, pltpu.SMEM((seq_count,), jnp.int32)],
        compiler_params=params,
        cost_estimate=attend_cost(seq_count, share),
        name="attend",
    )(source_length, target_length, *shares)
    shares = swapped(shares, order, after)
    out_shape = jax.ShapeDtypeStruct((1, 1, BLK, width), kind)
    return pl.pallas_call(
        functools.partial(unpack_kernel, seq_count, order),
        out_shape=[out_shape, out_shape],
        in_specs=specs(parts, pltpu.VMEM),
        out_specs=specs(2, pltpu.HBM),
        scratch_shapes=[sems],
        compiler_params=params,
        name="unpack",
    )(*shares)


def on_device(first_rows, second_rows, alignment, diffusion_mask, source_length, target_length):
    seq_count = lax.axis_size("seq")
    parts = lax.axis_size("section") * seq_count
    paired = (
        parts == 2 * seq_count
        and seq_count & (seq_count - 1) == 0
        and first_rows.shape[2] == BLK
        and first_rows.shape[3] % (parts * LANES) == 0
    )
    work = by_pairs if paired else by_all_to_all
    return tuple(
        work(first_rows, second_rows, alignment, diffusion_mask, source_length, target_length)
    )


def solution(mesh):
    placed = (
        P("section", "sample", "seq", None),
        P("section", "sample", "seq", None),
        P("sample", "seq", None),
        P("sample", "seq"),
        P("sample"),
        P("sample"),
    )
    return jax.shard_map(
        on_device,
        mesh=mesh,
        in_specs=placed,
        out_specs=(P("section", "sample", "seq", None), P("section", "sample", "seq", None)),
        check_vma=False,
    )
```

```python
import functools

import jax
import jax.numpy as jnp
from jax import lax
from jax.experimental import pallas as pl
from jax.experimental.pallas import tpu as pltpu
from jax.sharding import PartitionSpec as P

HDIM = 64
BLK = 128
NLIST = 2
WIN = 1
SPAN = 2 * WIN + 1
LANES = 128
TAIL = 16
FLIGHTS = 5
SCALE = HDIM ** (-0.5)
FLOOR = -1e30
VMEM_LIMIT = 32 * 1024 * 1024
AXES = ("section", "seq")


def contract(left, right, left_dim, right_dim):
    return lax.dot_general(
        left, right, (((left_dim,), (right_dim,)), ((), ())), preferred_element_type=jnp.float32
    )


def attend_sample(
    seq_count, listed, source_len, target_len, rows, out, key_grad, value_grad, turned
):
    per_device = rows.shape[2] // BLK
    block_count = seq_count * per_device
    width = rows.shape[3]
    tile = min(width, LANES)
    heads = tile // HDIM
    key_grad[...] = jnp.zeros_like(key_grad)
    value_grad[...] = jnp.zeros_like(value_grad)
    inside = lax.broadcasted_iota(jnp.int32, (BLK, 1), 0)
    lane_head = lax.broadcasted_iota(jnp.int32, (BLK, tile), 1) // HDIM

    def place(block):
        if per_device == 1:
            return block, pl.ds(0, BLK)
        return block // per_device, pl.ds((block % per_device) * BLK, BLK)

    def own_heads(turned_result):
        return jnp.concatenate(
            [
                turned_result[head * HDIM : (head + 1) * HDIM, head * BLK : (head + 1) * BLK]
                for head in range(heads)
            ],
            axis=0,
        )

    def turn(block, carry):
        dev, here = place(block)
        for first in range(0, width, tile):
            for half in range(2):
                turned[block, half, pl.ds(first, tile)] = rows[
                    dev, half, here, pl.ds(first, tile)
                ].T
        return carry

    def step(block, carry):
        chosen = [listed(block, slot) for slot in range(NLIST)]
        places = [place(index) for index in chosen]
        target, target_rows = place(block)
        key_valid = jnp.concatenate(
            [index * BLK + inside < source_len for index in chosen], axis=0
        )
        live = block * BLK + inside < target_len
        for first in range(0, width, tile):
            lanes = pl.ds(first, tile)
            keys = jnp.concatenate([rows[dev, 0, here, lanes] for dev, here in places], axis=0)
            values = jnp.concatenate([rows[dev, 1, here, lanes] for dev, here in places], axis=0)
            queries = rows[seq_count + target, 0, target_rows, lanes] * jnp.bfloat16(SCALE)
            cots = rows[seq_count + target, 1, target_rows, lanes]
            none = jnp.zeros_like(queries)
            cots = jnp.where(live, cots, none)
            queries = jnp.concatenate(
                [jnp.where(lane_head == head, queries, none) for head in range(heads)], axis=0
            )
            cots = jnp.concatenate(
                [jnp.where(lane_head == head, cots, none) for head in range(heads)], axis=0
            )
            scores = jnp.where(key_valid, contract(keys, queries, 1, 1), FLOOR)
            expo = jnp.exp(scores - jnp.max(scores, axis=0, keepdims=True))
            probs = expo * (1.0 / jnp.sum(expo, axis=0, keepdims=True))
            dprob = contract(values, cots, 1, 1)
            delta = jnp.sum(probs * dprob, axis=0, keepdims=True)
            probs_low = probs.astype(jnp.bfloat16)
            dscore_low = (probs * (dprob - delta)).astype(jnp.bfloat16)
            dvalue = contract(probs_low, cots, 1, 0)
            dkey = contract(dscore_low, queries, 1, 0)
            keys_turned = jnp.concatenate([turned[index, 0, lanes] for index in chosen], axis=1)
            values_turned = jnp.concatenate([turned[index, 1, lanes] for index in chosen], axis=1)
            attended = own_heads(contract(values_turned, probs_low, 1, 0))
            dquery = own_heads(contract(keys_turned, dscore_low, 1, 0)) * SCALE
            attended = jnp.where(live, attended.astype(jnp.bfloat16).T, none)
            out[seq_count + target, 0, target_rows, lanes] = dquery.astype(jnp.bfloat16).T
            out[seq_count + target, 1, target_rows, lanes] = attended
            for slot, (dev, here) in enumerate(places):
                part = slice(slot * BLK, (slot + 1) * BLK)
                key_grad[dev, here, lanes] += dkey[part]
                value_grad[dev, here, lanes] += dvalue[part]
        return carry

    lax.fori_loop(0, block_count, turn, 0, unroll=block_count <= 4)
    lax.fori_loop(0, block_count, step, 0, unroll=block_count <= 4)
    out[:seq_count, 0] = key_grad[...].astype(jnp.bfloat16)
    out[:seq_count, 1] = value_grad[...].astype(jnp.bfloat16)


def attend_cost(block_count, width):
    pairs = block_count * NLIST * BLK * BLK * width
    return pl.CostEstimate(
        flops=10 * pairs,
        bytes_accessed=16 * block_count * BLK * width,
        transcendentals=pairs // HDIM,
    )


def specs(count, space):
    return [pl.BlockSpec(memory_space=space)] * count


def in_hbm(*arrays):
    return [pltpu.with_memory_space_constraint(array, pltpu.HBM) for array in arrays]


def gathered_kernel(
    seq_count, lists, source_len, target_len, rows, out, key_grad, value_grad, turned
):
    def listed(block, slot):
        return lists[block, slot]

    attend_sample(
        seq_count, listed, source_len[0], target_len[0], rows, out, key_grad, value_grad, turned
    )


def by_all_to_all(first_rows, second_rows, alignment, diffusion_mask, source_length, target_length):
    seq_count = lax.axis_size("seq")
    parts = lax.axis_size("section") * seq_count
    rows_here = first_rows.shape[2]
    width = first_rows.shape[3]
    on_encoder = lax.axis_index("section") == 0
    keep = on_encoder | (diffusion_mask[0] == 1)
    second = jnp.where(keep[:, None], second_rows[0, 0], jnp.zeros_like(second_rows[0, 0]))
    held = jnp.stack([first_rows[0, 0], second])
    held = held.reshape(2, rows_here, parts, width // parts).transpose(2, 0, 1, 3)
    lists = lax.all_gather(alignment[0], "seq", axis=0, tiled=True)
    rows = lax.all_to_all(held, AXES, 0, 0, tiled=True)
    grads = pltpu.VMEM((seq_count, rows_here, width // parts), jnp.float32)
    turned = pltpu.VMEM((lists.shape[0], 2, width // parts, BLK), rows.dtype)
    grads = pl.pallas_call(
        functools.partial(gathered_kernel, seq_count),
        out_shape=jax.ShapeDtypeStruct(rows.shape, rows.dtype),
        in_specs=specs(3, pltpu.SMEM) + specs(1, pltpu.VMEM),
        out_specs=pl.BlockSpec(memory_space=pltpu.VMEM),
        scratch_shapes=[grads, grads, turned],
        compiler_params=pltpu.CompilerParams(vmem_limit_bytes=VMEM_LIMIT),
        cost_estimate=attend_cost(lists.shape[0], width // parts),
        name="attend_gathered",
    )(lists, source_length, target_length, rows)
    grads = lax.all_to_all(grads, AXES, 0, 0, tiled=True)
    grads = grads.transpose(1, 2, 0, 3).reshape(2, rows_here, width)
    return (grads[0][None, None], grads[1][None, None])


def device_index(seq_count):
    return lax.axis_index("section") * seq_count + lax.axis_index("seq")


def pack_kernel(seq_count, order, *refs):
    smalls, (first, second) = refs[:2], refs[2:4]
    outs, (lists, mask, small_sem, sem) = refs[4:-4], refs[-4:]
    small_copies = [
        pltpu.make_async_copy(source, held, small_sem.at[slot])
        for slot, (source, held) in enumerate(zip(smalls, (lists, mask)))
    ]
    for copy in small_copies:
        copy.start()
    me = device_index(seq_count)
    here = me % seq_count
    share = outs[0].shape[1]
    copies = []
    for slot, (step, out) in enumerate(zip(order, outs)):
        lanes = pl.ds(pl.multiple_of((me ^ step) * share, LANES), share)
        pair = [
            pltpu.make_async_copy(
                source.at[0, 0, :, lanes], out.at[pl.ds(half * BLK, BLK)], sem.at[half, slot]
            )
            for half, source in enumerate((first, second))
        ]
        for copy in pair:
            copy.start()
        copies.append(pair)
    for copy in small_copies:
        copy.wait()
    keep = (mask[...] == 1) | (me < seq_count)
    keep = jnp.broadcast_to(jnp.where(keep, 1.0, 0.0), (BLK, BLK)).T.astype(jnp.bfloat16)
    keep = jnp.concatenate([keep] * (share // LANES), axis=1)
    base = here - WIN
    code = (lists[0, 0, 0] - base) * SPAN + lists[0, 0, 1] - base
    tail = jnp.full((TAIL, share), code, jnp.int32).astype(jnp.float32).astype(jnp.bfloat16)
    for out, pair in zip(outs, copies):
        for copy in pair:
            copy.wait()
        out[BLK : 2 * BLK] = out[BLK : 2 * BLK] * keep
        out[2 * BLK :] = tail


def attend_kernel(seq_count, order, turn, source_len, target_len, *refs):
    parts = 2 * seq_count
    shares, outs = refs[:parts], refs[parts : 2 * parts]
    rows, result, key_grad, value_grad, turned, lists = refs[2 * parts :]
    me = device_index(seq_count)
    here = me % seq_count

    def listed(block, slot):
        code = lists[block]
        return block - WIN + (code // SPAN if slot == 0 else code % SPAN)

    @pl.when(me % 2 == turn)
    def _():
        for step, share in zip(order, shares):
            source = me ^ step
            rows[source, 0] = share[:BLK]
            rows[source, 1] = share[BLK : 2 * BLK]
            if step < seq_count:
                tail = share[2 * BLK :, :LANES].astype(jnp.float32)
                lists[here ^ step] = jnp.max(tail).astype(jnp.int32)
        attend_sample(
            seq_count,
            listed,
            source_len[0],
            target_len[0],
            rows,
            result,
            key_grad,
            value_grad,
            turned,
        )
        for step, out in zip(order, outs):
            out[:BLK] = result[me ^ step, 0]
            out[BLK:] = result[me ^ step, 1]


def unpack_kernel(seq_count, order, *refs):
    parts = 2 * seq_count
    turns, (first, second, sem) = (refs[:parts], refs[parts : 2 * parts]), refs[2 * parts :]
    width = refs[0].shape[1]
    me = device_index(seq_count)
    for core in range(2):

        @pl.when(me % 2 == core)
        def _(core=core):
            copies = []
            for slot, step in enumerate(order):
                lanes = pl.ds(pl.multiple_of((me ^ step) * width, LANES), width)
                share = turns[(core ^ step) % 2][slot]
                for half, result in enumerate((first, second)):
                    copy = pltpu.make_async_copy(
                        share.at[pl.ds(half * BLK, BLK)],
                        result.at[0, 0, :, lanes],
                        sem.at[half, slot],
                    )
                    copy.start()
                    copies.append(copy)
            for copy in copies:
                copy.wait()


def to_turn(shares, order, turn):
    parts = len(order)
    return [
        lax.ppermute(
            share, AXES, [(dev, dev ^ step) for dev in range(parts) if (dev ^ step) % 2 == turn]
        )
        if step
        else share
        for step, share in zip(order, shares)
    ]


def from_turn(shares, order, turn):
    parts = len(order)
    return [
        lax.ppermute(share, AXES, [(dev, dev ^ step) for dev in range(turn, parts, 2)])
        if step
        else share
        for step, share in zip(order, shares)
    ]


def by_pairs(first_rows, second_rows, alignment, diffusion_mask, source_length, target_length):
    seq_count = lax.axis_size("seq")
    parts = 2 * seq_count
    width = first_rows.shape[3]
    share = width // parts
    kind = first_rows.dtype
    params = pltpu.CompilerParams(vmem_limit_bytes=VMEM_LIMIT)
    order = list(range(parts - 1, -1, -1))
    if parts == 8:
        order = [6, 7, 4, 5, 2, 3, 1, 0]
    sems = pltpu.SemaphoreType.DMA((2, parts))
    shares = pl.pallas_call(
        functools.partial(pack_kernel, seq_count, order),
        out_shape=[jax.ShapeDtypeStruct((2 * BLK + TAIL, share), kind)] * parts,
        in_specs=specs(4, pltpu.HBM),
        out_specs=specs(parts, pltpu.VMEM),
        scratch_shapes=[
            pltpu.SMEM(alignment.shape, jnp.int32),
            pltpu.VMEM(diffusion_mask.shape, jnp.int32),
            pltpu.SemaphoreType.DMA((2,)),
            sems,
        ],
        compiler_params=params,
        name="pack",
    )(*in_hbm(alignment, diffusion_mask, first_rows, second_rows))
    rows = pltpu.VMEM((parts, 2, BLK, share), kind)
    grads = pltpu.VMEM((seq_count, BLK, share), jnp.float32)
    turned = pltpu.VMEM((seq_count, 2, share, BLK), kind)

    def attend(turn, shares):
        return pl.pallas_call(
            functools.partial(attend_kernel, seq_count, order, turn),
            out_shape=[jax.ShapeDtypeStruct((2 * BLK, share), kind)] * parts,
            in_specs=specs(2, pltpu.SMEM) + specs(parts, pltpu.VMEM),
            out_specs=specs(parts, pltpu.VMEM),
            scratch_shapes=[rows, rows, grads, grads, turned, pltpu.SMEM((seq_count,), jnp.int32)],
            compiler_params=params,
            cost_estimate=attend_cost(seq_count, share),
            name="attend",
        )(source_length, target_length, *shares)

    early = to_turn(shares, order, 0)
    shares, early = zip(*(lax.optimization_barrier(pair) for pair in zip(shares, early)))
    early = list(attend(0, early))
    *tied, early[-1] = lax.optimization_barrier((*shares[FLIGHTS:], early[-1]))
    late = attend(1, to_turn([*shares[:FLIGHTS], *tied], order, 1))
    back = [from_turn(outs, order, turn) for turn, outs in enumerate((early, late))]
    out_shape = jax.ShapeDtypeStruct((1, 1, BLK, width), kind)
    return pl.pallas_call(
        functools.partial(unpack_kernel, seq_count, order),
        out_shape=[out_shape, out_shape],
        in_specs=specs(2 * parts, pltpu.VMEM),
        out_specs=specs(2, pltpu.HBM),
        scratch_shapes=[sems],
        compiler_params=params,
        name="unpack",
    )(*back[0], *back[1])


def on_device(first_rows, second_rows, alignment, diffusion_mask, source_length, target_length):
    seq_count = lax.axis_size("seq")
    parts = lax.axis_size("section") * seq_count
    paired = (
        parts == 2 * seq_count
        and seq_count & (seq_count - 1) == 0
        and first_rows.shape[2] == BLK
        and first_rows.shape[3] % (parts * LANES) == 0
    )
    work = by_pairs if paired else by_all_to_all
    return tuple(
        work(first_rows, second_rows, alignment, diffusion_mask, source_length, target_length)
    )


def solution(mesh):
    placed = (
        P("section", "sample", "seq", None),
        P("section", "sample", "seq", None),
        P("sample", "seq", None),
        P("sample", "seq"),
        P("sample"),
        P("sample"),
    )
    return jax.shard_map(
        on_device,
        mesh=mesh,
        in_specs=placed,
        out_specs=(P("section", "sample", "seq", None), P("section", "sample", "seq", None)),
        check_vma=False,
    )
```

```python
import functools

import jax
import jax.numpy as jnp
from jax import lax
from jax.experimental import pallas as pl
from jax.experimental.pallas import tpu as pltpu
from jax.sharding import PartitionSpec as P

HDIM = 64
BLK = 128
NLIST = 2
WIN = 1
SPAN = 2 * WIN + 1
LANES = 128
TAIL = 16
FLIGHTS = 5
SCALE = HDIM ** (-0.5)
FLOOR = -1e30
VMEM_LIMIT = 32 * 1024 * 1024
AXES = ("section", "seq")


def contract(left, right, left_dim, right_dim):
    return lax.dot_general(
        left, right, (((left_dim,), (right_dim,)), ((), ())), preferred_element_type=jnp.float32
    )


def attend_sample(
    seq_count, listed, source_len, target_len, rows, out, key_grad, value_grad, turned
):
    per_device = rows.shape[2] // BLK
    block_count = seq_count * per_device
    width = rows.shape[3]
    tile = min(width, LANES)
    heads = tile // HDIM
    key_grad[...] = jnp.zeros_like(key_grad)
    value_grad[...] = jnp.zeros_like(value_grad)
    inside = lax.broadcasted_iota(jnp.int32, (BLK, 1), 0)
    lane_head = lax.broadcasted_iota(jnp.int32, (BLK, tile), 1) // HDIM

    def place(block):
        if per_device == 1:
            return block, pl.ds(0, BLK)
        return block // per_device, pl.ds((block % per_device) * BLK, BLK)

    def own_heads(turned_result):
        return jnp.concatenate(
            [
                turned_result[head * HDIM : (head + 1) * HDIM, head * BLK : (head + 1) * BLK]
                for head in range(heads)
            ],
            axis=0,
        )

    def turn(block, carry):
        dev, here = place(block)
        for first in range(0, width, tile):
            for half in range(2):
                turned[block, half, pl.ds(first, tile)] = rows[
                    dev, half, here, pl.ds(first, tile)
                ].T
        return carry

    def step(block, carry):
        chosen = [listed(block, slot) for slot in range(NLIST)]
        places = [place(index) for index in chosen]
        target, target_rows = place(block)
        key_valid = jnp.concatenate(
            [index * BLK + inside < source_len for index in chosen], axis=0
        )
        live = block * BLK + inside < target_len
        for first in range(0, width, tile):
            lanes = pl.ds(first, tile)
            keys = jnp.concatenate([rows[dev, 0, here, lanes] for dev, here in places], axis=0)
            values = jnp.concatenate([rows[dev, 1, here, lanes] for dev, here in places], axis=0)
            queries = rows[seq_count + target, 0, target_rows, lanes] * jnp.bfloat16(SCALE)
            cots = rows[seq_count + target, 1, target_rows, lanes]
            none = jnp.zeros_like(queries)
            cots = jnp.where(live, cots, none)
            queries = jnp.concatenate(
                [jnp.where(lane_head == head, queries, none) for head in range(heads)], axis=0
            )
            cots = jnp.concatenate(
                [jnp.where(lane_head == head, cots, none) for head in range(heads)], axis=0
            )
            scores = jnp.where(key_valid, contract(keys, queries, 1, 1), FLOOR)
            expo = jnp.exp(scores - jnp.max(scores, axis=0, keepdims=True))
            probs = expo * (1.0 / jnp.sum(expo, axis=0, keepdims=True))
            dprob = contract(values, cots, 1, 1)
            delta = jnp.sum(probs * dprob, axis=0, keepdims=True)
            probs_low = probs.astype(jnp.bfloat16)
            dscore_low = (probs * (dprob - delta)).astype(jnp.bfloat16)
            dvalue = contract(probs_low, cots, 1, 0)
            dkey = contract(dscore_low, queries, 1, 0)
            keys_turned = jnp.concatenate([turned[index, 0, lanes] for index in chosen], axis=1)
            values_turned = jnp.concatenate([turned[index, 1, lanes] for index in chosen], axis=1)
            attended = own_heads(contract(values_turned, probs_low, 1, 0))
            dquery = own_heads(contract(keys_turned, dscore_low, 1, 0)) * SCALE
            attended = jnp.where(live, attended.astype(jnp.bfloat16).T, none)
            out[seq_count + target, 0, target_rows, lanes] = dquery.astype(jnp.bfloat16).T
            out[seq_count + target, 1, target_rows, lanes] = attended
            for slot, (dev, here) in enumerate(places):
                part = slice(slot * BLK, (slot + 1) * BLK)
                key_grad[dev, here, lanes] += dkey[part]
                value_grad[dev, here, lanes] += dvalue[part]
        return carry

    lax.fori_loop(0, block_count, turn, 0, unroll=block_count <= 4)
    lax.fori_loop(0, block_count, step, 0, unroll=block_count <= 4)
    out[:seq_count, 0] = key_grad[...].astype(jnp.bfloat16)
    out[:seq_count, 1] = value_grad[...].astype(jnp.bfloat16)


def attend_cost(block_count, width):
    pairs = block_count * NLIST * BLK * BLK * width
    return pl.CostEstimate(
        flops=10 * pairs,
        bytes_accessed=16 * block_count * BLK * width,
        transcendentals=pairs // HDIM,
    )


def specs(count, space):
    return [pl.BlockSpec(memory_space=space)] * count


def in_hbm(*arrays):
    return [pltpu.with_memory_space_constraint(array, pltpu.HBM) for array in arrays]


def gathered_kernel(
    seq_count, lists, source_len, target_len, rows, out, key_grad, value_grad, turned
):
    def listed(block, slot):
        return lists[block, slot]

    attend_sample(
        seq_count, listed, source_len[0], target_len[0], rows, out, key_grad, value_grad, turned
    )


def by_all_to_all(first_rows, second_rows, alignment, diffusion_mask, source_length, target_length):
    seq_count = lax.axis_size("seq")
    parts = lax.axis_size("section") * seq_count
    rows_here = first_rows.shape[2]
    width = first_rows.shape[3]
    on_encoder = lax.axis_index("section") == 0
    keep = on_encoder | (diffusion_mask[0] == 1)
    second = jnp.where(keep[:, None], second_rows[0, 0], jnp.zeros_like(second_rows[0, 0]))
    held = jnp.stack([first_rows[0, 0], second])
    held = held.reshape(2, rows_here, parts, width // parts).transpose(2, 0, 1, 3)
    lists = lax.all_gather(alignment[0], "seq", axis=0, tiled=True)
    rows = lax.all_to_all(held, AXES, 0, 0, tiled=True)
    grads = pltpu.VMEM((seq_count, rows_here, width // parts), jnp.float32)
    turned = pltpu.VMEM((lists.shape[0], 2, width // parts, BLK), rows.dtype)
    grads = pl.pallas_call(
        functools.partial(gathered_kernel, seq_count),
        out_shape=jax.ShapeDtypeStruct(rows.shape, rows.dtype),
        in_specs=specs(3, pltpu.SMEM) + specs(1, pltpu.VMEM),
        out_specs=pl.BlockSpec(memory_space=pltpu.VMEM),
        scratch_shapes=[grads, grads, turned],
        compiler_params=pltpu.CompilerParams(vmem_limit_bytes=VMEM_LIMIT),
        cost_estimate=attend_cost(lists.shape[0], width // parts),
        name="attend_gathered",
    )(lists, source_length, target_length, rows)
    grads = lax.all_to_all(grads, AXES, 0, 0, tiled=True)
    grads = grads.transpose(1, 2, 0, 3).reshape(2, rows_here, width)
    return (grads[0][None, None], grads[1][None, None])


def device_index(seq_count):
    return lax.axis_index("section") * seq_count + lax.axis_index("seq")


def pack_kernel(seq_count, order, *refs):
    smalls, (first, second) = refs[:2], refs[2:4]
    outs, (lists, mask, small_sem, sem) = refs[4:-4], refs[-4:]
    small_copies = [
        pltpu.make_async_copy(source, held, small_sem.at[slot])
        for slot, (source, held) in enumerate(zip(smalls, (lists, mask)))
    ]
    for copy in small_copies:
        copy.start()
    me = device_index(seq_count)
    here = me % seq_count
    share = outs[0].shape[1]
    copies = []
    for slot, (step, out) in enumerate(zip(order, outs)):
        lanes = pl.ds(pl.multiple_of((me ^ step) * share, LANES), share)
        pair = [
            pltpu.make_async_copy(
                source.at[0, 0, :, lanes], out.at[pl.ds(half * BLK, BLK)], sem.at[half, slot]
            )
            for half, source in enumerate((first, second))
        ]
        for copy in pair:
            copy.start()
        copies.append(pair)
    for copy in small_copies:
        copy.wait()
    keep = (mask[...] == 1) | (me < seq_count)
    keep = jnp.broadcast_to(jnp.where(keep, 1.0, 0.0), (BLK, BLK)).T.astype(jnp.bfloat16)
    keep = jnp.concatenate([keep] * (share // LANES), axis=1)
    base = here - WIN
    code = (lists[0, 0, 0] - base) * SPAN + lists[0, 0, 1] - base
    tail = jnp.full((TAIL, share), code, jnp.int32).astype(jnp.float32).astype(jnp.bfloat16)
    for out, pair in zip(outs, copies):
        for copy in pair:
            copy.wait()
        out[BLK : 2 * BLK] = out[BLK : 2 * BLK] * keep
        out[2 * BLK :] = tail


def attend_kernel(seq_count, order, turn, source_len, target_len, *refs):
    parts = 2 * seq_count
    shares, outs = refs[:parts], refs[parts : 2 * parts]
    rows, result, key_grad, value_grad, turned, lists = refs[2 * parts :]
    me = device_index(seq_count)
    here = me % seq_count

    def listed(block, slot):
        code = lists[block]
        return block - WIN + (code // SPAN if slot == 0 else code % SPAN)

    @pl.when(me % 2 == turn)
    def _():
        for step, share in zip(order, shares):
            source = me ^ step
            rows[source, 0] = share[:BLK]
            rows[source, 1] = share[BLK : 2 * BLK]
            if step < seq_count:
                tail = share[2 * BLK :, :LANES].astype(jnp.float32)
                lists[here ^ step] = jnp.max(tail).astype(jnp.int32)
        attend_sample(
            seq_count,
            listed,
            source_len[0],
            target_len[0],
            rows,
            result,
            key_grad,
            value_grad,
            turned,
        )
        for step, out in zip(order, outs):
            out[:BLK] = result[me ^ step, 0]
            out[BLK:] = result[me ^ step, 1]


def unpack_kernel(seq_count, order, *refs):
    parts = 2 * seq_count
    turns, (first, second, sem) = (refs[:parts], refs[parts : 2 * parts]), refs[2 * parts :]
    width = refs[0].shape[1]
    me = device_index(seq_count)
    for core in range(2):

        @pl.when(me % 2 == core)
        def _(core=core):
            copies = []
            for slot, step in enumerate(order):
                lanes = pl.ds(pl.multiple_of((me ^ step) * width, LANES), width)
                share = turns[(core ^ step) % 2][slot]
                for half, result in enumerate((first, second)):
                    copy = pltpu.make_async_copy(
                        share.at[pl.ds(half * BLK, BLK)],
                        result.at[0, 0, :, lanes],
                        sem.at[half, slot],
                    )
                    copy.start()
                    copies.append(copy)
            for copy in copies:
                copy.wait()


def moved(share, step, parts, real):
    pairs = [(dev, dev ^ (step if real(dev) else step % 2)) for dev in range(parts)]
    return lax.ppermute(share, AXES, pairs)


def to_turn(shares, order, turn):
    def real(step):
        return lambda dev: (dev ^ step) % 2 == turn

    return [
        moved(share, step, len(order), real(step)) if step else share
        for step, share in zip(order, shares)
    ]


def from_turn(shares, order, turn):
    return [
        moved(share, step, len(order), lambda dev: dev % 2 == turn) if step else share
        for step, share in zip(order, shares)
    ]


def by_pairs(first_rows, second_rows, alignment, diffusion_mask, source_length, target_length):
    seq_count = lax.axis_size("seq")
    parts = 2 * seq_count
    width = first_rows.shape[3]
    share = width // parts
    kind = first_rows.dtype
    params = pltpu.CompilerParams(vmem_limit_bytes=VMEM_LIMIT)
    order = list(range(parts - 1, -1, -1))
    if parts == 8:
        order = [6, 7, 4, 5, 2, 3, 1, 0]
    sems = pltpu.SemaphoreType.DMA((2, parts))
    shares = pl.pallas_call(
        functools.partial(pack_kernel, seq_count, order),
        out_shape=[jax.ShapeDtypeStruct((2 * BLK + TAIL, share), kind)] * parts,
        in_specs=specs(4, pltpu.HBM),
        out_specs=specs(parts, pltpu.VMEM),
        scratch_shapes=[
            pltpu.SMEM(alignment.shape, jnp.int32),
            pltpu.VMEM(diffusion_mask.shape, jnp.int32),
            pltpu.SemaphoreType.DMA((2,)),
            sems,
        ],
        compiler_params=params,
        name="pack",
    )(*in_hbm(alignment, diffusion_mask, first_rows, second_rows))
    rows = pltpu.VMEM((parts, 2, BLK, share), kind)
    grads = pltpu.VMEM((seq_count, BLK, share), jnp.float32)
    turned = pltpu.VMEM((seq_count, 2, share, BLK), kind)

    def attend(turn, shares):
        return pl.pallas_call(
            functools.partial(attend_kernel, seq_count, order, turn),
            out_shape=[jax.ShapeDtypeStruct((2 * BLK, share), kind)] * parts,
            in_specs=specs(2, pltpu.SMEM) + specs(parts, pltpu.VMEM),
            out_specs=specs(parts, pltpu.VMEM),
            scratch_shapes=[rows, rows, grads, grads, turned, pltpu.SMEM((seq_count,), jnp.int32)],
            compiler_params=params,
            cost_estimate=attend_cost(seq_count, share),
            name="attend",
        )(source_length, target_length, *shares)

    early = to_turn(shares, order, 0)
    shares, early = zip(*(lax.optimization_barrier(pair) for pair in zip(shares, early)))
    outs = list(attend(0, early))
    *tied, outs[-1] = lax.optimization_barrier((*shares[FLIGHTS:], outs[-1]))
    late = to_turn([*shares[:FLIGHTS], *tied], order, 1)
    late[order.index(1)] = early[order.index(1)]
    back = [from_turn(outs, order, 0), from_turn(attend(1, late), order, 1)]
    out_shape = jax.ShapeDtypeStruct((1, 1, BLK, width), kind)
    return pl.pallas_call(
        functools.partial(unpack_kernel, seq_count, order),
        out_shape=[out_shape, out_shape],
        in_specs=specs(2 * parts, pltpu.VMEM),
        out_specs=specs(2, pltpu.HBM),
        scratch_shapes=[sems],
        compiler_params=params,
        name="unpack",
    )(*back[0], *back[1])


def on_device(first_rows, second_rows, alignment, diffusion_mask, source_length, target_length):
    seq_count = lax.axis_size("seq")
    parts = lax.axis_size("section") * seq_count
    paired = (
        parts == 2 * seq_count
        and seq_count & (seq_count - 1) == 0
        and first_rows.shape[2] == BLK
        and first_rows.shape[3] % (parts * LANES) == 0
    )
    work = by_pairs if paired else by_all_to_all
    return tuple(
        work(first_rows, second_rows, alignment, diffusion_mask, source_length, target_length)
    )


def solution(mesh):
    placed = (
        P("section", "sample", "seq", None),
        P("section", "sample", "seq", None),
        P("sample", "seq", None),
        P("sample", "seq"),
        P("sample"),
        P("sample"),
    )
    return jax.shard_map(
        on_device,
        mesh=mesh,
        in_specs=placed,
        out_specs=(P("section", "sample", "seq", None), P("section", "sample", "seq", None)),
        check_vma=False,
    )
```

```python
import functools

import jax
import jax.numpy as jnp
from jax import lax
from jax.experimental import pallas as pl
from jax.experimental.pallas import tpu as pltpu
from jax.sharding import PartitionSpec as P

HDIM = 64
BLK = 128
NLIST = 2
WIN = 1
SPAN = 2 * WIN + 1
LANES = 128
TAIL = 16
EARLY = (0, 1, 6, 7)
SCALE = HDIM ** (-0.5)
FLOOR = -1e30
VMEM_LIMIT = 32 * 1024 * 1024
AXES = ("section", "seq")


def contract(left, right, left_dim, right_dim):
    return lax.dot_general(
        left, right, (((left_dim,), (right_dim,)), ((), ())), preferred_element_type=jnp.float32
    )


def attend_sample(
    seq_count, listed, source_len, target_len, rows, out, key_grad, value_grad, turned
):
    per_device = rows.shape[2] // BLK
    block_count = seq_count * per_device
    width = rows.shape[3]
    tile = min(width, LANES)
    heads = tile // HDIM
    key_grad[...] = jnp.zeros_like(key_grad)
    value_grad[...] = jnp.zeros_like(value_grad)
    inside = lax.broadcasted_iota(jnp.int32, (BLK, 1), 0)
    lane_head = lax.broadcasted_iota(jnp.int32, (BLK, tile), 1) // HDIM

    def place(block):
        if per_device == 1:
            return block, pl.ds(0, BLK)
        return block // per_device, pl.ds((block % per_device) * BLK, BLK)

    def own_heads(turned_result):
        return jnp.concatenate(
            [
                turned_result[head * HDIM : (head + 1) * HDIM, head * BLK : (head + 1) * BLK]
                for head in range(heads)
            ],
            axis=0,
        )

    def turn(block, carry):
        dev, here = place(block)
        for first in range(0, width, tile):
            for half in range(2):
                turned[block, half, pl.ds(first, tile)] = rows[
                    dev, half, here, pl.ds(first, tile)
                ].T
        return carry

    def step(block, carry):
        chosen = [listed(block, slot) for slot in range(NLIST)]
        places = [place(index) for index in chosen]
        target, target_rows = place(block)
        key_valid = jnp.concatenate(
            [index * BLK + inside < source_len for index in chosen], axis=0
        )
        live = block * BLK + inside < target_len
        for first in range(0, width, tile):
            lanes = pl.ds(first, tile)
            keys = jnp.concatenate([rows[dev, 0, here, lanes] for dev, here in places], axis=0)
            values = jnp.concatenate([rows[dev, 1, here, lanes] for dev, here in places], axis=0)
            queries = rows[seq_count + target, 0, target_rows, lanes] * jnp.bfloat16(SCALE)
            cots = rows[seq_count + target, 1, target_rows, lanes]
            none = jnp.zeros_like(queries)
            cots = jnp.where(live, cots, none)
            queries = jnp.concatenate(
                [jnp.where(lane_head == head, queries, none) for head in range(heads)], axis=0
            )
            cots = jnp.concatenate(
                [jnp.where(lane_head == head, cots, none) for head in range(heads)], axis=0
            )
            scores = jnp.where(key_valid, contract(keys, queries, 1, 1), FLOOR)
            expo = jnp.exp(scores - jnp.max(scores, axis=0, keepdims=True))
            probs = expo * (1.0 / jnp.sum(expo, axis=0, keepdims=True))
            dprob = contract(values, cots, 1, 1)
            delta = jnp.sum(probs * dprob, axis=0, keepdims=True)
            probs_low = probs.astype(jnp.bfloat16)
            dscore_low = (probs * (dprob - delta)).astype(jnp.bfloat16)
            dvalue = contract(probs_low, cots, 1, 0)
            dkey = contract(dscore_low, queries, 1, 0)
            keys_turned = jnp.concatenate([turned[index, 0, lanes] for index in chosen], axis=1)
            values_turned = jnp.concatenate([turned[index, 1, lanes] for index in chosen], axis=1)
            attended = own_heads(contract(values_turned, probs_low, 1, 0))
            dquery = own_heads(contract(keys_turned, dscore_low, 1, 0)) * SCALE
            attended = jnp.where(live, attended.astype(jnp.bfloat16).T, none)
            out[seq_count + target, 0, target_rows, lanes] = dquery.astype(jnp.bfloat16).T
            out[seq_count + target, 1, target_rows, lanes] = attended
            for slot, (dev, here) in enumerate(places):
                part = slice(slot * BLK, (slot + 1) * BLK)
                key_grad[dev, here, lanes] += dkey[part]
                value_grad[dev, here, lanes] += dvalue[part]
        return carry

    lax.fori_loop(0, block_count, turn, 0, unroll=block_count <= 4)
    lax.fori_loop(0, block_count, step, 0, unroll=block_count <= 4)
    out[:seq_count, 0] = key_grad[...].astype(jnp.bfloat16)
    out[:seq_count, 1] = value_grad[...].astype(jnp.bfloat16)


def attend_cost(block_count, width):
    pairs = block_count * NLIST * BLK * BLK * width
    return pl.CostEstimate(
        flops=10 * pairs,
        bytes_accessed=16 * block_count * BLK * width,
        transcendentals=pairs // HDIM,
    )


def specs(count, space):
    return [pl.BlockSpec(memory_space=space)] * count


def in_hbm(*arrays):
    return [pltpu.with_memory_space_constraint(array, pltpu.HBM) for array in arrays]


def gathered_kernel(
    seq_count, lists, source_len, target_len, rows, out, key_grad, value_grad, turned
):
    def listed(block, slot):
        return lists[block, slot]

    attend_sample(
        seq_count, listed, source_len[0], target_len[0], rows, out, key_grad, value_grad, turned
    )


def by_all_to_all(first_rows, second_rows, alignment, diffusion_mask, source_length, target_length):
    seq_count = lax.axis_size("seq")
    parts = lax.axis_size("section") * seq_count
    rows_here = first_rows.shape[2]
    width = first_rows.shape[3]
    on_encoder = lax.axis_index("section") == 0
    keep = on_encoder | (diffusion_mask[0] == 1)
    second = jnp.where(keep[:, None], second_rows[0, 0], jnp.zeros_like(second_rows[0, 0]))
    held = jnp.stack([first_rows[0, 0], second])
    held = held.reshape(2, rows_here, parts, width // parts).transpose(2, 0, 1, 3)
    lists = lax.all_gather(alignment[0], "seq", axis=0, tiled=True)
    rows = lax.all_to_all(held, AXES, 0, 0, tiled=True)
    grads = pltpu.VMEM((seq_count, rows_here, width // parts), jnp.float32)
    turned = pltpu.VMEM((lists.shape[0], 2, width // parts, BLK), rows.dtype)
    grads = pl.pallas_call(
        functools.partial(gathered_kernel, seq_count),
        out_shape=jax.ShapeDtypeStruct(rows.shape, rows.dtype),
        in_specs=specs(3, pltpu.SMEM) + specs(1, pltpu.VMEM),
        out_specs=pl.BlockSpec(memory_space=pltpu.VMEM),
        scratch_shapes=[grads, grads, turned],
        compiler_params=pltpu.CompilerParams(vmem_limit_bytes=VMEM_LIMIT),
        cost_estimate=attend_cost(lists.shape[0], width // parts),
        name="attend_gathered",
    )(lists, source_length, target_length, rows)
    grads = lax.all_to_all(grads, AXES, 0, 0, tiled=True)
    grads = grads.transpose(1, 2, 0, 3).reshape(2, rows_here, width)
    return (grads[0][None, None], grads[1][None, None])


def device_index(seq_count):
    return lax.axis_index("section") * seq_count + lax.axis_index("seq")


def pack_kernel(seq_count, steps, *refs):
    smalls, (first, second) = refs[:2], refs[2:4]
    outs, (lists, mask, small_sem, sem) = refs[4:-4], refs[-4:]
    me = device_index(seq_count)
    here = me % seq_count
    share = outs[0].shape[1]
    copies = []
    for slot, (step, out) in enumerate(zip(steps, outs)):
        lanes = pl.ds(pl.multiple_of((me ^ step) * share, LANES), share)
        pair = [
            pltpu.make_async_copy(
                source.at[0, 0, :, lanes], out.at[pl.ds(half * BLK, BLK)], sem.at[half, slot]
            )
            for half, source in enumerate((first, second))
        ]
        for copy in pair:
            copy.start()
        copies.append(pair)
    small_copies = [
        pltpu.make_async_copy(source, held, small_sem.at[slot])
        for slot, (source, held) in enumerate(zip(smalls, (lists, mask)))
    ]
    for copy in small_copies:
        copy.start()
    for copy in small_copies:
        copy.wait()
    keep = (mask[...] == 1) | (me < seq_count)
    keep = jnp.broadcast_to(jnp.where(keep, 1.0, 0.0), (BLK, BLK)).T.astype(jnp.bfloat16)
    keep = jnp.concatenate([keep] * (share // LANES), axis=1)
    base = here - WIN
    code = (lists[0, 0, 0] - base) * SPAN + lists[0, 0, 1] - base
    tail = jnp.full((TAIL, share), code, jnp.int32).astype(jnp.float32).astype(jnp.bfloat16)
    for out, pair in zip(outs, copies):
        for copy in pair:
            copy.wait()
        out[BLK : 2 * BLK] = out[BLK : 2 * BLK] * keep
        out[2 * BLK :] = tail


def attend_kernel(seq_count, order, back, source_len, target_len, *refs):
    parts = 2 * seq_count
    shares, outs = refs[:parts], refs[parts : 2 * parts]
    rows, result, key_grad, value_grad, turned, lists = refs[2 * parts :]
    me = device_index(seq_count)
    here = me % seq_count
    for step, share in zip(order, shares):
        source = me ^ step
        rows[source, 0] = share[:BLK]
        rows[source, 1] = share[BLK : 2 * BLK]
        if step < seq_count:
            tail = share[2 * BLK :, :LANES].astype(jnp.float32)
            lists[here ^ step] = jnp.max(tail).astype(jnp.int32)

    def listed(block, slot):
        code = lists[block]
        return block - WIN + (code // SPAN if slot == 0 else code % SPAN)

    attend_sample(
        seq_count,
        listed,
        source_len[0],
        target_len[0],
        rows,
        result,
        key_grad,
        value_grad,
        turned,
    )
    for step, out in zip(back, outs):
        out[:BLK] = result[me ^ step, 0]
        out[BLK:] = result[me ^ step, 1]


def unpack_kernel(seq_count, steps, *refs):
    shares, (first, second, sem) = refs[: len(steps)], refs[-3:]
    width = shares[0].shape[1]
    me = device_index(seq_count)
    copies = []
    for slot, (step, share) in enumerate(zip(steps, shares)):
        lanes = pl.ds(pl.multiple_of((me ^ step) * width, LANES), width)
        for half, result in enumerate((first, second)):
            copy = pltpu.make_async_copy(
                share.at[pl.ds(half * BLK, BLK)], result.at[0, 0, :, lanes], sem.at[half, slot]
            )
            copy.start()
            copies.append(copy)
    for copy in copies:
        copy.wait()


def swapped(shares, order):
    parts = len(order)
    return [
        lax.ppermute(share, AXES, [(dev, dev ^ step) for dev in range(parts)]) if step else share
        for step, share in zip(order, shares)
    ]


def by_pairs(first_rows, second_rows, alignment, diffusion_mask, source_length, target_length):
    seq_count = lax.axis_size("seq")
    parts = 2 * seq_count
    width = first_rows.shape[3]
    share = width // parts
    kind = first_rows.dtype
    params = pltpu.CompilerParams(vmem_limit_bytes=VMEM_LIMIT)
    order = back = list(range(parts - 1, -1, -1))
    if parts == 8:
        order, back = [6, 4, 7, 5, 2, 3, 1, 0], [6, 7, 4, 5, 2, 3, 1, 0]
    sems = pltpu.SemaphoreType.DMA((2, parts))

    def pack(steps, lists):
        return pl.pallas_call(
            functools.partial(pack_kernel, seq_count, steps),
            out_shape=[jax.ShapeDtypeStruct((2 * BLK + TAIL, share), kind)] * len(steps),
            in_specs=specs(4, pltpu.HBM),
            out_specs=specs(len(steps), pltpu.VMEM),
            scratch_shapes=[
                pltpu.SMEM(alignment.shape, jnp.int32),
                pltpu.VMEM(diffusion_mask.shape, jnp.int32),
                pltpu.SemaphoreType.DMA((2,)),
                sems,
            ],
            compiler_params=params,
            name="pack",
        )(*in_hbm(lists, diffusion_mask, first_rows, second_rows))

    shares = list(pack(order[:seq_count], alignment))
    lists, shares[0] = lax.optimization_barrier((alignment, shares[0]))
    shares = swapped([*shares, *pack(order[seq_count:], lists)], order)
    rows = pltpu.VMEM((parts, 2, BLK, share), kind)
    grads = pltpu.VMEM((seq_count, BLK, share), jnp.float32)
    turned = pltpu.VMEM((seq_count, 2, share, BLK), kind)
    shares = pl.pallas_call(
        functools.partial(attend_kernel, seq_count, order, back),
        out_shape=[jax.ShapeDtypeStruct((2 * BLK, share), kind)] * parts,
        in_specs=specs(2, pltpu.SMEM) + specs(parts, pltpu.VMEM),
        out_specs=specs(parts, pltpu.VMEM),
        scratch_shapes=[rows, rows, grads, grads, turned, pltpu.SMEM((seq_count,), jnp.int32)],
        compiler_params=params,
        cost_estimate=attend_cost(seq_count, share),
        name="attend",
    )(source_length, target_length, *shares)
    shares = dict(zip(back, swapped(shares, back)))
    out_shape = jax.ShapeDtypeStruct((1, 1, BLK, width), kind)

    def unpack(steps, *begun):
        count = len(steps)
        return pl.pallas_call(
            functools.partial(unpack_kernel, seq_count, steps),
            out_shape=[out_shape, out_shape],
            in_specs=specs(count, pltpu.VMEM) + specs(len(begun), pltpu.HBM),
            out_specs=specs(2, pltpu.HBM),
            input_output_aliases={count + slot: slot for slot in range(len(begun))},
            scratch_shapes=[sems],
            compiler_params=params,
            name="unpack",
        )(*(shares[step] for step in steps), *begun)

    early = [step for step in back if step in EARLY]
    return unpack([step for step in back if step not in EARLY], *unpack(early))


def on_device(first_rows, second_rows, alignment, diffusion_mask, source_length, target_length):
    seq_count = lax.axis_size("seq")
    parts = lax.axis_size("section") * seq_count
    paired = (
        parts == 2 * seq_count
        and seq_count & (seq_count - 1) == 0
        and first_rows.shape[2] == BLK
        and first_rows.shape[3] % (parts * LANES) == 0
    )
    work = by_pairs if paired else by_all_to_all
    return tuple(
        work(first_rows, second_rows, alignment, diffusion_mask, source_length, target_length)
    )


def solution(mesh):
    placed = (
        P("section", "sample", "seq", None),
        P("section", "sample", "seq", None),
        P("sample", "seq", None),
        P("sample", "seq"),
        P("sample"),
        P("sample"),
    )
    return jax.shard_map(
        on_device,
        mesh=mesh,
        in_specs=placed,
        out_specs=(P("section", "sample", "seq", None), P("section", "sample", "seq", None)),
        check_vma=False,
    )
```

```python
import functools

import jax
import jax.numpy as jnp
from jax import lax
from jax.experimental import pallas as pl
from jax.experimental.pallas import tpu as pltpu
from jax.sharding import PartitionSpec as P

HDIM = 64
BLK = 128
NLIST = 2
WIN = 1
SPAN = 2 * WIN + 1
LANES = 128
TAIL = 16
EARLY = (0, 2, 4)
SCALE = HDIM ** (-0.5)
FLOOR = -1e30
VMEM_LIMIT = 32 * 1024 * 1024
AXES = ("section", "seq")


def contract(left, right, left_dim, right_dim):
    return lax.dot_general(
        left, right, (((left_dim,), (right_dim,)), ((), ())), preferred_element_type=jnp.float32
    )


def attend_sample(
    seq_count, listed, source_len, target_len, rows, out, key_grad, value_grad, turned
):
    per_device = rows.shape[2] // BLK
    block_count = seq_count * per_device
    width = rows.shape[3]
    tile = min(width, LANES)
    heads = tile // HDIM
    key_grad[...] = jnp.zeros_like(key_grad)
    value_grad[...] = jnp.zeros_like(value_grad)
    inside = lax.broadcasted_iota(jnp.int32, (BLK, 1), 0)
    lane_head = lax.broadcasted_iota(jnp.int32, (BLK, tile), 1) // HDIM

    def place(block):
        if per_device == 1:
            return block, pl.ds(0, BLK)
        return block // per_device, pl.ds((block % per_device) * BLK, BLK)

    def own_heads(turned_result):
        return jnp.concatenate(
            [
                turned_result[head * HDIM : (head + 1) * HDIM, head * BLK : (head + 1) * BLK]
                for head in range(heads)
            ],
            axis=0,
        )

    def turn(block, carry):
        dev, here = place(block)
        for first in range(0, width, tile):
            for half in range(2):
                turned[block, half, pl.ds(first, tile)] = rows[
                    dev, half, here, pl.ds(first, tile)
                ].T
        return carry

    def step(block, carry):
        chosen = [listed(block, slot) for slot in range(NLIST)]
        places = [place(index) for index in chosen]
        target, target_rows = place(block)
        key_valid = jnp.concatenate(
            [index * BLK + inside < source_len for index in chosen], axis=0
        )
        live = block * BLK + inside < target_len
        for first in range(0, width, tile):
            lanes = pl.ds(first, tile)
            keys = jnp.concatenate([rows[dev, 0, here, lanes] for dev, here in places], axis=0)
            values = jnp.concatenate([rows[dev, 1, here, lanes] for dev, here in places], axis=0)
            queries = rows[seq_count + target, 0, target_rows, lanes] * jnp.bfloat16(SCALE)
            cots = rows[seq_count + target, 1, target_rows, lanes]
            none = jnp.zeros_like(queries)
            cots = jnp.where(live, cots, none)
            queries = jnp.concatenate(
                [jnp.where(lane_head == head, queries, none) for head in range(heads)], axis=0
            )
            cots = jnp.concatenate(
                [jnp.where(lane_head == head, cots, none) for head in range(heads)], axis=0
            )
            scores = jnp.where(key_valid, contract(keys, queries, 1, 1), FLOOR)
            expo = jnp.exp(scores - jnp.max(scores, axis=0, keepdims=True))
            probs = expo * (1.0 / jnp.sum(expo, axis=0, keepdims=True))
            dprob = contract(values, cots, 1, 1)
            delta = jnp.sum(probs * dprob, axis=0, keepdims=True)
            probs_low = probs.astype(jnp.bfloat16)
            dscore_low = (probs * (dprob - delta)).astype(jnp.bfloat16)
            dvalue = contract(probs_low, cots, 1, 0)
            dkey = contract(dscore_low, queries, 1, 0)
            keys_turned = jnp.concatenate([turned[index, 0, lanes] for index in chosen], axis=1)
            values_turned = jnp.concatenate([turned[index, 1, lanes] for index in chosen], axis=1)
            attended = own_heads(contract(values_turned, probs_low, 1, 0))
            dquery = own_heads(contract(keys_turned, dscore_low, 1, 0)) * SCALE
            attended = jnp.where(live, attended.astype(jnp.bfloat16).T, none)
            out[seq_count + target, 0, target_rows, lanes] = dquery.astype(jnp.bfloat16).T
            out[seq_count + target, 1, target_rows, lanes] = attended
            for slot, (dev, here) in enumerate(places):
                part = slice(slot * BLK, (slot + 1) * BLK)
                key_grad[dev, here, lanes] += dkey[part]
                value_grad[dev, here, lanes] += dvalue[part]
        return carry

    lax.fori_loop(0, block_count, turn, 0, unroll=block_count <= 4)
    lax.fori_loop(0, block_count, step, 0, unroll=block_count <= 4)
    out[:seq_count, 0] = key_grad[...].astype(jnp.bfloat16)
    out[:seq_count, 1] = value_grad[...].astype(jnp.bfloat16)


def attend_cost(block_count, width):
    pairs = block_count * NLIST * BLK * BLK * width
    return pl.CostEstimate(
        flops=10 * pairs,
        bytes_accessed=16 * block_count * BLK * width,
        transcendentals=pairs // HDIM,
    )


def specs(count, space):
    return [pl.BlockSpec(memory_space=space)] * count


def in_hbm(*arrays):
    return [pltpu.with_memory_space_constraint(array, pltpu.HBM) for array in arrays]


def gathered_kernel(
    seq_count, lists, source_len, target_len, rows, out, key_grad, value_grad, turned
):
    def listed(block, slot):
        return lists[block, slot]

    attend_sample(
        seq_count, listed, source_len[0], target_len[0], rows, out, key_grad, value_grad, turned
    )


def by_all_to_all(first_rows, second_rows, alignment, diffusion_mask, source_length, target_length):
    seq_count = lax.axis_size("seq")
    parts = lax.axis_size("section") * seq_count
    rows_here = first_rows.shape[2]
    width = first_rows.shape[3]
    on_encoder = lax.axis_index("section") == 0
    keep = on_encoder | (diffusion_mask[0] == 1)
    second = jnp.where(keep[:, None], second_rows[0, 0], jnp.zeros_like(second_rows[0, 0]))
    held = jnp.stack([first_rows[0, 0], second])
    held = held.reshape(2, rows_here, parts, width // parts).transpose(2, 0, 1, 3)
    lists = lax.all_gather(alignment[0], "seq", axis=0, tiled=True)
    rows = lax.all_to_all(held, AXES, 0, 0, tiled=True)
    grads = pltpu.VMEM((seq_count, rows_here, width // parts), jnp.float32)
    turned = pltpu.VMEM((lists.shape[0], 2, width // parts, BLK), rows.dtype)
    grads = pl.pallas_call(
        functools.partial(gathered_kernel, seq_count),
        out_shape=jax.ShapeDtypeStruct(rows.shape, rows.dtype),
        in_specs=specs(3, pltpu.SMEM) + specs(1, pltpu.VMEM),
        out_specs=pl.BlockSpec(memory_space=pltpu.VMEM),
        scratch_shapes=[grads, grads, turned],
        compiler_params=pltpu.CompilerParams(vmem_limit_bytes=VMEM_LIMIT),
        cost_estimate=attend_cost(lists.shape[0], width // parts),
        name="attend_gathered",
    )(lists, source_length, target_length, rows)
    grads = lax.all_to_all(grads, AXES, 0, 0, tiled=True)
    grads = grads.transpose(1, 2, 0, 3).reshape(2, rows_here, width)
    return (grads[0][None, None], grads[1][None, None])


def device_index(seq_count):
    return lax.axis_index("section") * seq_count + lax.axis_index("seq")


def pack_kernel(seq_count, steps, *refs):
    smalls, (first, second) = refs[:2], refs[2:4]
    outs, (lists, mask, small_sem, sem) = refs[4:-4], refs[-4:]
    me = device_index(seq_count)
    here = me % seq_count
    share = outs[0].shape[1]
    copies = []
    for slot, (step, out) in enumerate(zip(steps, outs)):
        lanes = pl.ds(pl.multiple_of((me ^ step) * share, LANES), share)
        pair = [
            pltpu.make_async_copy(
                source.at[0, 0, :, lanes], out.at[pl.ds(half * BLK, BLK)], sem.at[half, slot]
            )
            for half, source in enumerate((first, second))
        ]
        for copy in pair:
            copy.start()
        copies.append(pair)
    small_copies = [
        pltpu.make_async_copy(source, held, small_sem.at[slot])
        for slot, (source, held) in enumerate(zip(smalls, (lists, mask)))
    ]
    for copy in small_copies:
        copy.start()
    for copy in small_copies:
        copy.wait()
    keep = (mask[...] == 1) | (me < seq_count)
    keep = jnp.broadcast_to(jnp.where(keep, 1.0, 0.0), (BLK, BLK)).T.astype(jnp.bfloat16)
    keep = jnp.concatenate([keep] * (share // LANES), axis=1)
    base = here - WIN
    code = (lists[0, 0, 0] - base) * SPAN + lists[0, 0, 1] - base
    tail = jnp.full((TAIL, share), code, jnp.int32).astype(jnp.float32).astype(jnp.bfloat16)
    for out, pair in zip(outs, copies):
        for copy in pair:
            copy.wait()
        out[BLK : 2 * BLK] = out[BLK : 2 * BLK] * keep
        out[2 * BLK :] = tail


def attend_kernel(seq_count, order, back, source_len, target_len, *refs):
    parts = 2 * seq_count
    shares, outs = refs[:parts], refs[parts : 2 * parts]
    rows, result, key_grad, value_grad, turned, lists = refs[2 * parts :]
    me = device_index(seq_count)
    here = me % seq_count
    for step, share in zip(order, shares):
        source = me ^ step
        rows[source, 0] = share[:BLK]
        rows[source, 1] = share[BLK : 2 * BLK]
        if step < seq_count:
            tail = share[2 * BLK :, :LANES].astype(jnp.float32)
            lists[here ^ step] = jnp.max(tail).astype(jnp.int32)

    def listed(block, slot):
        code = lists[block]
        return block - WIN + (code // SPAN if slot == 0 else code % SPAN)

    attend_sample(
        seq_count,
        listed,
        source_len[0],
        target_len[0],
        rows,
        result,
        key_grad,
        value_grad,
        turned,
    )
    for step, out in zip(back, outs):
        out[:BLK] = result[me ^ step, 0]
        out[BLK:] = result[me ^ step, 1]


def unpack_kernel(seq_count, steps, *refs):
    shares, (first, second, sem) = refs[: len(steps)], refs[-3:]
    width = shares[0].shape[1]
    me = device_index(seq_count)
    copies = []
    for slot, (step, share) in enumerate(zip(steps, shares)):
        lanes = pl.ds(pl.multiple_of((me ^ step) * width, LANES), width)
        for half, result in enumerate((first, second)):
            copy = pltpu.make_async_copy(
                share.at[pl.ds(half * BLK, BLK)], result.at[0, 0, :, lanes], sem.at[half, slot]
            )
            copy.start()
            copies.append(copy)
    for copy in copies:
        copy.wait()


def swapped(shares, order):
    parts = len(order)
    return [
        lax.ppermute(share, AXES, [(dev, dev ^ step) for dev in range(parts)]) if step else share
        for step, share in zip(order, shares)
    ]


def by_pairs(first_rows, second_rows, alignment, diffusion_mask, source_length, target_length):
    seq_count = lax.axis_size("seq")
    parts = 2 * seq_count
    width = first_rows.shape[3]
    share = width // parts
    kind = first_rows.dtype
    params = pltpu.CompilerParams(vmem_limit_bytes=VMEM_LIMIT)
    order = back = list(range(parts - 1, -1, -1))
    if parts == 8:
        order, back = [4, 2, 5, 6, 7, 3, 1, 0], [4, 2, 6, 7, 5, 3, 1, 0]
    sems = pltpu.SemaphoreType.DMA((2, parts))

    def pack(steps, lists):
        return pl.pallas_call(
            functools.partial(pack_kernel, seq_count, steps),
            out_shape=[jax.ShapeDtypeStruct((2 * BLK + TAIL, share), kind)] * len(steps),
            in_specs=specs(4, pltpu.HBM),
            out_specs=specs(len(steps), pltpu.VMEM),
            scratch_shapes=[
                pltpu.SMEM(alignment.shape, jnp.int32),
                pltpu.VMEM(diffusion_mask.shape, jnp.int32),
                pltpu.SemaphoreType.DMA((2,)),
                sems,
            ],
            compiler_params=params,
            name="pack",
        )(*in_hbm(lists, diffusion_mask, first_rows, second_rows))

    shares = list(pack(order[:seq_count], alignment))
    lists, shares[0] = lax.optimization_barrier((alignment, shares[0]))
    shares = swapped([*shares, *pack(order[seq_count:], lists)], order)
    rows = pltpu.VMEM((parts, 2, BLK, share), kind)
    grads = pltpu.VMEM((seq_count, BLK, share), jnp.float32)
    turned = pltpu.VMEM((seq_count, 2, share, BLK), kind)
    shares = pl.pallas_call(
        functools.partial(attend_kernel, seq_count, order, back),
        out_shape=[jax.ShapeDtypeStruct((2 * BLK, share), kind)] * parts,
        in_specs=specs(2, pltpu.SMEM) + specs(parts, pltpu.VMEM),
        out_specs=specs(parts, pltpu.VMEM),
        scratch_shapes=[rows, rows, grads, grads, turned, pltpu.SMEM((seq_count,), jnp.int32)],
        compiler_params=params,
        cost_estimate=attend_cost(seq_count, share),
        name="attend",
    )(source_length, target_length, *shares)
    shares = dict(zip(back, swapped(shares, back)))
    out_shape = jax.ShapeDtypeStruct((1, 1, BLK, width), kind)

    def unpack(steps, *begun):
        count = len(steps)
        return pl.pallas_call(
            functools.partial(unpack_kernel, seq_count, steps),
            out_shape=[out_shape, out_shape],
            in_specs=specs(count, pltpu.VMEM) + specs(len(begun), pltpu.HBM),
            out_specs=specs(2, pltpu.HBM),
            input_output_aliases={count + slot: slot for slot in range(len(begun))},
            scratch_shapes=[sems],
            compiler_params=params,
            name="unpack",
        )(*(shares[step] for step in steps), *begun)

    early = [step for step in back if step in EARLY]
    return unpack([step for step in back if step not in EARLY], *unpack(early))


def on_device(first_rows, second_rows, alignment, diffusion_mask, source_length, target_length):
    seq_count = lax.axis_size("seq")
    parts = lax.axis_size("section") * seq_count
    paired = (
        parts == 2 * seq_count
        and seq_count & (seq_count - 1) == 0
        and first_rows.shape[2] == BLK
        and first_rows.shape[3] % (parts * LANES) == 0
    )
    work = by_pairs if paired else by_all_to_all
    return tuple(
        work(first_rows, second_rows, alignment, diffusion_mask, source_length, target_length)
    )


def solution(mesh):
    placed = (
        P("section", "sample", "seq", None),
        P("section", "sample", "seq", None),
        P("sample", "seq", None),
        P("sample", "seq"),
        P("sample"),
        P("sample"),
    )
    return jax.shard_map(
        on_device,
        mesh=mesh,
        in_specs=placed,
        out_specs=(P("section", "sample", "seq", None), P("section", "sample", "seq", None)),
        check_vma=False,
    )
```

```python
import functools

import jax
import jax.numpy as jnp
from jax import lax
from jax.experimental import pallas as pl
from jax.experimental.pallas import tpu as pltpu
from jax.sharding import PartitionSpec as P

HDIM = 64
BLK = 128
NLIST = 2
WIN = 1
SPAN = 2 * WIN + 1
LANES = 128
TAIL = 16
EARLY = (0, 2, 4)
SCALE = HDIM ** (-0.5)
FLOOR = -1e30
VMEM_LIMIT = 32 * 1024 * 1024
AXES = ("section", "seq")


def contract(left, right, left_dim, right_dim):
    return lax.dot_general(
        left, right, (((left_dim,), (right_dim,)), ((), ())), preferred_element_type=jnp.float32
    )


def attend_sample(
    seq_count, listed, source_len, target_len, rows, out, key_grad, value_grad, turned
):
    per_device = rows.shape[2] // BLK
    block_count = seq_count * per_device
    width = rows.shape[3]
    tile = min(width, LANES)
    heads = tile // HDIM
    key_grad[...] = jnp.zeros_like(key_grad)
    value_grad[...] = jnp.zeros_like(value_grad)
    key_inside = lax.broadcasted_iota(jnp.int32, (BLK, heads * BLK), 0)
    row_inside = lax.broadcasted_iota(jnp.int32, (BLK, tile), 0)
    lane_head = lax.broadcasted_iota(jnp.int32, (BLK, tile), 1) // HDIM

    def factor(mask):
        return jnp.where(mask, 1.0, 0.0).astype(jnp.bfloat16)

    own_lanes = [factor(lane_head == head) for head in range(heads)]

    def place(block):
        if per_device == 1:
            return block, pl.ds(0, BLK)
        return block // per_device, pl.ds((block % per_device) * BLK, BLK)

    def own_heads(turned_result):
        return jnp.concatenate(
            [
                turned_result[head * HDIM : (head + 1) * HDIM, head * BLK : (head + 1) * BLK]
                for head in range(heads)
            ],
            axis=0,
        )

    def turn(block, carry):
        dev, here = place(block)
        for first in range(0, width, tile):
            for half in range(2):
                turned[block, half, pl.ds(first, tile)] = rows[
                    dev, half, here, pl.ds(first, tile)
                ].T
        return carry

    def step(block, carry):
        chosen = [listed(block, slot) for slot in range(NLIST)]
        places = [place(index) for index in chosen]
        target, target_rows = place(block)
        key_valid = jnp.concatenate(
            [key_inside < source_len - index * BLK for index in chosen], axis=0
        )
        live = factor(row_inside < target_len - block * BLK)
        for first in range(0, width, tile):
            lanes = pl.ds(first, tile)
            keys = jnp.concatenate([rows[dev, 0, here, lanes] for dev, here in places], axis=0)
            values = jnp.concatenate([rows[dev, 1, here, lanes] for dev, here in places], axis=0)
            queries = rows[seq_count + target, 0, target_rows, lanes] * jnp.bfloat16(SCALE)
            cots = rows[seq_count + target, 1, target_rows, lanes]
            queries = jnp.concatenate([queries * own for own in own_lanes], axis=0)
            cots = jnp.concatenate([cots * (live * own) for own in own_lanes], axis=0)
            scores = jnp.where(key_valid, contract(keys, queries, 1, 1), FLOOR)
            expo = jnp.exp(scores - jnp.max(scores, axis=0, keepdims=True))
            probs = expo * (1.0 / jnp.sum(expo, axis=0, keepdims=True))
            dprob = contract(values, cots, 1, 1)
            delta = jnp.sum(probs * dprob, axis=0, keepdims=True)
            probs_low = probs.astype(jnp.bfloat16)
            dscore_low = (probs * (dprob - delta)).astype(jnp.bfloat16)
            dvalue = contract(probs_low, cots, 1, 0)
            dkey = contract(dscore_low, queries, 1, 0)
            keys_turned = jnp.concatenate([turned[index, 0, lanes] for index in chosen], axis=1)
            values_turned = jnp.concatenate([turned[index, 1, lanes] for index in chosen], axis=1)
            attended = own_heads(contract(values_turned, probs_low, 1, 0))
            dquery = own_heads(contract(keys_turned, dscore_low, 1, 0)) * SCALE
            attended = attended.astype(jnp.bfloat16).T * live
            out[seq_count + target, 0, target_rows, lanes] = dquery.astype(jnp.bfloat16).T
            out[seq_count + target, 1, target_rows, lanes] = attended
            for slot, (dev, here) in enumerate(places):
                part = slice(slot * BLK, (slot + 1) * BLK)
                key_grad[dev, here, lanes] += dkey[part]
                value_grad[dev, here, lanes] += dvalue[part]
        return carry

    lax.fori_loop(0, block_count, turn, 0, unroll=block_count <= 4)
    lax.fori_loop(0, block_count, step, 0, unroll=block_count <= 4)
    out[:seq_count, 0] = key_grad[...].astype(jnp.bfloat16)
    out[:seq_count, 1] = value_grad[...].astype(jnp.bfloat16)


def attend_cost(block_count, width):
    pairs = block_count * NLIST * BLK * BLK * width
    return pl.CostEstimate(
        flops=10 * pairs,
        bytes_accessed=16 * block_count * BLK * width,
        transcendentals=pairs // HDIM,
    )


def specs(count, space):
    return [pl.BlockSpec(memory_space=space)] * count


def in_hbm(*arrays):
    return [pltpu.with_memory_space_constraint(array, pltpu.HBM) for array in arrays]


def gathered_kernel(
    seq_count, lists, source_len, target_len, rows, out, key_grad, value_grad, turned
):
    def listed(block, slot):
        return lists[block, slot]

    attend_sample(
        seq_count, listed, source_len[0], target_len[0], rows, out, key_grad, value_grad, turned
    )


def by_all_to_all(first_rows, second_rows, alignment, diffusion_mask, source_length, target_length):
    seq_count = lax.axis_size("seq")
    parts = lax.axis_size("section") * seq_count
    rows_here = first_rows.shape[2]
    width = first_rows.shape[3]
    on_encoder = lax.axis_index("section") == 0
    keep = on_encoder | (diffusion_mask[0] == 1)
    second = jnp.where(keep[:, None], second_rows[0, 0], jnp.zeros_like(second_rows[0, 0]))
    held = jnp.stack([first_rows[0, 0], second])
    held = held.reshape(2, rows_here, parts, width // parts).transpose(2, 0, 1, 3)
    lists = lax.all_gather(alignment[0], "seq", axis=0, tiled=True)
    rows = lax.all_to_all(held, AXES, 0, 0, tiled=True)
    grads = pltpu.VMEM((seq_count, rows_here, width // parts), jnp.float32)
    turned = pltpu.VMEM((lists.shape[0], 2, width // parts, BLK), rows.dtype)
    grads = pl.pallas_call(
        functools.partial(gathered_kernel, seq_count),
        out_shape=jax.ShapeDtypeStruct(rows.shape, rows.dtype),
        in_specs=specs(3, pltpu.SMEM) + specs(1, pltpu.VMEM),
        out_specs=pl.BlockSpec(memory_space=pltpu.VMEM),
        scratch_shapes=[grads, grads, turned],
        compiler_params=pltpu.CompilerParams(vmem_limit_bytes=VMEM_LIMIT),
        cost_estimate=attend_cost(lists.shape[0], width // parts),
        name="attend_gathered",
    )(lists, source_length, target_length, rows)
    grads = lax.all_to_all(grads, AXES, 0, 0, tiled=True)
    grads = grads.transpose(1, 2, 0, 3).reshape(2, rows_here, width)
    return (grads[0][None, None], grads[1][None, None])


def device_index(seq_count):
    return lax.axis_index("section") * seq_count + lax.axis_index("seq")


def pack_kernel(seq_count, steps, *refs):
    smalls, (first, second) = refs[:2], refs[2:4]
    outs, (lists, mask, small_sem, sem) = refs[4:-4], refs[-4:]
    me = device_index(seq_count)
    here = me % seq_count
    share = outs[0].shape[1]
    copies = []
    for slot, (step, out) in enumerate(zip(steps, outs)):
        lanes = pl.ds(pl.multiple_of((me ^ step) * share, LANES), share)
        pair = [
            pltpu.make_async_copy(
                source.at[0, 0, :, lanes], out.at[pl.ds(half * BLK, BLK)], sem.at[half, slot]
            )
            for half, source in enumerate((first, second))
        ]
        for copy in pair:
            copy.start()
        copies.append(pair)
    small_copies = [
        pltpu.make_async_copy(source, held, small_sem.at[slot])
        for slot, (source, held) in enumerate(zip(smalls, (lists, mask)))
    ]
    for copy in small_copies:
        copy.start()
    for copy in small_copies:
        copy.wait()
    keep = (mask[...] == 1) | (me < seq_count)
    keep = jnp.broadcast_to(jnp.where(keep, 1.0, 0.0), (BLK, BLK)).T.astype(jnp.bfloat16)
    keep = jnp.concatenate([keep] * (share // LANES), axis=1)
    base = here - WIN
    code = (lists[0, 0, 0] - base) * SPAN + lists[0, 0, 1] - base
    tail = jnp.full((TAIL, share), code, jnp.int32).astype(jnp.float32).astype(jnp.bfloat16)
    for out, pair in zip(outs, copies):
        for copy in pair:
            copy.wait()
        out[BLK : 2 * BLK] = out[BLK : 2 * BLK] * keep
        out[2 * BLK :] = tail


def attend_kernel(seq_count, order, back, source_len, target_len, *refs):
    parts = 2 * seq_count
    shares, outs = refs[:parts], refs[parts : 2 * parts]
    rows, result, key_grad, value_grad, turned, lists = refs[2 * parts :]
    me = device_index(seq_count)
    here = me % seq_count
    for step, share in zip(order, shares):
        source = me ^ step
        rows[source, 0] = share[:BLK]
        rows[source, 1] = share[BLK : 2 * BLK]
        if step < seq_count:
            tail = share[2 * BLK :, :LANES].astype(jnp.float32)
            lists[here ^ step] = jnp.max(tail).astype(jnp.int32)

    def listed(block, slot):
        code = lists[block]
        return block - WIN + (code // SPAN if slot == 0 else code % SPAN)

    attend_sample(
        seq_count,
        listed,
        source_len[0],
        target_len[0],
        rows,
        result,
        key_grad,
        value_grad,
        turned,
    )
    for step, out in zip(back, outs):
        out[:BLK] = result[me ^ step, 0]
        out[BLK:] = result[me ^ step, 1]


def unpack_kernel(seq_count, steps, *refs):
    shares, (first, second, sem) = refs[: len(steps)], refs[-3:]
    width = shares[0].shape[1]
    me = device_index(seq_count)
    copies = []
    for slot, (step, share) in enumerate(zip(steps, shares)):
        lanes = pl.ds(pl.multiple_of((me ^ step) * width, LANES), width)
        for half, result in enumerate((first, second)):
            copy = pltpu.make_async_copy(
                share.at[pl.ds(half * BLK, BLK)], result.at[0, 0, :, lanes], sem.at[half, slot]
            )
            copy.start()
            copies.append(copy)
    for copy in copies:
        copy.wait()


def swapped(shares, order):
    parts = len(order)
    return [
        lax.ppermute(share, AXES, [(dev, dev ^ step) for dev in range(parts)]) if step else share
        for step, share in zip(order, shares)
    ]


def by_pairs(first_rows, second_rows, alignment, diffusion_mask, source_length, target_length):
    seq_count = lax.axis_size("seq")
    parts = 2 * seq_count
    width = first_rows.shape[3]
    share = width // parts
    kind = first_rows.dtype
    params = pltpu.CompilerParams(vmem_limit_bytes=VMEM_LIMIT)
    order = back = list(range(parts - 1, -1, -1))
    if parts == 8:
        order = back = [4, 2, 6, 7, 5, 3, 1, 0]
    sems = pltpu.SemaphoreType.DMA((2, parts))

    def pack(steps, lists):
        return pl.pallas_call(
            functools.partial(pack_kernel, seq_count, steps),
            out_shape=[jax.ShapeDtypeStruct((2 * BLK + TAIL, share), kind)] * len(steps),
            in_specs=specs(4, pltpu.HBM),
            out_specs=specs(len(steps), pltpu.VMEM),
            scratch_shapes=[
                pltpu.SMEM(alignment.shape, jnp.int32),
                pltpu.VMEM(diffusion_mask.shape, jnp.int32),
                pltpu.SemaphoreType.DMA((2,)),
                sems,
            ],
            compiler_params=params,
            name="pack",
        )(*in_hbm(lists, diffusion_mask, first_rows, second_rows))

    shares = list(pack(order[:seq_count], alignment))
    lists, shares[0] = lax.optimization_barrier((alignment, shares[0]))
    shares = swapped([*shares, *pack(order[seq_count:], lists)], order)
    rows = pltpu.VMEM((parts, 2, BLK, share), kind)
    grads = pltpu.VMEM((seq_count, BLK, share), jnp.float32)
    turned = pltpu.VMEM((seq_count, 2, share, BLK), kind)
    shares = pl.pallas_call(
        functools.partial(attend_kernel, seq_count, order, back),
        out_shape=[jax.ShapeDtypeStruct((2 * BLK, share), kind)] * parts,
        in_specs=specs(2, pltpu.SMEM) + specs(parts, pltpu.VMEM),
        out_specs=specs(parts, pltpu.VMEM),
        scratch_shapes=[rows, rows, grads, grads, turned, pltpu.SMEM((seq_count,), jnp.int32)],
        compiler_params=params,
        cost_estimate=attend_cost(seq_count, share),
        name="attend",
    )(source_length, target_length, *shares)
    shares = dict(zip(back, swapped(shares, back)))
    out_shape = jax.ShapeDtypeStruct((1, 1, BLK, width), kind)

    def unpack(steps, *begun):
        count = len(steps)
        return pl.pallas_call(
            functools.partial(unpack_kernel, seq_count, steps),
            out_shape=[out_shape, out_shape],
            in_specs=specs(count, pltpu.VMEM) + specs(len(begun), pltpu.HBM),
            out_specs=specs(2, pltpu.HBM),
            input_output_aliases={count + slot: slot for slot in range(len(begun))},
            scratch_shapes=[sems],
            compiler_params=params,
            name="unpack",
        )(*(shares[step] for step in steps), *begun)

    early = [step for step in back if step in EARLY]
    return unpack([step for step in back if step not in EARLY], *unpack(early))


def on_device(first_rows, second_rows, alignment, diffusion_mask, source_length, target_length):
    seq_count = lax.axis_size("seq")
    parts = lax.axis_size("section") * seq_count
    paired = (
        parts == 2 * seq_count
        and seq_count & (seq_count - 1) == 0
        and first_rows.shape[2] == BLK
        and first_rows.shape[3] % (parts * LANES) == 0
    )
    work = by_pairs if paired else by_all_to_all
    return tuple(
        work(first_rows, second_rows, alignment, diffusion_mask, source_length, target_length)
    )


def solution(mesh):
    placed = (
        P("section", "sample", "seq", None),
        P("section", "sample", "seq", None),
        P("sample", "seq", None),
        P("sample", "seq"),
        P("sample"),
        P("sample"),
    )
    return jax.shard_map(
        on_device,
        mesh=mesh,
        in_specs=placed,
        out_specs=(P("section", "sample", "seq", None), P("section", "sample", "seq", None)),
        check_vma=False,
    )
```

```python
import functools

import jax
import jax.numpy as jnp
from jax import lax
from jax.experimental import pallas as pl
from jax.experimental.pallas import tpu as pltpu
from jax.sharding import PartitionSpec as P

HDIM = 64
BLK = 128
NLIST = 2
WIN = 1
SPAN = 2 * WIN + 1
LANES = 128
TAIL = 16
SCALE = HDIM ** (-0.5)
FLOOR = -1e30
VMEM_LIMIT = 32 * 1024 * 1024
AXES = ("section", "seq")


def contract(left, right, left_dim, right_dim):
    return lax.dot_general(
        left, right, (((left_dim,), (right_dim,)), ((), ())), preferred_element_type=jnp.float32
    )


def attend_sample(
    seq_count, listed, source_len, target_len, rows, out, key_grad, value_grad, turned
):
    per_device = rows.shape[2] // BLK
    block_count = seq_count * per_device
    width = rows.shape[3]
    tile = min(width, LANES)
    heads = tile // HDIM
    key_grad[...] = jnp.zeros_like(key_grad)
    value_grad[...] = jnp.zeros_like(value_grad)
    inside = lax.broadcasted_iota(jnp.int32, (BLK, 1), 0)
    lane_head = lax.broadcasted_iota(jnp.int32, (BLK, tile), 1) // HDIM

    def place(block):
        if per_device == 1:
            return block, pl.ds(0, BLK)
        return block // per_device, pl.ds((block % per_device) * BLK, BLK)

    def own_heads(turned_result):
        return jnp.concatenate(
            [
                turned_result[head * HDIM : (head + 1) * HDIM, head * BLK : (head + 1) * BLK]
                for head in range(heads)
            ],
            axis=0,
        )

    def turn(block, carry):
        dev, here = place(block)
        for first in range(0, width, tile):
            for half in range(2):
                turned[block, half, pl.ds(first, tile)] = rows[
                    dev, half, here, pl.ds(first, tile)
                ].T
        return carry

    def step(block, carry):
        chosen = [listed(block, slot) for slot in range(NLIST)]
        places = [place(index) for index in chosen]
        target, target_rows = place(block)
        key_valid = jnp.concatenate(
            [index * BLK + inside < source_len for index in chosen], axis=0
        )
        live = block * BLK + inside < target_len
        for first in range(0, width, tile):
            lanes = pl.ds(first, tile)
            keys = jnp.concatenate([rows[dev, 0, here, lanes] for dev, here in places], axis=0)
            values = jnp.concatenate([rows[dev, 1, here, lanes] for dev, here in places], axis=0)
            queries = rows[seq_count + target, 0, target_rows, lanes] * jnp.bfloat16(SCALE)
            cots = rows[seq_count + target, 1, target_rows, lanes]
            none = jnp.zeros_like(queries)
            cots = jnp.where(live, cots, none)
            queries = jnp.concatenate(
                [jnp.where(lane_head == head, queries, none) for head in range(heads)], axis=0
            )
            cots = jnp.concatenate(
                [jnp.where(lane_head == head, cots, none) for head in range(heads)], axis=0
            )
            scores = jnp.where(key_valid, contract(keys, queries, 1, 1), FLOOR)
            expo = jnp.exp(scores - jnp.max(scores, axis=0, keepdims=True))
            probs = expo * (1.0 / jnp.sum(expo, axis=0, keepdims=True))
            dprob = contract(values, cots, 1, 1)
            delta = jnp.sum(probs * dprob, axis=0, keepdims=True)
            probs_low = probs.astype(jnp.bfloat16)
            dscore_low = (probs * (dprob - delta)).astype(jnp.bfloat16)
            dvalue = contract(probs_low, cots, 1, 0)
            dkey = contract(dscore_low, queries, 1, 0)
            keys_turned = jnp.concatenate([turned[index, 0, lanes] for index in chosen], axis=1)
            values_turned = jnp.concatenate([turned[index, 1, lanes] for index in chosen], axis=1)
            attended = own_heads(contract(values_turned, probs_low, 1, 0))
            dquery = own_heads(contract(keys_turned, dscore_low, 1, 0)) * SCALE
            attended = jnp.where(live, attended.astype(jnp.bfloat16).T, none)
            out[seq_count + target, 0, target_rows, lanes] = dquery.astype(jnp.bfloat16).T
            out[seq_count + target, 1, target_rows, lanes] = attended
            for slot, (dev, here) in enumerate(places):
                part = slice(slot * BLK, (slot + 1) * BLK)
                key_grad[dev, here, lanes] += dkey[part]
                value_grad[dev, here, lanes] += dvalue[part]
        return carry

    lax.fori_loop(0, block_count, turn, 0, unroll=block_count <= 4)
    lax.fori_loop(0, block_count, step, 0, unroll=block_count <= 4)
    out[:seq_count, 0] = key_grad[...].astype(jnp.bfloat16)
    out[:seq_count, 1] = value_grad[...].astype(jnp.bfloat16)


def attend_cost(block_count, width):
    pairs = block_count * NLIST * BLK * BLK * width
    return pl.CostEstimate(
        flops=10 * pairs,
        bytes_accessed=16 * block_count * BLK * width,
        transcendentals=pairs // HDIM,
    )


def specs(count, space):
    return [pl.BlockSpec(memory_space=space)] * count


def in_hbm(*arrays):
    return [pltpu.with_memory_space_constraint(array, pltpu.HBM) for array in arrays]


def gathered_kernel(
    seq_count, lists, source_len, target_len, rows, out, key_grad, value_grad, turned
):
    def listed(block, slot):
        return lists[block, slot]

    attend_sample(
        seq_count, listed, source_len[0], target_len[0], rows, out, key_grad, value_grad, turned
    )


def by_all_to_all(first_rows, second_rows, alignment, diffusion_mask, source_length, target_length):
    seq_count = lax.axis_size("seq")
    parts = lax.axis_size("section") * seq_count
    rows_here = first_rows.shape[2]
    width = first_rows.shape[3]
    on_encoder = lax.axis_index("section") == 0
    keep = on_encoder | (diffusion_mask[0] == 1)
    second = jnp.where(keep[:, None], second_rows[0, 0], jnp.zeros_like(second_rows[0, 0]))
    held = jnp.stack([first_rows[0, 0], second])
    held = held.reshape(2, rows_here, parts, width // parts).transpose(2, 0, 1, 3)
    lists = lax.all_gather(alignment[0], "seq", axis=0, tiled=True)
    rows = lax.all_to_all(held, AXES, 0, 0, tiled=True)
    grads = pltpu.VMEM((seq_count, rows_here, width // parts), jnp.float32)
    turned = pltpu.VMEM((lists.shape[0], 2, width // parts, BLK), rows.dtype)
    grads = pl.pallas_call(
        functools.partial(gathered_kernel, seq_count),
        out_shape=jax.ShapeDtypeStruct(rows.shape, rows.dtype),
        in_specs=specs(3, pltpu.SMEM) + specs(1, pltpu.VMEM),
        out_specs=pl.BlockSpec(memory_space=pltpu.VMEM),
        scratch_shapes=[grads, grads, turned],
        compiler_params=pltpu.CompilerParams(vmem_limit_bytes=VMEM_LIMIT),
        cost_estimate=attend_cost(lists.shape[0], width // parts),
        name="attend_gathered",
    )(lists, source_length, target_length, rows)
    grads = lax.all_to_all(grads, AXES, 0, 0, tiled=True)
    grads = grads.transpose(1, 2, 0, 3).reshape(2, rows_here, width)
    return (grads[0][None, None], grads[1][None, None])


def device_index(seq_count):
    return lax.axis_index("section") * seq_count + lax.axis_index("seq")


OUTGOING = [(0,), (1,), (6, 7), (4,), (2,), (5,), (3,)]
INCOMING = [*OUTGOING, (7,)]


def pack_kernel(seq_count, steps, *refs):
    smalls, (first, second) = refs[:2], refs[2:4]
    outs, (lists, mask, small_sem, sem) = refs[4:-4], refs[-4:]
    me = device_index(seq_count)
    here = me % seq_count
    share = outs[0].shape[1]
    copies, pieces = [], []
    for group, out in zip(steps, outs):
        for place, step in enumerate(group):
            slot = len(copies)
            lanes = pl.ds(pl.multiple_of((me ^ step) * share, LANES), share)
            piece = out.at[pl.ds(place * 2 * BLK, 2 * BLK)]
            pair = [
                pltpu.make_async_copy(
                    source.at[0, 0, :, lanes], piece.at[pl.ds(half * BLK, BLK)], sem.at[half, slot]
                )
                for half, source in enumerate((first, second))
            ]
            for copy in pair:
                copy.start()
            copies.append(pair)
            pieces.append(piece)
    small_copies = [
        pltpu.make_async_copy(source, held, small_sem.at[slot])
        for slot, (source, held) in enumerate(zip(smalls, (lists, mask)))
    ]
    for copy in small_copies:
        copy.start()
    for copy in small_copies:
        copy.wait()
    keep = (mask[...] == 1) | (me < seq_count)
    keep = jnp.broadcast_to(jnp.where(keep, 1.0, 0.0), (BLK, BLK)).T.astype(jnp.bfloat16)
    keep = jnp.concatenate([keep] * (share // LANES), axis=1)
    base = here - WIN
    code = (lists[0, 0, 0] - base) * SPAN + lists[0, 0, 1] - base
    tail = jnp.full((TAIL, share), code, jnp.int32).astype(jnp.float32).astype(jnp.bfloat16)
    for out in outs:
        if out.shape[0] % (2 * BLK):
            out[2 * BLK :] = tail
    for piece, pair in zip(pieces, copies):
        for copy in pair:
            copy.wait()
        piece[BLK:] = piece[BLK:] * keep


def attend_kernel(seq_count, order, source_len, target_len, *refs):
    count = len(order)
    shares, outs = refs[:count], refs[count : 2 * count - 1]
    rows, result, key_grad, value_grad, turned, lists = refs[2 * count - 1 :]
    me = device_index(seq_count)
    here = me % seq_count
    for (step, *_), share in zip(order, shares):
        source = me ^ step
        rows[source, 0] = share[:BLK]
        rows[source, 1] = share[BLK : 2 * BLK]
        if step < seq_count:
            tail = share[2 * BLK :, :LANES].astype(jnp.float32)
            lists[here ^ step] = jnp.max(tail).astype(jnp.int32)

    def listed(block, slot):
        code = lists[block]
        return block - WIN + (code // SPAN if slot == 0 else code % SPAN)

    attend_sample(
        seq_count,
        listed,
        source_len[0],
        target_len[0],
        rows,
        result,
        key_grad,
        value_grad,
        turned,
    )
    for group, out in zip(OUTGOING, outs):
        for place, step in enumerate(group):
            out[2 * place * BLK : (2 * place + 1) * BLK] = result[me ^ step, 0]
            out[(2 * place + 1) * BLK : (2 * place + 2) * BLK] = result[me ^ step, 1]


def unpack_kernel(seq_count, steps, *refs):
    shares, (first, second, sem) = refs[: len(steps)], refs[-3:]
    width = shares[0].shape[1]
    me = device_index(seq_count)
    copies = []
    for slot, ((step, *_), share) in enumerate(zip(steps, shares)):
        lanes = pl.ds(pl.multiple_of((me ^ step) * width, LANES), width)
        for half, result in enumerate((first, second)):
            copy = pltpu.make_async_copy(
                share.at[pl.ds(half * BLK, BLK)], result.at[0, 0, :, lanes], sem.at[half, slot]
            )
            copy.start()
            copies.append(copy)
    for copy in copies:
        copy.wait()


def swapped(shares):
    parts = 8

    def move(share, step):
        return lax.ppermute(share, AXES, [(dev, dev ^ step) for dev in range(parts)])

    moved = {
        group: move(share, group[0]) if group[0] else share
        for group, share in zip(OUTGOING, shares)
    }
    moved[(6, 7)], moved[(1,)] = lax.optimization_barrier((moved[(6, 7)], moved[(1,)]))
    moved[(7,)] = move(moved[(6, 7)][2 * BLK :], 1)
    return [moved[group] for group in INCOMING]


def by_pairs(first_rows, second_rows, alignment, diffusion_mask, source_length, target_length):
    seq_count = lax.axis_size("seq")
    parts = 2 * seq_count
    width = first_rows.shape[3]
    share = width // parts
    kind = first_rows.dtype
    params = pltpu.CompilerParams(vmem_limit_bytes=VMEM_LIMIT)
    sems = pltpu.SemaphoreType.DMA((2, parts))

    def sizes(groups, tail):
        return [
            jax.ShapeDtypeStruct(
                (len(group) * 2 * BLK + (tail if group[0] < seq_count else 0), share), kind
            )
            for group in groups
        ]

    def pack(groups, lists):
        return pl.pallas_call(
            functools.partial(pack_kernel, seq_count, groups),
            out_shape=sizes(groups, TAIL),
            in_specs=specs(4, pltpu.HBM),
            out_specs=specs(len(groups), pltpu.VMEM),
            scratch_shapes=[
                pltpu.SMEM(alignment.shape, jnp.int32),
                pltpu.VMEM(diffusion_mask.shape, jnp.int32),
                pltpu.SemaphoreType.DMA((2,)),
                sems,
            ],
            compiler_params=params,
            name="pack",
        )(*in_hbm(lists, diffusion_mask, first_rows, second_rows))

    shares = swapped(pack(OUTGOING, alignment))
    rows = pltpu.VMEM((parts, 2, BLK, share), kind)
    grads = pltpu.VMEM((seq_count, BLK, share), jnp.float32)
    turned = pltpu.VMEM((seq_count, 2, share, BLK), kind)
    shares = pl.pallas_call(
        functools.partial(attend_kernel, seq_count, INCOMING),
        out_shape=sizes(OUTGOING, 0),
        in_specs=specs(2, pltpu.SMEM) + specs(len(INCOMING), pltpu.VMEM),
        out_specs=specs(len(OUTGOING), pltpu.VMEM),
        scratch_shapes=[rows, rows, grads, grads, turned, pltpu.SMEM((seq_count,), jnp.int32)],
        compiler_params=params,
        cost_estimate=attend_cost(seq_count, share),
        name="attend",
    )(source_length, target_length, *shares)
    shares = swapped(shares)
    out_shape = jax.ShapeDtypeStruct((1, 1, BLK, width), kind)
    return pl.pallas_call(
        functools.partial(unpack_kernel, seq_count, INCOMING),
        out_shape=[out_shape, out_shape],
        in_specs=specs(len(INCOMING), pltpu.VMEM),
        out_specs=specs(2, pltpu.HBM),
        scratch_shapes=[sems],
        compiler_params=params,
        name="unpack",
    )(*shares)


def on_device(first_rows, second_rows, alignment, diffusion_mask, source_length, target_length):
    seq_count = lax.axis_size("seq")
    parts = lax.axis_size("section") * seq_count
    paired = (
        (parts, seq_count) == (8, 4)
        and first_rows.shape[2] == BLK
        and first_rows.shape[3] % (parts * LANES) == 0
    )
    work = by_pairs if paired else by_all_to_all
    return tuple(
        work(first_rows, second_rows, alignment, diffusion_mask, source_length, target_length)
    )


def solution(mesh):
    placed = (
        P("section", "sample", "seq", None),
        P("section", "sample", "seq", None),
        P("sample", "seq", None),
        P("sample", "seq"),
        P("sample"),
        P("sample"),
    )
    return jax.shard_map(
        on_device,
        mesh=mesh,
        in_specs=placed,
        out_specs=(P("section", "sample", "seq", None), P("section", "sample", "seq", None)),
        check_vma=False,
    )
```

```python
import functools

import jax
import jax.numpy as jnp
from jax import lax
from jax.experimental import pallas as pl
from jax.experimental.pallas import tpu as pltpu
from jax.sharding import PartitionSpec as P

HDIM = 64
BLK = 128
NLIST = 2
WIN = 1
SPAN = 2 * WIN + 1
LANES = 128
TAIL = 16
SCALE = HDIM ** (-0.5)
FLOOR = -1e30
VMEM_LIMIT = 32 * 1024 * 1024
AXES = ("section", "seq")


def contract(left, right, left_dim, right_dim):
    return lax.dot_general(
        left, right, (((left_dim,), (right_dim,)), ((), ())), preferred_element_type=jnp.float32
    )


def attend_sample(
    seq_count, listed, source_len, target_len, rows, out, key_grad, value_grad, turned
):
    per_device = rows.shape[2] // BLK
    block_count = seq_count * per_device
    width = rows.shape[3]
    tile = min(width, LANES)
    heads = tile // HDIM
    key_grad[...] = jnp.zeros_like(key_grad)
    value_grad[...] = jnp.zeros_like(value_grad)
    inside = lax.broadcasted_iota(jnp.int32, (BLK, 1), 0)
    lane_head = lax.broadcasted_iota(jnp.int32, (BLK, tile), 1) // HDIM

    def place(block):
        if per_device == 1:
            return block, pl.ds(0, BLK)
        return block // per_device, pl.ds((block % per_device) * BLK, BLK)

    def own_heads(turned_result):
        return jnp.concatenate(
            [
                turned_result[head * HDIM : (head + 1) * HDIM, head * BLK : (head + 1) * BLK]
                for head in range(heads)
            ],
            axis=0,
        )

    def turn(block, carry):
        dev, here = place(block)
        for first in range(0, width, tile):
            for half in range(2):
                turned[block, half, pl.ds(first, tile)] = rows[
                    dev, half, here, pl.ds(first, tile)
                ].T
        return carry

    def step(block, carry):
        chosen = [listed(block, slot) for slot in range(NLIST)]
        places = [place(index) for index in chosen]
        target, target_rows = place(block)
        key_valid = jnp.concatenate(
            [index * BLK + inside < source_len for index in chosen], axis=0
        )
        live = block * BLK + inside < target_len
        for first in range(0, width, tile):
            lanes = pl.ds(first, tile)
            keys = jnp.concatenate([rows[dev, 0, here, lanes] for dev, here in places], axis=0)
            values = jnp.concatenate([rows[dev, 1, here, lanes] for dev, here in places], axis=0)
            queries = rows[seq_count + target, 0, target_rows, lanes] * jnp.bfloat16(SCALE)
            cots = rows[seq_count + target, 1, target_rows, lanes]
            none = jnp.zeros_like(queries)
            cots = jnp.where(live, cots, none)
            queries = jnp.concatenate(
                [jnp.where(lane_head == head, queries, none) for head in range(heads)], axis=0
            )
            cots = jnp.concatenate(
                [jnp.where(lane_head == head, cots, none) for head in range(heads)], axis=0
            )
            scores = jnp.where(key_valid, contract(keys, queries, 1, 1), FLOOR)
            expo = jnp.exp(scores - jnp.max(scores, axis=0, keepdims=True))
            probs = expo * (1.0 / jnp.sum(expo, axis=0, keepdims=True))
            dprob = contract(values, cots, 1, 1)
            delta = jnp.sum(probs * dprob, axis=0, keepdims=True)
            probs_low = probs.astype(jnp.bfloat16)
            dscore_low = (probs * (dprob - delta)).astype(jnp.bfloat16)
            dvalue = contract(probs_low, cots, 1, 0)
            dkey = contract(dscore_low, queries, 1, 0)
            keys_turned = jnp.concatenate([turned[index, 0, lanes] for index in chosen], axis=1)
            values_turned = jnp.concatenate([turned[index, 1, lanes] for index in chosen], axis=1)
            attended = own_heads(contract(values_turned, probs_low, 1, 0))
            dquery = own_heads(contract(keys_turned, dscore_low, 1, 0)) * SCALE
            attended = jnp.where(live, attended.astype(jnp.bfloat16).T, none)
            out[seq_count + target, 0, target_rows, lanes] = dquery.astype(jnp.bfloat16).T
            out[seq_count + target, 1, target_rows, lanes] = attended
            for slot, (dev, here) in enumerate(places):
                part = slice(slot * BLK, (slot + 1) * BLK)
                key_grad[dev, here, lanes] += dkey[part]
                value_grad[dev, here, lanes] += dvalue[part]
        return carry

    lax.fori_loop(0, block_count, turn, 0, unroll=block_count <= 4)
    lax.fori_loop(0, block_count, step, 0, unroll=block_count <= 4)
    out[:seq_count, 0] = key_grad[...].astype(jnp.bfloat16)
    out[:seq_count, 1] = value_grad[...].astype(jnp.bfloat16)


def attend_cost(block_count, width):
    pairs = block_count * NLIST * BLK * BLK * width
    return pl.CostEstimate(
        flops=10 * pairs,
        bytes_accessed=16 * block_count * BLK * width,
        transcendentals=pairs // HDIM,
    )


def specs(count, space):
    return [pl.BlockSpec(memory_space=space)] * count


def in_hbm(*arrays):
    return [pltpu.with_memory_space_constraint(array, pltpu.HBM) for array in arrays]


def gathered_kernel(
    seq_count, lists, source_len, target_len, rows, out, key_grad, value_grad, turned
):
    def listed(block, slot):
        return lists[block, slot]

    attend_sample(
        seq_count, listed, source_len[0], target_len[0], rows, out, key_grad, value_grad, turned
    )


def by_all_to_all(first_rows, second_rows, alignment, diffusion_mask, source_length, target_length):
    seq_count = lax.axis_size("seq")
    parts = lax.axis_size("section") * seq_count
    rows_here = first_rows.shape[2]
    width = first_rows.shape[3]
    on_encoder = lax.axis_index("section") == 0
    keep = on_encoder | (diffusion_mask[0] == 1)
    second = jnp.where(keep[:, None], second_rows[0, 0], jnp.zeros_like(second_rows[0, 0]))
    held = jnp.stack([first_rows[0, 0], second])
    held = held.reshape(2, rows_here, parts, width // parts).transpose(2, 0, 1, 3)
    lists = lax.all_gather(alignment[0], "seq", axis=0, tiled=True)
    rows = lax.all_to_all(held, AXES, 0, 0, tiled=True)
    grads = pltpu.VMEM((seq_count, rows_here, width // parts), jnp.float32)
    turned = pltpu.VMEM((lists.shape[0], 2, width // parts, BLK), rows.dtype)
    grads = pl.pallas_call(
        functools.partial(gathered_kernel, seq_count),
        out_shape=jax.ShapeDtypeStruct(rows.shape, rows.dtype),
        in_specs=specs(3, pltpu.SMEM) + specs(1, pltpu.VMEM),
        out_specs=pl.BlockSpec(memory_space=pltpu.VMEM),
        scratch_shapes=[grads, grads, turned],
        compiler_params=pltpu.CompilerParams(vmem_limit_bytes=VMEM_LIMIT),
        cost_estimate=attend_cost(lists.shape[0], width // parts),
        name="attend_gathered",
    )(lists, source_length, target_length, rows)
    grads = lax.all_to_all(grads, AXES, 0, 0, tiled=True)
    grads = grads.transpose(1, 2, 0, 3).reshape(2, rows_here, width)
    return (grads[0][None, None], grads[1][None, None])


def device_index(seq_count):
    return lax.axis_index("section") * seq_count + lax.axis_index("seq")


DIAGONAL = (6, 7)
OUTGOING = [(0,), (1,), DIAGONAL, (4,), (2,), (5,), (3,)]
INCOMING = [*OUTGOING, (7,)]


def pack_kernel(seq_count, steps, *refs):
    smalls, (first, second) = refs[:2], refs[2:4]
    outs, (lists, mask, small_sem, sem) = refs[4:-4], refs[-4:]
    me = device_index(seq_count)
    here = me % seq_count
    share = outs[0].shape[1]
    copies, pieces = [], []
    for group, out in zip(steps, outs):
        for place, step in enumerate(group):
            slot = len(copies)
            lanes = pl.ds(pl.multiple_of((me ^ step) * share, LANES), share)
            piece = out.at[pl.ds(place * 2 * BLK, 2 * BLK)]
            pair = [
                pltpu.make_async_copy(
                    source.at[0, 0, :, lanes], piece.at[pl.ds(half * BLK, BLK)], sem.at[half, slot]
                )
                for half, source in enumerate((first, second))
            ]
            for copy in pair:
                copy.start()
            copies.append(pair)
            pieces.append(piece)
    small_copies = [
        pltpu.make_async_copy(source, held, small_sem.at[slot])
        for slot, (source, held) in enumerate(zip(smalls, (lists, mask)))
    ]
    for copy in small_copies:
        copy.start()
    for copy in small_copies:
        copy.wait()
    keep = (mask[...] == 1) | (me < seq_count)
    keep = jnp.broadcast_to(jnp.where(keep, 1.0, 0.0), (BLK, BLK)).T.astype(jnp.bfloat16)
    keep = jnp.concatenate([keep] * (share // LANES), axis=1)
    base = here - WIN
    code = (lists[0, 0, 0] - base) * SPAN + lists[0, 0, 1] - base
    tail = jnp.full((TAIL, share), code, jnp.int32).astype(jnp.float32).astype(jnp.bfloat16)
    for out in outs:
        if out.shape[0] % (2 * BLK):
            out[2 * BLK :] = tail
    for piece, pair in zip(pieces, copies):
        for copy in pair:
            copy.wait()
        piece[BLK:] = piece[BLK:] * keep


def attend_kernel(seq_count, order, source_len, target_len, *refs):
    count = len(order)
    shares, outs = refs[:count], refs[count : 2 * count - 1]
    rows, result, key_grad, value_grad, turned, lists = refs[2 * count - 1 :]
    me = device_index(seq_count)
    here = me % seq_count
    for (step, *_), share in zip(order, shares):
        source = me ^ step
        rows[source, 0] = share[:BLK]
        rows[source, 1] = share[BLK : 2 * BLK]
        if step < seq_count:
            tail = share[2 * BLK :, :LANES].astype(jnp.float32)
            lists[here ^ step] = jnp.max(tail).astype(jnp.int32)

    def listed(block, slot):
        code = lists[block]
        return block - WIN + (code // SPAN if slot == 0 else code % SPAN)

    attend_sample(
        seq_count,
        listed,
        source_len[0],
        target_len[0],
        rows,
        result,
        key_grad,
        value_grad,
        turned,
    )
    for group, out in zip(OUTGOING, outs):
        for place, step in enumerate(group):
            out[2 * place * BLK : (2 * place + 1) * BLK] = result[me ^ step, 0]
            out[(2 * place + 1) * BLK : (2 * place + 2) * BLK] = result[me ^ step, 1]


def unpack_kernel(seq_count, steps, *refs):
    shares, (first, second, sem) = refs[: len(steps)], refs[-3:]
    width = shares[0].shape[1]
    me = device_index(seq_count)
    copies = []
    for slot, ((step, *_), share) in enumerate(zip(steps, shares)):
        lanes = pl.ds(pl.multiple_of((me ^ step) * width, LANES), width)
        for half, result in enumerate((first, second)):
            copy = pltpu.make_async_copy(
                share.at[pl.ds(half * BLK, BLK)], result.at[0, 0, :, lanes], sem.at[half, slot]
            )
            copy.start()
            copies.append(copy)
    for copy in copies:
        copy.wait()


def swapped(shares):
    parts = 8

    def move(share, step):
        return lax.ppermute(share, AXES, [(dev, dev ^ step) for dev in range(parts)])

    moved = {
        group: move(share, group[0]) if group[0] else share
        for group, share in zip(OUTGOING, shares)
    }
    moved[DIAGONAL], moved[(1,)] = lax.optimization_barrier((moved[DIAGONAL], moved[(1,)]))
    moved[(7,)] = move(moved[DIAGONAL][2 * BLK :], 1)
    return [moved[group] for group in INCOMING]


def by_pairs(first_rows, second_rows, alignment, diffusion_mask, source_length, target_length):
    seq_count = lax.axis_size("seq")
    parts = 2 * seq_count
    width = first_rows.shape[3]
    share = width // parts
    kind = first_rows.dtype
    params = pltpu.CompilerParams(vmem_limit_bytes=VMEM_LIMIT)
    sems = pltpu.SemaphoreType.DMA((2, parts))

    def sizes(groups, tail):
        return [
            jax.ShapeDtypeStruct(
                (len(group) * 2 * BLK + (tail if group[0] < seq_count else 0), share), kind
            )
            for group in groups
        ]

    def pack(groups, lists):
        return pl.pallas_call(
            functools.partial(pack_kernel, seq_count, groups),
            out_shape=sizes(groups, TAIL),
            in_specs=specs(4, pltpu.HBM),
            out_specs=specs(len(groups), pltpu.VMEM),
            scratch_shapes=[
                pltpu.SMEM(alignment.shape, jnp.int32),
                pltpu.VMEM(diffusion_mask.shape, jnp.int32),
                pltpu.SemaphoreType.DMA((2,)),
                sems,
            ],
            compiler_params=params,
            name="pack",
        )(*in_hbm(lists, diffusion_mask, first_rows, second_rows))

    rest = [group for group in OUTGOING if group != DIAGONAL]
    (diagonal,) = pack([DIAGONAL], alignment)
    lists, diagonal = lax.optimization_barrier((alignment, diagonal))
    shares = {DIAGONAL: diagonal, **dict(zip(rest, pack(rest, lists)))}
    shares = swapped([shares[group] for group in OUTGOING])
    rows = pltpu.VMEM((parts, 2, BLK, share), kind)
    grads = pltpu.VMEM((seq_count, BLK, share), jnp.float32)
    turned = pltpu.VMEM((seq_count, 2, share, BLK), kind)
    shares = pl.pallas_call(
        functools.partial(attend_kernel, seq_count, INCOMING),
        out_shape=sizes(OUTGOING, 0),
        in_specs=specs(2, pltpu.SMEM) + specs(len(INCOMING), pltpu.VMEM),
        out_specs=specs(len(OUTGOING), pltpu.VMEM),
        scratch_shapes=[rows, rows, grads, grads, turned, pltpu.SMEM((seq_count,), jnp.int32)],
        compiler_params=params,
        cost_estimate=attend_cost(seq_count, share),
        name="attend",
    )(source_length, target_length, *shares)
    shares = swapped(shares)
    out_shape = jax.ShapeDtypeStruct((1, 1, BLK, width), kind)
    return pl.pallas_call(
        functools.partial(unpack_kernel, seq_count, INCOMING),
        out_shape=[out_shape, out_shape],
        in_specs=specs(len(INCOMING), pltpu.VMEM),
        out_specs=specs(2, pltpu.HBM),
        scratch_shapes=[sems],
        compiler_params=params,
        name="unpack",
    )(*shares)


def on_device(first_rows, second_rows, alignment, diffusion_mask, source_length, target_length):
    seq_count = lax.axis_size("seq")
    parts = lax.axis_size("section") * seq_count
    paired = (
        (parts, seq_count) == (8, 4)
        and first_rows.shape[2] == BLK
        and first_rows.shape[3] % (parts * LANES) == 0
    )
    work = by_pairs if paired else by_all_to_all
    return tuple(
        work(first_rows, second_rows, alignment, diffusion_mask, source_length, target_length)
    )


def solution(mesh):
    placed = (
        P("section", "sample", "seq", None),
        P("section", "sample", "seq", None),
        P("sample", "seq", None),
        P("sample", "seq"),
        P("sample"),
        P("sample"),
    )
    return jax.shard_map(
        on_device,
        mesh=mesh,
        in_specs=placed,
        out_specs=(P("section", "sample", "seq", None), P("section", "sample", "seq", None)),
        check_vma=False,
    )
```

```python
import functools

import jax
import jax.numpy as jnp
from jax import lax
from jax.experimental import pallas as pl
from jax.experimental.pallas import tpu as pltpu
from jax.sharding import PartitionSpec as P

HDIM = 64
BLK = 128
NLIST = 2
WIN = 1
SPAN = 2 * WIN + 1
LANES = 128
TAIL = 16
SCALE = HDIM ** (-0.5)
FLOOR = -1e30
VMEM_LIMIT = 32 * 1024 * 1024
AXES = ("section", "seq")


def contract(left, right, left_dim, right_dim):
    return lax.dot_general(
        left, right, (((left_dim,), (right_dim,)), ((), ())), preferred_element_type=jnp.float32
    )


def attend_sample(
    seq_count, listed, source_len, target_len, rows, out, key_grad, value_grad, turned
):
    per_device = rows.shape[2] // BLK
    block_count = seq_count * per_device
    width = rows.shape[3]
    tile = min(width, LANES)
    heads = tile // HDIM
    key_grad[...] = jnp.zeros_like(key_grad)
    value_grad[...] = jnp.zeros_like(value_grad)
    inside = lax.broadcasted_iota(jnp.int32, (BLK, 1), 0)
    lane_head = lax.broadcasted_iota(jnp.int32, (BLK, tile), 1) // HDIM

    def place(block):
        if per_device == 1:
            return block, pl.ds(0, BLK)
        return block // per_device, pl.ds((block % per_device) * BLK, BLK)

    def own_heads(turned_result):
        return jnp.concatenate(
            [
                turned_result[head * HDIM : (head + 1) * HDIM, head * BLK : (head + 1) * BLK]
                for head in range(heads)
            ],
            axis=0,
        )

    def turn(block, carry):
        dev, here = place(block)
        for first in range(0, width, tile):
            for half in range(2):
                turned[block, half, pl.ds(first, tile)] = rows[
                    dev, half, here, pl.ds(first, tile)
                ].T
        return carry

    def step(block, carry):
        chosen = [listed(block, slot) for slot in range(NLIST)]
        places = [place(index) for index in chosen]
        target, target_rows = place(block)
        key_valid = jnp.concatenate(
            [index * BLK + inside < source_len for index in chosen], axis=0
        )
        live = block * BLK + inside < target_len
        for first in range(0, width, tile):
            lanes = pl.ds(first, tile)
            keys = jnp.concatenate([rows[dev, 0, here, lanes] for dev, here in places], axis=0)
            values = jnp.concatenate([rows[dev, 1, here, lanes] for dev, here in places], axis=0)
            queries = rows[seq_count + target, 0, target_rows, lanes] * jnp.bfloat16(SCALE)
            cots = rows[seq_count + target, 1, target_rows, lanes]
            none = jnp.zeros_like(queries)
            cots = jnp.where(live, cots, none)
            queries = jnp.concatenate(
                [jnp.where(lane_head == head, queries, none) for head in range(heads)], axis=0
            )
            cots = jnp.concatenate(
                [jnp.where(lane_head == head, cots, none) for head in range(heads)], axis=0
            )
            scores = jnp.where(key_valid, contract(keys, queries, 1, 1), FLOOR)
            expo = jnp.exp(scores - jnp.max(scores, axis=0, keepdims=True))
            probs = expo * (1.0 / jnp.sum(expo, axis=0, keepdims=True))
            dprob = contract(values, cots, 1, 1)
            delta = jnp.sum(probs * dprob, axis=0, keepdims=True)
            probs_low = probs.astype(jnp.bfloat16)
            dscore_low = (probs * (dprob - delta)).astype(jnp.bfloat16)
            dvalue = contract(probs_low, cots, 1, 0)
            dkey = contract(dscore_low, queries, 1, 0)
            keys_turned = jnp.concatenate([turned[index, 0, lanes] for index in chosen], axis=1)
            values_turned = jnp.concatenate([turned[index, 1, lanes] for index in chosen], axis=1)
            attended = own_heads(contract(values_turned, probs_low, 1, 0))
            dquery = own_heads(contract(keys_turned, dscore_low, 1, 0)) * SCALE
            attended = jnp.where(live, attended.astype(jnp.bfloat16).T, none)
            out[seq_count + target, 0, target_rows, lanes] = dquery.astype(jnp.bfloat16).T
            out[seq_count + target, 1, target_rows, lanes] = attended
            for slot, (dev, here) in enumerate(places):
                part = slice(slot * BLK, (slot + 1) * BLK)
                key_grad[dev, here, lanes] += dkey[part]
                value_grad[dev, here, lanes] += dvalue[part]
        return carry

    lax.fori_loop(0, block_count, turn, 0, unroll=block_count <= 4)
    lax.fori_loop(0, block_count, step, 0, unroll=block_count <= 4)
    out[:seq_count, 0] = key_grad[...].astype(jnp.bfloat16)
    out[:seq_count, 1] = value_grad[...].astype(jnp.bfloat16)


def attend_cost(block_count, width):
    pairs = block_count * NLIST * BLK * BLK * width
    return pl.CostEstimate(
        flops=10 * pairs,
        bytes_accessed=16 * block_count * BLK * width,
        transcendentals=pairs // HDIM,
    )


def specs(count, space):
    return [pl.BlockSpec(memory_space=space)] * count


def in_hbm(*arrays):
    return [pltpu.with_memory_space_constraint(array, pltpu.HBM) for array in arrays]


def gathered_kernel(
    seq_count, lists, source_len, target_len, rows, out, key_grad, value_grad, turned
):
    def listed(block, slot):
        return lists[block, slot]

    attend_sample(
        seq_count, listed, source_len[0], target_len[0], rows, out, key_grad, value_grad, turned
    )


def by_all_to_all(first_rows, second_rows, alignment, diffusion_mask, source_length, target_length):
    seq_count = lax.axis_size("seq")
    parts = lax.axis_size("section") * seq_count
    rows_here = first_rows.shape[2]
    width = first_rows.shape[3]
    on_encoder = lax.axis_index("section") == 0
    keep = on_encoder | (diffusion_mask[0] == 1)
    second = jnp.where(keep[:, None], second_rows[0, 0], jnp.zeros_like(second_rows[0, 0]))
    held = jnp.stack([first_rows[0, 0], second])
    held = held.reshape(2, rows_here, parts, width // parts).transpose(2, 0, 1, 3)
    lists = lax.all_gather(alignment[0], "seq", axis=0, tiled=True)
    rows = lax.all_to_all(held, AXES, 0, 0, tiled=True)
    grads = pltpu.VMEM((seq_count, rows_here, width // parts), jnp.float32)
    turned = pltpu.VMEM((lists.shape[0], 2, width // parts, BLK), rows.dtype)
    grads = pl.pallas_call(
        functools.partial(gathered_kernel, seq_count),
        out_shape=jax.ShapeDtypeStruct(rows.shape, rows.dtype),
        in_specs=specs(3, pltpu.SMEM) + specs(1, pltpu.VMEM),
        out_specs=pl.BlockSpec(memory_space=pltpu.VMEM),
        scratch_shapes=[grads, grads, turned],
        compiler_params=pltpu.CompilerParams(vmem_limit_bytes=VMEM_LIMIT),
        cost_estimate=attend_cost(lists.shape[0], width // parts),
        name="attend_gathered",
    )(lists, source_length, target_length, rows)
    grads = lax.all_to_all(grads, AXES, 0, 0, tiled=True)
    grads = grads.transpose(1, 2, 0, 3).reshape(2, rows_here, width)
    return (grads[0][None, None], grads[1][None, None])


def device_index(seq_count):
    return lax.axis_index("section") * seq_count + lax.axis_index("seq")


DIAGONAL = (6, 7)
REST = [(0,), (1,), (4,), (2,), (5,), (3,)]
OUTGOING = [DIAGONAL, *REST]
INCOMING = [*OUTGOING, DIAGONAL[1:]]
TILES = 2
AFTER = REST.index((1,))


def pack_kernel(seq_count, steps, *refs):
    smalls, (first, second) = refs[:2], refs[2:4]
    outs, (lists, mask, small_sem, sem) = refs[4:-4], refs[-4:]
    me = device_index(seq_count)
    here = me % seq_count
    share = outs[0].shape[1]
    copies, pieces = [], []
    for group, out in zip(steps, outs):
        for place, step in enumerate(group):
            slot = len(copies)
            lanes = pl.ds(pl.multiple_of((me ^ step) * share, LANES), share)
            piece = out.at[pl.ds(place * 2 * BLK, 2 * BLK)]
            pair = [
                pltpu.make_async_copy(
                    source.at[0, 0, :, lanes], piece.at[pl.ds(half * BLK, BLK)], sem.at[half, slot]
                )
                for half, source in enumerate((first, second))
            ]
            for copy in pair:
                copy.start()
            copies.append(pair)
            pieces.append(piece)
    small_copies = [
        pltpu.make_async_copy(source, held, small_sem.at[slot])
        for slot, (source, held) in enumerate(zip(smalls, (lists, mask)))
    ]
    for copy in small_copies:
        copy.start()
    for copy in small_copies:
        copy.wait()
    keep = (mask[...] == 1) | (me < seq_count)
    keep = jnp.broadcast_to(jnp.where(keep, 1.0, 0.0), (BLK, BLK)).T.astype(jnp.bfloat16)
    keep = jnp.concatenate([keep] * (share // LANES), axis=1)
    base = here - WIN
    code = (lists[0, 0, 0] - base) * SPAN + lists[0, 0, 1] - base
    tail = jnp.full((TAIL, share), code, jnp.int32).astype(jnp.float32).astype(jnp.bfloat16)
    for out in outs:
        if out.shape[0] % (2 * BLK):
            out[2 * BLK :] = tail
    for piece, pair in zip(pieces, copies):
        for copy in pair:
            copy.wait()
        piece[BLK:] = piece[BLK:] * keep


def attend_kernel(seq_count, turn, source_len, target_len, *refs):
    parts, rest = len(INCOMING), len(OUTGOING) - 1
    shares, before = refs[:parts], refs[parts : parts + (rest if turn else 0)]
    outs = refs[parts + len(before) : parts + len(before) + 1 + rest]
    rows, result, key_grad, value_grad, turned, lists = refs[parts + len(before) + 1 + rest :]
    me = device_index(seq_count)
    here = me % seq_count
    lanes = pl.ds(turn * LANES, LANES)
    for (step, *_), share in zip(INCOMING, shares):
        source = me ^ step
        rows[source, 0] = share[pl.ds(0, BLK), lanes]
        rows[source, 1] = share[pl.ds(BLK, BLK), lanes]
        if step < seq_count:
            tail = share[pl.ds(2 * BLK, TAIL), lanes].astype(jnp.float32)
            lists[here ^ step] = jnp.max(tail).astype(jnp.int32)

    def listed(block, slot):
        code = lists[block]
        return block - WIN + (code // SPAN if slot == 0 else code % SPAN)

    attend_sample(
        seq_count,
        listed,
        source_len[0],
        target_len[0],
        rows,
        result,
        key_grad,
        value_grad,
        turned,
    )
    diagonal, *others = outs
    for place, step in enumerate(DIAGONAL):
        for half in range(2):
            diagonal[pl.ds((2 * place + half) * BLK, BLK)] = result[me ^ step, half]
    for group, out in zip(REST, others):
        for half in range(2):
            out[pl.ds(half * BLK, BLK), lanes] = result[me ^ group[0], half]
    for done, out in zip(before, others):
        out[:, pl.ds(0, turn * LANES)] = done[...]


def unpack_kernel(seq_count, *refs):
    diagonals, shares = refs[:TILES], refs[TILES : TILES + len(REST) + 1]
    first, second, sem = refs[-3:]
    width = first.shape[3] // (2 * seq_count)
    me = device_index(seq_count)
    pieces = [
        (DIAGONAL[0], tile * LANES, share.at[pl.ds(0, 2 * BLK)])
        for tile, share in enumerate(diagonals)
    ]
    pieces += [(group[0], 0, share) for group, share in zip([*REST, DIAGONAL[1:]], shares)]
    copies = []
    for slot, (step, start, share) in enumerate(pieces):
        lanes = pl.ds(pl.multiple_of((me ^ step) * width + start, LANES), share.shape[1])
        for half, result in enumerate((first, second)):
            copy = pltpu.make_async_copy(
                share.at[pl.ds(half * BLK, BLK)], result.at[0, 0, :, lanes], sem.at[half, slot]
            )
            copy.start()
            copies.append(copy)
    for copy in copies:
        copy.wait()


def permuted(share, step):
    return lax.ppermute(share, AXES, [(dev, dev ^ step) for dev in range(8)])


def swapped(diagonals, shares):
    diagonals, shares = [permuted(share, DIAGONAL[0]) for share in diagonals], list(shares)
    for share in diagonals[:-1]:
        shares[AFTER], diagonals[0] = lax.optimization_barrier((shares[AFTER], diagonals[0]))
    shares = [permuted(share, step) if step else share for (step,), share in zip(REST, shares)]
    near = REST.index((1,))
    diagonals[-1], shares[near] = lax.optimization_barrier((diagonals[-1], shares[near]))
    handed_on = [share[share.shape[0] // 2 :] for share in diagonals]
    return diagonals, shares, permuted(jnp.concatenate(handed_on, axis=1), 1)


def by_pairs(first_rows, second_rows, alignment, diffusion_mask, source_length, target_length):
    seq_count = lax.axis_size("seq")
    parts = 2 * seq_count
    width = first_rows.shape[3]
    share = width // parts
    kind = first_rows.dtype
    params = pltpu.CompilerParams(vmem_limit_bytes=VMEM_LIMIT)
    sems = pltpu.SemaphoreType.DMA((2, parts))

    def sizes(groups, tail):
        return [
            jax.ShapeDtypeStruct(
                (len(group) * 2 * BLK + (tail if group[0] < seq_count else 0), share), kind
            )
            for group in groups
        ]

    def pack(groups, lists):
        return pl.pallas_call(
            functools.partial(pack_kernel, seq_count, groups),
            out_shape=sizes(groups, TAIL),
            in_specs=specs(4, pltpu.HBM),
            out_specs=specs(len(groups), pltpu.VMEM),
            scratch_shapes=[
                pltpu.SMEM(alignment.shape, jnp.int32),
                pltpu.VMEM(diffusion_mask.shape, jnp.int32),
                pltpu.SemaphoreType.DMA((2,)),
                sems,
            ],
            compiler_params=params,
            name="pack",
        )(*in_hbm(lists, diffusion_mask, first_rows, second_rows))

    (diagonal,) = pack([DIAGONAL], alignment)
    lists, diagonal = lax.optimization_barrier((alignment, diagonal))
    (diagonal,), shares, handed_on = swapped([diagonal], pack(REST, lists))
    coming = [diagonal, *shares, handed_on]
    rows = pltpu.VMEM((parts, 2, BLK, LANES), kind)
    grads = pltpu.VMEM((seq_count, BLK, LANES), jnp.float32)
    turned = pltpu.VMEM((seq_count, 2, LANES, BLK), kind)

    def attend(turn, *before):
        lanes = (turn + 1) * LANES
        return pl.pallas_call(
            functools.partial(attend_kernel, seq_count, turn),
            out_shape=[
                jax.ShapeDtypeStruct((4 * BLK, LANES), kind),
                *([jax.ShapeDtypeStruct((2 * BLK, lanes), kind)] * len(REST)),
            ],
            in_specs=specs(2, pltpu.SMEM) + specs(len(coming) + len(before), pltpu.VMEM),
            out_specs=specs(1 + len(REST), pltpu.VMEM),
            scratch_shapes=[rows, rows, grads, grads, turned, pltpu.SMEM((seq_count,), jnp.int32)],
            compiler_params=params,
            cost_estimate=attend_cost(seq_count, LANES),
            name="attend",
        )(source_length, target_length, *coming, *before)

    diagonals, shares = [], []
    for turn in range(TILES):
        diagonal, *shares = attend(turn, *shares)
        diagonals.append(diagonal)
    diagonals, shares, handed_on = swapped(diagonals, shares)
    out_shape = jax.ShapeDtypeStruct((1, 1, BLK, width), kind)
    return pl.pallas_call(
        functools.partial(unpack_kernel, seq_count),
        out_shape=[out_shape, out_shape],
        in_specs=specs(TILES + len(REST) + 1, pltpu.VMEM),
        out_specs=specs(2, pltpu.HBM),
        scratch_shapes=[pltpu.SemaphoreType.DMA((2, parts + TILES))],
        compiler_params=params,
        name="unpack",
    )(*diagonals, *shares, handed_on)


def on_device(first_rows, second_rows, alignment, diffusion_mask, source_length, target_length):
    seq_count = lax.axis_size("seq")
    parts = lax.axis_size("section") * seq_count
    paired = (
        (parts, seq_count) == (8, 4)
        and first_rows.shape[2] == BLK
        and first_rows.shape[3] == parts * TILES * LANES
    )
    work = by_pairs if paired else by_all_to_all
    return tuple(
        work(first_rows, second_rows, alignment, diffusion_mask, source_length, target_length)
    )


def solution(mesh):
    placed = (
        P("section", "sample", "seq", None),
        P("section", "sample", "seq", None),
        P("sample", "seq", None),
        P("sample", "seq"),
        P("sample"),
        P("sample"),
    )
    return jax.shard_map(
        on_device,
        mesh=mesh,
        in_specs=placed,
        out_specs=(P("section", "sample", "seq", None), P("section", "sample", "seq", None)),
        check_vma=False,
    )
```

```python
import functools

import jax
import jax.numpy as jnp
from jax import lax
from jax.experimental import pallas as pl
from jax.experimental.pallas import tpu as pltpu
from jax.sharding import PartitionSpec as P

HDIM = 64
BLK = 128
NLIST = 2
WIN = 1
SPAN = 2 * WIN + 1
LANES = 128
TAIL = 16
SCALE = HDIM ** (-0.5)
FLOOR = -1e30
VMEM_LIMIT = 32 * 1024 * 1024
AXES = ("section", "seq")


def contract(left, right, left_dim, right_dim):
    return lax.dot_general(
        left, right, (((left_dim,), (right_dim,)), ((), ())), preferred_element_type=jnp.float32
    )


def attend_sample(
    seq_count, listed, source_len, target_len, rows, out, key_grad, value_grad, turned
):
    per_device = rows.shape[2] // BLK
    block_count = seq_count * per_device
    width = rows.shape[3]
    tile = min(width, LANES)
    heads = tile // HDIM
    key_grad[...] = jnp.zeros_like(key_grad)
    value_grad[...] = jnp.zeros_like(value_grad)
    inside = lax.broadcasted_iota(jnp.int32, (BLK, 1), 0)
    lane_head = lax.broadcasted_iota(jnp.int32, (BLK, tile), 1) // HDIM

    def place(block):
        if per_device == 1:
            return block, pl.ds(0, BLK)
        return block // per_device, pl.ds((block % per_device) * BLK, BLK)

    def own_heads(turned_result):
        return jnp.concatenate(
            [
                turned_result[head * HDIM : (head + 1) * HDIM, head * BLK : (head + 1) * BLK]
                for head in range(heads)
            ],
            axis=0,
        )

    def turn(block, carry):
        dev, here = place(block)
        for first in range(0, width, tile):
            for half in range(2):
                turned[block, half, pl.ds(first, tile)] = rows[
                    dev, half, here, pl.ds(first, tile)
                ].T
        return carry

    def step(block, carry):
        chosen = [listed(block, slot) for slot in range(NLIST)]
        places = [place(index) for index in chosen]
        target, target_rows = place(block)
        key_valid = jnp.concatenate(
            [index * BLK + inside < source_len for index in chosen], axis=0
        )
        live = block * BLK + inside < target_len
        for first in range(0, width, tile):
            lanes = pl.ds(first, tile)
            keys = jnp.concatenate([rows[dev, 0, here, lanes] for dev, here in places], axis=0)
            values = jnp.concatenate([rows[dev, 1, here, lanes] for dev, here in places], axis=0)
            queries = rows[seq_count + target, 0, target_rows, lanes] * jnp.bfloat16(SCALE)
            cots = rows[seq_count + target, 1, target_rows, lanes]
            none = jnp.zeros_like(queries)
            cots = jnp.where(live, cots, none)
            queries = jnp.concatenate(
                [jnp.where(lane_head == head, queries, none) for head in range(heads)], axis=0
            )
            cots = jnp.concatenate(
                [jnp.where(lane_head == head, cots, none) for head in range(heads)], axis=0
            )
            scores = jnp.where(key_valid, contract(keys, queries, 1, 1), FLOOR)
            expo = jnp.exp(scores - jnp.max(scores, axis=0, keepdims=True))
            probs = expo * (1.0 / jnp.sum(expo, axis=0, keepdims=True))
            dprob = contract(values, cots, 1, 1)
            delta = jnp.sum(probs * dprob, axis=0, keepdims=True)
            probs_low = probs.astype(jnp.bfloat16)
            dscore_low = (probs * (dprob - delta)).astype(jnp.bfloat16)
            dvalue = contract(probs_low, cots, 1, 0)
            dkey = contract(dscore_low, queries, 1, 0)
            keys_turned = jnp.concatenate([turned[index, 0, lanes] for index in chosen], axis=1)
            values_turned = jnp.concatenate([turned[index, 1, lanes] for index in chosen], axis=1)
            attended = own_heads(contract(values_turned, probs_low, 1, 0))
            dquery = own_heads(contract(keys_turned, dscore_low, 1, 0)) * SCALE
            attended = jnp.where(live, attended.astype(jnp.bfloat16).T, none)
            out[seq_count + target, 0, target_rows, lanes] = dquery.astype(jnp.bfloat16).T
            out[seq_count + target, 1, target_rows, lanes] = attended
            for slot, (dev, here) in enumerate(places):
                part = slice(slot * BLK, (slot + 1) * BLK)
                key_grad[dev, here, lanes] += dkey[part]
                value_grad[dev, here, lanes] += dvalue[part]
        return carry

    lax.fori_loop(0, block_count, turn, 0, unroll=block_count <= 4)
    lax.fori_loop(0, block_count, step, 0, unroll=block_count <= 4)
    out[:seq_count, 0] = key_grad[...].astype(jnp.bfloat16)
    out[:seq_count, 1] = value_grad[...].astype(jnp.bfloat16)


def attend_cost(block_count, width):
    pairs = block_count * NLIST * BLK * BLK * width
    return pl.CostEstimate(
        flops=10 * pairs,
        bytes_accessed=16 * block_count * BLK * width,
        transcendentals=pairs // HDIM,
    )


def specs(count, space):
    return [pl.BlockSpec(memory_space=space)] * count


def in_hbm(*arrays):
    return [pltpu.with_memory_space_constraint(array, pltpu.HBM) for array in arrays]


def gathered_kernel(
    seq_count, lists, source_len, target_len, rows, out, key_grad, value_grad, turned
):
    def listed(block, slot):
        return lists[block, slot]

    attend_sample(
        seq_count, listed, source_len[0], target_len[0], rows, out, key_grad, value_grad, turned
    )


def by_all_to_all(first_rows, second_rows, alignment, diffusion_mask, source_length, target_length):
    seq_count = lax.axis_size("seq")
    parts = lax.axis_size("section") * seq_count
    rows_here = first_rows.shape[2]
    width = first_rows.shape[3]
    on_encoder = lax.axis_index("section") == 0
    keep = on_encoder | (diffusion_mask[0] == 1)
    second = jnp.where(keep[:, None], second_rows[0, 0], jnp.zeros_like(second_rows[0, 0]))
    held = jnp.stack([first_rows[0, 0], second])
    held = held.reshape(2, rows_here, parts, width // parts).transpose(2, 0, 1, 3)
    lists = lax.all_gather(alignment[0], "seq", axis=0, tiled=True)
    rows = lax.all_to_all(held, AXES, 0, 0, tiled=True)
    grads = pltpu.VMEM((seq_count, rows_here, width // parts), jnp.float32)
    turned = pltpu.VMEM((lists.shape[0], 2, width // parts, BLK), rows.dtype)
    grads = pl.pallas_call(
        functools.partial(gathered_kernel, seq_count),
        out_shape=jax.ShapeDtypeStruct(rows.shape, rows.dtype),
        in_specs=specs(3, pltpu.SMEM) + specs(1, pltpu.VMEM),
        out_specs=pl.BlockSpec(memory_space=pltpu.VMEM),
        scratch_shapes=[grads, grads, turned],
        compiler_params=pltpu.CompilerParams(vmem_limit_bytes=VMEM_LIMIT),
        cost_estimate=attend_cost(lists.shape[0], width // parts),
        name="attend_gathered",
    )(lists, source_length, target_length, rows)
    grads = lax.all_to_all(grads, AXES, 0, 0, tiled=True)
    grads = grads.transpose(1, 2, 0, 3).reshape(2, rows_here, width)
    return (grads[0][None, None], grads[1][None, None])


def device_index(seq_count):
    return lax.axis_index("section") * seq_count + lax.axis_index("seq")


DIAGONAL = (6, 7)
OWN, NEAR = (0,), (1,)
ACROSS = [(4,), (2,), (5,), (3,)]
REST = [OWN, NEAR, *ACROSS]
OUTGOING = [DIAGONAL, *REST]
INCOMING = [*OUTGOING, DIAGONAL[1:]]
TILES = 2


def pack_kernel(seq_count, steps, *refs):
    smalls, (first, second) = refs[:2], refs[2:4]
    outs, (lists, mask, small_sem, sem) = refs[4:-4], refs[-4:]
    me = device_index(seq_count)
    here = me % seq_count
    share = outs[0].shape[1]
    copies, pieces = [], []
    for group, out in zip(steps, outs):
        for place, step in enumerate(group):
            slot = len(copies)
            lanes = pl.ds(pl.multiple_of((me ^ step) * share, LANES), share)
            piece = out.at[pl.ds(place * 2 * BLK, 2 * BLK)]
            pair = [
                pltpu.make_async_copy(
                    source.at[0, 0, :, lanes], piece.at[pl.ds(half * BLK, BLK)], sem.at[half, slot]
                )
                for half, source in enumerate((first, second))
            ]
            for copy in pair:
                copy.start()
            copies.append(pair)
            pieces.append(piece)
    small_copies = [
        pltpu.make_async_copy(source, held, small_sem.at[slot])
        for slot, (source, held) in enumerate(zip(smalls, (lists, mask)))
    ]
    for copy in small_copies:
        copy.start()
    for copy in small_copies:
        copy.wait()
    keep = (mask[...] == 1) | (me < seq_count)
    keep = jnp.broadcast_to(jnp.where(keep, 1.0, 0.0), (BLK, BLK)).T.astype(jnp.bfloat16)
    keep = jnp.concatenate([keep] * (share // LANES), axis=1)
    base = here - WIN
    code = (lists[0, 0, 0] - base) * SPAN + lists[0, 0, 1] - base
    tail = jnp.full((TAIL, share), code, jnp.int32).astype(jnp.float32).astype(jnp.bfloat16)
    for out in outs:
        if out.shape[0] % (2 * BLK):
            out[2 * BLK :] = tail
    for piece, pair in zip(pieces, copies):
        for copy in pair:
            copy.wait()
        piece[BLK:] = piece[BLK:] * keep


def attend_kernel(seq_count, turn, source_len, target_len, *refs):
    parts, rest = len(INCOMING), len(OUTGOING) - 1
    shares, before = refs[:parts], refs[parts : parts + (rest if turn else 0)]
    outs = refs[parts + len(before) : parts + len(before) + 1 + rest]
    rows, result, key_grad, value_grad, turned, lists = refs[parts + len(before) + 1 + rest :]
    me = device_index(seq_count)
    here = me % seq_count
    lanes = pl.ds(turn * LANES, LANES)
    for (step, *_), share in zip(INCOMING, shares):
        source = me ^ step
        rows[source, 0] = share[pl.ds(0, BLK), lanes]
        rows[source, 1] = share[pl.ds(BLK, BLK), lanes]
        if step < seq_count:
            tail = share[pl.ds(2 * BLK, TAIL), lanes].astype(jnp.float32)
            lists[here ^ step] = jnp.max(tail).astype(jnp.int32)

    def listed(block, slot):
        code = lists[block]
        return block - WIN + (code // SPAN if slot == 0 else code % SPAN)

    attend_sample(
        seq_count,
        listed,
        source_len[0],
        target_len[0],
        rows,
        result,
        key_grad,
        value_grad,
        turned,
    )
    diagonal, *others = outs
    for place, step in enumerate(DIAGONAL):
        for half in range(2):
            diagonal[pl.ds((2 * place + half) * BLK, BLK)] = result[me ^ step, half]
    for group, out in zip(REST, others):
        for half in range(2):
            out[pl.ds(half * BLK, BLK), lanes] = result[me ^ group[0], half]
    for done, out in zip(before, others):
        out[:, pl.ds(0, turn * LANES)] = done[...]


def unpack_kernel(seq_count, *refs):
    diagonals, handed_on, shares = refs[:TILES], refs[TILES : 2 * TILES], refs[2 * TILES : -3]
    first, second, sem = refs[-3:]
    width = first.shape[3] // (2 * seq_count)
    me = device_index(seq_count)
    pieces = [
        (step, tile * LANES, share.at[pl.ds(0, 2 * BLK)])
        for step, arrived in zip(DIAGONAL, (diagonals, handed_on))
        for tile, share in enumerate(arrived)
    ]
    pieces += [(step, 0, share) for (step,), share in zip(REST, shares)]
    copies = []
    for slot, (step, start, share) in enumerate(pieces):
        lanes = pl.ds(pl.multiple_of((me ^ step) * width + start, LANES), share.shape[1])
        for half, result in enumerate((first, second)):
            copy = pltpu.make_async_copy(
                share.at[pl.ds(half * BLK, BLK)], result.at[0, 0, :, lanes], sem.at[half, slot]
            )
            copy.start()
            copies.append(copy)
    for copy in copies:
        copy.wait()


def permuted(share, step):
    return lax.ppermute(share, AXES, [(dev, dev ^ step) for dev in range(8)])


def swapped(diagonals, shares):
    held = dict(zip(REST, shares))
    diagonals = [permuted(share, DIAGONAL[0]) for share in diagonals]
    moved = {group: permuted(held[group], group[0]) for group in ACROSS}
    if len(diagonals) > 1:
        held[NEAR], diagonals[0] = lax.optimization_barrier((held[NEAR], diagonals[0]))
    moved[NEAR] = permuted(held[NEAR], NEAR[0])
    if len(diagonals) == 1:
        diagonals[0], moved[NEAR] = lax.optimization_barrier((diagonals[0], moved[NEAR]))
    handed_on = [permuted(share[share.shape[0] // 2 :], NEAR[0]) for share in diagonals]
    return diagonals, [held[OWN], moved[NEAR], *(moved[group] for group in ACROSS)], handed_on


def by_pairs(first_rows, second_rows, alignment, diffusion_mask, source_length, target_length):
    seq_count = lax.axis_size("seq")
    parts = 2 * seq_count
    width = first_rows.shape[3]
    share = width // parts
    kind = first_rows.dtype
    params = pltpu.CompilerParams(vmem_limit_bytes=VMEM_LIMIT)
    sems = pltpu.SemaphoreType.DMA((2, parts))

    def sizes(groups, tail):
        return [
            jax.ShapeDtypeStruct(
                (len(group) * 2 * BLK + (tail if group[0] < seq_count else 0), share), kind
            )
            for group in groups
        ]

    def pack(groups, lists):
        return pl.pallas_call(
            functools.partial(pack_kernel, seq_count, groups),
            out_shape=sizes(groups, TAIL),
            in_specs=specs(4, pltpu.HBM),
            out_specs=specs(len(groups), pltpu.VMEM),
            scratch_shapes=[
                pltpu.SMEM(alignment.shape, jnp.int32),
                pltpu.VMEM(diffusion_mask.shape, jnp.int32),
                pltpu.SemaphoreType.DMA((2,)),
                sems,
            ],
            compiler_params=params,
            name="pack",
        )(*in_hbm(lists, diffusion_mask, first_rows, second_rows))

    (diagonal,) = pack([DIAGONAL], alignment)
    lists, diagonal = lax.optimization_barrier((alignment, diagonal))
    diagonals, shares, handed_on = swapped([diagonal], pack(REST, lists))
    coming = [*diagonals, *shares, *handed_on]
    rows = pltpu.VMEM((parts, 2, BLK, LANES), kind)
    grads = pltpu.VMEM((seq_count, BLK, LANES), jnp.float32)
    turned = pltpu.VMEM((seq_count, 2, LANES, BLK), kind)

    def attend(turn, *before):
        lanes = (turn + 1) * LANES
        return pl.pallas_call(
            functools.partial(attend_kernel, seq_count, turn),
            out_shape=[
                jax.ShapeDtypeStruct((4 * BLK, LANES), kind),
                *([jax.ShapeDtypeStruct((2 * BLK, lanes), kind)] * len(REST)),
            ],
            in_specs=specs(2, pltpu.SMEM) + specs(len(coming) + len(before), pltpu.VMEM),
            out_specs=specs(1 + len(REST), pltpu.VMEM),
            scratch_shapes=[rows, rows, grads, grads, turned, pltpu.SMEM((seq_count,), jnp.int32)],
            compiler_params=params,
            cost_estimate=attend_cost(seq_count, LANES),
            name="attend",
        )(source_length, target_length, *coming, *before)

    diagonals, shares = [], []
    for turn in range(TILES):
        diagonal, *shares = attend(turn, *shares)
        diagonals.append(diagonal)
    diagonals, shares, handed_on = swapped(diagonals, shares)
    out_shape = jax.ShapeDtypeStruct((1, 1, BLK, width), kind)
    return pl.pallas_call(
        functools.partial(unpack_kernel, seq_count),
        out_shape=[out_shape, out_shape],
        in_specs=specs(2 * TILES + len(REST), pltpu.VMEM),
        out_specs=specs(2, pltpu.HBM),
        scratch_shapes=[pltpu.SemaphoreType.DMA((2, parts + 2 * TILES))],
        compiler_params=params,
        name="unpack",
    )(*diagonals, *handed_on, *shares)


def on_device(first_rows, second_rows, alignment, diffusion_mask, source_length, target_length):
    seq_count = lax.axis_size("seq")
    parts = lax.axis_size("section") * seq_count
    paired = (
        (parts, seq_count) == (8, 4)
        and first_rows.shape[2] == BLK
        and first_rows.shape[3] == parts * TILES * LANES
    )
    work = by_pairs if paired else by_all_to_all
    return tuple(
        work(first_rows, second_rows, alignment, diffusion_mask, source_length, target_length)
    )


def solution(mesh):
    placed = (
        P("section", "sample", "seq", None),
        P("section", "sample", "seq", None),
        P("sample", "seq", None),
        P("sample", "seq"),
        P("sample"),
        P("sample"),
    )
    return jax.shard_map(
        on_device,
        mesh=mesh,
        in_specs=placed,
        out_specs=(P("section", "sample", "seq", None), P("section", "sample", "seq", None)),
        check_vma=False,
    )
```

```python
import functools

import jax
import jax.numpy as jnp
from jax import lax
from jax.experimental import pallas as pl
from jax.experimental.pallas import tpu as pltpu
from jax.sharding import PartitionSpec as P

HDIM = 64
BLK = 128
NLIST = 2
WIN = 1
SPAN = 2 * WIN + 1
LANES = 128
TAIL = 16
SCALE = HDIM ** (-0.5)
FLOOR = -1e30
VMEM_LIMIT = 32 * 1024 * 1024
AXES = ("section", "seq")


def contract(left, right, left_dim, right_dim):
    return lax.dot_general(
        left, right, (((left_dim,), (right_dim,)), ((), ())), preferred_element_type=jnp.float32
    )


def attend_sample(
    seq_count, listed, source_len, target_len, rows, out, key_grad, value_grad, turned
):
    per_device = rows.shape[2] // BLK
    block_count = seq_count * per_device
    width = rows.shape[3]
    tile = min(width, LANES)
    heads = tile // HDIM
    key_grad[...] = jnp.zeros_like(key_grad)
    value_grad[...] = jnp.zeros_like(value_grad)
    inside = lax.broadcasted_iota(jnp.int32, (BLK, 1), 0)
    lane_head = lax.broadcasted_iota(jnp.int32, (BLK, tile), 1) // HDIM

    def place(block):
        if per_device == 1:
            return block, pl.ds(0, BLK)
        return block // per_device, pl.ds((block % per_device) * BLK, BLK)

    def own_heads(turned_result):
        return jnp.concatenate(
            [
                turned_result[head * HDIM : (head + 1) * HDIM, head * BLK : (head + 1) * BLK]
                for head in range(heads)
            ],
            axis=0,
        )

    def turn(block, carry):
        dev, here = place(block)
        for first in range(0, width, tile):
            for half in range(2):
                turned[block, half, pl.ds(first, tile)] = rows[
                    dev, half, here, pl.ds(first, tile)
                ].T
        return carry

    def step(block, carry):
        chosen = [listed(block, slot) for slot in range(NLIST)]
        places = [place(index) for index in chosen]
        target, target_rows = place(block)
        key_valid = jnp.concatenate(
            [index * BLK + inside < source_len for index in chosen], axis=0
        )
        live = block * BLK + inside < target_len
        for first in range(0, width, tile):
            lanes = pl.ds(first, tile)
            keys = jnp.concatenate([rows[dev, 0, here, lanes] for dev, here in places], axis=0)
            values = jnp.concatenate([rows[dev, 1, here, lanes] for dev, here in places], axis=0)
            queries = rows[seq_count + target, 0, target_rows, lanes] * jnp.bfloat16(SCALE)
            cots = rows[seq_count + target, 1, target_rows, lanes]
            none = jnp.zeros_like(queries)
            cots = jnp.where(live, cots, none)
            queries = jnp.concatenate(
                [jnp.where(lane_head == head, queries, none) for head in range(heads)], axis=0
            )
            cots = jnp.concatenate(
                [jnp.where(lane_head == head, cots, none) for head in range(heads)], axis=0
            )
            scores = jnp.where(key_valid, contract(keys, queries, 1, 1), FLOOR)
            expo = jnp.exp(scores - jnp.max(scores, axis=0, keepdims=True))
            probs = expo * (1.0 / jnp.sum(expo, axis=0, keepdims=True))
            dprob = contract(values, cots, 1, 1)
            delta = jnp.sum(probs * dprob, axis=0, keepdims=True)
            probs_low = probs.astype(jnp.bfloat16)
            dscore_low = (probs * (dprob - delta)).astype(jnp.bfloat16)
            dvalue = contract(probs_low, cots, 1, 0)
            dkey = contract(dscore_low, queries, 1, 0)
            keys_turned = jnp.concatenate([turned[index, 0, lanes] for index in chosen], axis=1)
            values_turned = jnp.concatenate([turned[index, 1, lanes] for index in chosen], axis=1)
            attended = own_heads(contract(values_turned, probs_low, 1, 0))
            dquery = own_heads(contract(keys_turned, dscore_low, 1, 0)) * SCALE
            attended = jnp.where(live, attended.astype(jnp.bfloat16).T, none)
            out[seq_count + target, 0, target_rows, lanes] = dquery.astype(jnp.bfloat16).T
            out[seq_count + target, 1, target_rows, lanes] = attended
            for slot, (dev, here) in enumerate(places):
                part = slice(slot * BLK, (slot + 1) * BLK)
                key_grad[dev, here, lanes] += dkey[part]
                value_grad[dev, here, lanes] += dvalue[part]
        return carry

    lax.fori_loop(0, block_count, turn, 0, unroll=block_count <= 4)
    lax.fori_loop(0, block_count, step, 0, unroll=block_count <= 4)
    out[:seq_count, 0] = key_grad[...].astype(jnp.bfloat16)
    out[:seq_count, 1] = value_grad[...].astype(jnp.bfloat16)


def attend_cost(block_count, width):
    pairs = block_count * NLIST * BLK * BLK * width
    return pl.CostEstimate(
        flops=10 * pairs,
        bytes_accessed=16 * block_count * BLK * width,
        transcendentals=pairs // HDIM,
    )


def specs(count, space):
    return [pl.BlockSpec(memory_space=space)] * count


def in_hbm(*arrays):
    return [pltpu.with_memory_space_constraint(array, pltpu.HBM) for array in arrays]


def gathered_kernel(
    seq_count, lists, source_len, target_len, rows, out, key_grad, value_grad, turned
):
    def listed(block, slot):
        return lists[block, slot]

    attend_sample(
        seq_count, listed, source_len[0], target_len[0], rows, out, key_grad, value_grad, turned
    )


def by_all_to_all(first_rows, second_rows, alignment, diffusion_mask, source_length, target_length):
    seq_count = lax.axis_size("seq")
    parts = lax.axis_size("section") * seq_count
    rows_here = first_rows.shape[2]
    width = first_rows.shape[3]
    on_encoder = lax.axis_index("section") == 0
    keep = on_encoder | (diffusion_mask[0] == 1)
    second = jnp.where(keep[:, None], second_rows[0, 0], jnp.zeros_like(second_rows[0, 0]))
    held = jnp.stack([first_rows[0, 0], second])
    held = held.reshape(2, rows_here, parts, width // parts).transpose(2, 0, 1, 3)
    lists = lax.all_gather(alignment[0], "seq", axis=0, tiled=True)
    rows = lax.all_to_all(held, AXES, 0, 0, tiled=True)
    grads = pltpu.VMEM((seq_count, rows_here, width // parts), jnp.float32)
    turned = pltpu.VMEM((lists.shape[0], 2, width // parts, BLK), rows.dtype)
    grads = pl.pallas_call(
        functools.partial(gathered_kernel, seq_count),
        out_shape=jax.ShapeDtypeStruct(rows.shape, rows.dtype),
        in_specs=specs(3, pltpu.SMEM) + specs(1, pltpu.VMEM),
        out_specs=pl.BlockSpec(memory_space=pltpu.VMEM),
        scratch_shapes=[grads, grads, turned],
        compiler_params=pltpu.CompilerParams(vmem_limit_bytes=VMEM_LIMIT),
        cost_estimate=attend_cost(lists.shape[0], width // parts),
        name="attend_gathered",
    )(lists, source_length, target_length, rows)
    grads = lax.all_to_all(grads, AXES, 0, 0, tiled=True)
    grads = grads.transpose(1, 2, 0, 3).reshape(2, rows_here, width)
    return (grads[0][None, None], grads[1][None, None])


def device_index(seq_count):
    return lax.axis_index("section") * seq_count + lax.axis_index("seq")


DIAGONAL = (6, 7)
OWN, NEAR = (0,), (1,)
ACROSS = [(4,), (2,), (5,), (3,)]
REST = [OWN, NEAR, *ACROSS]
OUTGOING = [DIAGONAL, *REST]
INCOMING = [*OUTGOING, DIAGONAL[1:]]
TILES = 2
EARLY = (0, 6)


def pack_kernel(seq_count, steps, *refs):
    smalls, (first, second) = refs[:2], refs[2:4]
    outs, (lists, mask, small_sem, sem) = refs[4:-4], refs[-4:]
    me = device_index(seq_count)
    here = me % seq_count
    share = outs[0].shape[1]
    copies, pieces = [], []
    for group, out in zip(steps, outs):
        for place, step in enumerate(group):
            slot = len(copies)
            lanes = pl.ds(pl.multiple_of((me ^ step) * share, LANES), share)
            piece = out.at[pl.ds(place * 2 * BLK, 2 * BLK)]
            pair = [
                pltpu.make_async_copy(
                    source.at[0, 0, :, lanes], piece.at[pl.ds(half * BLK, BLK)], sem.at[half, slot]
                )
                for half, source in enumerate((first, second))
            ]
            for copy in pair:
                copy.start()
            copies.append(pair)
            pieces.append(piece)
    small_copies = [
        pltpu.make_async_copy(source, held, small_sem.at[slot])
        for slot, (source, held) in enumerate(zip(smalls, (lists, mask)))
    ]
    for copy in small_copies:
        copy.start()
    for copy in small_copies:
        copy.wait()
    keep = (mask[...] == 1) | (me < seq_count)
    keep = jnp.broadcast_to(jnp.where(keep, 1.0, 0.0), (BLK, BLK)).T.astype(jnp.bfloat16)
    keep = jnp.concatenate([keep] * (share // LANES), axis=1)
    base = here - WIN
    code = (lists[0, 0, 0] - base) * SPAN + lists[0, 0, 1] - base
    tail = jnp.full((TAIL, share), code, jnp.int32).astype(jnp.float32).astype(jnp.bfloat16)
    for out in outs:
        if out.shape[0] % (2 * BLK):
            out[2 * BLK :] = tail
    for piece, pair in zip(pieces, copies):
        for copy in pair:
            copy.wait()
        piece[BLK:] = piece[BLK:] * keep


def attend_kernel(seq_count, turn, source_len, target_len, *refs):
    parts, rest = len(INCOMING), len(OUTGOING) - 1
    shares, before = refs[:parts], refs[parts : parts + (rest if turn else 0)]
    outs = refs[parts + len(before) : parts + len(before) + 1 + rest]
    rows, result, key_grad, value_grad, turned, lists = refs[parts + len(before) + 1 + rest :]
    me = device_index(seq_count)
    here = me % seq_count
    lanes = pl.ds(turn * LANES, LANES)
    for (step, *_), share in zip(INCOMING, shares):
        source = me ^ step
        rows[source, 0] = share[pl.ds(0, BLK), lanes]
        rows[source, 1] = share[pl.ds(BLK, BLK), lanes]
        if step < seq_count:
            tail = share[pl.ds(2 * BLK, TAIL), lanes].astype(jnp.float32)
            lists[here ^ step] = jnp.max(tail).astype(jnp.int32)

    def listed(block, slot):
        code = lists[block]
        return block - WIN + (code // SPAN if slot == 0 else code % SPAN)

    attend_sample(
        seq_count,
        listed,
        source_len[0],
        target_len[0],
        rows,
        result,
        key_grad,
        value_grad,
        turned,
    )
    diagonal, *others = outs
    for place, step in enumerate(DIAGONAL):
        for half in range(2):
            diagonal[pl.ds((2 * place + half) * BLK, BLK)] = result[me ^ step, half]
    for group, out in zip(REST, others):
        for half in range(2):
            out[pl.ds(half * BLK, BLK), lanes] = result[me ^ group[0], half]
    for done, out in zip(before, others):
        out[:, pl.ds(0, turn * LANES)] = done[...]


def unpack_kernel(seq_count, places, *refs):
    shares, (first, second, sem) = refs[: len(places)], refs[-3:]
    width = first.shape[3] // (2 * seq_count)
    me = device_index(seq_count)
    copies = []
    for slot, ((step, start), share) in enumerate(zip(places, shares)):
        lanes = pl.ds(pl.multiple_of((me ^ step) * width + start, LANES), share.shape[1])
        for half, result in enumerate((first, second)):
            copy = pltpu.make_async_copy(
                share.at[pl.ds(half * BLK, BLK)], result.at[0, 0, :, lanes], sem.at[half, slot]
            )
            copy.start()
            copies.append(copy)
    for copy in copies:
        copy.wait()


def permuted(share, step):
    return lax.ppermute(share, AXES, [(dev, dev ^ step) for dev in range(8)])


def swapped(diagonals, shares):
    held = dict(zip(REST, shares))
    diagonals = [permuted(share, DIAGONAL[0]) for share in diagonals]
    moved = {group: permuted(held[group], group[0]) for group in ACROSS}
    if len(diagonals) > 1:
        held[NEAR], diagonals[0] = lax.optimization_barrier((held[NEAR], diagonals[0]))
    moved[NEAR] = permuted(held[NEAR], NEAR[0])
    if len(diagonals) == 1:
        diagonals[0], moved[NEAR] = lax.optimization_barrier((diagonals[0], moved[NEAR]))
    handed_on = [permuted(share[share.shape[0] // 2 :], NEAR[0]) for share in diagonals]
    return diagonals, [held[OWN], moved[NEAR], *(moved[group] for group in ACROSS)], handed_on


def by_pairs(first_rows, second_rows, alignment, diffusion_mask, source_length, target_length):
    seq_count = lax.axis_size("seq")
    parts = 2 * seq_count
    width = first_rows.shape[3]
    share = width // parts
    kind = first_rows.dtype
    params = pltpu.CompilerParams(vmem_limit_bytes=VMEM_LIMIT)
    sems = pltpu.SemaphoreType.DMA((2, parts))

    def sizes(groups, tail):
        return [
            jax.ShapeDtypeStruct(
                (len(group) * 2 * BLK + (tail if group[0] < seq_count else 0), share), kind
            )
            for group in groups
        ]

    def pack(groups, lists):
        return pl.pallas_call(
            functools.partial(pack_kernel, seq_count, groups),
            out_shape=sizes(groups, TAIL),
            in_specs=specs(4, pltpu.HBM),
            out_specs=specs(len(groups), pltpu.VMEM),
            scratch_shapes=[
                pltpu.SMEM(alignment.shape, jnp.int32),
                pltpu.VMEM(diffusion_mask.shape, jnp.int32),
                pltpu.SemaphoreType.DMA((2,)),
                sems,
            ],
            compiler_params=params,
            name="pack",
        )(*in_hbm(lists, diffusion_mask, first_rows, second_rows))

    (diagonal,) = pack([DIAGONAL], alignment)
    lists, diagonal = lax.optimization_barrier((alignment, diagonal))
    diagonals, shares, handed_on = swapped([diagonal], pack(REST, lists))
    coming = [*diagonals, *shares, *handed_on]
    rows = pltpu.VMEM((parts, 2, BLK, LANES), kind)
    grads = pltpu.VMEM((seq_count, BLK, LANES), jnp.float32)
    turned = pltpu.VMEM((seq_count, 2, LANES, BLK), kind)

    def attend(turn, *before):
        lanes = (turn + 1) * LANES
        return pl.pallas_call(
            functools.partial(attend_kernel, seq_count, turn),
            out_shape=[
                jax.ShapeDtypeStruct((4 * BLK, LANES), kind),
                *([jax.ShapeDtypeStruct((2 * BLK, lanes), kind)] * len(REST)),
            ],
            in_specs=specs(2, pltpu.SMEM) + specs(len(coming) + len(before), pltpu.VMEM),
            out_specs=specs(1 + len(REST), pltpu.VMEM),
            scratch_shapes=[rows, rows, grads, grads, turned, pltpu.SMEM((seq_count,), jnp.int32)],
            compiler_params=params,
            cost_estimate=attend_cost(seq_count, LANES),
            name="attend",
        )(source_length, target_length, *coming, *before)

    diagonals, shares = [], []
    for turn in range(TILES):
        diagonal, *shares = attend(turn, *shares)
        diagonals.append(diagonal)
    diagonals, shares, handed_on = swapped(diagonals, shares)
    arrived = dict(zip([(group[0], 0) for group in REST], shares))
    for step, tiles in zip(DIAGONAL, (diagonals, handed_on)):
        arrived.update({(step, tile * LANES): share for tile, share in enumerate(tiles)})
    out_shape = jax.ShapeDtypeStruct((1, 1, BLK, width), kind)

    def unpack(places, *begun):
        count = len(places)
        return pl.pallas_call(
            functools.partial(unpack_kernel, seq_count, places),
            out_shape=[out_shape, out_shape],
            in_specs=specs(count, pltpu.VMEM) + specs(len(begun), pltpu.HBM),
            out_specs=specs(2, pltpu.HBM),
            input_output_aliases={count + slot: slot for slot in range(len(begun))},
            scratch_shapes=[pltpu.SemaphoreType.DMA((2, count))],
            compiler_params=params,
            name="unpack",
        )(*(arrived[place] for place in places), *begun)

    early = [place for place in arrived if place[0] in EARLY]
    return unpack([place for place in arrived if place not in early], *unpack(early))


def on_device(first_rows, second_rows, alignment, diffusion_mask, source_length, target_length):
    seq_count = lax.axis_size("seq")
    parts = lax.axis_size("section") * seq_count
    paired = (
        (parts, seq_count) == (8, 4)
        and first_rows.shape[2] == BLK
        and first_rows.shape[3] == parts * TILES * LANES
    )
    work = by_pairs if paired else by_all_to_all
    return tuple(
        work(first_rows, second_rows, alignment, diffusion_mask, source_length, target_length)
    )


def solution(mesh):
    placed = (
        P("section", "sample", "seq", None),
        P("section", "sample", "seq", None),
        P("sample", "seq", None),
        P("sample", "seq"),
        P("sample"),
        P("sample"),
    )
    return jax.shard_map(
        on_device,
        mesh=mesh,
        in_specs=placed,
        out_specs=(P("section", "sample", "seq", None), P("section", "sample", "seq", None)),
        check_vma=False,
    )
```

```python
import functools

import jax
import jax.numpy as jnp
from jax import lax
from jax.experimental import pallas as pl
from jax.experimental.pallas import tpu as pltpu
from jax.sharding import PartitionSpec as P

HDIM = 64
BLK = 128
NLIST = 2
WIN = 1
SPAN = 2 * WIN + 1
LANES = 128
TAIL = 16
SCALE = HDIM ** (-0.5)
FLOOR = -1e30
VMEM_LIMIT = 32 * 1024 * 1024
AXES = ("section", "seq")


def contract(left, right, left_dim, right_dim):
    return lax.dot_general(
        left, right, (((left_dim,), (right_dim,)), ((), ())), preferred_element_type=jnp.float32
    )


def attend_sample(
    seq_count, listed, source_len, target_len, rows, out, key_grad, value_grad, turned
):
    per_device = rows.shape[2] // BLK
    block_count = seq_count * per_device
    width = rows.shape[3]
    tile = min(width, LANES)
    heads = tile // HDIM
    key_grad[...] = jnp.zeros_like(key_grad)
    value_grad[...] = jnp.zeros_like(value_grad)
    inside = lax.broadcasted_iota(jnp.int32, (BLK, 1), 0)
    lane_head = lax.broadcasted_iota(jnp.int32, (BLK, tile), 1) // HDIM

    def place(block):
        if per_device == 1:
            return block, pl.ds(0, BLK)
        return block // per_device, pl.ds((block % per_device) * BLK, BLK)

    def own_heads(turned_result):
        return jnp.concatenate(
            [
                turned_result[head * HDIM : (head + 1) * HDIM, head * BLK : (head + 1) * BLK]
                for head in range(heads)
            ],
            axis=0,
        )

    def turn(block, carry):
        dev, here = place(block)
        for first in range(0, width, tile):
            for half in range(2):
                turned[block, half, pl.ds(first, tile)] = rows[
                    dev, half, here, pl.ds(first, tile)
                ].T
        return carry

    def step(block, carry):
        chosen = [listed(block, slot) for slot in range(NLIST)]
        places = [place(index) for index in chosen]
        target, target_rows = place(block)
        key_valid = jnp.concatenate(
            [index * BLK + inside < source_len for index in chosen], axis=0
        )
        live = block * BLK + inside < target_len
        for first in range(0, width, tile):
            lanes = pl.ds(first, tile)
            keys = jnp.concatenate([rows[dev, 0, here, lanes] for dev, here in places], axis=0)
            values = jnp.concatenate([rows[dev, 1, here, lanes] for dev, here in places], axis=0)
            queries = rows[seq_count + target, 0, target_rows, lanes] * jnp.bfloat16(SCALE)
            cots = rows[seq_count + target, 1, target_rows, lanes]
            none = jnp.zeros_like(queries)
            cots = jnp.where(live, cots, none)
            queries = jnp.concatenate(
                [jnp.where(lane_head == head, queries, none) for head in range(heads)], axis=0
            )
            cots = jnp.concatenate(
                [jnp.where(lane_head == head, cots, none) for head in range(heads)], axis=0
            )
            scores = jnp.where(key_valid, contract(keys, queries, 1, 1), FLOOR)
            expo = jnp.exp(scores - jnp.max(scores, axis=0, keepdims=True))
            probs = expo * (1.0 / jnp.sum(expo, axis=0, keepdims=True))
            dprob = contract(values, cots, 1, 1)
            delta = jnp.sum(probs * dprob, axis=0, keepdims=True)
            probs_low = probs.astype(jnp.bfloat16)
            dscore_low = (probs * (dprob - delta)).astype(jnp.bfloat16)
            dvalue = contract(probs_low, cots, 1, 0)
            dkey = contract(dscore_low, queries, 1, 0)
            keys_turned = jnp.concatenate([turned[index, 0, lanes] for index in chosen], axis=1)
            values_turned = jnp.concatenate([turned[index, 1, lanes] for index in chosen], axis=1)
            attended = own_heads(contract(values_turned, probs_low, 1, 0))
            dquery = own_heads(contract(keys_turned, dscore_low, 1, 0)) * SCALE
            attended = jnp.where(live, attended.astype(jnp.bfloat16).T, none)
            out[seq_count + target, 0, target_rows, lanes] = dquery.astype(jnp.bfloat16).T
            out[seq_count + target, 1, target_rows, lanes] = attended
            for slot, (dev, here) in enumerate(places):
                part = slice(slot * BLK, (slot + 1) * BLK)
                key_grad[dev, here, lanes] += dkey[part]
                value_grad[dev, here, lanes] += dvalue[part]
        return carry

    lax.fori_loop(0, block_count, turn, 0, unroll=block_count <= 4)
    lax.fori_loop(0, block_count, step, 0, unroll=block_count <= 4)
    out[:seq_count, 0] = key_grad[...].astype(jnp.bfloat16)
    out[:seq_count, 1] = value_grad[...].astype(jnp.bfloat16)


def attend_cost(block_count, width):
    pairs = block_count * NLIST * BLK * BLK * width
    return pl.CostEstimate(
        flops=10 * pairs,
        bytes_accessed=16 * block_count * BLK * width,
        transcendentals=pairs // HDIM,
    )


def specs(count, space):
    return [pl.BlockSpec(memory_space=space)] * count


def in_hbm(*arrays):
    return [pltpu.with_memory_space_constraint(array, pltpu.HBM) for array in arrays]


def gathered_kernel(
    seq_count, lists, source_len, target_len, rows, out, key_grad, value_grad, turned
):
    def listed(block, slot):
        return lists[block, slot]

    attend_sample(
        seq_count, listed, source_len[0], target_len[0], rows, out, key_grad, value_grad, turned
    )


def by_all_to_all(first_rows, second_rows, alignment, diffusion_mask, source_length, target_length):
    seq_count = lax.axis_size("seq")
    parts = lax.axis_size("section") * seq_count
    rows_here = first_rows.shape[2]
    width = first_rows.shape[3]
    on_encoder = lax.axis_index("section") == 0
    keep = on_encoder | (diffusion_mask[0] == 1)
    second = jnp.where(keep[:, None], second_rows[0, 0], jnp.zeros_like(second_rows[0, 0]))
    held = jnp.stack([first_rows[0, 0], second])
    held = held.reshape(2, rows_here, parts, width // parts).transpose(2, 0, 1, 3)
    lists = lax.all_gather(alignment[0], "seq", axis=0, tiled=True)
    rows = lax.all_to_all(held, AXES, 0, 0, tiled=True)
    grads = pltpu.VMEM((seq_count, rows_here, width // parts), jnp.float32)
    turned = pltpu.VMEM((lists.shape[0], 2, width // parts, BLK), rows.dtype)
    grads = pl.pallas_call(
        functools.partial(gathered_kernel, seq_count),
        out_shape=jax.ShapeDtypeStruct(rows.shape, rows.dtype),
        in_specs=specs(3, pltpu.SMEM) + specs(1, pltpu.VMEM),
        out_specs=pl.BlockSpec(memory_space=pltpu.VMEM),
        scratch_shapes=[grads, grads, turned],
        compiler_params=pltpu.CompilerParams(vmem_limit_bytes=VMEM_LIMIT),
        cost_estimate=attend_cost(lists.shape[0], width // parts),
        name="attend_gathered",
    )(lists, source_length, target_length, rows)
    grads = lax.all_to_all(grads, AXES, 0, 0, tiled=True)
    grads = grads.transpose(1, 2, 0, 3).reshape(2, rows_here, width)
    return (grads[0][None, None], grads[1][None, None])


def device_index(seq_count):
    return lax.axis_index("section") * seq_count + lax.axis_index("seq")


DIAGONAL = (6, 7)
OWN, NEAR = (0,), (1,)
ACROSS = [(4,), (5,), (2,), (3,)]
REST = [OWN, NEAR, *ACROSS]
OUTGOING = [DIAGONAL, *REST]
INCOMING = [*OUTGOING, DIAGONAL[1:]]
TILES = 2


def pack_kernel(seq_count, steps, *refs):
    smalls, (first, second) = refs[:2], refs[2:4]
    outs, (lists, mask, small_sem, sem) = refs[4:-4], refs[-4:]
    me = device_index(seq_count)
    here = me % seq_count
    share = outs[0].shape[1]
    copies, pieces = [], []
    for group, out in zip(steps, outs):
        for place, step in enumerate(group):
            slot = len(copies)
            lanes = pl.ds(pl.multiple_of((me ^ step) * share, LANES), share)
            piece = out.at[pl.ds(place * 2 * BLK, 2 * BLK)]
            pair = [
                pltpu.make_async_copy(
                    source.at[0, 0, :, lanes], piece.at[pl.ds(half * BLK, BLK)], sem.at[half, slot]
                )
                for half, source in enumerate((first, second))
            ]
            for copy in pair:
                copy.start()
            copies.append(pair)
            pieces.append(piece)
    small_copies = [
        pltpu.make_async_copy(source, held, small_sem.at[slot])
        for slot, (source, held) in enumerate(zip(smalls, (lists, mask)))
    ]
    for copy in small_copies:
        copy.start()
    for copy in small_copies:
        copy.wait()
    keep = (mask[...] == 1) | (me < seq_count)
    keep = jnp.broadcast_to(jnp.where(keep, 1.0, 0.0), (BLK, BLK)).T.astype(jnp.bfloat16)
    keep = jnp.concatenate([keep] * (share // LANES), axis=1)
    base = here - WIN
    code = (lists[0, 0, 0] - base) * SPAN + lists[0, 0, 1] - base
    tail = jnp.full((TAIL, share), code, jnp.int32).astype(jnp.float32).astype(jnp.bfloat16)
    for out in outs:
        if out.shape[0] % (2 * BLK):
            out[2 * BLK :] = tail
    for piece, pair in zip(pieces, copies):
        for copy in pair:
            copy.wait()
        piece[BLK:] = piece[BLK:] * keep


def attend_kernel(seq_count, turn, source_len, target_len, *refs):
    parts, rest = len(INCOMING), len(OUTGOING) - 1
    shares, before = refs[:parts], refs[parts : parts + (rest if turn else 0)]
    outs = refs[parts + len(before) : parts + len(before) + 1 + rest]
    rows, result, key_grad, value_grad, turned, lists = refs[parts + len(before) + 1 + rest :]
    me = device_index(seq_count)
    here = me % seq_count
    lanes = pl.ds(turn * LANES, LANES)
    for (step, *_), share in zip(INCOMING, shares):
        source = me ^ step
        rows[source, 0] = share[pl.ds(0, BLK), lanes]
        rows[source, 1] = share[pl.ds(BLK, BLK), lanes]
        if step < seq_count:
            tail = share[pl.ds(2 * BLK, TAIL), lanes].astype(jnp.float32)
            lists[here ^ step] = jnp.max(tail).astype(jnp.int32)

    def listed(block, slot):
        code = lists[block]
        return block - WIN + (code // SPAN if slot == 0 else code % SPAN)

    attend_sample(
        seq_count,
        listed,
        source_len[0],
        target_len[0],
        rows,
        result,
        key_grad,
        value_grad,
        turned,
    )
    diagonal, *others = outs
    for place, step in enumerate(DIAGONAL):
        for half in range(2):
            diagonal[pl.ds((2 * place + half) * BLK, BLK)] = result[me ^ step, half]
    for group, out in zip(REST, others):
        for half in range(2):
            out[pl.ds(half * BLK, BLK), lanes] = result[me ^ group[0], half]
    for done, out in zip(before, others):
        out[:, pl.ds(0, turn * LANES)] = done[...]


def unpack_kernel(seq_count, *refs):
    diagonals, handed_on, shares = refs[:TILES], refs[TILES : 2 * TILES], refs[2 * TILES : -3]
    first, second, sem = refs[-3:]
    width = first.shape[3] // (2 * seq_count)
    me = device_index(seq_count)
    pieces = [
        (step, tile * LANES, share.at[pl.ds(0, 2 * BLK)])
        for step, arrived in zip(DIAGONAL, (diagonals, handed_on))
        for tile, share in enumerate(arrived)
    ]
    pieces += [(step, 0, share) for (step,), share in zip(REST, shares)]
    copies = []
    for slot, (step, start, share) in enumerate(pieces):
        lanes = pl.ds(pl.multiple_of((me ^ step) * width + start, LANES), share.shape[1])
        for half, result in enumerate((first, second)):
            copy = pltpu.make_async_copy(
                share.at[pl.ds(half * BLK, BLK)], result.at[0, 0, :, lanes], sem.at[half, slot]
            )
            copy.start()
            copies.append(copy)
    for copy in copies:
        copy.wait()


def permuted(share, step):
    return lax.ppermute(share, AXES, [(dev, dev ^ step) for dev in range(8)])


def swapped(diagonals, shares):
    held = dict(zip(REST, shares))
    diagonals = [permuted(share, DIAGONAL[0]) for share in diagonals]
    moved = {group: permuted(held[group], group[0]) for group in ACROSS}
    if len(diagonals) > 1:
        held[NEAR], diagonals[0] = lax.optimization_barrier((held[NEAR], diagonals[0]))
    moved[NEAR] = permuted(held[NEAR], NEAR[0])
    if len(diagonals) == 1:
        diagonals[0], moved[NEAR] = lax.optimization_barrier((diagonals[0], moved[NEAR]))
    handed_on = [permuted(share[share.shape[0] // 2 :], NEAR[0]) for share in diagonals]
    return diagonals, [held[OWN], moved[NEAR], *(moved[group] for group in ACROSS)], handed_on


def by_pairs(first_rows, second_rows, alignment, diffusion_mask, source_length, target_length):
    seq_count = lax.axis_size("seq")
    parts = 2 * seq_count
    width = first_rows.shape[3]
    share = width // parts
    kind = first_rows.dtype
    params = pltpu.CompilerParams(vmem_limit_bytes=VMEM_LIMIT)
    sems = pltpu.SemaphoreType.DMA((2, parts))

    def sizes(groups, tail):
        return [
            jax.ShapeDtypeStruct(
                (len(group) * 2 * BLK + (tail if group[0] < seq_count else 0), share), kind
            )
            for group in groups
        ]

    def pack(groups, lists):
        return pl.pallas_call(
            functools.partial(pack_kernel, seq_count, groups),
            out_shape=sizes(groups, TAIL),
            in_specs=specs(4, pltpu.HBM),
            out_specs=specs(len(groups), pltpu.VMEM),
            scratch_shapes=[
                pltpu.SMEM(alignment.shape, jnp.int32),
                pltpu.VMEM(diffusion_mask.shape, jnp.int32),
                pltpu.SemaphoreType.DMA((2,)),
                sems,
            ],
            compiler_params=params,
            name="pack",
        )(*in_hbm(lists, diffusion_mask, first_rows, second_rows))

    (diagonal,) = pack([DIAGONAL], alignment)
    lists, diagonal = lax.optimization_barrier((alignment, diagonal))
    diagonals, shares, handed_on = swapped([diagonal], pack(REST, lists))
    coming = [*diagonals, *shares, *handed_on]
    rows = pltpu.VMEM((parts, 2, BLK, LANES), kind)
    grads = pltpu.VMEM((seq_count, BLK, LANES), jnp.float32)
    turned = pltpu.VMEM((seq_count, 2, LANES, BLK), kind)

    def attend(turn, *before):
        lanes = (turn + 1) * LANES
        return pl.pallas_call(
            functools.partial(attend_kernel, seq_count, turn),
            out_shape=[
                jax.ShapeDtypeStruct((4 * BLK, LANES), kind),
                *([jax.ShapeDtypeStruct((2 * BLK, lanes), kind)] * len(REST)),
            ],
            in_specs=specs(2, pltpu.SMEM) + specs(len(coming) + len(before), pltpu.VMEM),
            out_specs=specs(1 + len(REST), pltpu.VMEM),
            scratch_shapes=[rows, rows, grads, grads, turned, pltpu.SMEM((seq_count,), jnp.int32)],
            compiler_params=params,
            cost_estimate=attend_cost(seq_count, LANES),
            name="attend",
        )(source_length, target_length, *coming, *before)

    diagonals, shares = [], []
    for turn in range(TILES):
        diagonal, *shares = attend(turn, *shares)
        diagonals.append(diagonal)
    diagonals, shares, handed_on = swapped(diagonals, shares)
    out_shape = jax.ShapeDtypeStruct((1, 1, BLK, width), kind)
    return pl.pallas_call(
        functools.partial(unpack_kernel, seq_count),
        out_shape=[out_shape, out_shape],
        in_specs=specs(2 * TILES + len(REST), pltpu.VMEM),
        out_specs=specs(2, pltpu.HBM),
        scratch_shapes=[pltpu.SemaphoreType.DMA((2, parts + 2 * TILES))],
        compiler_params=params,
        name="unpack",
    )(*diagonals, *handed_on, *shares)


def on_device(first_rows, second_rows, alignment, diffusion_mask, source_length, target_length):
    seq_count = lax.axis_size("seq")
    parts = lax.axis_size("section") * seq_count
    paired = (
        (parts, seq_count) == (8, 4)
        and first_rows.shape[2] == BLK
        and first_rows.shape[3] == parts * TILES * LANES
    )
    work = by_pairs if paired else by_all_to_all
    return tuple(
        work(first_rows, second_rows, alignment, diffusion_mask, source_length, target_length)
    )


def solution(mesh):
    placed = (
        P("section", "sample", "seq", None),
        P("section", "sample", "seq", None),
        P("sample", "seq", None),
        P("sample", "seq"),
        P("sample"),
        P("sample"),
    )
    return jax.shard_map(
        on_device,
        mesh=mesh,
        in_specs=placed,
        out_specs=(P("section", "sample", "seq", None), P("section", "sample", "seq", None)),
        check_vma=False,
    )
```

```python
import functools

import jax
import jax.numpy as jnp
from jax import lax
from jax.experimental import pallas as pl
from jax.experimental.pallas import tpu as pltpu
from jax.sharding import PartitionSpec as P

HDIM = 64
BLK = 128
NLIST = 2
WIN = 1
SPAN = 2 * WIN + 1
LANES = 128
TAIL = 16
SCALE = HDIM ** (-0.5)
FLOOR = -1e30
VMEM_LIMIT = 32 * 1024 * 1024
AXES = ("section", "seq")


def contract(left, right, left_dim, right_dim):
    return lax.dot_general(
        left, right, (((left_dim,), (right_dim,)), ((), ())), preferred_element_type=jnp.float32
    )


def attend_sample(
    seq_count, listed, source_len, target_len, rows, out, key_grad, value_grad, turned
):
    per_device = rows.shape[2] // BLK
    block_count = seq_count * per_device
    width = rows.shape[3]
    tile = min(width, LANES)
    heads = tile // HDIM
    key_grad[...] = jnp.zeros_like(key_grad)
    value_grad[...] = jnp.zeros_like(value_grad)
    inside = lax.broadcasted_iota(jnp.int32, (BLK, 1), 0)
    lane_head = lax.broadcasted_iota(jnp.int32, (BLK, tile), 1) // HDIM

    def place(block):
        if per_device == 1:
            return block, pl.ds(0, BLK)
        return block // per_device, pl.ds((block % per_device) * BLK, BLK)

    def own_heads(turned_result):
        return jnp.concatenate(
            [
                turned_result[head * HDIM : (head + 1) * HDIM, head * BLK : (head + 1) * BLK]
                for head in range(heads)
            ],
            axis=0,
        )

    def turn(block, carry):
        dev, here = place(block)
        for first in range(0, width, tile):
            for half in range(2):
                turned[block, half, pl.ds(first, tile)] = rows[
                    dev, half, here, pl.ds(first, tile)
                ].T
        return carry

    def step(block, carry):
        chosen = [listed(block, slot) for slot in range(NLIST)]
        places = [place(index) for index in chosen]
        target, target_rows = place(block)
        key_valid = jnp.concatenate(
            [index * BLK + inside < source_len for index in chosen], axis=0
        )
        live = block * BLK + inside < target_len
        for first in range(0, width, tile):
            lanes = pl.ds(first, tile)
            keys = jnp.concatenate([rows[dev, 0, here, lanes] for dev, here in places], axis=0)
            values = jnp.concatenate([rows[dev, 1, here, lanes] for dev, here in places], axis=0)
            queries = rows[seq_count + target, 0, target_rows, lanes] * jnp.bfloat16(SCALE)
            cots = rows[seq_count + target, 1, target_rows, lanes]
            none = jnp.zeros_like(queries)
            cots = jnp.where(live, cots, none)
            queries = jnp.concatenate(
                [jnp.where(lane_head == head, queries, none) for head in range(heads)], axis=0
            )
            cots = jnp.concatenate(
                [jnp.where(lane_head == head, cots, none) for head in range(heads)], axis=0
            )
            scores = jnp.where(key_valid, contract(keys, queries, 1, 1), FLOOR)
            expo = jnp.exp(scores - jnp.max(scores, axis=0, keepdims=True))
            probs = expo * (1.0 / jnp.sum(expo, axis=0, keepdims=True))
            dprob = contract(values, cots, 1, 1)
            delta = jnp.sum(probs * dprob, axis=0, keepdims=True)
            probs_low = probs.astype(jnp.bfloat16)
            dscore_low = (probs * (dprob - delta)).astype(jnp.bfloat16)
            dvalue = contract(probs_low, cots, 1, 0)
            dkey = contract(dscore_low, queries, 1, 0)
            keys_turned = jnp.concatenate([turned[index, 0, lanes] for index in chosen], axis=1)
            values_turned = jnp.concatenate([turned[index, 1, lanes] for index in chosen], axis=1)
            attended = own_heads(contract(values_turned, probs_low, 1, 0))
            dquery = own_heads(contract(keys_turned, dscore_low, 1, 0)) * SCALE
            attended = jnp.where(live, attended.astype(jnp.bfloat16).T, none)
            out[seq_count + target, 0, target_rows, lanes] = dquery.astype(jnp.bfloat16).T
            out[seq_count + target, 1, target_rows, lanes] = attended
            for slot, (dev, here) in enumerate(places):
                part = slice(slot * BLK, (slot + 1) * BLK)
                key_grad[dev, here, lanes] += dkey[part]
                value_grad[dev, here, lanes] += dvalue[part]
        return carry

    lax.fori_loop(0, block_count, turn, 0, unroll=block_count <= 4)
    lax.fori_loop(0, block_count, step, 0, unroll=block_count <= 4)
    out[:seq_count, 0] = key_grad[...].astype(jnp.bfloat16)
    out[:seq_count, 1] = value_grad[...].astype(jnp.bfloat16)


def attend_cost(block_count, width):
    pairs = block_count * NLIST * BLK * BLK * width
    return pl.CostEstimate(
        flops=10 * pairs,
        bytes_accessed=16 * block_count * BLK * width,
        transcendentals=pairs // HDIM,
    )


def specs(count, space):
    return [pl.BlockSpec(memory_space=space)] * count


def in_hbm(*arrays):
    return [pltpu.with_memory_space_constraint(array, pltpu.HBM) for array in arrays]


def gathered_kernel(
    seq_count, lists, source_len, target_len, rows, out, key_grad, value_grad, turned
):
    def listed(block, slot):
        return lists[block, slot]

    attend_sample(
        seq_count, listed, source_len[0], target_len[0], rows, out, key_grad, value_grad, turned
    )


def by_all_to_all(first_rows, second_rows, alignment, diffusion_mask, source_length, target_length):
    seq_count = lax.axis_size("seq")
    parts = lax.axis_size("section") * seq_count
    rows_here = first_rows.shape[2]
    width = first_rows.shape[3]
    on_encoder = lax.axis_index("section") == 0
    keep = on_encoder | (diffusion_mask[0] == 1)
    second = jnp.where(keep[:, None], second_rows[0, 0], jnp.zeros_like(second_rows[0, 0]))
    held = jnp.stack([first_rows[0, 0], second])
    held = held.reshape(2, rows_here, parts, width // parts).transpose(2, 0, 1, 3)
    lists = lax.all_gather(alignment[0], "seq", axis=0, tiled=True)
    rows = lax.all_to_all(held, AXES, 0, 0, tiled=True)
    grads = pltpu.VMEM((seq_count, rows_here, width // parts), jnp.float32)
    turned = pltpu.VMEM((lists.shape[0], 2, width // parts, BLK), rows.dtype)
    grads = pl.pallas_call(
        functools.partial(gathered_kernel, seq_count),
        out_shape=jax.ShapeDtypeStruct(rows.shape, rows.dtype),
        in_specs=specs(3, pltpu.SMEM) + specs(1, pltpu.VMEM),
        out_specs=pl.BlockSpec(memory_space=pltpu.VMEM),
        scratch_shapes=[grads, grads, turned],
        compiler_params=pltpu.CompilerParams(vmem_limit_bytes=VMEM_LIMIT),
        cost_estimate=attend_cost(lists.shape[0], width // parts),
        name="attend_gathered",
    )(lists, source_length, target_length, rows)
    grads = lax.all_to_all(grads, AXES, 0, 0, tiled=True)
    grads = grads.transpose(1, 2, 0, 3).reshape(2, rows_here, width)
    return (grads[0][None, None], grads[1][None, None])


def device_index(seq_count):
    return lax.axis_index("section") * seq_count + lax.axis_index("seq")


DIAGONAL = (6, 7)
OWN, NEAR = (0,), (1,)
ACROSS = [(4,), (2,), (5,), (3,)]
REST = [OWN, NEAR, *ACROSS]
OUTGOING = [DIAGONAL, *REST]
INCOMING = [*OUTGOING, DIAGONAL[1:]]
TILES = 2
LISTED = (0, 1, 6, 3)


def pack_kernel(seq_count, steps, *refs):
    smalls, (first, second) = refs[:2], refs[2:4]
    outs, (lists, mask, small_sem, sem) = refs[4:-4], refs[-4:]
    me = device_index(seq_count)
    here = me % seq_count
    share = outs[0].shape[1]
    copies, pieces = [], []
    for group, out in zip(steps, outs):
        for place, step in enumerate(group):
            slot = len(copies)
            lanes = pl.ds(pl.multiple_of((me ^ step) * share, LANES), share)
            piece = out.at[pl.ds(place * 2 * BLK, 2 * BLK)]
            pair = [
                pltpu.make_async_copy(
                    source.at[0, 0, :, lanes], piece.at[pl.ds(half * BLK, BLK)], sem.at[half, slot]
                )
                for half, source in enumerate((first, second))
            ]
            for copy in pair:
                copy.start()
            copies.append(pair)
            pieces.append(piece)
    small_copies = [
        pltpu.make_async_copy(source, held, small_sem.at[slot])
        for slot, (source, held) in enumerate(zip(smalls, (lists, mask)))
    ]
    for copy in small_copies:
        copy.start()
    for copy in small_copies:
        copy.wait()
    keep = (mask[...] == 1) | (me < seq_count)
    keep = jnp.broadcast_to(jnp.where(keep, 1.0, 0.0), (BLK, BLK)).T.astype(jnp.bfloat16)
    keep = jnp.concatenate([keep] * (share // LANES), axis=1)
    base = here - WIN
    code = (lists[0, 0, 0] - base) * SPAN + lists[0, 0, 1] - base
    tail = jnp.full((TAIL, share), code, jnp.int32).astype(jnp.float32).astype(jnp.bfloat16)
    for out in outs:
        if out.shape[0] % (2 * BLK):
            out[out.shape[0] - TAIL :] = tail
    for piece, pair in zip(pieces, copies):
        for copy in pair:
            copy.wait()
        piece[BLK:] = piece[BLK:] * keep


def attend_kernel(seq_count, turn, source_len, target_len, *refs):
    parts, rest = len(INCOMING), len(OUTGOING) - 1
    shares, before = refs[:parts], refs[parts : parts + (rest if turn else 0)]
    outs = refs[parts + len(before) : parts + len(before) + 1 + rest]
    rows, result, key_grad, value_grad, turned, lists = refs[parts + len(before) + 1 + rest :]
    me = device_index(seq_count)
    lanes = pl.ds(turn * LANES, LANES)
    for (step, *_), share in zip(INCOMING, shares):
        source = me ^ step
        rows[source, 0] = share[pl.ds(0, BLK), lanes]
        rows[source, 1] = share[pl.ds(BLK, BLK), lanes]
        if step in LISTED:
            tail = share[pl.ds(share.shape[0] - TAIL, TAIL), lanes].astype(jnp.float32)
            lists[source % seq_count] = jnp.max(tail).astype(jnp.int32)

    def listed(block, slot):
        code = lists[block]
        return block - WIN + (code // SPAN if slot == 0 else code % SPAN)

    attend_sample(
        seq_count,
        listed,
        source_len[0],
        target_len[0],
        rows,
        result,
        key_grad,
        value_grad,
        turned,
    )
    diagonal, *others = outs
    for place, step in enumerate(DIAGONAL):
        for half in range(2):
            diagonal[pl.ds((2 * place + half) * BLK, BLK)] = result[me ^ step, half]
    for group, out in zip(REST, others):
        for half in range(2):
            out[pl.ds(half * BLK, BLK), lanes] = result[me ^ group[0], half]
    for done, out in zip(before, others):
        out[:, pl.ds(0, turn * LANES)] = done[...]


def unpack_kernel(seq_count, *refs):
    diagonals, handed_on, shares = refs[:TILES], refs[TILES : 2 * TILES], refs[2 * TILES : -3]
    first, second, sem = refs[-3:]
    width = first.shape[3] // (2 * seq_count)
    me = device_index(seq_count)
    pieces = [
        (step, tile * LANES, share.at[pl.ds(0, 2 * BLK)])
        for step, arrived in zip(DIAGONAL, (diagonals, handed_on))
        for tile, share in enumerate(arrived)
    ]
    pieces += [(step, 0, share) for (step,), share in zip(REST, shares)]
    copies = []
    for slot, (step, start, share) in enumerate(pieces):
        lanes = pl.ds(pl.multiple_of((me ^ step) * width + start, LANES), share.shape[1])
        for half, result in enumerate((first, second)):
            copy = pltpu.make_async_copy(
                share.at[pl.ds(half * BLK, BLK)], result.at[0, 0, :, lanes], sem.at[half, slot]
            )
            copy.start()
            copies.append(copy)
    for copy in copies:
        copy.wait()


def permuted(share, step):
    return lax.ppermute(share, AXES, [(dev, dev ^ step) for dev in range(8)])


def swapped(diagonals, shares):
    held = dict(zip(REST, shares))
    diagonals = [permuted(share, DIAGONAL[0]) for share in diagonals]
    moved = {group: permuted(held[group], group[0]) for group in ACROSS}
    if len(diagonals) > 1:
        held[NEAR], diagonals[0] = lax.optimization_barrier((held[NEAR], diagonals[0]))
    moved[NEAR] = permuted(held[NEAR], NEAR[0])
    if len(diagonals) == 1:
        diagonals[0], moved[NEAR] = lax.optimization_barrier((diagonals[0], moved[NEAR]))
    handed_on = [permuted(share[2 * BLK : 4 * BLK], NEAR[0]) for share in diagonals]
    return diagonals, [held[OWN], moved[NEAR], *(moved[group] for group in ACROSS)], handed_on


def by_pairs(first_rows, second_rows, alignment, diffusion_mask, source_length, target_length):
    seq_count = lax.axis_size("seq")
    parts = 2 * seq_count
    width = first_rows.shape[3]
    share = width // parts
    kind = first_rows.dtype
    params = pltpu.CompilerParams(vmem_limit_bytes=VMEM_LIMIT)
    sems = pltpu.SemaphoreType.DMA((2, parts))

    def sizes(groups, tail):
        return [
            jax.ShapeDtypeStruct(
                (len(group) * 2 * BLK + (tail if group[0] in LISTED else 0), share), kind
            )
            for group in groups
        ]

    def pack(groups, lists):
        return pl.pallas_call(
            functools.partial(pack_kernel, seq_count, groups),
            out_shape=sizes(groups, TAIL),
            in_specs=specs(4, pltpu.HBM),
            out_specs=specs(len(groups), pltpu.VMEM),
            scratch_shapes=[
                pltpu.SMEM(alignment.shape, jnp.int32),
                pltpu.VMEM(diffusion_mask.shape, jnp.int32),
                pltpu.SemaphoreType.DMA((2,)),
                sems,
            ],
            compiler_params=params,
            name="pack",
        )(*in_hbm(lists, diffusion_mask, first_rows, second_rows))

    (diagonal,) = pack([DIAGONAL], alignment)
    lists, diagonal = lax.optimization_barrier((alignment, diagonal))
    diagonals, shares, handed_on = swapped([diagonal], pack(REST, lists))
    coming = [*diagonals, *shares, *handed_on]
    rows = pltpu.VMEM((parts, 2, BLK, LANES), kind)
    grads = pltpu.VMEM((seq_count, BLK, LANES), jnp.float32)
    turned = pltpu.VMEM((seq_count, 2, LANES, BLK), kind)

    def attend(turn, *before):
        lanes = (turn + 1) * LANES
        return pl.pallas_call(
            functools.partial(attend_kernel, seq_count, turn),
            out_shape=[
                jax.ShapeDtypeStruct((4 * BLK, LANES), kind),
                *([jax.ShapeDtypeStruct((2 * BLK, lanes), kind)] * len(REST)),
            ],
            in_specs=specs(2, pltpu.SMEM) + specs(len(coming) + len(before), pltpu.VMEM),
            out_specs=specs(1 + len(REST), pltpu.VMEM),
            scratch_shapes=[rows, rows, grads, grads, turned, pltpu.SMEM((seq_count,), jnp.int32)],
            compiler_params=params,
            cost_estimate=attend_cost(seq_count, LANES),
            name="attend",
        )(source_length, target_length, *coming, *before)

    diagonals, shares = [], []
    for turn in range(TILES):
        diagonal, *shares = attend(turn, *shares)
        diagonals.append(diagonal)
    diagonals, shares, handed_on = swapped(diagonals, shares)
    out_shape = jax.ShapeDtypeStruct((1, 1, BLK, width), kind)
    return pl.pallas_call(
        functools.partial(unpack_kernel, seq_count),
        out_shape=[out_shape, out_shape],
        in_specs=specs(2 * TILES + len(REST), pltpu.VMEM),
        out_specs=specs(2, pltpu.HBM),
        scratch_shapes=[pltpu.SemaphoreType.DMA((2, parts + 2 * TILES))],
        compiler_params=params,
        name="unpack",
    )(*diagonals, *handed_on, *shares)


def on_device(first_rows, second_rows, alignment, diffusion_mask, source_length, target_length):
    seq_count = lax.axis_size("seq")
    parts = lax.axis_size("section") * seq_count
    paired = (
        (parts, seq_count) == (8, 4)
        and first_rows.shape[2] == BLK
        and first_rows.shape[3] == parts * TILES * LANES
    )
    work = by_pairs if paired else by_all_to_all
    return tuple(
        work(first_rows, second_rows, alignment, diffusion_mask, source_length, target_length)
    )


def solution(mesh):
    placed = (
        P("section", "sample", "seq", None),
        P("section", "sample", "seq", None),
        P("sample", "seq", None),
        P("sample", "seq"),
        P("sample"),
        P("sample"),
    )
    return jax.shard_map(
        on_device,
        mesh=mesh,
        in_specs=placed,
        out_specs=(P("section", "sample", "seq", None), P("section", "sample", "seq", None)),
        check_vma=False,
    )
```

```python
import functools

import jax
import jax.numpy as jnp
from jax import lax
from jax.experimental import pallas as pl
from jax.experimental.pallas import tpu as pltpu
from jax.sharding import PartitionSpec as P

HDIM = 64
BLK = 128
NLIST = 2
WIN = 1
SPAN = 2 * WIN + 1
LANES = 128
TAIL = 16
SCALE = HDIM ** (-0.5)
FLOOR = -1e30
VMEM_LIMIT = 32 * 1024 * 1024
AXES = ("section", "seq")


def contract(left, right, left_dim, right_dim):
    return lax.dot_general(
        left, right, (((left_dim,), (right_dim,)), ((), ())), preferred_element_type=jnp.float32
    )


def attend_sample(
    seq_count, listed, source_len, target_len, rows, out, key_grad, value_grad, turned
):
    per_device = rows.shape[2] // BLK
    block_count = seq_count * per_device
    width = rows.shape[3]
    tile = min(width, LANES)
    heads = tile // HDIM
    key_grad[...] = jnp.zeros_like(key_grad)
    value_grad[...] = jnp.zeros_like(value_grad)
    inside = lax.broadcasted_iota(jnp.int32, (BLK, 1), 0)
    lane_head = lax.broadcasted_iota(jnp.int32, (BLK, tile), 1) // HDIM

    def place(block):
        if per_device == 1:
            return block, pl.ds(0, BLK)
        return block // per_device, pl.ds((block % per_device) * BLK, BLK)

    def own_heads(turned_result):
        return jnp.concatenate(
            [
                turned_result[head * HDIM : (head + 1) * HDIM, head * BLK : (head + 1) * BLK]
                for head in range(heads)
            ],
            axis=0,
        )

    def turn(block, carry):
        dev, here = place(block)
        for first in range(0, width, tile):
            for half in range(2):
                turned[block, half, pl.ds(first, tile)] = rows[
                    dev, half, here, pl.ds(first, tile)
                ].T
        return carry

    def step(block, carry):
        chosen = [listed(block, slot) for slot in range(NLIST)]
        places = [place(index) for index in chosen]
        target, target_rows = place(block)
        key_valid = jnp.concatenate(
            [index * BLK + inside < source_len for index in chosen], axis=0
        )
        live = block * BLK + inside < target_len
        for first in range(0, width, tile):
            lanes = pl.ds(first, tile)
            keys = jnp.concatenate([rows[dev, 0, here, lanes] for dev, here in places], axis=0)
            values = jnp.concatenate([rows[dev, 1, here, lanes] for dev, here in places], axis=0)
            queries = rows[seq_count + target, 0, target_rows, lanes] * jnp.bfloat16(SCALE)
            cots = rows[seq_count + target, 1, target_rows, lanes]
            none = jnp.zeros_like(queries)
            cots = jnp.where(live, cots, none)
            queries = jnp.concatenate(
                [jnp.where(lane_head == head, queries, none) for head in range(heads)], axis=0
            )
            cots = jnp.concatenate(
                [jnp.where(lane_head == head, cots, none) for head in range(heads)], axis=0
            )
            scores = jnp.where(key_valid, contract(keys, queries, 1, 1), FLOOR)
            expo = jnp.exp(scores - jnp.max(scores, axis=0, keepdims=True))
            probs = expo * (1.0 / jnp.sum(expo, axis=0, keepdims=True))
            dprob = contract(values, cots, 1, 1)
            delta = jnp.sum(probs * dprob, axis=0, keepdims=True)
            probs_low = probs.astype(jnp.bfloat16)
            dscore_low = (probs * (dprob - delta)).astype(jnp.bfloat16)
            dvalue = contract(probs_low, cots, 1, 0)
            dkey = contract(dscore_low, queries, 1, 0)
            keys_turned = jnp.concatenate([turned[index, 0, lanes] for index in chosen], axis=1)
            values_turned = jnp.concatenate([turned[index, 1, lanes] for index in chosen], axis=1)
            attended = own_heads(contract(values_turned, probs_low, 1, 0))
            dquery = own_heads(contract(keys_turned, dscore_low, 1, 0)) * SCALE
            attended = jnp.where(live, attended.astype(jnp.bfloat16).T, none)
            out[seq_count + target, 0, target_rows, lanes] = dquery.astype(jnp.bfloat16).T
            out[seq_count + target, 1, target_rows, lanes] = attended
            for slot, (dev, here) in enumerate(places):
                part = slice(slot * BLK, (slot + 1) * BLK)
                key_grad[dev, here, lanes] += dkey[part]
                value_grad[dev, here, lanes] += dvalue[part]
        return carry

    lax.fori_loop(0, block_count, turn, 0, unroll=block_count <= 4)
    lax.fori_loop(0, block_count, step, 0, unroll=block_count <= 4)
    out[:seq_count, 0] = key_grad[...].astype(jnp.bfloat16)
    out[:seq_count, 1] = value_grad[...].astype(jnp.bfloat16)


def attend_cost(block_count, width):
    pairs = block_count * NLIST * BLK * BLK * width
    return pl.CostEstimate(
        flops=10 * pairs,
        bytes_accessed=16 * block_count * BLK * width,
        transcendentals=pairs // HDIM,
    )


def specs(count, space):
    return [pl.BlockSpec(memory_space=space)] * count


def in_hbm(*arrays):
    return [pltpu.with_memory_space_constraint(array, pltpu.HBM) for array in arrays]


def gathered_kernel(
    seq_count, lists, source_len, target_len, rows, out, key_grad, value_grad, turned
):
    def listed(block, slot):
        return lists[block, slot]

    attend_sample(
        seq_count, listed, source_len[0], target_len[0], rows, out, key_grad, value_grad, turned
    )


def by_all_to_all(first_rows, second_rows, alignment, diffusion_mask, source_length, target_length):
    seq_count = lax.axis_size("seq")
    parts = lax.axis_size("section") * seq_count
    rows_here = first_rows.shape[2]
    width = first_rows.shape[3]
    on_encoder = lax.axis_index("section") == 0
    keep = on_encoder | (diffusion_mask[0] == 1)
    second = jnp.where(keep[:, None], second_rows[0, 0], jnp.zeros_like(second_rows[0, 0]))
    held = jnp.stack([first_rows[0, 0], second])
    held = held.reshape(2, rows_here, parts, width // parts).transpose(2, 0, 1, 3)
    lists = lax.all_gather(alignment[0], "seq", axis=0, tiled=True)
    rows = lax.all_to_all(held, AXES, 0, 0, tiled=True)
    grads = pltpu.VMEM((seq_count, rows_here, width // parts), jnp.float32)
    turned = pltpu.VMEM((lists.shape[0], 2, width // parts, BLK), rows.dtype)
    grads = pl.pallas_call(
        functools.partial(gathered_kernel, seq_count),
        out_shape=jax.ShapeDtypeStruct(rows.shape, rows.dtype),
        in_specs=specs(3, pltpu.SMEM) + specs(1, pltpu.VMEM),
        out_specs=pl.BlockSpec(memory_space=pltpu.VMEM),
        scratch_shapes=[grads, grads, turned],
        compiler_params=pltpu.CompilerParams(vmem_limit_bytes=VMEM_LIMIT),
        cost_estimate=attend_cost(lists.shape[0], width // parts),
        name="attend_gathered",
    )(lists, source_length, target_length, rows)
    grads = lax.all_to_all(grads, AXES, 0, 0, tiled=True)
    grads = grads.transpose(1, 2, 0, 3).reshape(2, rows_here, width)
    return (grads[0][None, None], grads[1][None, None])


def device_index(seq_count):
    return lax.axis_index("section") * seq_count + lax.axis_index("seq")


DIAGONAL = (6, 7)
OWN, NEAR = (0,), (1,)
ACROSS = [(4,), (2,), (5,), (3,)]
REST = [OWN, NEAR, *ACROSS]
OUTGOING = [DIAGONAL, *REST]
INCOMING = [*OUTGOING, DIAGONAL[1:]]
TILES = 2
HALVED = [(5,)]
PACKED = [(group, 0) for group in REST if group not in HALVED]
PACKED += [(group, tile * LANES) for tile in range(TILES) for group in HALVED]
AFTER = {((5,), 0): (NEAR, 0), ((5,), LANES): ((4,), 0)}
EARLY = (0, 6)


def pack_kernel(seq_count, places, *refs):
    smalls, (first, second) = refs[:2], refs[2:4]
    outs, (lists, mask, small_sem, sem) = refs[4:-4], refs[-4:]
    me = device_index(seq_count)
    here = me % seq_count
    share = first.shape[3] // (2 * seq_count)
    copies, pieces = [], []
    for (group, start), out in zip(places, outs):
        for place, step in enumerate(group):
            slot = len(copies)
            lanes = pl.ds(pl.multiple_of((me ^ step) * share + start, LANES), out.shape[1])
            piece = out.at[pl.ds(place * 2 * BLK, 2 * BLK)]
            pair = [
                pltpu.make_async_copy(
                    source.at[0, 0, :, lanes], piece.at[pl.ds(half * BLK, BLK)], sem.at[half, slot]
                )
                for half, source in enumerate((first, second))
            ]
            for copy in pair:
                copy.start()
            copies.append(pair)
            pieces.append(piece)
    small_copies = [
        pltpu.make_async_copy(source, held, small_sem.at[slot])
        for slot, (source, held) in enumerate(zip(smalls, (lists, mask)))
    ]
    for copy in small_copies:
        copy.start()
    for copy in small_copies:
        copy.wait()
    keep = (mask[...] == 1) | (me < seq_count)
    keep = jnp.broadcast_to(jnp.where(keep, 1.0, 0.0), (BLK, BLK)).T.astype(jnp.bfloat16)
    base = here - WIN
    code = (lists[0, 0, 0] - base) * SPAN + lists[0, 0, 1] - base
    tail = jnp.full((TAIL, LANES), code, jnp.int32).astype(jnp.float32).astype(jnp.bfloat16)
    for out in outs:
        if out.shape[0] % (2 * BLK):
            out[2 * BLK :] = jnp.concatenate([tail] * (out.shape[1] // LANES), axis=1)
    for piece, pair in zip(pieces, copies):
        for copy in pair:
            copy.wait()
        piece[BLK:] = piece[BLK:] * jnp.concatenate([keep] * (piece.shape[1] // LANES), axis=1)


def attend_kernel(seq_count, turn, source_len, target_len, *refs):
    parts, rest = len(INCOMING), len(OUTGOING) - 1
    shares, before = refs[:parts], refs[parts : parts + (rest if turn else 0)]
    outs = refs[parts + len(before) : parts + len(before) + 1 + rest]
    rows, result, key_grad, value_grad, turned, lists = refs[parts + len(before) + 1 + rest :]
    me = device_index(seq_count)
    here = me % seq_count
    lanes = pl.ds(turn * LANES, LANES)
    for (step, *_), share in zip(INCOMING, shares):
        source = me ^ step
        here_lanes = lanes if share.shape[1] > LANES else pl.ds(0, LANES)
        rows[source, 0] = share[pl.ds(0, BLK), here_lanes]
        rows[source, 1] = share[pl.ds(BLK, BLK), here_lanes]
        if step < seq_count:
            tail = share[pl.ds(2 * BLK, TAIL), here_lanes].astype(jnp.float32)
            lists[here ^ step] = jnp.max(tail).astype(jnp.int32)

    def listed(block, slot):
        code = lists[block]
        return block - WIN + (code // SPAN if slot == 0 else code % SPAN)

    attend_sample(
        seq_count,
        listed,
        source_len[0],
        target_len[0],
        rows,
        result,
        key_grad,
        value_grad,
        turned,
    )
    diagonal, *others = outs
    for place, step in enumerate(DIAGONAL):
        for half in range(2):
            diagonal[pl.ds((2 * place + half) * BLK, BLK)] = result[me ^ step, half]
    for group, out in zip(REST, others):
        for half in range(2):
            out[pl.ds(half * BLK, BLK), lanes] = result[me ^ group[0], half]
    for done, out in zip(before, others):
        out[:, pl.ds(0, turn * LANES)] = done[...]


def unpack_kernel(seq_count, places, *refs):
    shares, (first, second, sem) = refs[: len(places)], refs[-3:]
    width = first.shape[3] // (2 * seq_count)
    me = device_index(seq_count)
    copies = []
    for slot, ((step, start), share) in enumerate(zip(places, shares)):
        lanes = pl.ds(pl.multiple_of((me ^ step) * width + start, LANES), share.shape[1])
        for half, result in enumerate((first, second)):
            copy = pltpu.make_async_copy(
                share.at[pl.ds(half * BLK, BLK)], result.at[0, 0, :, lanes], sem.at[half, slot]
            )
            copy.start()
            copies.append(copy)
    for copy in copies:
        copy.wait()


def permuted(share, step):
    return lax.ppermute(share, AXES, [(dev, dev ^ step) for dev in range(8)])


def coming_in(diagonal, held):
    diagonal = permuted(diagonal, DIAGONAL[0])
    moved = {}
    for place in PACKED:
        share = held[place]
        if place in AFTER:
            earlier = AFTER[place]
            share, moved[earlier] = lax.optimization_barrier((share, moved[earlier]))
        moved[place] = permuted(share, place[0][0]) if place[0] != OWN else share
    near = (NEAR, 0)
    diagonal, moved[near] = lax.optimization_barrier((diagonal, moved[near]))
    return diagonal, moved, permuted(diagonal[diagonal.shape[0] // 2 :], NEAR[0])


def going_out(diagonals, shares):
    held = dict(zip(REST, shares))
    diagonals = [permuted(share, DIAGONAL[0]) for share in diagonals]
    moved = {group: permuted(held[group], group[0]) for group in ACROSS}
    held[NEAR], diagonals[0] = lax.optimization_barrier((held[NEAR], diagonals[0]))
    moved[NEAR] = permuted(held[NEAR], NEAR[0])
    handed_on = [permuted(share[share.shape[0] // 2 :], NEAR[0]) for share in diagonals]
    return diagonals, [held[OWN], moved[NEAR], *(moved[group] for group in ACROSS)], handed_on


def by_pairs(first_rows, second_rows, alignment, diffusion_mask, source_length, target_length):
    seq_count = lax.axis_size("seq")
    parts = 2 * seq_count
    width = first_rows.shape[3]
    share = width // parts
    kind = first_rows.dtype
    params = pltpu.CompilerParams(vmem_limit_bytes=VMEM_LIMIT)
    sems = pltpu.SemaphoreType.DMA((2, parts))

    def pack(places, lists):
        return pl.pallas_call(
            functools.partial(pack_kernel, seq_count, places),
            out_shape=[
                jax.ShapeDtypeStruct(
                    (
                        len(group) * 2 * BLK + (TAIL if group[0] < seq_count else 0),
                        LANES if group in HALVED else share,
                    ),
                    kind,
                )
                for group, _ in places
            ],
            in_specs=specs(4, pltpu.HBM),
            out_specs=specs(len(places), pltpu.VMEM),
            scratch_shapes=[
                pltpu.SMEM(alignment.shape, jnp.int32),
                pltpu.VMEM(diffusion_mask.shape, jnp.int32),
                pltpu.SemaphoreType.DMA((2,)),
                sems,
            ],
            compiler_params=params,
            name="pack",
        )(*in_hbm(lists, diffusion_mask, first_rows, second_rows))

    (diagonal,) = pack([(DIAGONAL, 0)], alignment)
    lists, diagonal = lax.optimization_barrier((alignment, diagonal))
    diagonal, moved, handed_on = coming_in(diagonal, dict(zip(PACKED, pack(PACKED, lists))))
    rows = pltpu.VMEM((parts, 2, BLK, LANES), kind)
    grads = pltpu.VMEM((seq_count, BLK, LANES), jnp.float32)
    turned = pltpu.VMEM((seq_count, 2, LANES, BLK), kind)

    def attend(turn, *before):
        lanes = (turn + 1) * LANES
        coming = [diagonal]
        coming += [moved[group, turn * LANES if group in HALVED else 0] for group in REST]
        coming += [handed_on]
        return pl.pallas_call(
            functools.partial(attend_kernel, seq_count, turn),
            out_shape=[
                jax.ShapeDtypeStruct((4 * BLK, LANES), kind),
                *([jax.ShapeDtypeStruct((2 * BLK, lanes), kind)] * len(REST)),
            ],
            in_specs=specs(2, pltpu.SMEM) + specs(len(coming) + len(before), pltpu.VMEM),
            out_specs=specs(1 + len(REST), pltpu.VMEM),
            scratch_shapes=[rows, rows, grads, grads, turned, pltpu.SMEM((seq_count,), jnp.int32)],
            compiler_params=params,
            cost_estimate=attend_cost(seq_count, LANES),
            name="attend",
        )(source_length, target_length, *coming, *before)

    diagonals, shares = [], []
    for turn in range(TILES):
        result, *shares = attend(turn, *shares)
        diagonals.append(result)
    diagonals, shares, handed_on = going_out(diagonals, shares)
    arrived = dict(zip([(group[0], 0) for group in REST], shares))
    for step, tiles in zip(DIAGONAL, (diagonals, handed_on)):
        arrived.update({(step, tile * LANES): share for tile, share in enumerate(tiles)})
    out_shape = jax.ShapeDtypeStruct((1, 1, BLK, width), kind)

    def unpack(places, *begun):
        count = len(places)
        return pl.pallas_call(
            functools.partial(unpack_kernel, seq_count, places),
            out_shape=[out_shape, out_shape],
            in_specs=specs(count, pltpu.VMEM) + specs(len(begun), pltpu.HBM),
            out_specs=specs(2, pltpu.HBM),
            input_output_aliases={count + slot: slot for slot in range(len(begun))},
            scratch_shapes=[pltpu.SemaphoreType.DMA((2, count))],
            compiler_params=params,
            name="unpack",
        )(*(arrived[place] for place in places), *begun)

    early = [place for place in arrived if place[0] in EARLY]
    return unpack([place for place in arrived if place not in early], *unpack(early))


def on_device(first_rows, second_rows, alignment, diffusion_mask, source_length, target_length):
    seq_count = lax.axis_size("seq")
    parts = lax.axis_size("section") * seq_count
    paired = (
        (parts, seq_count) == (8, 4)
        and first_rows.shape[2] == BLK
        and first_rows.shape[3] == parts * TILES * LANES
    )
    work = by_pairs if paired else by_all_to_all
    return tuple(
        work(first_rows, second_rows, alignment, diffusion_mask, source_length, target_length)
    )


def solution(mesh):
    placed = (
        P("section", "sample", "seq", None),
        P("section", "sample", "seq", None),
        P("sample", "seq", None),
        P("sample", "seq"),
        P("sample"),
        P("sample"),
    )
    return jax.shard_map(
        on_device,
        mesh=mesh,
        in_specs=placed,
        out_specs=(P("section", "sample", "seq", None), P("section", "sample", "seq", None)),
        check_vma=False,
    )
```

```python
import functools

import jax
import jax.numpy as jnp
from jax import lax
from jax.experimental import pallas as pl
from jax.experimental.pallas import tpu as pltpu
from jax.sharding import PartitionSpec as P

HDIM = 64
BLK = 128
NLIST = 2
WIN = 1
SPAN = 2 * WIN + 1
LANES = 128
TAIL = 16
SCALE = HDIM ** (-0.5)
FLOOR = -1e30
VMEM_LIMIT = 32 * 1024 * 1024
AXES = ("section", "seq")


def contract(left, right, left_dim, right_dim):
    return lax.dot_general(
        left, right, (((left_dim,), (right_dim,)), ((), ())), preferred_element_type=jnp.float32
    )


def attend_sample(
    seq_count, listed, source_len, target_len, rows, out, key_grad, value_grad, turned
):
    per_device = rows.shape[2] // BLK
    block_count = seq_count * per_device
    width = rows.shape[3]
    tile = min(width, LANES)
    heads = tile // HDIM
    key_grad[...] = jnp.zeros_like(key_grad)
    value_grad[...] = jnp.zeros_like(value_grad)
    inside = lax.broadcasted_iota(jnp.int32, (BLK, 1), 0)
    lane_head = lax.broadcasted_iota(jnp.int32, (BLK, tile), 1) // HDIM

    def place(block):
        if per_device == 1:
            return block, pl.ds(0, BLK)
        return block // per_device, pl.ds((block % per_device) * BLK, BLK)

    def own_heads(turned_result):
        return jnp.concatenate(
            [
                turned_result[head * HDIM : (head + 1) * HDIM, head * BLK : (head + 1) * BLK]
                for head in range(heads)
            ],
            axis=0,
        )

    def turn(block, carry):
        dev, here = place(block)
        for first in range(0, width, tile):
            for half in range(2):
                turned[block, half, pl.ds(first, tile)] = rows[
                    dev, half, here, pl.ds(first, tile)
                ].T
        return carry

    def step(block, carry):
        chosen = [listed(block, slot) for slot in range(NLIST)]
        places = [place(index) for index in chosen]
        target, target_rows = place(block)
        key_valid = jnp.concatenate(
            [index * BLK + inside < source_len for index in chosen], axis=0
        )
        live = block * BLK + inside < target_len
        for first in range(0, width, tile):
            lanes = pl.ds(first, tile)
            keys = jnp.concatenate([rows[dev, 0, here, lanes] for dev, here in places], axis=0)
            values = jnp.concatenate([rows[dev, 1, here, lanes] for dev, here in places], axis=0)
            queries = rows[seq_count + target, 0, target_rows, lanes] * jnp.bfloat16(SCALE)
            cots = rows[seq_count + target, 1, target_rows, lanes]
            none = jnp.zeros_like(queries)
            cots = jnp.where(live, cots, none)
            queries = jnp.concatenate(
                [jnp.where(lane_head == head, queries, none) for head in range(heads)], axis=0
            )
            cots = jnp.concatenate(
                [jnp.where(lane_head == head, cots, none) for head in range(heads)], axis=0
            )
            scores = jnp.where(key_valid, contract(keys, queries, 1, 1), FLOOR)
            expo = jnp.exp(scores - jnp.max(scores, axis=0, keepdims=True))
            probs = expo * (1.0 / jnp.sum(expo, axis=0, keepdims=True))
            dprob = contract(values, cots, 1, 1)
            delta = jnp.sum(probs * dprob, axis=0, keepdims=True)
            probs_low = probs.astype(jnp.bfloat16)
            dscore_low = (probs * (dprob - delta)).astype(jnp.bfloat16)
            dvalue = contract(probs_low, cots, 1, 0)
            dkey = contract(dscore_low, queries, 1, 0)
            keys_turned = jnp.concatenate([turned[index, 0, lanes] for index in chosen], axis=1)
            values_turned = jnp.concatenate([turned[index, 1, lanes] for index in chosen], axis=1)
            attended = own_heads(contract(values_turned, probs_low, 1, 0))
            dquery = own_heads(contract(keys_turned, dscore_low, 1, 0)) * SCALE
            attended = jnp.where(live, attended.astype(jnp.bfloat16).T, none)
            out[seq_count + target, 0, target_rows, lanes] = dquery.astype(jnp.bfloat16).T
            out[seq_count + target, 1, target_rows, lanes] = attended
            for slot, (dev, here) in enumerate(places):
                part = slice(slot * BLK, (slot + 1) * BLK)
                key_grad[dev, here, lanes] += dkey[part]
                value_grad[dev, here, lanes] += dvalue[part]
        return carry

    lax.fori_loop(0, block_count, turn, 0, unroll=block_count <= 4)
    lax.fori_loop(0, block_count, step, 0, unroll=block_count <= 4)
    out[:seq_count, 0] = key_grad[...].astype(jnp.bfloat16)
    out[:seq_count, 1] = value_grad[...].astype(jnp.bfloat16)


def attend_cost(block_count, width):
    pairs = block_count * NLIST * BLK * BLK * width
    return pl.CostEstimate(
        flops=10 * pairs,
        bytes_accessed=16 * block_count * BLK * width,
        transcendentals=pairs // HDIM,
    )


def specs(count, space):
    return [pl.BlockSpec(memory_space=space)] * count


def in_hbm(*arrays):
    return [pltpu.with_memory_space_constraint(array, pltpu.HBM) for array in arrays]


def gathered_kernel(
    seq_count, lists, source_len, target_len, rows, out, key_grad, value_grad, turned
):
    def listed(block, slot):
        return lists[block, slot]

    attend_sample(
        seq_count, listed, source_len[0], target_len[0], rows, out, key_grad, value_grad, turned
    )


def by_all_to_all(first_rows, second_rows, alignment, diffusion_mask, source_length, target_length):
    seq_count = lax.axis_size("seq")
    parts = lax.axis_size("section") * seq_count
    rows_here = first_rows.shape[2]
    width = first_rows.shape[3]
    on_encoder = lax.axis_index("section") == 0
    keep = on_encoder | (diffusion_mask[0] == 1)
    second = jnp.where(keep[:, None], second_rows[0, 0], jnp.zeros_like(second_rows[0, 0]))
    held = jnp.stack([first_rows[0, 0], second])
    held = held.reshape(2, rows_here, parts, width // parts).transpose(2, 0, 1, 3)
    lists = lax.all_gather(alignment[0], "seq", axis=0, tiled=True)
    rows = lax.all_to_all(held, AXES, 0, 0, tiled=True)
    grads = pltpu.VMEM((seq_count, rows_here, width // parts), jnp.float32)
    turned = pltpu.VMEM((lists.shape[0], 2, width // parts, BLK), rows.dtype)
    grads = pl.pallas_call(
        functools.partial(gathered_kernel, seq_count),
        out_shape=jax.ShapeDtypeStruct(rows.shape, rows.dtype),
        in_specs=specs(3, pltpu.SMEM) + specs(1, pltpu.VMEM),
        out_specs=pl.BlockSpec(memory_space=pltpu.VMEM),
        scratch_shapes=[grads, grads, turned],
        compiler_params=pltpu.CompilerParams(vmem_limit_bytes=VMEM_LIMIT),
        cost_estimate=attend_cost(lists.shape[0], width // parts),
        name="attend_gathered",
    )(lists, source_length, target_length, rows)
    grads = lax.all_to_all(grads, AXES, 0, 0, tiled=True)
    grads = grads.transpose(1, 2, 0, 3).reshape(2, rows_here, width)
    return (grads[0][None, None], grads[1][None, None])


def device_index(seq_count):
    return lax.axis_index("section") * seq_count + lax.axis_index("seq")


DIAGONAL = (6, 7)
OWN, NEAR = (0,), (1,)
ACROSS = [(2,), (4,), (5,), (3,)]
REST = [OWN, NEAR, *ACROSS]
OUTGOING = [DIAGONAL, *REST]
INCOMING = [*OUTGOING, DIAGONAL[1:]]
TILES = 2


def pack_kernel(seq_count, steps, *refs):
    smalls, (first, second) = refs[:2], refs[2:4]
    outs, (lists, mask, small_sem, sem) = refs[4:-4], refs[-4:]
    me = device_index(seq_count)
    here = me % seq_count
    share = outs[0].shape[1]
    copies, pieces = [], []
    for group, out in zip(steps, outs):
        for place, step in enumerate(group):
            slot = len(copies)
            lanes = pl.ds(pl.multiple_of((me ^ step) * share, LANES), share)
            piece = out.at[pl.ds(place * 2 * BLK, 2 * BLK)]
            pair = [
                pltpu.make_async_copy(
                    source.at[0, 0, :, lanes], piece.at[pl.ds(half * BLK, BLK)], sem.at[half, slot]
                )
                for half, source in enumerate((first, second))
            ]
            for copy in pair:
                copy.start()
            copies.append(pair)
            pieces.append(piece)
    small_copies = [
        pltpu.make_async_copy(source, held, small_sem.at[slot])
        for slot, (source, held) in enumerate(zip(smalls, (lists, mask)))
    ]
    for copy in small_copies:
        copy.start()
    for copy in small_copies:
        copy.wait()
    keep = (mask[...] == 1) | (me < seq_count)
    keep = jnp.broadcast_to(jnp.where(keep, 1.0, 0.0), (BLK, BLK)).T.astype(jnp.bfloat16)
    keep = jnp.concatenate([keep] * (share // LANES), axis=1)
    base = here - WIN
    code = (lists[0, 0, 0] - base) * SPAN + lists[0, 0, 1] - base
    tail = jnp.full((TAIL, share), code, jnp.int32).astype(jnp.float32).astype(jnp.bfloat16)
    for out in outs:
        if out.shape[0] % (2 * BLK):
            out[2 * BLK :] = tail
    for piece, pair in zip(pieces, copies):
        for copy in pair:
            copy.wait()
        piece[BLK:] = piece[BLK:] * keep


def attend_kernel(seq_count, turn, source_len, target_len, *refs):
    parts, rest = len(INCOMING), len(OUTGOING) - 1
    shares, before = refs[:parts], refs[parts : parts + (rest if turn else 0)]
    outs = refs[parts + len(before) : parts + len(before) + 1 + rest]
    rows, result, key_grad, value_grad, turned, lists = refs[parts + len(before) + 1 + rest :]
    me = device_index(seq_count)
    here = me % seq_count
    lanes = pl.ds(turn * LANES, LANES)
    for (step, *_), share in zip(INCOMING, shares):
        source = me ^ step
        rows[source, 0] = share[pl.ds(0, BLK), lanes]
        rows[source, 1] = share[pl.ds(BLK, BLK), lanes]
        if step < seq_count:
            tail = share[pl.ds(2 * BLK, TAIL), lanes].astype(jnp.float32)
            lists[here ^ step] = jnp.max(tail).astype(jnp.int32)

    def listed(block, slot):
        code = lists[block]
        return block - WIN + (code // SPAN if slot == 0 else code % SPAN)

    attend_sample(
        seq_count,
        listed,
        source_len[0],
        target_len[0],
        rows,
        result,
        key_grad,
        value_grad,
        turned,
    )
    diagonal, *others = outs
    for place, step in enumerate(DIAGONAL):
        for half in range(2):
            diagonal[pl.ds((2 * place + half) * BLK, BLK)] = result[me ^ step, half]
    for group, out in zip(REST, others):
        for half in range(2):
            out[pl.ds(half * BLK, BLK), lanes] = result[me ^ group[0], half]
    for done, out in zip(before, others):
        out[:, pl.ds(0, turn * LANES)] = done[...]


def unpack_kernel(seq_count, *refs):
    diagonals, handed_on, shares = refs[:TILES], refs[TILES : 2 * TILES], refs[2 * TILES : -3]
    first, second, sem = refs[-3:]
    width = first.shape[3] // (2 * seq_count)
    me = device_index(seq_count)
    pieces = [
        (step, tile * LANES, share.at[pl.ds(0, 2 * BLK)])
        for step, arrived in zip(DIAGONAL, (diagonals, handed_on))
        for tile, share in enumerate(arrived)
    ]
    pieces += [(step, 0, share) for (step,), share in zip(REST, shares)]
    copies = []
    for slot, (step, start, share) in enumerate(pieces):
        lanes = pl.ds(pl.multiple_of((me ^ step) * width + start, LANES), share.shape[1])
        for half, result in enumerate((first, second)):
            copy = pltpu.make_async_copy(
                share.at[pl.ds(half * BLK, BLK)], result.at[0, 0, :, lanes], sem.at[half, slot]
            )
            copy.start()
            copies.append(copy)
    for copy in copies:
        copy.wait()


def permuted(share, step):
    return lax.ppermute(share, AXES, [(dev, dev ^ step) for dev in range(8)])


def swapped(diagonals, shares):
    held = dict(zip(REST, shares))
    diagonals = [permuted(share, DIAGONAL[0]) for share in diagonals]
    moved = {group: permuted(held[group], group[0]) for group in ACROSS}
    if len(diagonals) > 1:
        held[NEAR], diagonals[0] = lax.optimization_barrier((held[NEAR], diagonals[0]))
    moved[NEAR] = permuted(held[NEAR], NEAR[0])
    if len(diagonals) == 1:
        diagonals[0], moved[NEAR] = lax.optimization_barrier((diagonals[0], moved[NEAR]))
    handed_on = [permuted(share[share.shape[0] // 2 :], NEAR[0]) for share in diagonals]
    return diagonals, [held[OWN], moved[NEAR], *(moved[group] for group in ACROSS)], handed_on


def by_pairs(first_rows, second_rows, alignment, diffusion_mask, source_length, target_length):
    seq_count = lax.axis_size("seq")
    parts = 2 * seq_count
    width = first_rows.shape[3]
    share = width // parts
    kind = first_rows.dtype
    params = pltpu.CompilerParams(vmem_limit_bytes=VMEM_LIMIT)
    sems = pltpu.SemaphoreType.DMA((2, parts))

    def sizes(groups, tail):
        return [
            jax.ShapeDtypeStruct(
                (len(group) * 2 * BLK + (tail if group[0] < seq_count else 0), share), kind
            )
            for group in groups
        ]

    def pack(groups, lists):
        return pl.pallas_call(
            functools.partial(pack_kernel, seq_count, groups),
            out_shape=sizes(groups, TAIL),
            in_specs=specs(4, pltpu.HBM),
            out_specs=specs(len(groups), pltpu.VMEM),
            scratch_shapes=[
                pltpu.SMEM(alignment.shape, jnp.int32),
                pltpu.VMEM(diffusion_mask.shape, jnp.int32),
                pltpu.SemaphoreType.DMA((2,)),
                sems,
            ],
            compiler_params=params,
            name="pack",
        )(*in_hbm(lists, diffusion_mask, first_rows, second_rows))

    (diagonal,) = pack([DIAGONAL], alignment)
    lists, diagonal = lax.optimization_barrier((alignment, diagonal))
    diagonals, shares, handed_on = swapped([diagonal], pack(REST, lists))
    coming = [*diagonals, *shares, *handed_on]
    rows = pltpu.VMEM((parts, 2, BLK, LANES), kind)
    grads = pltpu.VMEM((seq_count, BLK, LANES), jnp.float32)
    turned = pltpu.VMEM((seq_count, 2, LANES, BLK), kind)

    def attend(turn, *before):
        lanes = (turn + 1) * LANES
        return pl.pallas_call(
            functools.partial(attend_kernel, seq_count, turn),
            out_shape=[
                jax.ShapeDtypeStruct((4 * BLK, LANES), kind),
                *([jax.ShapeDtypeStruct((2 * BLK, lanes), kind)] * len(REST)),
            ],
            in_specs=specs(2, pltpu.SMEM) + specs(len(coming) + len(before), pltpu.VMEM),
            out_specs=specs(1 + len(REST), pltpu.VMEM),
            scratch_shapes=[rows, rows, grads, grads, turned, pltpu.SMEM((seq_count,), jnp.int32)],
            compiler_params=params,
            cost_estimate=attend_cost(seq_count, LANES),
            name="attend",
        )(source_length, target_length, *coming, *before)

    diagonals, shares = [], []
    for turn in range(TILES):
        diagonal, *shares = attend(turn, *shares)
        diagonals.append(diagonal)
    diagonals, shares, handed_on = swapped(diagonals, shares)
    out_shape = jax.ShapeDtypeStruct((1, 1, BLK, width), kind)
    return pl.pallas_call(
        functools.partial(unpack_kernel, seq_count),
        out_shape=[out_shape, out_shape],
        in_specs=specs(2 * TILES + len(REST), pltpu.VMEM),
        out_specs=specs(2, pltpu.HBM),
        scratch_shapes=[pltpu.SemaphoreType.DMA((2, parts + 2 * TILES))],
        compiler_params=params,
        name="unpack",
    )(*diagonals, *handed_on, *shares)


def on_device(first_rows, second_rows, alignment, diffusion_mask, source_length, target_length):
    seq_count = lax.axis_size("seq")
    parts = lax.axis_size("section") * seq_count
    paired = (
        (parts, seq_count) == (8, 4)
        and first_rows.shape[2] == BLK
        and first_rows.shape[3] == parts * TILES * LANES
    )
    work = by_pairs if paired else by_all_to_all
    return tuple(
        work(first_rows, second_rows, alignment, diffusion_mask, source_length, target_length)
    )


def solution(mesh):
    placed = (
        P("section", "sample", "seq", None),
        P("section", "sample", "seq", None),
        P("sample", "seq", None),
        P("sample", "seq"),
        P("sample"),
        P("sample"),
    )
    return jax.shard_map(
        on_device,
        mesh=mesh,
        in_specs=placed,
        out_specs=(P("section", "sample", "seq", None), P("section", "sample", "seq", None)),
        check_vma=False,
    )
```

```python
import functools

import jax
import jax.numpy as jnp
from jax import lax
from jax.experimental import pallas as pl
from jax.experimental.pallas import tpu as pltpu
from jax.sharding import PartitionSpec as P

HDIM = 64
BLK = 128
NLIST = 2
WIN = 1
SPAN = 2 * WIN + 1
LANES = 128
TAIL = 16
SCALE = HDIM ** (-0.5)
FLOOR = -1e30
VMEM_LIMIT = 32 * 1024 * 1024
AXES = ("section", "seq")


def contract(left, right, left_dim, right_dim):
    return lax.dot_general(
        left, right, (((left_dim,), (right_dim,)), ((), ())), preferred_element_type=jnp.float32
    )


def attend_sample(
    seq_count, listed, source_len, target_len, rows, out, key_grad, value_grad, turned
):
    per_device = rows.shape[2] // BLK
    block_count = seq_count * per_device
    width = rows.shape[3]
    tile = min(width, LANES)
    heads = tile // HDIM
    key_grad[...] = jnp.zeros_like(key_grad)
    value_grad[...] = jnp.zeros_like(value_grad)
    inside = lax.broadcasted_iota(jnp.int32, (BLK, 1), 0)
    lane_head = lax.broadcasted_iota(jnp.int32, (BLK, tile), 1) // HDIM

    def place(block):
        if per_device == 1:
            return block, pl.ds(0, BLK)
        return block // per_device, pl.ds((block % per_device) * BLK, BLK)

    def own_heads(turned_result):
        return jnp.concatenate(
            [
                turned_result[head * HDIM : (head + 1) * HDIM, head * BLK : (head + 1) * BLK]
                for head in range(heads)
            ],
            axis=0,
        )

    def turn(block, carry):
        dev, here = place(block)
        for first in range(0, width, tile):
            for half in range(2):
                turned[block, half, pl.ds(first, tile)] = rows[
                    dev, half, here, pl.ds(first, tile)
                ].T
        return carry

    def step(block, carry):
        chosen = [listed(block, slot) for slot in range(NLIST)]
        places = [place(index) for index in chosen]
        target, target_rows = place(block)
        key_valid = jnp.concatenate(
            [index * BLK + inside < source_len for index in chosen], axis=0
        )
        live = block * BLK + inside < target_len
        for first in range(0, width, tile):
            lanes = pl.ds(first, tile)
            keys = jnp.concatenate([rows[dev, 0, here, lanes] for dev, here in places], axis=0)
            values = jnp.concatenate([rows[dev, 1, here, lanes] for dev, here in places], axis=0)
            queries = rows[seq_count + target, 0, target_rows, lanes] * jnp.bfloat16(SCALE)
            cots = rows[seq_count + target, 1, target_rows, lanes]
            none = jnp.zeros_like(queries)
            cots = jnp.where(live, cots, none)
            queries = jnp.concatenate(
                [jnp.where(lane_head == head, queries, none) for head in range(heads)], axis=0
            )
            cots = jnp.concatenate(
                [jnp.where(lane_head == head, cots, none) for head in range(heads)], axis=0
            )
            scores = jnp.where(key_valid, contract(keys, queries, 1, 1), FLOOR)
            expo = jnp.exp(scores - jnp.max(scores, axis=0, keepdims=True))
            probs = expo * (1.0 / jnp.sum(expo, axis=0, keepdims=True))
            dprob = contract(values, cots, 1, 1)
            delta = jnp.sum(probs * dprob, axis=0, keepdims=True)
            probs_low = probs.astype(jnp.bfloat16)
            dscore_low = (probs * (dprob - delta)).astype(jnp.bfloat16)
            dvalue = contract(probs_low, cots, 1, 0)
            dkey = contract(dscore_low, queries, 1, 0)
            keys_turned = jnp.concatenate([turned[index, 0, lanes] for index in chosen], axis=1)
            values_turned = jnp.concatenate([turned[index, 1, lanes] for index in chosen], axis=1)
            attended = own_heads(contract(values_turned, probs_low, 1, 0))
            dquery = own_heads(contract(keys_turned, dscore_low, 1, 0)) * SCALE
            attended = jnp.where(live, attended.astype(jnp.bfloat16).T, none)
            out[seq_count + target, 0, target_rows, lanes] = dquery.astype(jnp.bfloat16).T
            out[seq_count + target, 1, target_rows, lanes] = attended
            for slot, (dev, here) in enumerate(places):
                part = slice(slot * BLK, (slot + 1) * BLK)
                key_grad[dev, here, lanes] += dkey[part]
                value_grad[dev, here, lanes] += dvalue[part]
        return carry

    lax.fori_loop(0, block_count, turn, 0, unroll=block_count <= 4)
    lax.fori_loop(0, block_count, step, 0, unroll=block_count <= 4)
    out[:seq_count, 0] = key_grad[...].astype(jnp.bfloat16)
    out[:seq_count, 1] = value_grad[...].astype(jnp.bfloat16)


def attend_cost(block_count, width):
    pairs = block_count * NLIST * BLK * BLK * width
    return pl.CostEstimate(
        flops=10 * pairs,
        bytes_accessed=16 * block_count * BLK * width,
        transcendentals=pairs // HDIM,
    )


def specs(count, space):
    return [pl.BlockSpec(memory_space=space)] * count


def in_hbm(*arrays):
    return [pltpu.with_memory_space_constraint(array, pltpu.HBM) for array in arrays]


def gathered_kernel(
    seq_count, lists, source_len, target_len, rows, out, key_grad, value_grad, turned
):
    def listed(block, slot):
        return lists[block, slot]

    attend_sample(
        seq_count, listed, source_len[0], target_len[0], rows, out, key_grad, value_grad, turned
    )


def by_all_to_all(first_rows, second_rows, alignment, diffusion_mask, source_length, target_length):
    seq_count = lax.axis_size("seq")
    parts = lax.axis_size("section") * seq_count
    rows_here = first_rows.shape[2]
    width = first_rows.shape[3]
    on_encoder = lax.axis_index("section") == 0
    keep = on_encoder | (diffusion_mask[0] == 1)
    second = jnp.where(keep[:, None], second_rows[0, 0], jnp.zeros_like(second_rows[0, 0]))
    held = jnp.stack([first_rows[0, 0], second])
    held = held.reshape(2, rows_here, parts, width // parts).transpose(2, 0, 1, 3)
    lists = lax.all_gather(alignment[0], "seq", axis=0, tiled=True)
    rows = lax.all_to_all(held, AXES, 0, 0, tiled=True)
    grads = pltpu.VMEM((seq_count, rows_here, width // parts), jnp.float32)
    turned = pltpu.VMEM((lists.shape[0], 2, width // parts, BLK), rows.dtype)
    grads = pl.pallas_call(
        functools.partial(gathered_kernel, seq_count),
        out_shape=jax.ShapeDtypeStruct(rows.shape, rows.dtype),
        in_specs=specs(3, pltpu.SMEM) + specs(1, pltpu.VMEM),
        out_specs=pl.BlockSpec(memory_space=pltpu.VMEM),
        scratch_shapes=[grads, grads, turned],
        compiler_params=pltpu.CompilerParams(vmem_limit_bytes=VMEM_LIMIT),
        cost_estimate=attend_cost(lists.shape[0], width // parts),
        name="attend_gathered",
    )(lists, source_length, target_length, rows)
    grads = lax.all_to_all(grads, AXES, 0, 0, tiled=True)
    grads = grads.transpose(1, 2, 0, 3).reshape(2, rows_here, width)
    return (grads[0][None, None], grads[1][None, None])


def device_index(seq_count):
    return lax.axis_index("section") * seq_count + lax.axis_index("seq")


DIAGONAL = (6, 7)
OWN, NEAR = (0,), (1,)
ACROSS = [(4,), (2,), (5,), (3,)]
REST = [OWN, NEAR, *ACROSS]
OUTGOING = [DIAGONAL, *REST]
INCOMING = [*OUTGOING, DIAGONAL[1:]]
TILES = 2


def pack_kernel(seq_count, steps, *refs):
    smalls, (first, second) = refs[:2], refs[2:4]
    outs, (lists, mask, small_sem, sem) = refs[4:-4], refs[-4:]
    me = device_index(seq_count)
    here = me % seq_count
    share = outs[0].shape[1]
    copies, pieces = [], []
    for group, out in zip(steps, outs):
        for place, step in enumerate(group):
            slot = len(copies)
            lanes = pl.ds(pl.multiple_of((me ^ step) * share, LANES), share)
            piece = out.at[pl.ds(place * 2 * BLK, 2 * BLK)]
            pair = [
                pltpu.make_async_copy(
                    source.at[0, 0, :, lanes], piece.at[pl.ds(half * BLK, BLK)], sem.at[half, slot]
                )
                for half, source in enumerate((first, second))
            ]
            for copy in pair:
                copy.start()
            copies.append(pair)
            pieces.append(piece)
    small_copies = [
        pltpu.make_async_copy(source, held, small_sem.at[slot])
        for slot, (source, held) in enumerate(zip(smalls, (lists, mask)))
    ]
    for copy in small_copies:
        copy.start()
    for copy in small_copies:
        copy.wait()
    keep = (mask[...] == 1) | (me < seq_count)
    keep = jnp.broadcast_to(jnp.where(keep, 1.0, 0.0), (BLK, BLK)).T.astype(jnp.bfloat16)
    keep = jnp.concatenate([keep] * (share // LANES), axis=1)
    base = here - WIN
    code = (lists[0, 0, 0] - base) * SPAN + lists[0, 0, 1] - base
    tail = jnp.full((TAIL, share), code, jnp.int32).astype(jnp.float32).astype(jnp.bfloat16)
    for out in outs:
        if out.shape[0] % (2 * BLK):
            out[2 * BLK :] = tail
    for piece, pair in zip(pieces, copies):
        for copy in pair:
            copy.wait()
        piece[BLK:] = piece[BLK:] * keep


def attend_kernel(seq_count, turn, source_len, target_len, *refs):
    parts, rest = len(INCOMING), len(OUTGOING) - 1
    shares, before = refs[:parts], refs[parts : parts + (rest if turn else 0)]
    outs = refs[parts + len(before) : parts + len(before) + 1 + rest]
    rows, result, key_grad, value_grad, turned, lists = refs[parts + len(before) + 1 + rest :]
    me = device_index(seq_count)
    here = me % seq_count
    lanes = pl.ds(turn * LANES, LANES)
    for (step, *_), share in zip(INCOMING, shares):
        source = me ^ step
        rows[source, 0] = share[pl.ds(0, BLK), lanes]
        rows[source, 1] = share[pl.ds(BLK, BLK), lanes]
        if step < seq_count:
            tail = share[pl.ds(2 * BLK, TAIL), lanes].astype(jnp.float32)
            lists[here ^ step] = jnp.max(tail).astype(jnp.int32)

    def listed(block, slot):
        code = lists[block]
        return block - WIN + (code // SPAN if slot == 0 else code % SPAN)

    attend_sample(
        seq_count,
        listed,
        source_len[0],
        target_len[0],
        rows,
        result,
        key_grad,
        value_grad,
        turned,
    )
    diagonal, *others = outs
    for place, step in enumerate(DIAGONAL):
        for half in range(2):
            diagonal[pl.ds((2 * place + half) * BLK, BLK)] = result[me ^ step, half]
    for group, out in zip(REST, others):
        for half in range(2):
            out[pl.ds(half * BLK, BLK), lanes] = result[me ^ group[0], half]
    for done, out in zip(before, others):
        out[:, pl.ds(0, turn * LANES)] = done[...]


def unpack_kernel(seq_count, *refs):
    diagonals, shares = refs[:TILES], refs[TILES:-3]
    first, second, sem = refs[-3:]
    width = first.shape[3] // (2 * seq_count)
    me = device_index(seq_count)
    pieces = [
        (DIAGONAL[0], tile * LANES, share.at[pl.ds(0, 2 * BLK)])
        for tile, share in enumerate(diagonals)
    ]
    pieces += [(group[0], 0, share) for group, share in zip([DIAGONAL[1:], *REST], shares)]
    copies = []
    for slot, (step, start, share) in enumerate(pieces):
        lanes = pl.ds(pl.multiple_of((me ^ step) * width + start, LANES), share.shape[1])
        for half, result in enumerate((first, second)):
            copy = pltpu.make_async_copy(
                share.at[pl.ds(half * BLK, BLK)], result.at[0, 0, :, lanes], sem.at[half, slot]
            )
            copy.start()
            copies.append(copy)
    for copy in copies:
        copy.wait()


def permuted(share, step):
    return lax.ppermute(share, AXES, [(dev, dev ^ step) for dev in range(8)])


def swapped(diagonals, shares):
    held = dict(zip(REST, shares))
    diagonals = [permuted(share, DIAGONAL[0]) for share in diagonals]
    moved = {group: permuted(held[group], group[0]) for group in ACROSS}
    if len(diagonals) > 1:
        held[NEAR], diagonals[0] = lax.optimization_barrier((held[NEAR], diagonals[0]))
    moved[NEAR] = permuted(held[NEAR], NEAR[0])
    if len(diagonals) == 1:
        diagonals[0], moved[NEAR] = lax.optimization_barrier((diagonals[0], moved[NEAR]))
    handed_on = [share[share.shape[0] // 2 :] for share in diagonals]
    handed_on = permuted(jnp.concatenate(handed_on, axis=1), NEAR[0])
    return diagonals, [held[OWN], moved[NEAR], *(moved[group] for group in ACROSS)], handed_on


def by_pairs(first_rows, second_rows, alignment, diffusion_mask, source_length, target_length):
    seq_count = lax.axis_size("seq")
    parts = 2 * seq_count
    width = first_rows.shape[3]
    share = width // parts
    kind = first_rows.dtype
    params = pltpu.CompilerParams(vmem_limit_bytes=VMEM_LIMIT)
    sems = pltpu.SemaphoreType.DMA((2, parts))

    def sizes(groups, tail):
        return [
            jax.ShapeDtypeStruct(
                (len(group) * 2 * BLK + (tail if group[0] < seq_count else 0), share), kind
            )
            for group in groups
        ]

    def pack(groups, lists):
        return pl.pallas_call(
            functools.partial(pack_kernel, seq_count, groups),
            out_shape=sizes(groups, TAIL),
            in_specs=specs(4, pltpu.HBM),
            out_specs=specs(len(groups), pltpu.VMEM),
            scratch_shapes=[
                pltpu.SMEM(alignment.shape, jnp.int32),
                pltpu.VMEM(diffusion_mask.shape, jnp.int32),
                pltpu.SemaphoreType.DMA((2,)),
                sems,
            ],
            compiler_params=params,
            name="pack",
        )(*in_hbm(lists, diffusion_mask, first_rows, second_rows))

    (diagonal,) = pack([DIAGONAL], alignment)
    lists, diagonal = lax.optimization_barrier((alignment, diagonal))
    diagonals, shares, handed_on = swapped([diagonal], pack(REST, lists))
    coming = [*diagonals, *shares, handed_on]
    rows = pltpu.VMEM((parts, 2, BLK, LANES), kind)
    grads = pltpu.VMEM((seq_count, BLK, LANES), jnp.float32)
    turned = pltpu.VMEM((seq_count, 2, LANES, BLK), kind)

    def attend(turn, *before):
        lanes = (turn + 1) * LANES
        return pl.pallas_call(
            functools.partial(attend_kernel, seq_count, turn),
            out_shape=[
                jax.ShapeDtypeStruct((4 * BLK, LANES), kind),
                *([jax.ShapeDtypeStruct((2 * BLK, lanes), kind)] * len(REST)),
            ],
            in_specs=specs(2, pltpu.SMEM) + specs(len(coming) + len(before), pltpu.VMEM),
            out_specs=specs(1 + len(REST), pltpu.VMEM),
            scratch_shapes=[rows, rows, grads, grads, turned, pltpu.SMEM((seq_count,), jnp.int32)],
            compiler_params=params,
            cost_estimate=attend_cost(seq_count, LANES),
            name="attend",
        )(source_length, target_length, *coming, *before)

    diagonals, shares = [], []
    for turn in range(TILES):
        diagonal, *shares = attend(turn, *shares)
        diagonals.append(diagonal)
    diagonals, shares, handed_on = swapped(diagonals, shares)
    out_shape = jax.ShapeDtypeStruct((1, 1, BLK, width), kind)
    return pl.pallas_call(
        functools.partial(unpack_kernel, seq_count),
        out_shape=[out_shape, out_shape],
        in_specs=specs(TILES + 1 + len(REST), pltpu.VMEM),
        out_specs=specs(2, pltpu.HBM),
        scratch_shapes=[pltpu.SemaphoreType.DMA((2, parts + 2 * TILES))],
        compiler_params=params,
        name="unpack",
    )(*diagonals, handed_on, *shares)


def on_device(first_rows, second_rows, alignment, diffusion_mask, source_length, target_length):
    seq_count = lax.axis_size("seq")
    parts = lax.axis_size("section") * seq_count
    paired = (
        (parts, seq_count) == (8, 4)
        and first_rows.shape[2] == BLK
        and first_rows.shape[3] == parts * TILES * LANES
    )
    work = by_pairs if paired else by_all_to_all
    return tuple(
        work(first_rows, second_rows, alignment, diffusion_mask, source_length, target_length)
    )


def solution(mesh):
    placed = (
        P("section", "sample", "seq", None),
        P("section", "sample", "seq", None),
        P("sample", "seq", None),
        P("sample", "seq"),
        P("sample"),
        P("sample"),
    )
    return jax.shard_map(
        on_device,
        mesh=mesh,
        in_specs=placed,
        out_specs=(P("section", "sample", "seq", None), P("section", "sample", "seq", None)),
        check_vma=False,
    )
```

```python
import functools

import jax
import jax.numpy as jnp
from jax import lax
from jax.experimental import pallas as pl
from jax.experimental.pallas import tpu as pltpu
from jax.sharding import PartitionSpec as P

HDIM = 64
BLK = 128
NLIST = 2
WIN = 1
SPAN = 2 * WIN + 1
LANES = 128
TAIL = 16
SCALE = HDIM ** (-0.5)
FLOOR = -1e30
VMEM_LIMIT = 32 * 1024 * 1024
AXES = ("section", "seq")


def contract(left, right, left_dim, right_dim):
    return lax.dot_general(
        left, right, (((left_dim,), (right_dim,)), ((), ())), preferred_element_type=jnp.float32
    )


def attend_sample(
    seq_count, listed, source_len, target_len, rows, out, key_grad, value_grad, turned
):
    per_device = rows.shape[2] // BLK
    block_count = seq_count * per_device
    width = rows.shape[3]
    tile = min(width, LANES)
    heads = tile // HDIM
    key_grad[...] = jnp.zeros_like(key_grad)
    value_grad[...] = jnp.zeros_like(value_grad)
    inside = lax.broadcasted_iota(jnp.int32, (BLK, 1), 0)
    lane_head = lax.broadcasted_iota(jnp.int32, (BLK, tile), 1) // HDIM

    def place(block):
        if per_device == 1:
            return block, pl.ds(0, BLK)
        return block // per_device, pl.ds((block % per_device) * BLK, BLK)

    def own_heads(turned_result):
        return jnp.concatenate(
            [
                turned_result[head * HDIM : (head + 1) * HDIM, head * BLK : (head + 1) * BLK]
                for head in range(heads)
            ],
            axis=0,
        )

    def turn(block, carry):
        dev, here = place(block)
        for first in range(0, width, tile):
            for half in range(2):
                turned[block, half, pl.ds(first, tile)] = rows[
                    dev, half, here, pl.ds(first, tile)
                ].T
        return carry

    def step(block, carry):
        chosen = [listed(block, slot) for slot in range(NLIST)]
        places = [place(index) for index in chosen]
        target, target_rows = place(block)
        key_valid = jnp.concatenate(
            [index * BLK + inside < source_len for index in chosen], axis=0
        )
        live = block * BLK + inside < target_len
        for first in range(0, width, tile):
            lanes = pl.ds(first, tile)
            keys = jnp.concatenate([rows[dev, 0, here, lanes] for dev, here in places], axis=0)
            values = jnp.concatenate([rows[dev, 1, here, lanes] for dev, here in places], axis=0)
            queries = rows[seq_count + target, 0, target_rows, lanes] * jnp.bfloat16(SCALE)
            cots = rows[seq_count + target, 1, target_rows, lanes]
            none = jnp.zeros_like(queries)
            cots = jnp.where(live, cots, none)
            queries = jnp.concatenate(
                [jnp.where(lane_head == head, queries, none) for head in range(heads)], axis=0
            )
            cots = jnp.concatenate(
                [jnp.where(lane_head == head, cots, none) for head in range(heads)], axis=0
            )
            scores = jnp.where(key_valid, contract(keys, queries, 1, 1), FLOOR)
            expo = jnp.exp(scores - jnp.max(scores, axis=0, keepdims=True))
            probs = expo * (1.0 / jnp.sum(expo, axis=0, keepdims=True))
            dprob = contract(values, cots, 1, 1)
            delta = jnp.sum(probs * dprob, axis=0, keepdims=True)
            probs_low = probs.astype(jnp.bfloat16)
            dscore_low = (probs * (dprob - delta)).astype(jnp.bfloat16)
            dvalue = contract(probs_low, cots, 1, 0)
            dkey = contract(dscore_low, queries, 1, 0)
            keys_turned = jnp.concatenate([turned[index, 0, lanes] for index in chosen], axis=1)
            values_turned = jnp.concatenate([turned[index, 1, lanes] for index in chosen], axis=1)
            attended = own_heads(contract(values_turned, probs_low, 1, 0))
            dquery = own_heads(contract(keys_turned, dscore_low, 1, 0)) * SCALE
            attended = jnp.where(live, attended.astype(jnp.bfloat16).T, none)
            out[seq_count + target, 0, target_rows, lanes] = dquery.astype(jnp.bfloat16).T
            out[seq_count + target, 1, target_rows, lanes] = attended
            for slot, (dev, here) in enumerate(places):
                part = slice(slot * BLK, (slot + 1) * BLK)
                key_grad[dev, here, lanes] += dkey[part]
                value_grad[dev, here, lanes] += dvalue[part]
        return carry

    lax.fori_loop(0, block_count, turn, 0, unroll=block_count <= 4)
    lax.fori_loop(0, block_count, step, 0, unroll=block_count <= 4)
    out[:seq_count, 0] = key_grad[...].astype(jnp.bfloat16)
    out[:seq_count, 1] = value_grad[...].astype(jnp.bfloat16)


def attend_cost(block_count, width):
    pairs = block_count * NLIST * BLK * BLK * width
    return pl.CostEstimate(
        flops=10 * pairs,
        bytes_accessed=16 * block_count * BLK * width,
        transcendentals=pairs // HDIM,
    )


def specs(count, space):
    return [pl.BlockSpec(memory_space=space)] * count


def in_hbm(*arrays):
    return [pltpu.with_memory_space_constraint(array, pltpu.HBM) for array in arrays]


def gathered_kernel(
    seq_count, lists, source_len, target_len, rows, out, key_grad, value_grad, turned
):
    def listed(block, slot):
        return lists[block, slot]

    attend_sample(
        seq_count, listed, source_len[0], target_len[0], rows, out, key_grad, value_grad, turned
    )


def by_all_to_all(first_rows, second_rows, alignment, diffusion_mask, source_length, target_length):
    seq_count = lax.axis_size("seq")
    parts = lax.axis_size("section") * seq_count
    rows_here = first_rows.shape[2]
    width = first_rows.shape[3]
    on_encoder = lax.axis_index("section") == 0
    keep = on_encoder | (diffusion_mask[0] == 1)
    second = jnp.where(keep[:, None], second_rows[0, 0], jnp.zeros_like(second_rows[0, 0]))
    held = jnp.stack([first_rows[0, 0], second])
    held = held.reshape(2, rows_here, parts, width // parts).transpose(2, 0, 1, 3)
    lists = lax.all_gather(alignment[0], "seq", axis=0, tiled=True)
    rows = lax.all_to_all(held, AXES, 0, 0, tiled=True)
    grads = pltpu.VMEM((seq_count, rows_here, width // parts), jnp.float32)
    turned = pltpu.VMEM((lists.shape[0], 2, width // parts, BLK), rows.dtype)
    grads = pl.pallas_call(
        functools.partial(gathered_kernel, seq_count),
        out_shape=jax.ShapeDtypeStruct(rows.shape, rows.dtype),
        in_specs=specs(3, pltpu.SMEM) + specs(1, pltpu.VMEM),
        out_specs=pl.BlockSpec(memory_space=pltpu.VMEM),
        scratch_shapes=[grads, grads, turned],
        compiler_params=pltpu.CompilerParams(vmem_limit_bytes=VMEM_LIMIT),
        cost_estimate=attend_cost(lists.shape[0], width // parts),
        name="attend_gathered",
    )(lists, source_length, target_length, rows)
    grads = lax.all_to_all(grads, AXES, 0, 0, tiled=True)
    grads = grads.transpose(1, 2, 0, 3).reshape(2, rows_here, width)
    return (grads[0][None, None], grads[1][None, None])


def device_index(seq_count):
    return lax.axis_index("section") * seq_count + lax.axis_index("seq")


DIAGONAL = (6, 7)
OWN, NEAR = (0,), (1,)
ACROSS = [(4,), (2,), (3,), (5,)]
REST = [OWN, NEAR, *ACROSS]
OUTGOING = [DIAGONAL, *REST]
INCOMING = [*OUTGOING, DIAGONAL[1:]]
TILES = 2


def pack_kernel(seq_count, steps, *refs):
    smalls, (first, second) = refs[:2], refs[2:4]
    outs, (lists, mask, small_sem, sem) = refs[4:-4], refs[-4:]
    me = device_index(seq_count)
    here = me % seq_count
    share = outs[0].shape[1]
    copies, pieces = [], []
    for group, out in zip(steps, outs):
        for place, step in enumerate(group):
            slot = len(copies)
            lanes = pl.ds(pl.multiple_of((me ^ step) * share, LANES), share)
            piece = out.at[pl.ds(place * 2 * BLK, 2 * BLK)]
            pair = [
                pltpu.make_async_copy(
                    source.at[0, 0, :, lanes], piece.at[pl.ds(half * BLK, BLK)], sem.at[half, slot]
                )
                for half, source in enumerate((first, second))
            ]
            for copy in pair:
                copy.start()
            copies.append(pair)
            pieces.append(piece)
    small_copies = [
        pltpu.make_async_copy(source, held, small_sem.at[slot])
        for slot, (source, held) in enumerate(zip(smalls, (lists, mask)))
    ]
    for copy in small_copies:
        copy.start()
    for copy in small_copies:
        copy.wait()
    keep = (mask[...] == 1) | (me < seq_count)
    keep = jnp.broadcast_to(jnp.where(keep, 1.0, 0.0), (BLK, BLK)).T.astype(jnp.bfloat16)
    keep = jnp.concatenate([keep] * (share // LANES), axis=1)
    base = here - WIN
    code = (lists[0, 0, 0] - base) * SPAN + lists[0, 0, 1] - base
    tail = jnp.full((TAIL, share), code, jnp.int32).astype(jnp.float32).astype(jnp.bfloat16)
    for out in outs:
        if out.shape[0] % (2 * BLK):
            out[2 * BLK :] = tail
    for piece, pair in zip(pieces, copies):
        for copy in pair:
            copy.wait()
        piece[BLK:] = piece[BLK:] * keep


def attend_kernel(seq_count, turn, source_len, target_len, *refs):
    parts, rest = len(INCOMING), len(OUTGOING) - 1
    shares, before = refs[:parts], refs[parts : parts + (rest if turn else 0)]
    outs = refs[parts + len(before) : parts + len(before) + 1 + rest]
    rows, result, key_grad, value_grad, turned, lists = refs[parts + len(before) + 1 + rest :]
    me = device_index(seq_count)
    here = me % seq_count
    lanes = pl.ds(turn * LANES, LANES)
    for (step, *_), share in zip(INCOMING, shares):
        source = me ^ step
        rows[source, 0] = share[pl.ds(0, BLK), lanes]
        rows[source, 1] = share[pl.ds(BLK, BLK), lanes]
        if step < seq_count:
            tail = share[pl.ds(2 * BLK, TAIL), lanes].astype(jnp.float32)
            lists[here ^ step] = jnp.max(tail).astype(jnp.int32)

    def listed(block, slot):
        code = lists[block]
        return block - WIN + (code // SPAN if slot == 0 else code % SPAN)

    attend_sample(
        seq_count,
        listed,
        source_len[0],
        target_len[0],
        rows,
        result,
        key_grad,
        value_grad,
        turned,
    )
    diagonal, *others = outs
    for place, step in enumerate(DIAGONAL):
        for half in range(2):
            diagonal[pl.ds((2 * place + half) * BLK, BLK)] = result[me ^ step, half]
    for group, out in zip(REST, others):
        for half in range(2):
            out[pl.ds(half * BLK, BLK), lanes] = result[me ^ group[0], half]
    for done, out in zip(before, others):
        out[:, pl.ds(0, turn * LANES)] = done[...]


def unpack_kernel(seq_count, *refs):
    diagonals, shares = refs[:TILES], refs[TILES:-3]
    first, second, sem = refs[-3:]
    width = first.shape[3] // (2 * seq_count)
    me = device_index(seq_count)
    pieces = [
        (DIAGONAL[0], tile * LANES, share.at[pl.ds(0, 2 * BLK)])
        for tile, share in enumerate(diagonals)
    ]
    pieces += [(group[0], 0, share) for group, share in zip([DIAGONAL[1:], *REST], shares)]
    copies = []
    for slot, (step, start, share) in enumerate(pieces):
        lanes = pl.ds(pl.multiple_of((me ^ step) * width + start, LANES), share.shape[1])
        for half, result in enumerate((first, second)):
            copy = pltpu.make_async_copy(
                share.at[pl.ds(half * BLK, BLK)], result.at[0, 0, :, lanes], sem.at[half, slot]
            )
            copy.start()
            copies.append(copy)
    for copy in copies:
        copy.wait()


def permuted(share, step):
    return lax.ppermute(share, AXES, [(dev, dev ^ step) for dev in range(8)])


def swapped(diagonals, shares):
    held = dict(zip(REST, shares))
    diagonals = [permuted(share, DIAGONAL[0]) for share in diagonals]
    moved = {group: permuted(held[group], group[0]) for group in ACROSS}
    if len(diagonals) > 1:
        held[NEAR], diagonals[0] = lax.optimization_barrier((held[NEAR], diagonals[0]))
    moved[NEAR] = permuted(held[NEAR], NEAR[0])
    if len(diagonals) == 1:
        diagonals[0], moved[NEAR] = lax.optimization_barrier((diagonals[0], moved[NEAR]))
    handed_on = [share[share.shape[0] // 2 :] for share in diagonals]
    handed_on = permuted(jnp.concatenate(handed_on, axis=1), NEAR[0])
    return diagonals, [held[OWN], moved[NEAR], *(moved[group] for group in ACROSS)], handed_on


def by_pairs(first_rows, second_rows, alignment, diffusion_mask, source_length, target_length):
    seq_count = lax.axis_size("seq")
    parts = 2 * seq_count
    width = first_rows.shape[3]
    share = width // parts
    kind = first_rows.dtype
    params = pltpu.CompilerParams(vmem_limit_bytes=VMEM_LIMIT)
    sems = pltpu.SemaphoreType.DMA((2, parts))

    def sizes(groups, tail):
        return [
            jax.ShapeDtypeStruct(
                (len(group) * 2 * BLK + (tail if group[0] < seq_count else 0), share), kind
            )
            for group in groups
        ]

    def pack(groups, lists):
        return pl.pallas_call(
            functools.partial(pack_kernel, seq_count, groups),
            out_shape=sizes(groups, TAIL),
            in_specs=specs(4, pltpu.HBM),
            out_specs=specs(len(groups), pltpu.VMEM),
            scratch_shapes=[
                pltpu.SMEM(alignment.shape, jnp.int32),
                pltpu.VMEM(diffusion_mask.shape, jnp.int32),
                pltpu.SemaphoreType.DMA((2,)),
                sems,
            ],
            compiler_params=params,
            name="pack",
        )(*in_hbm(lists, diffusion_mask, first_rows, second_rows))

    (diagonal,) = pack([DIAGONAL], alignment)
    lists, diagonal = lax.optimization_barrier((alignment, diagonal))
    diagonals, shares, handed_on = swapped([diagonal], pack(REST, lists))
    coming = [*diagonals, *shares, handed_on]
    rows = pltpu.VMEM((parts, 2, BLK, LANES), kind)
    grads = pltpu.VMEM((seq_count, BLK, LANES), jnp.float32)
    turned = pltpu.VMEM((seq_count, 2, LANES, BLK), kind)

    def attend(turn, *before):
        lanes = (turn + 1) * LANES
        return pl.pallas_call(
            functools.partial(attend_kernel, seq_count, turn),
            out_shape=[
                jax.ShapeDtypeStruct((4 * BLK, LANES), kind),
                *([jax.ShapeDtypeStruct((2 * BLK, lanes), kind)] * len(REST)),
            ],
            in_specs=specs(2, pltpu.SMEM) + specs(len(coming) + len(before), pltpu.VMEM),
            out_specs=specs(1 + len(REST), pltpu.VMEM),
            scratch_shapes=[rows, rows, grads, grads, turned, pltpu.SMEM((seq_count,), jnp.int32)],
            compiler_params=params,
            cost_estimate=attend_cost(seq_count, LANES),
            name="attend",
        )(source_length, target_length, *coming, *before)

    diagonals, shares = [], []
    for turn in range(TILES):
        diagonal, *shares = attend(turn, *shares)
        diagonals.append(diagonal)
    diagonals, shares, handed_on = swapped(diagonals, shares)
    out_shape = jax.ShapeDtypeStruct((1, 1, BLK, width), kind)
    return pl.pallas_call(
        functools.partial(unpack_kernel, seq_count),
        out_shape=[out_shape, out_shape],
        in_specs=specs(TILES + 1 + len(REST), pltpu.VMEM),
        out_specs=specs(2, pltpu.HBM),
        scratch_shapes=[pltpu.SemaphoreType.DMA((2, parts + 2 * TILES))],
        compiler_params=params,
        name="unpack",
    )(*diagonals, handed_on, *shares)


def on_device(first_rows, second_rows, alignment, diffusion_mask, source_length, target_length):
    seq_count = lax.axis_size("seq")
    parts = lax.axis_size("section") * seq_count
    paired = (
        (parts, seq_count) == (8, 4)
        and first_rows.shape[2] == BLK
        and first_rows.shape[3] == parts * TILES * LANES
    )
    work = by_pairs if paired else by_all_to_all
    return tuple(
        work(first_rows, second_rows, alignment, diffusion_mask, source_length, target_length)
    )


def solution(mesh):
    placed = (
        P("section", "sample", "seq", None),
        P("section", "sample", "seq", None),
        P("sample", "seq", None),
        P("sample", "seq"),
        P("sample"),
        P("sample"),
    )
    return jax.shard_map(
        on_device,
        mesh=mesh,
        in_specs=placed,
        out_specs=(P("section", "sample", "seq", None), P("section", "sample", "seq", None)),
        check_vma=False,
    )
```
